32 devices in a mesh: group: 2 (over y), shot: 4 (over z), line: 2 (over x), tm: 2 (over core).
Axes of the slice: x: 2, y: 2, z: 4, core: 2. Of those that a mesh axis runs over, the one named last changes fastest.
Arguments:
- initial_guess: bfloat16 [8, 256, 1024], P(('group', 'shot'), 'line', 'tm'), parts along dimension 0
- measured_mixtures: bfloat16 [4, 256, 1024], P('group', 'line'), parts along dimension 0
- launch_lags: int32 [8], P('group'), parts along dimension 0, may hold values from 0 to 127, as said below
- source_launch_order: int32 [8], P('group'), parts along dimension 0, may hold values from 0 to 3, each once
- station_portion_tallies: int32 [16], P('group'), parts along dimension 0, may hold values from 1 to 32, 128 in all
- source_entry_kernel: bfloat16 [4, 3, 64], replicated, may hold values from -1.75 to 1.75
- source_spaced_kernel: bfloat16 [3, 64, 64], replicated, may hold values from -0.4375 to 0.4375
- source_exit_kernel: bfloat16 [4, 64], replicated, may hold values from -0.5 to 0.5
- source_inner_offsets: float32 [2, 64], replicated, may hold values from -3 to 3
- station_entry_kernel: bfloat16 [4, 3, 64], replicated, may hold values from -1.75 to 1.75
- station_spaced_kernel: bfloat16 [3, 64, 64], replicated, may hold values from -0.4375 to 0.4375
- station_exit_kernel: bfloat16 [4, 64], replicated, may hold values from -0.5 to 0.5
- station_inner_offsets: float32 [2, 64], replicated, may hold values from -3 to 3
- learned_pace_factors: float32 [2], replicated, may hold values from 0.3 to 0.8
Outputs:
- deblended: bfloat16 [8, 256, 1024], P(('group', 'shot'), 'line', 'tm'), parts along dimension 0
The draws below stay inside these ranges and needn't reach their ends.
There are 2 independent parts, one for each index of `group`. The reference program is written for one: setup_inputs(seed, part) draws one part's arguments, and reference() takes and returns one part's arrays. A program takes and returns all parts, laid end to end along the dimension named above; an argument that names none is the same for every part. Nothing has to cross between parts.
Inputs may be any that keep to these rules, and one draw needn't show every extreme that they name: `launch_lags`: 0 and 127 both occur. `source_launch_order`: each shot once. `station_portion_tallies`: the counts sum to 128 and the largest equals 32.
All inputs are finite; a program needn't handle non-finite values.
Results may differ from the reference program's by a relative error of at most 0.013.
Values may be sent and summed in bfloat16 or wider, within the bound.
No kernel may reach another device: no remote copies, remote signals or barrier semaphores. Data moves between devices by JAX's collectives and lax.ppermute only.
A program may use at most 64 MiB of HBM per device.

```python
import math
import jax
import jax.numpy as jnp
import numpy as np
from jax import lax

LINES = 16
RPL = 16
NT = 1024
FEAT = 64
DMAX = 128
ITERS = 2
TILE_SOURCES = 4
NG = 2
RB = 128
NP = 8
RCAP = 32
N_LINE = 2


def receiver_scales(key):
    sub_key = jax.random.fold_in(key, 11)
    return jnp.exp(jax.random.uniform(sub_key, (LINES * RPL,), jnp.float32, math.log(0.3), math.log(3.0)))


def time_decay():
    fraction = jnp.arange(NT, dtype=jnp.float32) / NT
    return jnp.exp(-math.log(3.0) * fraction)


def draw_initial_guess(key, part):
    rscale = receiver_scales(key)
    shape_full = (TILE_SOURCES, LINES * RPL, NT)
    sscale = jnp.exp(jax.random.uniform(jax.random.fold_in(key, 12), (TILE_SOURCES,), jnp.float32, math.log(0.5), math.log(2.0)))
    noise = jax.random.normal(jax.random.fold_in(key, 13), shape_full, jnp.float32)
    values = noise * sscale[:, None, None] * rscale[None, :, None] * time_decay()[None, None, :]
    return values.astype(jnp.bfloat16)


def draw_measured_mixtures(key, part):
    rscale = receiver_scales(key)
    shape_full = (NG, LINES * RPL, NT)
    noise = 1.4 * jax.random.normal(jax.random.fold_in(key, 15), shape_full, jnp.float32)
    values = noise * rscale[None, :, None] * time_decay()[None, None, :]
    return values.astype(jnp.bfloat16)


def draw_launch_lags(key, part):
    base = jax.random.randint(jax.random.fold_in(key, 21), (TILE_SOURCES,), 0, DMAX)
    lowest = jax.random.randint(jax.random.fold_in(key, 22), (), 0, TILE_SOURCES)
    highest = (lowest + 1 + jax.random.randint(jax.random.fold_in(key, 23), (), 0, TILE_SOURCES - 1)) % TILE_SOURCES
    return base.at[lowest].set(0).at[highest].set(DMAX - 1).astype(jnp.int32)


def split_up(amount, total, bound, skew):
    weights = [(1 << 20) // math.isqrt(grade ** skew) + 1 for grade in range(2, amount + 1)]
    spare, given = total - bound - (amount - 1), [1] * (amount - 1)
    while spare > 0:
        free = [i for i in range(amount - 1) if given[i] < bound]
        pool, budget = sum([weights[i] for i in free]), spare
        for i in free:
            more = min(bound - given[i], max(1, budget * weights[i] // pool), spare)
            given[i] = given[i] + more
            spare = spare - more
    return np.array([bound] + given)


def ragged(own_key, number_of, total, limit, lean):
    if number_of == 2:
        one = jax.random.randint(own_key, (), max(1, total - limit), min(limit, total - 1) + 1)
        return jnp.stack([one, total - one])
    sizes = jnp.asarray(split_up(number_of, total, limit, lean), jnp.int32)
    pairs = (number_of - 1) // 2
    giver, sink = sizes[1:1 + 2 * pairs:2], sizes[2:2 + 2 * pairs:2]
    room = jnp.minimum(giver - 1, limit - sink)
    shifted = jax.random.randint(jax.random.fold_in(own_key, 1), (pairs,), 0, 1 << 20) % (room + 1)
    sizes = sizes.at[1:1 + 2 * pairs:2].set(giver - shifted).at[2:2 + 2 * pairs:2].set(sink + shifted)
    return sizes[jax.random.permutation(jax.random.fold_in(own_key, 2), number_of)]


def centred(key, extent, deviation, limit, kind=jnp.bfloat16):
    entries = jax.random.normal(key, extent, jnp.float32) * deviation
    return jnp.minimum(jnp.maximum(entries, -limit), limit).astype(kind)


def setup_inputs(seed: int = 0, part: int = 0) -> dict:
    splits = jax.random.split(jax.random.key(seed), 15)
    part_splits = jax.random.split(jax.random.fold_in(splits[14], part), 15)
    return {
        "initial_guess": draw_initial_guess(jax.random.fold_in(jax.random.fold_in(splits[14], part), 71), part),
        "measured_mixtures": draw_measured_mixtures(jax.random.fold_in(jax.random.fold_in(splits[14], part), 71), part),
        "launch_lags": draw_launch_lags(jax.random.fold_in(jax.random.fold_in(splits[14], part), 71), part),
        "source_launch_order": jax.random.permutation(part_splits[3], TILE_SOURCES).astype(jnp.int32),
        "station_portion_tallies": ragged(part_splits[4], NP, RB, RCAP, 2).astype(jnp.int32),
        "source_entry_kernel": centred(splits[5], (4, 3, FEAT), 12 ** -0.5, 1.75),
        "source_spaced_kernel": centred(splits[6], (3, FEAT, FEAT), (3 * FEAT) ** -0.5, 0.4375),
        "source_exit_kernel": centred(splits[7], (4, FEAT), (2 * FEAT) ** -0.5, 0.5),
        "source_inner_offsets": centred(splits[8], (2, FEAT), 0.5, 3.0, jnp.float32),
        "station_entry_kernel": centred(splits[9], (4, 3, FEAT), 12 ** -0.5, 1.75),
        "station_spaced_kernel": centred(splits[10], (3, FEAT, FEAT), (3 * FEAT) ** -0.5, 0.4375),
        "station_exit_kernel": centred(splits[11], (4, FEAT), (2 * FEAT) ** -0.5, 0.5),
        "station_inner_offsets": centred(splits[12], (2, FEAT), 0.5, 3.0, jnp.float32),
        "learned_pace_factors": jnp.clip(jnp.exp(jax.random.uniform(splits[13], (ITERS,), jnp.float32, math.log(0.3), math.log(0.8))), 0.3, 0.8),
    }


MARGIN = 7
EPSILON = 1e-05

def network(padded, first_sample, full_len, weight_in, weight_mid, weight_out, bias_pair):
    batch = padded.shape[0]
    sample_extent = padded.shape[2] - 2 * MARGIN
    half_len = sample_extent // 2
    count_one = half_len + 6
    count_two = half_len + 2
    wide_in = padded.astype(jnp.float32)
    total_sum = jnp.zeros((batch, weight_in.shape[2], count_one), jnp.float32)
    for tap_index in range(4):
        tap_slice = wide_in[:, :, tap_index:tap_index + 2 * count_one - 1:2]
        total_sum = total_sum + jnp.einsum('bcv,cf->bfv', tap_slice, weight_in[tap_index].astype(jnp.float32), precision=lax.Precision.HIGHEST)
    where_one = first_sample // 2 - 3 + jnp.arange(count_one)
    keep_one = (where_one >= 0) & (where_one < full_len // 2)
    layer_one = jnp.where(keep_one, jax.nn.relu(total_sum + bias_pair[0][None, :, None]), 0.0).astype(jnp.bfloat16)
    wide_one = layer_one.astype(jnp.float32)
    total_two = jnp.zeros((batch, weight_mid.shape[2], count_two), jnp.float32)
    for tap_index in range(3):
        total_two = total_two + jnp.einsum('bgw,gf->bfw', wide_one[:, :, 2 * tap_index:2 * tap_index + count_two], weight_mid[tap_index].astype(jnp.float32), precision=lax.Precision.HIGHEST)
    where_two = first_sample // 2 - 1 + jnp.arange(count_two)
    keep_two = (where_two >= 0) & (where_two < full_len // 2)
    layer_two = jnp.where(keep_two, jax.nn.relu(total_two + bias_pair[1][None, :, None]), 0.0).astype(jnp.bfloat16)
    projected = jnp.einsum('bgw,kg->bkw', layer_two.astype(jnp.float32), weight_out.astype(jnp.float32), precision=lax.Precision.HIGHEST)
    even_part = projected[:, 1, 1:half_len + 1] + projected[:, 3, 0:half_len]
    odd_part = projected[:, 0, 2:half_len + 2] + projected[:, 2, 1:half_len + 1]
    return jnp.stack([even_part, odd_part], axis=2).reshape(batch, sample_extent)

def sections(station_portion_tallies, block_size):
    offsets = jnp.cumsum(station_portion_tallies) - station_portion_tallies
    places = jnp.arange(block_size, dtype=jnp.int32)
    owner_of = lax.optimization_barrier(jnp.sum((offsets[None, :] <= places[:, None]).astype(jnp.int32), axis=1)) - 1
    return (offsets, owner_of)

def receiver_pass(sorting_choice, rms_scale, weights):
    normed = (sorting_choice.astype(jnp.float32) / rms_scale[:, None, None]).astype(jnp.bfloat16)

    def one_receiver(trace_set):
        shot_count = trace_set.shape[0]
        edged_set = jnp.pad(trace_set, ((1, 1), (0, 0)))
        stacked = jnp.stack([edged_set[channel:channel + shot_count] for channel in range(3)], axis=1)
        inputs = jnp.pad(stacked, ((0, 0), (0, 0), (MARGIN, MARGIN)))
        return network(inputs, 0, trace_set.shape[1], *weights)
    shaped = lax.map(one_receiver, normed)
    return (sorting_choice.astype(jnp.float32) + rms_scale[:, None, None] * shaped).astype(jnp.bfloat16)

def mixture_leftover(sorting_choice, measured_mixtures_here, source_launch_order, launch_lags, correction_pace):
    channel_total, shot_count, sample_extent = sorting_choice.shape
    mixture_batches = measured_mixtures_here.shape[1]
    sources_within_mixture = shot_count // mixture_batches
    widened = jnp.pad(sorting_choice.astype(jnp.float32), ((0, 0), (0, 0), (DMAX, 0)))

    def fire_shot(column, delay_at):
        return lax.dynamic_slice_in_dim(column, (DMAX - delay_at).astype(jnp.int32), sample_extent, axis=1)
    launched_source_collection = jax.vmap(fire_shot, in_axes=(1, 0), out_axes=1)(widened, launch_lags)
    recording_mismatch = jnp.take(launched_source_collection, source_launch_order, axis=1).reshape(channel_total, mixture_batches, sources_within_mixture, sample_extent).sum(axis=2) - measured_mixtures_here.astype(jnp.float32)
    place_labels = jnp.arange(shot_count, dtype=jnp.int32)
    source_location = lax.optimization_barrier(jnp.sum(jnp.where(source_launch_order[None, :] == place_labels[:, None], place_labels[None, :], 0), axis=1)).astype(jnp.int32)
    group_of = source_location // sources_within_mixture
    late_pad = jnp.pad(recording_mismatch, ((0, 0), (0, 0), (0, DMAX)))

    def spread(group_at, delay_at):
        group_row = jnp.take(late_pad, group_at, axis=1)
        return lax.dynamic_slice_in_dim(group_row, delay_at.astype(jnp.int32), sample_extent, axis=1)
    pulled = jax.vmap(spread, in_axes=(0, 0), out_axes=1)(group_of, launch_lags)
    return (sorting_choice.astype(jnp.float32) - correction_pace * pulled).astype(jnp.bfloat16)

def reference(initial_guess, measured_mixtures, launch_lags, source_launch_order, station_portion_tallies, source_entry_kernel, source_spaced_kernel, source_exit_kernel, source_inner_offsets, station_entry_kernel, station_spaced_kernel, station_exit_kernel, station_inner_offsets, learned_pace_factors):
    shot_count, recv_all, full_len = initial_guess.shape
    block_size = recv_all // N_LINE
    offsets, owner_of = sections(station_portion_tallies, block_size)
    shot_weights = (source_entry_kernel, source_spaced_kernel, source_exit_kernel, source_inner_offsets)
    receiver_weights = (station_entry_kernel, station_spaced_kernel, station_exit_kernel, station_inner_offsets)
    measured_mixtures_here = jnp.transpose(measured_mixtures, (1, 0, 2))
    ballot = (owner_of[:, None] == jnp.arange(station_portion_tallies.shape[0], dtype=jnp.int32)[None, :]).astype(jnp.float32)

    def shot_network(shot_traces):
        line_grid = shot_traces.reshape(LINES, RPL, full_len)
        edged_set = jnp.pad(line_grid, ((1, 1), (0, 0), (0, 0)))
        stacked = jnp.stack([edged_set[channel:channel + LINES] for channel in range(3)], axis=2)
        inputs = jnp.pad(stacked.reshape(recv_all, 3, full_len), ((0, 0), (0, 0), (MARGIN, MARGIN)))
        correction = network(inputs, 0, full_len, *shot_weights)
        return (shot_traces.astype(jnp.float32) + correction).astype(jnp.bfloat16)
    current = initial_guess
    for unrolled_round_ordinal in range(ITERS):
        after_shot = lax.map(shot_network, current)
        sorting_choice = jnp.transpose(after_shot, (1, 0, 2))
        energy = lax.optimization_barrier(jnp.sum(jnp.square(sorting_choice.astype(jnp.float32)), axis=(1, 2)))
        blocks = energy.reshape(N_LINE, block_size)
        section_sum = jnp.dot(blocks, ballot, precision=lax.Precision.HIGHEST)
        denominator = (jnp.take(station_portion_tallies, owner_of) * (shot_count * full_len)).astype(jnp.float32)
        mean_power = jnp.take(section_sum, owner_of, axis=1) / denominator[None, :]
        rms_scale = jnp.sqrt(mean_power.reshape(recv_all) + EPSILON)
        sorting_choice = receiver_pass(sorting_choice, rms_scale, receiver_weights)
        sorting_choice = mixture_leftover(sorting_choice, measured_mixtures_here, source_launch_order, launch_lags, learned_pace_factors[unrolled_round_ordinal])
        current = jnp.transpose(sorting_choice, (1, 0, 2))
    return current
```

```python
import functools

import jax
import jax.numpy as jnp
import numpy as np
from jax import lax
from jax.experimental import pallas as pl
from jax.experimental.pallas import tpu as pltpu
from jax.sharding import PartitionSpec as P

RPL = 16
DMAX = 128
ITERS = 2
EPSILON = 1e-05

SLAB = 128
HALF = 64
FEAT = 64
GROUP = 4
WIDE = GROUP * FEAT
QS = SLAB // (2 * GROUP)
QH = QS // 2
VMEM_LIMIT = 40 * 1024 * 1024

BF = jnp.bfloat16
F32 = jnp.float32


def entry_selector():
    picks = np.zeros((QH, WIDE, GROUP, 4, 8), np.float32)
    for q in range(QH):
        for p in range(GROUP):
            for j in range(4):
                i = 2 * (GROUP * q + p) + j - 1
                for c in range(3):
                    if i < 0:
                        lane = 3 * HALF + 2 * c
                    elif i >= HALF:
                        lane = 3 * HALF + 2 * c + 1
                    else:
                        lane = c * HALF + i
                    picks[q, lane, p, j, c] = 1
    return picks.reshape(QH * WIDE, GROUP * 4 * 8)


def exit_selector():
    picks = np.zeros((SLAB, QS + 2, SLAB), np.float32)
    for q in range(QS):
        for p in range(GROUP):
            for j in range(4):
                i = 2 * (GROUP * q + p) + j - 1
                if i < 0:
                    picks[p * 8 + j, QS + 1, SLAB - 1] = 1
                elif i >= SLAB:
                    picks[p * 8 + j, QS, 0] = 1
                else:
                    picks[p * 8 + j, q, i] = 1
    return picks.reshape(SLAB, (QS + 2) * SLAB)


def prepare_kernel(plan, place, sel_in, sel_out, mixes, *refs):
    nets, outs, (rhs, cols) = refs[:8], refs[8:-2], refs[-2:]
    for n in range(2):
        w_in, w_mid, w_out, bias = nets[4 * n : 4 * n + 4]
        o_in, o_mid, o_out, o_bias = outs[4 * n : 4 * n + 4]
        rhs[...] = jnp.zeros_like(rhs)
        cols[...] = jnp.zeros_like(cols)
        for p in range(GROUP):
            lanes = slice(p * FEAT, (p + 1) * FEAT)
            for j in range(4):
                rhs[p * 32 + j * 8 : p * 32 + j * 8 + 3, lanes] = w_in[j].astype(F32)
            cols[p * 8 : p * 8 + 4, lanes] = w_out[...].astype(F32)
            o_bias[:, lanes] = bias[...]
        taps = rhs[...].astype(BF)
        for q in range(QH):
            part = sel_in[q * WIDE : (q + 1) * WIDE, :]
            o_in[q] = jnp.dot(part, taps, preferred_element_type=F32).astype(BF)
        back = jnp.transpose(cols[...]).astype(BF)
        for q in range(QS + 2):
            part = sel_out[:, q * SLAB : (q + 1) * SLAB]
            o_out[q] = jnp.dot(back, part, preferred_element_type=F32).astype(BF)
        o_mid[...] = jnp.zeros_like(o_mid)
        for a, row in [(0, 0), (1, 1), (2, 2), (3, 3), (-2, 4), (-1, 5), (4, 6), (5, 7)]:
            for b in range(GROUP):
                if (a - b) % 2 == 0 and abs(a - b) <= 2:
                    o_mid[row * FEAT : (row + 1) * FEAT, b * FEAT : (b + 1) * FEAT] = w_mid[(a - b) // 2 + 1]
    picked = outs[8]
    pieces, mixtures, rows, _ = picked.shape
    block = mixes.shape[1]
    row = lax.broadcasted_iota(jnp.int32, (rows, block), 0)
    col = lax.broadcasted_iota(jnp.int32, (rows, block), 1)
    for n in range(pieces):
        want = (row + place[1]) * RPL + place[3 + n]
        choose = (col == want).astype(F32).astype(BF)
        for g in range(mixtures):
            picked[n, g] = jnp.dot(choose, mixes[g], preferred_element_type=F32).astype(BF)


def section_map(plan, place, tallies):
    shape = (plan.rows, SLAB)
    lane = lax.broadcasted_iota(jnp.int32, shape, 1)
    line = lax.broadcasted_iota(jnp.int32, shape, 0) % plan.lines + place[1]
    spot = (line % plan.block_lines) * RPL + place[0]
    block = line // plan.block_lines
    low = jnp.zeros(shape, jnp.int32)
    high = jnp.zeros(shape, jnp.int32)
    count = jnp.zeros(shape, jnp.int32)
    start = jnp.int32(0)
    for p in range(plan.sections):
        amount = tallies[p]
        for b in range(plan.blocks):
            here = lane == b * plan.sections + p
            low = jnp.where(here, start, low)
            high = jnp.where(here, start + amount, high)
            count = jnp.where(here, amount, count)
        start = start + amount
    member = (spot >= low) & (spot < high) & (lane // plan.sections == block)
    return member, count


def shifted(values, by, ok, edge):
    return jnp.where(ok, pltpu.roll(values, by % values.shape[0], 0), edge)


def pack_inputs(plan, channels, packed):
    lane = lax.broadcasted_iota(jnp.int32, (plan.rows, SLAB), 1)
    low = lane < HALF
    slabs = [[x[:, t * SLAB : (t + 1) * SLAB] for t in range(plan.slabs)] for x in channels]
    far = [[pltpu.roll(s, HALF + 1 + 2 * c, 1) for s in slabs[c]] for c in range(3)]
    for t in range(plan.slabs):
        v = [slabs[c][t] for c in range(3)]
        w = [pltpu.roll(s, HALF, 1) for s in v]
        even = jnp.where(low, v[2], 0.0)
        odd = jnp.where(low, w[2], 0.0)
        for c in range(3):
            left, right = lane == HALF + 2 * c, lane == HALF + 2 * c + 1
            near = pltpu.roll(v[c], 1 + 2 * c, 1)
            even = jnp.where(right, near, even)
            odd = jnp.where(left, near, odd)
            if t > 0:
                even = jnp.where(left, far[c][t - 1], even)
            if t < plan.slabs - 1:
                odd = jnp.where(right, far[c][t + 1], odd)
        packed[0, t, :, 0:SLAB] = jnp.where(low, v[0], w[1]).astype(BF)
        packed[0, t, :, SLAB:WIDE] = even.astype(BF)
        packed[1, t, :, 0:SLAB] = jnp.where(low, w[0], v[1]).astype(BF)
        packed[1, t, :, SLAB:WIDE] = odd.astype(BF)


def network(plan, weights, bias, scratch):
    w_in, w_mid, w_out = weights
    packed, hidden, total = scratch
    many, rows = plan.slabs * plan.rows, plan.rows
    grid = (plan.slabs, rows, WIDE)
    pitch = plan.slabs + 2
    bias_one, bias_two = bias

    def first(q):
        value = jnp.dot(packed[q // QH].reshape(many, WIDE), w_in[q % QH], preferred_element_type=F32)
        value = (value.reshape(grid) + bias_one[None]).astype(BF)
        hidden[pl.ds(q * pitch + 1, plan.slabs)] = jnp.maximum(value, 0)

    def second(q, left_at, right_at):
        middle = hidden[pl.ds(q * pitch + 1, plan.slabs)]
        left = hidden[pl.ds(left_at, plan.slabs), :, SLAB:WIDE]
        right = hidden[pl.ds(right_at, plan.slabs), :, 0:SLAB]
        window = jnp.concatenate([middle, left, right], axis=2).reshape(many, 2 * WIDE)
        value = jnp.dot(window, w_mid[...], preferred_element_type=F32)
        value = (value.reshape(grid) + bias_two[None]).astype(BF)
        return jnp.maximum(value, 0).reshape(many, WIDE)

    def onto(layer, q):
        return jnp.dot(layer, w_out[q], preferred_element_type=F32).reshape(plan.slabs, rows, SLAB)

    edge = jnp.zeros((rows, WIDE), BF)
    hidden[(QS - 1) * pitch] = edge
    hidden[pitch - 1] = edge
    lax.fori_loop(0, QS, lambda q, _: first(q), None, unroll=4)

    layer = second(0, (QS - 1) * pitch, pitch + 1)
    total[...] = onto(layer, 0)
    total[0 : plan.slabs - 1] += onto(layer, QS + 1)[1:]

    def step(q, _):
        total[...] += onto(second(q, (q - 1) * pitch + 1, (q + 1) * pitch + 1), q)

    lax.fori_loop(1, QS - 1, step, None, unroll=2)
    layer = second(QS - 1, (QS - 2) * pitch + 1, 2)
    total[...] += onto(layer, QS - 1)
    total[1 : plan.slabs] += onto(layer, QS)[: plan.slabs - 1]


def add_total(plan, now, total):
    for t in range(plan.slabs):
        lanes = slice(t * SLAB, (t + 1) * SLAB)
        now[:, lanes] = (now[:, lanes] + total[t]).astype(BF).astype(F32)


def shot_stage(plan, place, tallies, edges, weights, bias, now, scratch, energy):
    x = now[...]
    line = lax.broadcasted_iota(jnp.int32, x.shape, 0) % plan.lines
    above = 0.0 if edges is None else edges[0].astype(F32)
    below = 0.0 if edges is None else edges[1].astype(F32)
    channels = [
        shifted(x, 1, line > 0, above),
        x,
        shifted(x, -1, line < plan.lines - 1, below),
    ]
    pack_inputs(plan, channels, scratch[0])
    rows = [jnp.broadcast_to(bias[i : i + 1, :], (plan.rows, WIDE)) for i in range(2)]
    network(plan, weights, rows, scratch)
    add_total(plan, now, scratch[2])
    power = jnp.zeros((plan.rows, SLAB), F32)
    for t in range(plan.slabs):
        piece = now[:, t * SLAB : (t + 1) * SLAB]
        power = power + piece * piece
    member, _ = section_map(plan, place, tallies)
    each = jnp.where(member, jnp.sum(power, axis=1, keepdims=True), 0.0)
    energy[...] = jnp.sum(each, axis=0, keepdims=True)


def station_stage(plan, place, tallies, lags, order, pace, energies, mixes, weights, bias, now, scratch, blend):
    member, count = section_map(plan, place, tallies)
    totals = jnp.sum(energies[...], axis=0)
    denominator = jnp.maximum(count, 1) * (plan.shots * plan.slabs * SLAB)
    level = jnp.sqrt(totals / denominator.astype(F32) + EPSILON)
    rms = jnp.sum(jnp.where(member, level, 0.0), axis=1, keepdims=True)
    x = now[...]
    row = lax.broadcasted_iota(jnp.int32, x.shape, 0)
    channels = [
        shifted(x, plan.lines, row >= plan.lines, 0.0),
        x,
        shifted(x, -plan.lines, row < plan.rows - plan.lines, 0.0),
    ]
    pack_inputs(plan, channels, scratch[0])
    network(plan, weights, [rms * bias[i : i + 1, :] for i in range(2)], scratch)
    add_total(plan, now, scratch[2])

    fired, misfit, recorded = blend
    lane = lax.broadcasted_iota(jnp.int32, (plan.lines, SLAB), 1)
    pieces, mixtures = mixes.shape[:2]
    per = plan.shots // mixtures
    for n in range(pieces):
        recorded[(place[2] + n) % pieces] = mixes[n].astype(F32)
    for s in range(plan.shots):
        lag = lags[s]
        before = jnp.zeros((plan.lines, SLAB), F32)
        for t in range(plan.slabs):
            lanes = slice(t * SLAB, (t + 1) * SLAB)
            turned = pltpu.roll(now[s * plan.lines : (s + 1) * plan.lines, lanes], lag, 1)
            fired[s, :, lanes] = jnp.where(lane < lag, before, turned)
            before = turned
    for g in range(mixtures):
        value = fired[order[g * per]]
        for k in range(1, per):
            value = value + fired[order[g * per + k]]
        for n in range(pieces):
            here = slice(n * plan.piece_lines, (n + 1) * plan.piece_lines)
            misfit[g, here, :] = value[here] - recorded[n, g]
    for s in range(plan.shots):
        lag = lags[s]
        spot = jnp.int32(0)
        for k in range(plan.shots):
            spot = spot + jnp.where(order[k] == s, k, 0)
        which = spot // per
        back = (DMAX - lag) % DMAX
        after = jnp.zeros((plan.lines, SLAB), F32)
        rows = slice(s * plan.lines, (s + 1) * plan.lines)
        for t in range(plan.slabs - 1, -1, -1):
            lanes = slice(t * SLAB, (t + 1) * SLAB)
            turned = pltpu.roll(misfit[which, :, lanes], back, 1)
            pulled = jnp.where(lane < DMAX - lag, turned, after)
            after = turned
            now[rows, lanes] = (now[rows, lanes] - pace * pulled).astype(BF).astype(F32)


def stage_kernel(plan, station_round, with_shot, has_edges, split_in, split_out, *refs):
    refs = list(refs)
    take = lambda n: [refs.pop(0) for _ in range(n)]
    place, tallies, lags, order, paces, source = take(6)
    station = station_round is not None
    if station:
        energies, mixes, *station_weights, station_bias = take(6)
    edges = None
    if with_shot:
        if has_edges:
            (edges,) = take(1)
        *shot_weights, shot_bias = take(4)
    (result,) = take(1)
    if with_shot:
        (energy,) = take(1)
    now, packed, hidden, total = take(4)
    scratch = (packed, hidden, total)
    if split_in:
        for n, (row, lane, rows, lanes) in enumerate(plan.pieces):
            now[row : row + rows, lane : lane + lanes] = source[n].astype(F32)
    else:
        now[...] = source[...].astype(F32)
    if station:
        station_stage(plan, place, tallies, lags, order, paces[station_round], energies, mixes, station_weights, station_bias, now, scratch, refs)
    if with_shot:
        shot_stage(plan, place, tallies, edges, shot_weights, shot_bias, now, scratch, energy)
    if split_out:
        for n, (row, lane, rows, lanes) in enumerate(plan.pieces):
            result[n] = now[row : row + rows, lane : lane + lanes].astype(BF)
    else:
        result[...] = now[...].astype(BF)


SMEM = pl.BlockSpec(memory_space=pltpu.SMEM)
VMEM = pl.BlockSpec(memory_space=pltpu.VMEM)


def run_stage(plan, small, source, station=None, shot=None, split_in=False, split_out=False, name="stage"):
    operands = [*small, source]
    station_round, has_edges = None, False
    macs = 0
    pass_macs = plan.rows * plan.slabs * QS * WIDE * (WIDE * 3 + SLAB)
    if station is not None:
        station_round, energies, mixes, weights = station
        operands += [energies, mixes, *weights]
        macs += pass_macs
    if shot is not None:
        edges, weights = shot
        has_edges = edges is not None
        operands += ([edges] if has_edges else []) + list(weights)
        macs += pass_macs
    length = plan.slabs * SLAB
    if split_out:
        _, _, rows, lanes = plan.pieces[0]
        shapes = [jax.ShapeDtypeStruct((len(plan.pieces), rows, lanes), BF)]
    else:
        shapes = [jax.ShapeDtypeStruct((plan.rows, length), BF)]
    if shot is not None:
        shapes.append(jax.ShapeDtypeStruct((1, SLAB), F32))
    scratch = [
        pltpu.VMEM((plan.rows, length), F32),
        pltpu.VMEM((2, plan.slabs, plan.rows, WIDE), BF),
        pltpu.VMEM((QS * (plan.slabs + 2), plan.rows, WIDE), BF),
        pltpu.VMEM((plan.slabs, plan.rows, SLAB), F32),
    ]
    if station is not None:
        pieces, mixtures, lines, _ = mixes.shape
        scratch += [
            pltpu.VMEM((plan.shots, plan.lines, length), F32),
            pltpu.VMEM((mixtures, plan.lines, length), F32),
            pltpu.VMEM((pieces, mixtures, lines, length), F32),
        ]
    return pl.pallas_call(
        functools.partial(stage_kernel, plan, station_round, shot is not None, has_edges, split_in, split_out),
        out_shape=shapes,
        in_specs=[SMEM] * len(small) + [VMEM] * (len(operands) - len(small)),
        out_specs=[VMEM] * len(shapes),
        scratch_shapes=scratch,
        compiler_params=pltpu.CompilerParams(vmem_limit_bytes=VMEM_LIMIT),
        cost_estimate=pl.CostEstimate(flops=2 * macs, bytes_accessed=1 << 20, transcendentals=0),
        name=name,
    )(*operands)


def run_prepare(plan, place, mixtures, nets, pieces):
    groups, _, length = mixtures.shape
    shapes = []
    for _ in range(2):
        shapes += [
            jax.ShapeDtypeStruct((QH, WIDE, WIDE), BF),
            jax.ShapeDtypeStruct((2 * WIDE, WIDE), BF),
            jax.ShapeDtypeStruct((QS + 2, WIDE, SLAB), BF),
            jax.ShapeDtypeStruct((2, WIDE), F32),
        ]
    shapes.append(jax.ShapeDtypeStruct((pieces, groups, plan.piece_lines, length), BF))
    operands = [jnp.asarray(entry_selector(), BF), jnp.asarray(exit_selector(), BF), mixtures, *nets]
    outs = pl.pallas_call(
        functools.partial(prepare_kernel, plan),
        out_shape=shapes,
        in_specs=[SMEM] + [VMEM] * len(operands),
        out_specs=[VMEM] * len(shapes),
        scratch_shapes=[pltpu.VMEM((SLAB, WIDE), F32), pltpu.VMEM((SLAB, WIDE), F32)],
        compiler_params=pltpu.CompilerParams(vmem_limit_bytes=VMEM_LIMIT),
        cost_estimate=pl.CostEstimate(flops=2 * 2 * 8192 * WIDE * SLAB, bytes_accessed=8 << 20, transcendentals=0),
        name="prepare",
    )(place, *operands)
    return outs[0:4], outs[4:8], outs[8]


class Plan:
    def __init__(self, shots, lines, block_lines, blocks, sections, slabs, pieces, piece_lines):
        self.shots, self.lines, self.rows = shots, lines, shots * lines
        self.block_lines, self.blocks, self.sections = block_lines, blocks, sections
        self.slabs, self.pieces, self.piece_lines = slabs, pieces, piece_lines


def per_device(
    initial_guess,
    measured_mixtures,
    launch_lags,
    source_launch_order,
    station_portion_tallies,
    source_entry_kernel,
    source_spaced_kernel,
    source_exit_kernel,
    source_inner_offsets,
    station_entry_kernel,
    station_spaced_kernel,
    station_exit_kernel,
    station_inner_offsets,
    learned_pace_factors,
):
    shots_here, block, window = initial_guess.shape
    n_shot, n_line, n_tm = (lax.axis_size(a) for a in ("shot", "line", "tm"))
    at_shot, at_line, at_tm = (lax.axis_index(a) for a in ("shot", "line", "tm"))
    block_lines = block // RPL
    length = window * n_tm
    shots = shots_here * n_shot
    sections = station_portion_tallies.shape[0]
    whole_lines = n_shot * n_line * n_tm == RPL
    assert shots_here == 1 and (whole_lines or n_shot == RPL)
    if whole_lines:
        axes = ("shot", "line", "tm")
        piece_lines, lines, blocks = block_lines, block_lines * n_line, n_line
        position = (at_shot * n_line + at_line) * n_tm + at_tm
        first_line, piece_count = 0, n_line
        places = [(at_shot * n_line + (at_line + d) % n_line) * n_tm + at_tm for d in range(n_line)]
    else:
        axes = ("shot", "tm")
        piece_lines = lines = block_lines // n_tm
        blocks, position, piece_count = 1, at_shot, 1
        first_line = at_tm * lines
        places = [position]
    pieces = [
        (s * lines + a * block_lines, b * window, piece_lines, window)
        for s in range(n_shot)
        for a in range(blocks)
        for b in range(n_tm)
    ]
    plan = Plan(shots, lines, block_lines, blocks, sections, length // SLAB, pieces, piece_lines)

    grid = initial_guess.reshape(block_lines, RPL, window)
    if whole_lines:
        leaving = grid.transpose(1, 0, 2)
    else:
        leaving = grid.reshape(n_tm, lines, RPL, window).transpose(2, 0, 1, 3).reshape(RPL * n_tm, lines, window)
    arrived = lax.all_to_all(leaving, axes, split_axis=0, concat_axis=0, tiled=True)

    place = jnp.stack([jnp.asarray(v, jnp.int32) for v in [position, first_line, at_line, *places]])
    nets = (
        source_entry_kernel,
        source_spaced_kernel,
        source_exit_kernel,
        source_inner_offsets,
        station_entry_kernel,
        station_spaced_kernel,
        station_exit_kernel,
        station_inner_offsets,
    )
    shot_weights, station_weights, mixes = run_prepare(plan, place, measured_mixtures, nets, piece_count)
    if whole_lines and n_line > 1:
        parts = [mixes[0]]
        for d in range(1, n_line):
            parts.append(lax.ppermute(mixes[d], "line", [(i, (i + d) % n_line) for i in range(n_line)]))
        mixes = jnp.stack([parts[0], *parts[:0:-1]])

    small = (place, station_portion_tallies, launch_lags, source_launch_order, learned_pace_factors)
    split = whole_lines and piece_lines % 8 == 0
    if split:
        source = arrived
    else:
        source = arrived.reshape(n_shot, blocks, n_tm, piece_lines, window).transpose(0, 1, 3, 2, 4)
        source = source.reshape(plan.rows, length)

    def edges_of(current):
        if whole_lines:
            return None
        size = n_line * n_tm
        grid = current.reshape(shots, lines, length)
        up = [(i, i + 1) for i in range(size - 1)]
        down = [(j, i) for i, j in up]
        above = lax.ppermute(grid[:, -1], ("line", "tm"), up)
        below = lax.ppermute(grid[:, 0], ("line", "tm"), down)
        wide = jnp.broadcast_to(jnp.stack([above, below])[:, :, None, :], (2, shots, lines, length))
        return wide.reshape(2, plan.rows, length)

    def shared(energy):
        return lax.all_gather(energy, axes)

    current, energy = run_stage(
        plan, small, source, shot=(edges_of(source), shot_weights), split_in=split, name="shot_pass"
    )
    for i in range(ITERS):
        station = (i, shared(energy), mixes, station_weights)
        if i == ITERS - 1:
            (current,) = run_stage(plan, small, current, station=station, split_out=split, name="station_pass")
        elif whole_lines:
            current, energy = run_stage(
                plan, small, current, station=station, shot=(None, shot_weights), name="station_and_shot_pass"
            )
        else:
            (current,) = run_stage(plan, small, current, station=station, name="station_pass")
            current, energy = run_stage(plan, small, current, shot=(edges_of(current), shot_weights), name="shot_pass")
    if not split:
        current = current.reshape(n_shot, blocks, piece_lines, n_tm, window).transpose(0, 1, 3, 2, 4)
        current = current.reshape(len(pieces), piece_lines, window)
    back = lax.all_to_all(current, axes, split_axis=0, concat_axis=0, tiled=True)
    if whole_lines:
        back = back.transpose(1, 0, 2)
    else:
        back = back.reshape(RPL, n_tm, lines, window).transpose(1, 2, 0, 3)
    return back.reshape(shots_here, block, window)


def solution(mesh):
    placed = (P(("group", "shot"), "line", "tm"), P("group", "line", None), P("group"), P("group"), P("group"))
    return jax.shard_map(
        per_device,
        mesh=mesh,
        in_specs=placed + (P(),) * 9,
        out_specs=P(("group", "shot"), "line", "tm"),
        check_vma=False,
    )
```

```python
import functools

import jax
import jax.numpy as jnp
import numpy as np
from jax import lax
from jax.experimental import pallas as pl
from jax.experimental.pallas import tpu as pltpu
from jax.sharding import PartitionSpec as P

RPL = 16
DMAX = 128
ITERS = 2
EPSILON = 1e-05

SLAB = 128
HALF = 64
FEAT = 64
GROUP = 4
WIDE = GROUP * FEAT
QS = SLAB // (2 * GROUP)
QH = QS // 2
ONES = 3 * HALF + 6
VMEM_LIMIT = 20 * 1024 * 1024

BF = jnp.bfloat16
F32 = jnp.float32


def entry_selector():
    picks = np.zeros((QH, WIDE, GROUP, 4, 8), np.float32)
    for j in range(3):
        picks[:, ONES + j, :, 3, j] = 1
    for q in range(QH):
        for p in range(GROUP):
            for j in range(4):
                i = 2 * (GROUP * q + p) + j - 1
                for c in range(3):
                    if i < 0:
                        lane = 3 * HALF + 2 * c
                    elif i >= HALF:
                        lane = 3 * HALF + 2 * c + 1
                    else:
                        lane = c * HALF + i
                    picks[q, lane, p, c, j] = 1
    return picks.reshape(QH * WIDE, GROUP * 4 * 8)


def exit_selector():
    picks = np.zeros((SLAB, QS + 2, SLAB), np.float32)
    for q in range(QS):
        for p in range(GROUP):
            for j in range(4):
                i = 2 * (GROUP * q + p) + j - 1
                if i < 0:
                    picks[p * 8 + j, QS + 1, SLAB - 1] = 1
                elif i >= SLAB:
                    picks[p * 8 + j, QS, 0] = 1
                else:
                    picks[p * 8 + j, q, i] = 1
    return picks.reshape(SLAB, (QS + 2) * SLAB)


def split_bias(bias):
    high = bias.astype(BF).astype(F32)
    middle = (bias - high).astype(BF).astype(F32)
    return high, middle, bias - high - middle


def prepare_kernel(*refs):
    sources, outs = refs[:10], refs[10:16]
    (rhs, cols), held, done = refs[16:18], refs[18:28], refs[28]
    copies = [pltpu.make_async_copy(src, dst, done.at[i]) for i, (src, dst) in enumerate(zip(sources, held))]
    for copy in copies:
        copy.start()
    for copy in copies:
        copy.wait()
    sel_in, sel_out = held[:2]
    for n in range(2):
        w_in, w_mid, w_out, bias = held[2 + 4 * n : 6 + 4 * n]
        o_in, o_mid, o_out = outs[3 * n : 3 * n + 3]
        rhs[...] = jnp.zeros_like(rhs)
        cols[...] = jnp.zeros_like(cols)
        parts = split_bias(bias[0:1, :])
        for p in range(GROUP):
            lanes = slice(p * FEAT, (p + 1) * FEAT)
            for c in range(3):
                rhs[p * 32 + c * 8 : p * 32 + c * 8 + 4, lanes] = w_in[c].astype(F32)
                rhs[p * 32 + 24 + c : p * 32 + 25 + c, lanes] = parts[c]
            cols[p * 8 : p * 8 + 4, lanes] = w_out[...].astype(F32)
        taps = rhs[...].astype(BF)
        for q in range(QH):
            part = sel_in[q * WIDE : (q + 1) * WIDE, :]
            o_in[q] = jnp.dot(part, taps, preferred_element_type=F32).astype(BF)
        back = jnp.transpose(cols[...]).astype(BF)
        for q in range(QS + 2):
            part = sel_out[:, q * SLAB : (q + 1) * SLAB]
            o_out[q] = jnp.dot(back, part, preferred_element_type=F32).astype(BF)
        o_mid[...] = jnp.zeros_like(o_mid)
        for a, row in [(0, 0), (1, 1), (2, 2), (3, 3), (-2, 4), (-1, 5), (4, 6), (5, 7)]:
            for b in range(GROUP):
                if (a - b) % 2 == 0 and abs(a - b) <= 2:
                    o_mid[row * FEAT : (row + 1) * FEAT, b * FEAT : (b + 1) * FEAT] = w_mid[(a - b) // 2 + 1]


def pack_kernel(plan, place, traces, mixes, packet, held, done):
    window = traces.shape[1]
    share = (packet.shape[2] - window) // mixes.shape[0]
    copies = [pltpu.make_async_copy(traces, held.at[:, 0:window], done.at[0])]
    at = pl.multiple_of(place[2] * share, share)
    for g in range(mixes.shape[0]):
        into = held.at[:, window + g * share : window + (g + 1) * share]
        copies.append(pltpu.make_async_copy(mixes.at[g, :, pl.ds(at, share)], into, done.at[g + 1]))
    for copy in copies:
        copy.start()
    block = traces.shape[0]
    row = lax.broadcasted_iota(jnp.int32, (block, block), 0)
    col = lax.broadcasted_iota(jnp.int32, (block, block), 1)
    lines = plan.block_lines
    order = (col == (row % lines) * RPL + row // lines).astype(F32).astype(BF)
    for copy in copies:
        copy.wait()
    moved = jnp.dot(order, held[...], preferred_element_type=F32)
    packet[...] = moved.reshape(packet.shape).astype(BF)


def section_map(plan, place, tallies):
    shape = (plan.rows, SLAB)
    lane = lax.broadcasted_iota(jnp.int32, shape, 1)
    line = lax.broadcasted_iota(jnp.int32, shape, 0) % plan.lines + place[1]
    spot = (line % plan.block_lines) * RPL + place[0]
    block = line // plan.block_lines
    low = jnp.zeros(shape, jnp.int32)
    high = jnp.zeros(shape, jnp.int32)
    count = jnp.zeros(shape, jnp.int32)
    start = jnp.int32(0)
    for p in range(plan.sections):
        amount = tallies[p]
        for b in range(plan.blocks):
            here = lane == b * plan.sections + p
            low = jnp.where(here, start, low)
            high = jnp.where(here, start + amount, high)
            count = jnp.where(here, amount, count)
        start = start + amount
    member = (spot >= low) & (spot < high) & (lane // plan.sections == block)
    return member, count


def shifted(values, by, ok, edge):
    return jnp.where(ok, pltpu.roll(values, by % values.shape[0], 0), edge)


def pack_inputs(plan, channels, packed):
    lane = lax.broadcasted_iota(jnp.int32, (plan.rows, SLAB), 1)
    low = lane < HALF
    ones = ((lane >= ONES - SLAB) & (lane < ONES - SLAB + 3)).astype(F32)
    slabs = [[x[:, t * SLAB : (t + 1) * SLAB] for t in range(plan.slabs)] for x in channels]
    far = [[pltpu.roll(s, HALF + 1 + 2 * c, 1) for s in slabs[c]] for c in range(3)]
    for t in range(plan.slabs):
        v = [slabs[c][t] for c in range(3)]
        w = [pltpu.roll(s, HALF, 1) for s in v]
        even = jnp.where(low, v[2], ones)
        odd = jnp.where(low, w[2], ones)
        for c in range(3):
            left, right = lane == HALF + 2 * c, lane == HALF + 2 * c + 1
            near = pltpu.roll(v[c], 1 + 2 * c, 1)
            even = jnp.where(right, near, even)
            odd = jnp.where(left, near, odd)
            if t > 0:
                even = jnp.where(left, far[c][t - 1], even)
            if t < plan.slabs - 1:
                odd = jnp.where(right, far[c][t + 1], odd)
        packed[0, t, :, 0:SLAB] = jnp.where(low, v[0], w[1]).astype(BF)
        packed[0, t, :, SLAB:WIDE] = even.astype(BF)
        packed[1, t, :, 0:SLAB] = jnp.where(low, w[0], v[1]).astype(BF)
        packed[1, t, :, SLAB:WIDE] = odd.astype(BF)


def network(plan, weights, bias, scratch):
    w_in, w_mid, w_out = weights
    packed, hidden, total = scratch
    many, rows = plan.slabs * plan.rows, plan.rows
    grid = (plan.slabs, rows, WIDE)
    pitch = plan.slabs + 2
    bias_two = jnp.concatenate([bias[1:2, :]] * GROUP, axis=1)

    def first(q):
        value = jnp.dot(packed[q // QH].reshape(many, WIDE), w_in[q % QH], preferred_element_type=F32)
        hidden[pl.ds(q * pitch + 1, plan.slabs)] = jnp.maximum(value.astype(BF), 0).reshape(grid)

    def second(q, left_at, right_at):
        middle = hidden[pl.ds(q * pitch + 1, plan.slabs)]
        left = hidden[pl.ds(left_at, plan.slabs), :, SLAB:WIDE]
        right = hidden[pl.ds(right_at, plan.slabs), :, 0:SLAB]
        window = jnp.concatenate([middle, left, right], axis=2).reshape(many, 2 * WIDE)
        value = jnp.dot(window, w_mid[...], preferred_element_type=F32)
        return jnp.maximum((value + bias_two).astype(BF), 0)

    def onto(layer, q):
        return jnp.dot(layer, w_out[q], preferred_element_type=F32).reshape(plan.slabs, rows, SLAB)

    edge = jnp.zeros((rows, WIDE), BF)
    hidden[(QS - 1) * pitch] = edge
    hidden[pitch - 1] = edge
    for q in range(QS):
        first(q)

    layer = second(0, (QS - 1) * pitch, pitch + 1)
    total[...] = onto(layer, 0)
    total[0 : plan.slabs - 1] += onto(layer, QS + 1)[1:]

    for q in range(1, QS - 1):
        total[...] += onto(second(q, (q - 1) * pitch + 1, (q + 1) * pitch + 1), q)
    layer = second(QS - 1, (QS - 2) * pitch + 1, 2)
    total[...] += onto(layer, QS - 1)
    total[1 : plan.slabs] += onto(layer, QS)[: plan.slabs - 1]


def add_total(plan, now, total, scale=None):
    for t in range(plan.slabs):
        lanes = slice(t * SLAB, (t + 1) * SLAB)
        more = total[t] if scale is None else scale * total[t]
        now[:, lanes] = (now[:, lanes] + more).astype(BF).astype(F32)


def shot_stage(plan, place, tallies, edges, weights, bias, now, scratch, energy):
    x = now[...]
    line = lax.broadcasted_iota(jnp.int32, x.shape, 0) % plan.lines
    above = 0.0 if edges is None else edges[0].astype(F32)
    below = 0.0 if edges is None else edges[1].astype(F32)
    channels = [
        shifted(x, 1, line > 0, above),
        x,
        shifted(x, -1, line < plan.lines - 1, below),
    ]
    pack_inputs(plan, channels, scratch[0])
    network(plan, weights, bias, scratch)
    add_total(plan, now, scratch[2])
    power = jnp.zeros((plan.rows, SLAB), F32)
    for t in range(plan.slabs):
        piece = now[:, t * SLAB : (t + 1) * SLAB]
        power = power + piece * piece
    member, _ = section_map(plan, place, tallies)
    each = jnp.where(member, jnp.sum(power, axis=1, keepdims=True), 0.0)
    energy[...] = jnp.sum(each, axis=0, keepdims=True)


def station_stage(plan, place, tallies, lags, order, pace, energies, mixes, weights, bias, now, scratch, blend):
    member, count = section_map(plan, place, tallies)
    totals = energies[...]
    denominator = jnp.maximum(count, 1) * (plan.shots * plan.slabs * SLAB)
    level = jnp.sqrt(totals / denominator.astype(F32) + EPSILON)
    rms = jnp.sum(jnp.where(member, level, 0.0), axis=1, keepdims=True)
    x = (now[...] / rms).astype(BF).astype(F32)
    row = lax.broadcasted_iota(jnp.int32, x.shape, 0)
    channels = [
        shifted(x, plan.lines, row >= plan.lines, 0.0),
        x,
        shifted(x, -plan.lines, row < plan.rows - plan.lines, 0.0),
    ]
    pack_inputs(plan, channels, scratch[0])
    network(plan, weights, bias, scratch)
    add_total(plan, now, scratch[2], rms)

    fired, misfit = blend
    lane = lax.broadcasted_iota(jnp.int32, (plan.lines, SLAB), 1)
    mixtures = misfit.shape[0]
    per = plan.shots // mixtures
    if plan.whole_lines:
        for n, (row, _, rows, lanes) in enumerate(plan.pieces):
            share = (mixes.shape[2] - lanes) // mixtures
            spot = plan.spots[n] * share
            for g in range(mixtures):
                piece = mixes[n, :, lanes + g * share : lanes + (g + 1) * share]
                misfit[g, row % plan.lines : row % plan.lines + rows, spot : spot + share] = piece.astype(F32)
    else:
        misfit[...] = mixes[...].astype(F32)
    for s in range(plan.shots):
        lag = lags[s]
        before = jnp.zeros((plan.lines, SLAB), F32)
        for t in range(plan.slabs):
            lanes = slice(t * SLAB, (t + 1) * SLAB)
            turned = pltpu.roll(now[s * plan.lines : (s + 1) * plan.lines, lanes], lag, 1)
            fired[s, :, lanes] = jnp.where(lane < lag, before, turned)
            before = turned
    for g in range(mixtures):
        value = fired[order[g * per]]
        for k in range(1, per):
            value = value + fired[order[g * per + k]]
        misfit[g] = value - misfit[g]
    for s in range(plan.shots):
        lag = lags[s]
        spot = jnp.int32(0)
        for k in range(plan.shots):
            spot = spot + jnp.where(order[k] == s, k, 0)
        which = spot // per
        back = (DMAX - lag) % DMAX
        after = jnp.zeros((plan.lines, SLAB), F32)
        rows = slice(s * plan.lines, (s + 1) * plan.lines)
        for t in range(plan.slabs - 1, -1, -1):
            lanes = slice(t * SLAB, (t + 1) * SLAB)
            turned = pltpu.roll(misfit[which, :, lanes], back, 1)
            pulled = jnp.where(lane < DMAX - lag, turned, after)
            after = turned
            now[rows, lanes] = (now[rows, lanes] - pace * pulled).astype(BF).astype(F32)


def stage_kernel(plan, station_round, with_shot, has_edges, split_in, split_out, *refs):
    refs = list(refs)
    take = lambda n: [refs.pop(0) for _ in range(n)]
    place, tallies, lags, order, paces, source = take(6)
    station = station_round is not None
    if station:
        energies, mixes, *station_weights, station_bias = take(6)
    edges = None
    if with_shot:
        if has_edges:
            (edges,) = take(1)
        *shot_weights, shot_bias = take(4)
    (result,) = take(1)
    if with_shot:
        (energy,) = take(1)
    now, packed, hidden, total = take(4)
    scratch = (packed, hidden, total)
    if split_in:
        for n, (row, lane, rows, lanes) in enumerate(plan.pieces):
            now[row : row + rows, lane : lane + lanes] = source[n, :, 0:lanes].astype(F32)
    else:
        now[...] = source[...].astype(F32)
    if station:
        station_stage(plan, place, tallies, lags, order, paces[station_round], energies, mixes, station_weights, station_bias, now, scratch, refs)
    if with_shot:
        shot_stage(plan, place, tallies, edges, shot_weights, shot_bias, now, scratch, energy)
    if split_out:
        for n, (row, lane, rows, lanes) in enumerate(plan.pieces):
            result[n] = now[row : row + rows, lane : lane + lanes].astype(BF)
    else:
        result[...] = now[...].astype(BF)


SMEM = pl.BlockSpec(memory_space=pltpu.SMEM)
VMEM = pl.BlockSpec(memory_space=pltpu.VMEM)
ANY = pl.BlockSpec(memory_space=pl.ANY)


def run_stage(plan, small, source, station=None, shot=None, split_in=False, split_out=False, name="stage"):
    operands = [*small, source]
    station_round, has_edges = None, False
    macs = 0
    pass_macs = plan.rows * plan.slabs * QS * WIDE * (WIDE * 3 + SLAB)
    if station is not None:
        station_round, energies, mixes, weights = station
        operands += [energies, mixes, *weights]
        macs += pass_macs
    if shot is not None:
        edges, weights = shot
        has_edges = edges is not None
        operands += ([edges] if has_edges else []) + list(weights)
        macs += pass_macs
    length = plan.slabs * SLAB
    if split_out:
        _, _, rows, lanes = plan.pieces[0]
        shapes = [jax.ShapeDtypeStruct((len(plan.pieces), rows, lanes), BF)]
    else:
        shapes = [jax.ShapeDtypeStruct((plan.rows, length), BF)]
    if shot is not None:
        shapes.append(jax.ShapeDtypeStruct((1, SLAB), F32))
    scratch = [
        pltpu.VMEM((plan.rows, length), F32),
        pltpu.VMEM((2, plan.slabs, plan.rows, WIDE), BF),
        pltpu.VMEM((QS * (plan.slabs + 2), plan.rows, WIDE), BF),
        pltpu.VMEM((plan.slabs, plan.rows, SLAB), F32),
    ]
    if station is not None:
        scratch += [
            pltpu.VMEM((plan.shots, plan.lines, length), F32),
            pltpu.VMEM((plan.mixtures, plan.lines, length), F32),
        ]
    return pl.pallas_call(
        functools.partial(stage_kernel, plan, station_round, shot is not None, has_edges, split_in, split_out),
        out_shape=shapes,
        in_specs=[SMEM] * len(small) + [VMEM] * (len(operands) - len(small)),
        out_specs=[VMEM] * len(shapes),
        scratch_shapes=scratch,
        compiler_params=pltpu.CompilerParams(vmem_limit_bytes=VMEM_LIMIT),
        cost_estimate=pl.CostEstimate(flops=2 * macs, bytes_accessed=1 << 20, transcendentals=0),
        name=name,
    )(*operands)


def run_prepare(nets):
    shapes = []
    for _ in range(2):
        shapes += [
            jax.ShapeDtypeStruct((QH, WIDE, WIDE), BF),
            jax.ShapeDtypeStruct((2 * WIDE, WIDE), BF),
            jax.ShapeDtypeStruct((QS + 2, WIDE, SLAB), BF),
        ]
    operands = [jnp.asarray(entry_selector(), BF), jnp.asarray(exit_selector(), BF), *nets]
    scratch = [pltpu.VMEM((SLAB, WIDE), F32), pltpu.VMEM((SLAB, WIDE), F32)]
    scratch += [pltpu.VMEM(o.shape, o.dtype) for o in operands]
    scratch += [pltpu.SemaphoreType.DMA((len(operands),))]
    outs = pl.pallas_call(
        prepare_kernel,
        out_shape=shapes,
        in_specs=[ANY] * len(operands),
        out_specs=[VMEM] * len(shapes),
        scratch_shapes=scratch,
        compiler_params=pltpu.CompilerParams(vmem_limit_bytes=VMEM_LIMIT),
        cost_estimate=pl.CostEstimate(flops=2 * 2 * 8192 * WIDE * SLAB, bytes_accessed=8 << 20, transcendentals=0),
        name="prepare",
    )(*operands)
    return outs[0:3], outs[3:6]


def run_pack(plan, place, traces, mixtures, share):
    groups, block, _ = mixtures.shape
    width = traces.shape[1] + groups * share
    return pl.pallas_call(
        functools.partial(pack_kernel, plan),
        out_shape=jax.ShapeDtypeStruct((RPL, plan.block_lines, width), BF),
        in_specs=[SMEM, ANY, ANY],
        out_specs=VMEM,
        scratch_shapes=[pltpu.VMEM((block, width), BF), pltpu.SemaphoreType.DMA((groups + 1,))],
        compiler_params=pltpu.CompilerParams(vmem_limit_bytes=VMEM_LIMIT),
        cost_estimate=pl.CostEstimate(flops=2 * block * block * width, bytes_accessed=1 << 20, transcendentals=0),
        name="pack",
    )(place, traces, mixtures)


class Plan:
    def __init__(self, **sizes):
        self.__dict__.update(sizes)
        self.rows = self.shots * self.lines


def per_device(
    initial_guess,
    measured_mixtures,
    launch_lags,
    source_launch_order,
    station_portion_tallies,
    source_entry_kernel,
    source_spaced_kernel,
    source_exit_kernel,
    source_inner_offsets,
    station_entry_kernel,
    station_spaced_kernel,
    station_exit_kernel,
    station_inner_offsets,
    learned_pace_factors,
):
    shots_here, block, window = initial_guess.shape
    n_shot, n_line, n_tm = (lax.axis_size(a) for a in ("shot", "line", "tm"))
    at_shot, at_line, at_tm = (lax.axis_index(a) for a in ("shot", "line", "tm"))
    block_lines = block // RPL
    length = window * n_tm
    shots = shots_here * n_shot
    sections = station_portion_tallies.shape[0]
    mixtures = measured_mixtures.shape[0]
    whole_lines = n_shot * n_line * n_tm == RPL
    assert shots_here == 1 and (whole_lines or n_shot == RPL)
    if whole_lines:
        axes = ("shot", "line", "tm")
        piece_lines, lines, blocks = block_lines, block_lines * n_line, n_line
        position = (at_shot * n_line + at_line) * n_tm + at_tm
        first_line = 0
    else:
        axes = ("shot", "tm")
        piece_lines = lines = block_lines // n_tm
        blocks, position = 1, at_shot
        first_line = at_tm * lines
    turns = [(s, a, b) for s in range(n_shot) for a in range(blocks) for b in range(n_tm)]
    plan = Plan(
        whole_lines=whole_lines,
        shots=shots,
        lines=lines,
        block_lines=block_lines,
        blocks=blocks,
        sections=sections,
        mixtures=mixtures,
        slabs=length // SLAB,
        pieces=[(s * lines + a * block_lines, b * window, piece_lines, window) for s, a, b in turns],
        spots=[s * n_tm + b for s, a, b in turns],
    )
    place = jnp.stack([jnp.asarray(v, jnp.int32) for v in [position, first_line, at_shot * n_tm + at_tm]])

    share = length // (n_shot * n_tm)
    if whole_lines:
        assert share % SLAB == 0
        leaving = run_pack(plan, place, initial_guess.reshape(block, window), measured_mixtures, share)
    else:
        grid = initial_guess.reshape(n_tm, lines, RPL, window)
        leaving = grid.transpose(2, 0, 1, 3).reshape(RPL * n_tm, lines, window)
    arrived = lax.all_to_all(leaving, axes, split_axis=0, concat_axis=0, tiled=True)

    nets = (
        source_entry_kernel.transpose(1, 0, 2),
        source_spaced_kernel,
        source_exit_kernel,
        source_inner_offsets,
        station_entry_kernel.transpose(1, 0, 2),
        station_spaced_kernel,
        station_exit_kernel,
        station_inner_offsets,
    )
    shot_weights, station_weights = run_prepare(nets)
    shot_weights = (*shot_weights, source_inner_offsets)
    station_weights = (*station_weights, station_inner_offsets)
    small = (place, station_portion_tallies, launch_lags, source_launch_order, learned_pace_factors)
    split = whole_lines and piece_lines % 8 == 0
    if whole_lines:
        mixes = arrived
    else:
        grid = measured_mixtures.reshape(mixtures, n_tm, lines, RPL, length)
        mixes = lax.dynamic_slice(
            grid, (0, at_tm, 0, position, 0), (mixtures, 1, lines, 1, length)
        ).reshape(mixtures, lines, length)
    if split:
        source = arrived
    else:
        source = arrived.reshape(n_shot, blocks, n_tm, piece_lines, -1)[..., :window].transpose(0, 1, 3, 2, 4)
        source = source.reshape(plan.rows, length)

    def edges_of(current):
        if whole_lines:
            return None
        size = n_line * n_tm
        grid = current.reshape(shots, lines, length)
        up = [(i, i + 1) for i in range(size - 1)]
        down = [(j, i) for i, j in up]
        above = lax.ppermute(grid[:, -1], ("line", "tm"), up)
        below = lax.ppermute(grid[:, 0], ("line", "tm"), down)
        wide = jnp.broadcast_to(jnp.stack([above, below])[:, :, None, :], (2, shots, lines, length))
        return wide.reshape(2, plan.rows, length)

    def shared(energy):
        for axis in axes[::-1]:
            size = lax.axis_size(axis)
            step = 1
            while step < size:
                energy = energy + lax.ppermute(energy, axis, [(i, i ^ step) for i in range(size)])
                step *= 2
        return energy

    current, energy = run_stage(
        plan, small, source, shot=(edges_of(source), shot_weights), split_in=split, name="shot_pass"
    )
    for i in range(ITERS):
        station = (i, shared(energy), mixes, station_weights)
        if i == ITERS - 1:
            (current,) = run_stage(plan, small, current, station=station, split_out=split, name="station_pass")
        elif whole_lines:
            current, energy = run_stage(
                plan, small, current, station=station, shot=(None, shot_weights), name="station_and_shot_pass"
            )
        else:
            (current,) = run_stage(plan, small, current, station=station, name="station_pass")
            current, energy = run_stage(plan, small, current, shot=(edges_of(current), shot_weights), name="shot_pass")
    if not split:
        current = current.reshape(n_shot, blocks, piece_lines, n_tm, window).transpose(0, 1, 3, 2, 4)
        current = current.reshape(len(turns), piece_lines, window)
    back = lax.all_to_all(current, axes, split_axis=0, concat_axis=0, tiled=True)
    if whole_lines:
        back = back.transpose(1, 0, 2)
    else:
        back = back.reshape(RPL, n_tm, lines, window).transpose(1, 2, 0, 3)
    return back.reshape(shots_here, block, window)


def solution(mesh):
    placed = (P(("group", "shot"), "line", "tm"), P("group", "line", None), P("group"), P("group"), P("group"))
    return jax.shard_map(
        per_device,
        mesh=mesh,
        in_specs=placed + (P(),) * 9,
        out_specs=P(("group", "shot"), "line", "tm"),
        check_vma=False,
    )
```

```python
import functools

import jax
import jax.numpy as jnp
import numpy as np
from jax import lax
from jax.experimental import pallas as pl
from jax.experimental.pallas import tpu as pltpu
from jax.sharding import PartitionSpec as P

RPL = 16
DMAX = 128
ITERS = 2
EPSILON = 1e-05

SLAB = 128
HALF = 64
FEAT = 64
GROUP = 4
WIDE = GROUP * FEAT
QS = SLAB // (2 * GROUP)
QH = QS // 2
ONES = 3 * HALF + 6
VMEM_LIMIT = 53 * 1024 * 1024
VMEM_FULL = 63 * 1024 * 1024

BF = jnp.bfloat16
F32 = jnp.float32


def entry_selector():
    picks = np.zeros((QH, WIDE, GROUP, 4, 8), np.float32)
    for j in range(3):
        picks[:, ONES + j, :, 3, j] = 1
    for q in range(QH):
        for p in range(GROUP):
            for j in range(4):
                i = 2 * (GROUP * q + p) + j - 1
                for c in range(3):
                    if i < 0:
                        lane = 3 * HALF + 2 * c
                    elif i >= HALF:
                        lane = 3 * HALF + 2 * c + 1
                    else:
                        lane = c * HALF + i
                    picks[q, lane, p, c, j] = 1
    return picks.reshape(QH * WIDE, GROUP * 4 * 8)


def exit_selector():
    picks = np.zeros((QS + 2, SLAB, SLAB), np.float32)
    for q in range(QS):
        for p in range(GROUP):
            for j in range(4):
                i = 2 * (GROUP * q + p) + j - 1
                if i < 0:
                    picks[QS + 1, p * 8 + j, SLAB - 1] = 1
                elif i >= SLAB:
                    picks[QS, p * 8 + j, 0] = 1
                else:
                    picks[q, p * 8 + j, i] = 1
    return picks.reshape((QS + 2) * SLAB, SLAB)


def split_bias(bias):
    high = bias.astype(BF).astype(F32)
    middle = (bias - high).astype(BF).astype(F32)
    return high, middle, bias - high - middle


def prepare_kernel(*refs):
    sources, outs = refs[:10], refs[10:14]
    (rhs, cols), held, made = refs[14:16], refs[16:26], refs[26:30]
    done, sent = refs[30:32]
    copies = [pltpu.make_async_copy(src, dst, done.at[i]) for i, (src, dst) in enumerate(zip(sources, held))]
    for copy in copies:
        copy.start()
    for copy in copies:
        copy.wait()
    sel_in, sel_out = held[:2]
    for n in range(2):
        w_in, w_mid, w_out, bias = held[2 + 4 * n : 6 + 4 * n]
        o_in, o_out = made[2 * n : 2 * n + 2]
        leaving = [pltpu.make_async_copy(made[i], outs[i], sent.at[i]) for i in range(2 * n, 2 * n + 2)]
        rhs[...] = jnp.zeros_like(rhs)
        cols[...] = jnp.zeros_like(cols)
        parts = split_bias(bias[0:1, :])
        for p in range(GROUP):
            lanes = slice(p * FEAT, (p + 1) * FEAT)
            for c in range(3):
                rhs[p * 32 + c * 8 : p * 32 + c * 8 + 4, lanes] = w_in[c].astype(F32)
                rhs[p * 32 + 24 + c : p * 32 + 25 + c, lanes] = parts[c]
            cols[p * 8 : p * 8 + 4, lanes] = w_out[...].astype(F32)
        taps = rhs[...].astype(BF)
        for q in range(QH):
            part = sel_in[q * WIDE : (q + 1) * WIDE, :]
            o_in[q] = jnp.dot(part, taps, preferred_element_type=F32).astype(BF)
        back = jnp.transpose(cols[...]).astype(BF)
        for q in range(QS + 2):
            part = sel_out[q * SLAB : (q + 1) * SLAB, :]
            o_out[q] = jnp.dot(back, part, preferred_element_type=F32).astype(BF)
        leaving[1].start()
        o_in[QH:] = jnp.zeros((2, WIDE, WIDE), BF)
        for a, row in [(0, 0), (1, 1), (2, 2), (3, 3), (-2, 4), (-1, 5), (4, 6), (5, 7)]:
            for b in range(GROUP):
                if (a - b) % 2 == 0 and abs(a - b) <= 2:
                    o_in[QH + row // 4, row % 4 * FEAT : (row % 4 + 1) * FEAT, b * FEAT : (b + 1) * FEAT] = w_mid[
                        (a - b) // 2 + 1
                    ]
        leaving[0].start()
    for i in range(4):
        pltpu.make_async_copy(made[i], outs[i], sent.at[i]).wait()


def pack_kernel(plan, place, traces, mixes, packet, held, done):
    window = traces.shape[1]
    share = (packet.shape[2] - window) // mixes.shape[0]
    copies = [pltpu.make_async_copy(traces, held.at[:, 0:window], done.at[0])]
    at = pl.multiple_of(place[2] * share, share)
    for g in range(mixes.shape[0]):
        into = held.at[:, window + g * share : window + (g + 1) * share]
        copies.append(pltpu.make_async_copy(mixes.at[g, :, pl.ds(at, share)], into, done.at[g + 1]))
    for copy in copies:
        copy.start()
    block = traces.shape[0]
    row = lax.broadcasted_iota(jnp.int32, (block, block), 0)
    col = lax.broadcasted_iota(jnp.int32, (block, block), 1)
    lines = plan.block_lines
    order = (col == (row % lines) * RPL + row // lines).astype(F32).astype(BF)
    for copy in copies:
        copy.wait()
    moved = jnp.dot(order, held[...], preferred_element_type=F32)
    packet[...] = moved.reshape(packet.shape).astype(BF)


def split_index(value, size):
    if size & (size - 1):
        return value // size, value % size
    return value >> (size.bit_length() - 1), value & (size - 1)


def section_map(plan, place, tallies):
    shape = (plan.rows, SLAB)
    lane = lax.broadcasted_iota(jnp.int32, shape, 1)
    line = split_index(lax.broadcasted_iota(jnp.int32, shape, 0), plan.lines)[1] + place[1]
    block, line = split_index(line, plan.block_lines)
    spot = line * RPL + place[0]
    low = jnp.zeros(shape, jnp.int32)
    high = jnp.zeros(shape, jnp.int32)
    count = jnp.zeros(shape, jnp.int32)
    start = jnp.int32(0)
    for p in range(plan.sections):
        amount = tallies[p]
        for b in range(plan.blocks):
            here = lane == b * plan.sections + p
            low = jnp.where(here, start, low)
            high = jnp.where(here, start + amount, high)
            count = jnp.where(here, amount, count)
        start = start + amount
    member = (spot >= low) & (spot < high) & (split_index(lane, plan.sections)[0] == block)
    return member, count


def shifted(values, by, ok, edge):
    return jnp.where(ok, pltpu.roll(values, by % values.shape[0], 0), edge)


def pack_inputs(plan, channels, packed):
    lane = lax.broadcasted_iota(jnp.int32, (plan.rows, SLAB), 1)
    low = lane < HALF
    ones = ((lane >= ONES - SLAB) & (lane < ONES - SLAB + 3)).astype(F32)
    slabs = [[x[:, t * SLAB : (t + 1) * SLAB] for t in range(plan.slabs)] for x in channels]
    far = [[pltpu.roll(s, HALF + 1 + 2 * c, 1) for s in slabs[c]] for c in range(3)]
    for t in range(plan.slabs):
        v = [slabs[c][t] for c in range(3)]
        w = [pltpu.roll(s, HALF, 1) for s in v]
        even = jnp.where(low, v[2], ones)
        odd = jnp.where(low, w[2], ones)
        for c in range(3):
            left, right = lane == HALF + 2 * c, lane == HALF + 2 * c + 1
            near = pltpu.roll(v[c], 1 + 2 * c, 1)
            even = jnp.where(right, near, even)
            odd = jnp.where(left, near, odd)
            if t > 0:
                even = jnp.where(left, far[c][t - 1], even)
            if t < plan.slabs - 1:
                odd = jnp.where(right, far[c][t + 1], odd)
        packed[0, t, :, 0:SLAB] = jnp.where(low, v[0], w[1]).astype(BF)
        packed[0, t, :, SLAB:WIDE] = even.astype(BF)
        packed[1, t, :, 0:SLAB] = jnp.where(low, w[0], v[1]).astype(BF)
        packed[1, t, :, SLAB:WIDE] = odd.astype(BF)


def network(plan, weights, bias, scratch, ready=(lambda: None, lambda: None)):
    w_in, w_out = weights
    packed, hidden, total = scratch
    many, rows = plan.slabs * plan.rows, plan.rows
    grid = (plan.slabs, rows, WIDE)
    pitch = plan.slabs + 2
    bias_two = jnp.concatenate([bias[1:2, :]] * GROUP, axis=1)

    def first(q):
        value = jnp.dot(packed[q // QH].reshape(many, WIDE), w_in[q % QH], preferred_element_type=F32)
        hidden[pl.ds(q * pitch + 1, plan.slabs)] = jnp.maximum(value.astype(BF), 0).reshape(grid)

    def second(q, left_at, right_at):
        middle = hidden[pl.ds(q * pitch + 1, plan.slabs)]
        left = hidden[pl.ds(left_at, plan.slabs), :, SLAB:WIDE]
        right = hidden[pl.ds(right_at, plan.slabs), :, 0:SLAB]
        window = jnp.concatenate([middle, left, right], axis=2).reshape(many, 2 * WIDE)
        value = jnp.dot(window, w_in[QH:].reshape(2 * WIDE, WIDE), preferred_element_type=F32)
        return jnp.maximum((value + bias_two).astype(BF), 0)

    def onto(layer, q):
        return jnp.dot(layer, w_out[q], preferred_element_type=F32).reshape(plan.slabs, rows, SLAB)

    edge = jnp.zeros((rows, WIDE), BF)
    hidden[(QS - 1) * pitch] = edge
    hidden[pitch - 1] = edge
    ready[0]()
    for q in range(QS):
        first(q)
    ready[1]()

    layer = second(0, (QS - 1) * pitch, pitch + 1)
    total[...] = onto(layer, 0)
    total[0 : plan.slabs - 1] += onto(layer, QS + 1)[1:]

    for q in range(1, QS - 1):
        total[...] += onto(second(q, (q - 1) * pitch + 1, (q + 1) * pitch + 1), q)
    layer = second(QS - 1, (QS - 2) * pitch + 1, 2)
    total[...] += onto(layer, QS - 1)
    total[1 : plan.slabs] += onto(layer, QS)[: plan.slabs - 1]


def waits(fetches):
    return fetches[0].wait, fetches[1].wait


def add_total(plan, now, total, scale=None):
    for t in range(plan.slabs):
        lanes = slice(t * SLAB, (t + 1) * SLAB)
        more = total[t] if scale is None else scale * total[t]
        now[:, lanes] = (now[:, lanes] + more).astype(BF).astype(F32)


def shot_stage(plan, place, tallies, edges, weights, fetches, bias, now, scratch, energy):
    x = now[...]
    line = split_index(lax.broadcasted_iota(jnp.int32, x.shape, 0), plan.lines)[1]
    above = 0.0 if edges is None else edges[0].astype(F32)
    below = 0.0 if edges is None else edges[1].astype(F32)
    channels = [
        shifted(x, 1, line > 0, above),
        x,
        shifted(x, -1, line < plan.lines - 1, below),
    ]
    pack_inputs(plan, channels, scratch[0])
    network(plan, weights, bias, scratch, waits(fetches))
    add_total(plan, now, scratch[2])
    power = jnp.zeros((plan.rows, SLAB), F32)
    for t in range(plan.slabs):
        piece = now[:, t * SLAB : (t + 1) * SLAB]
        power = power + piece * piece
    member, _ = section_map(plan, place, tallies)
    each = jnp.where(member, jnp.sum(power, axis=1, keepdims=True), 0.0)
    energy[...] = jnp.sum(each, axis=0, keepdims=True)


def station_stage(
    plan, place, tallies, lags, order, pace, energies, mixes, weights, fetches, bias, now, scratch, blend
):
    member, count = section_map(plan, place, tallies)
    totals = energies[...]
    denominator = jnp.maximum(count, 1) * (plan.shots * plan.slabs * SLAB)
    level = jnp.sqrt(totals / denominator.astype(F32) + EPSILON)
    rms = jnp.sum(jnp.where(member, level, 0.0), axis=1, keepdims=True)
    x = (now[...] / rms).astype(BF).astype(F32)
    row = lax.broadcasted_iota(jnp.int32, x.shape, 0)
    channels = [
        shifted(x, plan.lines, row >= plan.lines, 0.0),
        x,
        shifted(x, -plan.lines, row < plan.rows - plan.lines, 0.0),
    ]
    pack_inputs(plan, channels, scratch[0])
    network(plan, weights, bias, scratch, waits(fetches))
    add_total(plan, now, scratch[2], rms)

    fired, misfit = blend
    lane = lax.broadcasted_iota(jnp.int32, (plan.lines, SLAB), 1)
    mixtures = misfit.shape[0]
    per = plan.shots // mixtures
    if plan.whole_lines:
        for n, (row, _, rows, lanes) in enumerate(plan.pieces):
            share = (mixes.shape[2] - lanes) // mixtures
            spot = plan.spots[n] * share
            for g in range(mixtures):
                piece = mixes[n, :, lanes + g * share : lanes + (g + 1) * share]
                misfit[g, row % plan.lines : row % plan.lines + rows, spot : spot + share] = piece.astype(F32)
    else:
        misfit[...] = mixes[...].astype(F32)
    for s in range(plan.shots):
        lag = lags[s]
        before = jnp.zeros((plan.lines, SLAB), F32)
        for t in range(plan.slabs):
            lanes = slice(t * SLAB, (t + 1) * SLAB)
            turned = pltpu.roll(now[s * plan.lines : (s + 1) * plan.lines, lanes], lag, 1)
            fired[s, :, lanes] = jnp.where(lane < lag, before, turned)
            before = turned
    for g in range(mixtures):
        value = fired[order[g * per]]
        for k in range(1, per):
            value = value + fired[order[g * per + k]]
        misfit[g] = value - misfit[g]
    for s in range(plan.shots):
        lag = lags[s]
        spot = jnp.int32(0)
        for k in range(plan.shots):
            spot = spot + jnp.where(order[k] == s, k, 0)
        which = spot // per
        back = (DMAX - lag) % DMAX
        after = jnp.zeros((plan.lines, SLAB), F32)
        rows = slice(s * plan.lines, (s + 1) * plan.lines)
        for t in range(plan.slabs - 1, -1, -1):
            lanes = slice(t * SLAB, (t + 1) * SLAB)
            turned = pltpu.roll(misfit[which, :, lanes], back, 1)
            pulled = jnp.where(lane < DMAX - lag, turned, after)
            after = turned
            now[rows, lanes] = (now[rows, lanes] - pace * pulled).astype(BF).astype(F32)


def stage_kernel(plan, station_round, with_shot, has_edges, split_in, split_out, *refs):
    refs = list(refs)
    take = lambda n: [refs.pop(0) for _ in range(n)]
    place, tallies, lags, order, paces, source = take(6)
    station = station_round is not None
    if station:
        energies, mixes, *station_weights, station_bias = take(5)
    edges = None
    if with_shot:
        if has_edges:
            (edges,) = take(1)
        *shot_weights, shot_bias = take(3)
    (result,) = take(1)
    if with_shot:
        (energy,) = take(1)
    now, packed, hidden, total = take(4)
    scratch = (packed, hidden, total)
    arrived = refs.pop()
    sets = ([station_weights] if station else []) + ([shot_weights] if with_shot else [])
    held = [[refs.pop(0) for _ in range(2)] for _ in sets]
    fetches = [
        [pltpu.make_async_copy(w, h, arrived.at[2 * n + i]) for i, (w, h) in enumerate(zip(sets[n], held[n]))]
        for n in range(len(sets))
    ]
    for fetch in sum(fetches, []):
        fetch.start()
    if split_in:
        for n, (row, lane, rows, lanes) in enumerate(plan.pieces):
            now[row : row + rows, lane : lane + lanes] = source[n, :, 0:lanes].astype(F32)
    else:
        now[...] = source[...].astype(F32)
    if station:
        station_stage(
            plan,
            place,
            tallies,
            lags,
            order,
            paces[station_round],
            energies,
            mixes,
            held[0],
            fetches[0],
            station_bias,
            now,
            scratch,
            refs,
        )
    if with_shot:
        shot_stage(plan, place, tallies, edges, held[-1], fetches[-1], shot_bias, now, scratch, energy)
    if split_out:
        for n, (row, lane, rows, lanes) in enumerate(plan.pieces):
            result[n] = now[row : row + rows, lane : lane + lanes].astype(BF)
    else:
        result[...] = now[...].astype(BF)


SMEM = pl.BlockSpec(memory_space=pltpu.SMEM)
VMEM = pl.BlockSpec(memory_space=pltpu.VMEM)
HBM = pl.BlockSpec(memory_space=pltpu.HBM)


def run_stage(plan, small, source, station=None, shot=None, split_in=False, split_out=False, name="stage"):
    operands = [*small, source]
    station_round, has_edges = None, False
    macs = 0
    pass_macs = plan.rows * plan.slabs * QS * WIDE * (WIDE * 3 + SLAB)
    if station is not None:
        station_round, energies, mixes, weights = station
        operands += [energies, mixes, *weights]
        macs += pass_macs
    if shot is not None:
        edges, weights = shot
        has_edges = edges is not None
        operands += ([edges] if has_edges else []) + list(weights)
        macs += pass_macs
    specs = [HBM if getattr(o, "ndim", 0) >= 2 and o.dtype == BF and o.shape[-2] == WIDE else VMEM for o in operands]
    specs[: len(small)] = [SMEM] * len(small)
    fetched = [o for o, spec in zip(operands, specs) if spec is HBM]
    length = plan.slabs * SLAB
    if split_out:
        _, _, rows, lanes = plan.pieces[0]
        shapes = [jax.ShapeDtypeStruct((len(plan.pieces), rows, lanes), BF)]
    else:
        shapes = [jax.ShapeDtypeStruct((plan.rows, length), BF)]
    if shot is not None:
        shapes.append(jax.ShapeDtypeStruct((1, SLAB), F32))
    scratch = [
        pltpu.VMEM((plan.rows, length), F32),
        pltpu.VMEM((2, plan.slabs, plan.rows, WIDE), BF),
        pltpu.VMEM((QS * (plan.slabs + 2), plan.rows, WIDE), BF),
        pltpu.VMEM((plan.slabs, plan.rows, SLAB), F32),
    ]
    scratch += [pltpu.VMEM(w.shape, w.dtype) for w in fetched]
    if station is not None:
        scratch += [
            pltpu.VMEM((plan.shots, plan.lines, length), F32),
            pltpu.VMEM((plan.mixtures, plan.lines, length), F32),
        ]
    scratch += [pltpu.SemaphoreType.DMA((len(fetched),))]
    return pl.pallas_call(
        functools.partial(stage_kernel, plan, station_round, shot is not None, has_edges, split_in, split_out),
        out_shape=shapes,
        in_specs=specs,
        out_specs=[VMEM] * len(shapes),
        scratch_shapes=scratch,
        compiler_params=pltpu.CompilerParams(vmem_limit_bytes=VMEM_LIMIT),
        cost_estimate=pl.CostEstimate(flops=2 * macs, bytes_accessed=1 << 20, transcendentals=0),
        name=name,
    )(*operands)


def run_prepare(nets):
    shapes = []
    for _ in range(2):
        shapes += [
            jax.ShapeDtypeStruct((QH + 2, WIDE, WIDE), BF),
            jax.ShapeDtypeStruct((QS + 2, WIDE, SLAB), BF),
        ]
    operands = [jnp.asarray(entry_selector(), BF), jnp.asarray(exit_selector(), BF), *nets]
    scratch = [pltpu.VMEM((SLAB, WIDE), F32), pltpu.VMEM((SLAB, WIDE), F32)]
    scratch += [pltpu.VMEM(o.shape, o.dtype) for o in operands]
    scratch += [pltpu.VMEM(o.shape, o.dtype) for o in shapes]
    scratch += [pltpu.SemaphoreType.DMA((len(operands),)), pltpu.SemaphoreType.DMA((len(shapes),))]
    outs = pl.pallas_call(
        prepare_kernel,
        out_shape=shapes,
        in_specs=[HBM] * len(operands),
        out_specs=[HBM] * len(shapes),
        scratch_shapes=scratch,
        compiler_params=pltpu.CompilerParams(vmem_limit_bytes=VMEM_FULL),
        cost_estimate=pl.CostEstimate(flops=2 * 2 * 8192 * WIDE * SLAB, bytes_accessed=8 << 20, transcendentals=0),
        name="prepare",
    )(*operands)
    return outs[0:2], outs[2:4]


def run_pack(plan, place, traces, mixtures, share):
    groups, block, _ = mixtures.shape
    width = traces.shape[1] + groups * share
    return pl.pallas_call(
        functools.partial(pack_kernel, plan),
        out_shape=jax.ShapeDtypeStruct((RPL, plan.block_lines, width), BF),
        in_specs=[SMEM, HBM, HBM],
        out_specs=VMEM,
        scratch_shapes=[pltpu.VMEM((block, width), BF), pltpu.SemaphoreType.DMA((groups + 1,))],
        compiler_params=pltpu.CompilerParams(vmem_limit_bytes=VMEM_FULL),
        cost_estimate=pl.CostEstimate(flops=2 * block * block * width, bytes_accessed=1 << 20, transcendentals=0),
        name="pack",
    )(place, traces, mixtures)


class Plan:
    def __init__(self, **sizes):
        self.__dict__.update(sizes)
        self.rows = self.shots * self.lines


def per_device(
    initial_guess,
    measured_mixtures,
    launch_lags,
    source_launch_order,
    station_portion_tallies,
    source_entry_kernel,
    source_spaced_kernel,
    source_exit_kernel,
    source_inner_offsets,
    station_entry_kernel,
    station_spaced_kernel,
    station_exit_kernel,
    station_inner_offsets,
    learned_pace_factors,
):
    shots_here, block, window = initial_guess.shape
    n_shot, n_line, n_tm = (lax.axis_size(a) for a in ("shot", "line", "tm"))
    at_shot, at_line, at_tm = (lax.axis_index(a) for a in ("shot", "line", "tm"))
    block_lines = block // RPL
    length = window * n_tm
    shots = shots_here * n_shot
    sections = station_portion_tallies.shape[0]
    mixtures = measured_mixtures.shape[0]
    whole_lines = n_shot * n_line * n_tm == RPL
    assert shots_here == 1 and (whole_lines or n_shot == RPL)
    if whole_lines:
        axes = ("shot", "line", "tm")
        piece_lines, lines, blocks = block_lines, block_lines * n_line, n_line
        position = (at_shot * n_line + at_line) * n_tm + at_tm
        first_line = 0
    else:
        axes = ("shot", "tm")
        piece_lines = lines = block_lines // n_tm
        blocks, position = 1, at_shot
        first_line = at_tm * lines
    turns = [(s, a, b) for s in range(n_shot) for a in range(blocks) for b in range(n_tm)]
    plan = Plan(
        whole_lines=whole_lines,
        shots=shots,
        lines=lines,
        block_lines=block_lines,
        blocks=blocks,
        sections=sections,
        mixtures=mixtures,
        slabs=length // SLAB,
        pieces=[(s * lines + a * block_lines, b * window, piece_lines, window) for s, a, b in turns],
        spots=[s * n_tm + b for s, a, b in turns],
    )
    place = jnp.stack([jnp.asarray(v, jnp.int32) for v in [position, first_line, at_shot * n_tm + at_tm]])

    share = length // (n_shot * n_tm)
    if whole_lines:
        assert share % SLAB == 0
        leaving = run_pack(plan, place, initial_guess.reshape(block, window), measured_mixtures, share)
    else:
        grid = initial_guess.reshape(n_tm, lines, RPL, window)
        leaving = grid.transpose(2, 0, 1, 3).reshape(RPL * n_tm, lines, window)
    arrived = lax.all_to_all(leaving, axes, split_axis=0, concat_axis=0, tiled=True)

    nets = (
        source_entry_kernel.transpose(1, 0, 2),
        source_spaced_kernel,
        source_exit_kernel,
        source_inner_offsets,
        station_entry_kernel.transpose(1, 0, 2),
        station_spaced_kernel,
        station_exit_kernel,
        station_inner_offsets,
    )
    shot_weights, station_weights = run_prepare(nets)
    shot_weights = (*shot_weights, source_inner_offsets)
    station_weights = (*station_weights, station_inner_offsets)
    small = (place, station_portion_tallies, launch_lags, source_launch_order, learned_pace_factors)
    split = whole_lines and piece_lines % 8 == 0
    if whole_lines:
        mixes = arrived
    else:
        grid = measured_mixtures.reshape(mixtures, n_tm, lines, RPL, length)
        mixes = lax.dynamic_slice(
            grid, (0, at_tm, 0, position, 0), (mixtures, 1, lines, 1, length)
        ).reshape(mixtures, lines, length)
    if split:
        source = arrived
    else:
        source = arrived.reshape(n_shot, blocks, n_tm, piece_lines, -1)[..., :window].transpose(0, 1, 3, 2, 4)
        source = source.reshape(plan.rows, length)

    def edges_of(current):
        if whole_lines:
            return None
        size = n_line * n_tm
        grid = current.reshape(shots, lines, length)
        up = [(i, i + 1) for i in range(size - 1)]
        down = [(j, i) for i, j in up]
        above = lax.ppermute(grid[:, -1], ("line", "tm"), up)
        below = lax.ppermute(grid[:, 0], ("line", "tm"), down)
        wide = jnp.broadcast_to(jnp.stack([above, below])[:, :, None, :], (2, shots, lines, length))
        return wide.reshape(2, plan.rows, length)

    def shared(energy):
        for axis in axes[::-1]:
            size = lax.axis_size(axis)
            if size <= 4:
                others = [lax.ppermute(energy, axis, [(i, i ^ d) for i in range(size)]) for d in range(1, size)]
                energy = sum(others, energy)
                continue
            step = 1
            while step < size:
                energy = energy + lax.ppermute(energy, axis, [(i, i ^ step) for i in range(size)])
                step *= 2
        return energy

    current, energy = run_stage(
        plan, small, source, shot=(edges_of(source), shot_weights), split_in=split, name="shot_pass"
    )
    for i in range(ITERS):
        station = (i, shared(energy), mixes, station_weights)
        if i == ITERS - 1:
            (current,) = run_stage(plan, small, current, station=station, split_out=split, name="station_pass")
        elif whole_lines:
            current, energy = run_stage(
                plan, small, current, station=station, shot=(None, shot_weights), name="station_and_shot_pass"
            )
        else:
            (current,) = run_stage(plan, small, current, station=station, name="station_pass")
            current, energy = run_stage(plan, small, current, shot=(edges_of(current), shot_weights), name="shot_pass")
    if not split:
        current = current.reshape(n_shot, blocks, piece_lines, n_tm, window).transpose(0, 1, 3, 2, 4)
        current = current.reshape(len(turns), piece_lines, window)
    back = lax.all_to_all(current, axes, split_axis=0, concat_axis=0, tiled=True)
    if whole_lines:
        back = back.transpose(1, 0, 2)
    else:
        back = back.reshape(RPL, n_tm, lines, window).transpose(1, 2, 0, 3)
    return back.reshape(shots_here, block, window)


def solution(mesh):
    placed = (P(("group", "shot"), "line", "tm"), P("group", "line", None), P("group"), P("group"), P("group"))
    return jax.shard_map(
        per_device,
        mesh=mesh,
        in_specs=placed + (P(),) * 9,
        out_specs=P(("group", "shot"), "line", "tm"),
        check_vma=False,
    )
```

```python
import functools

import jax
import jax.numpy as jnp
import numpy as np
from jax import lax
from jax.experimental import pallas as pl
from jax.experimental.pallas import tpu as pltpu
from jax.sharding import PartitionSpec as P

RPL = 16
DMAX = 128
ITERS = 2
EPSILON = 1e-05

SLAB = 128
HALF = 64
FEAT = 64
GROUP = 4
WIDE = GROUP * FEAT
QS = SLAB // (2 * GROUP)
QH = QS // 2
ONES = 3 * HALF + 6
VMEM_LIMIT = 53 * 1024 * 1024
VMEM_FULL = 63 * 1024 * 1024

BF = jnp.bfloat16
F32 = jnp.float32


def entry_selector():
    picks = np.zeros((QH, WIDE, GROUP, 4, 8), np.float32)
    for j in range(3):
        picks[:, ONES + j, :, 3, j] = 1
    for q in range(QH):
        for p in range(GROUP):
            for j in range(4):
                i = 2 * (GROUP * q + p) + j - 1
                for c in range(3):
                    if i < 0:
                        lane = 3 * HALF + 2 * c
                    elif i >= HALF:
                        lane = 3 * HALF + 2 * c + 1
                    else:
                        lane = c * HALF + i
                    picks[q, lane, p, c, j] = 1
    return picks.reshape(QH * WIDE, GROUP * 4 * 8)


def exit_selector():
    picks = np.zeros((QS + 2, SLAB, SLAB), np.float32)
    for q in range(QS):
        for p in range(GROUP):
            for j in range(4):
                i = 2 * (GROUP * q + p) + j - 1
                if i < 0:
                    picks[QS + 1, p * 8 + j, SLAB - 1] = 1
                elif i >= SLAB:
                    picks[QS, p * 8 + j, 0] = 1
                else:
                    picks[q, p * 8 + j, i] = 1
    return picks.reshape((QS + 2) * SLAB, SLAB)


def split_bias(bias):
    high = bias.astype(BF).astype(F32)
    middle = (bias - high).astype(BF).astype(F32)
    return high, middle, bias - high - middle


def prepare_kernel(*refs):
    sources, outs = refs[:10], refs[10:14]
    (rhs, cols), held, made = refs[14:16], refs[16:26], refs[26:30]
    done, sent = refs[30:32]
    copies = [pltpu.make_async_copy(src, dst, done.at[i]) for i, (src, dst) in enumerate(zip(sources, held))]
    for copy in copies:
        copy.start()
    for copy in copies:
        copy.wait()
    sel_in, sel_out = held[:2]
    for n in range(2):
        w_in, w_mid, w_out, bias = held[2 + 4 * n : 6 + 4 * n]
        o_in, o_out = made[2 * n : 2 * n + 2]
        leaving = [pltpu.make_async_copy(made[i], outs[i], sent.at[i]) for i in range(2 * n, 2 * n + 2)]
        rhs[...] = jnp.zeros_like(rhs)
        cols[...] = jnp.zeros_like(cols)
        parts = split_bias(bias[0:1, :])
        for p in range(GROUP):
            lanes = slice(p * FEAT, (p + 1) * FEAT)
            for c in range(3):
                rhs[p * 32 + c * 8 : p * 32 + c * 8 + 4, lanes] = w_in[c].astype(F32)
                rhs[p * 32 + 24 + c : p * 32 + 25 + c, lanes] = parts[c]
            cols[p * 8 : p * 8 + 4, lanes] = w_out[...].astype(F32)
        taps = rhs[...].astype(BF)
        for q in range(QH):
            part = sel_in[q * WIDE : (q + 1) * WIDE, :]
            o_in[q] = jnp.dot(part, taps, preferred_element_type=F32).astype(BF)
        back = jnp.transpose(cols[...]).astype(BF)
        for q in range(QS + 2):
            part = sel_out[q * SLAB : (q + 1) * SLAB, :]
            o_out[q] = jnp.dot(back, part, preferred_element_type=F32).astype(BF)
        leaving[1].start()
        o_in[QH:] = jnp.zeros((2, WIDE, WIDE), BF)
        for a, row in [(0, 0), (1, 1), (2, 2), (3, 3), (-2, 4), (-1, 5), (4, 6), (5, 7)]:
            for b in range(GROUP):
                if (a - b) % 2 == 0 and abs(a - b) <= 2:
                    o_in[QH + row // 4, row % 4 * FEAT : (row % 4 + 1) * FEAT, b * FEAT : (b + 1) * FEAT] = w_mid[
                        (a - b) // 2 + 1
                    ]
        leaving[0].start()
    for i in range(4):
        pltpu.make_async_copy(made[i], outs[i], sent.at[i]).wait()


def pack_kernel(plan, place, traces, mixes, packet, held, mixed, done):
    block, window = traces.shape
    groups = mixes.shape[0]
    share = packet.shape[2]
    copies = [pltpu.make_async_copy(traces, held, done.at[0])]
    at = pl.multiple_of(place[2] * share, share)
    for g in range(groups):
        into = mixed.at[g * block : (g + 1) * block, :]
        copies.append(pltpu.make_async_copy(mixes.at[g, :, pl.ds(at, share)], into, done.at[g + 1]))
    for copy in copies:
        copy.start()
    lines, each = plan.block_lines, plan.each
    row = lax.broadcasted_iota(jnp.int32, (block, block), 0)
    col = lax.broadcasted_iota(jnp.int32, (block, block), 1)
    spot, line = split_index(row, lines)
    order = (col == line * RPL + spot).astype(F32).astype(BF)
    rows = packet.shape[0] * groups * lines
    row = lax.broadcasted_iota(jnp.int32, (rows, groups * block), 0)
    col = lax.broadcasted_iota(jnp.int32, (rows, groups * block), 1)
    rest, line = split_index(row, lines)
    to, g = split_index(rest, groups)
    choose = (col == g * block + line * RPL + to * each + place[3]).astype(F32).astype(BF)
    for copy in copies:
        copy.wait()
    top = each * lines
    moved = jnp.dot(order, held[...], preferred_element_type=F32)
    packet[:, 0:top, :] = moved.reshape(packet.shape[0], top, share).astype(BF)
    moved = jnp.dot(choose, mixed[...], preferred_element_type=F32)
    packet[:, top:, :] = moved.reshape(packet.shape[0], groups * lines, share).astype(BF)


def split_index(value, size):
    if size & (size - 1):
        return value // size, value % size
    return value >> (size.bit_length() - 1), value & (size - 1)


def section_map(plan, place, tallies, stride):
    shape = (plan.rows, SLAB)
    lane = lax.broadcasted_iota(jnp.int32, shape, 1)
    apart, line = split_index(lax.broadcasted_iota(jnp.int32, shape, 0), plan.lines)
    block, line = split_index(line + place[1], plan.block_lines)
    spot = line * RPL + place[0] + apart * stride
    low = jnp.zeros(shape, jnp.int32)
    high = jnp.zeros(shape, jnp.int32)
    count = jnp.zeros(shape, jnp.int32)
    start = jnp.int32(0)
    for p in range(plan.sections):
        amount = tallies[p]
        for b in range(plan.blocks):
            here = lane == b * plan.sections + p
            low = jnp.where(here, start, low)
            high = jnp.where(here, start + amount, high)
            count = jnp.where(here, amount, count)
        start = start + amount
    member = (spot >= low) & (spot < high) & (split_index(lane, plan.sections)[0] == block)
    return member, count


def shifted(values, by, ok, edge):
    return jnp.where(ok, pltpu.roll(values, by % values.shape[0], 0), edge)


def pack_inputs(plan, channels, packed):
    lane = lax.broadcasted_iota(jnp.int32, (plan.rows, SLAB), 1)
    low = lane < HALF
    ones = ((lane >= ONES - SLAB) & (lane < ONES - SLAB + 3)).astype(F32)
    slabs = [[x[:, t * SLAB : (t + 1) * SLAB] for t in range(plan.slabs)] for x in channels]
    far = [[pltpu.roll(s, HALF + 1 + 2 * c, 1) for s in slabs[c]] for c in range(3)]
    for t in range(plan.slabs):
        v = [slabs[c][t] for c in range(3)]
        w = [pltpu.roll(s, HALF, 1) for s in v]
        even = jnp.where(low, v[2], ones)
        odd = jnp.where(low, w[2], ones)
        for c in range(3):
            left, right = lane == HALF + 2 * c, lane == HALF + 2 * c + 1
            near = pltpu.roll(v[c], 1 + 2 * c, 1)
            even = jnp.where(right, near, even)
            odd = jnp.where(left, near, odd)
            if t > 0:
                even = jnp.where(left, far[c][t - 1], even)
            if t < plan.slabs - 1:
                odd = jnp.where(right, far[c][t + 1], odd)
        packed[0, t, :, 0:SLAB] = jnp.where(low, v[0], w[1]).astype(BF)
        packed[0, t, :, SLAB:WIDE] = even.astype(BF)
        packed[1, t, :, 0:SLAB] = jnp.where(low, w[0], v[1]).astype(BF)
        packed[1, t, :, SLAB:WIDE] = odd.astype(BF)


def network(plan, weights, bias, scratch, ready=(lambda: None, lambda: None)):
    w_in, w_out = weights
    packed, hidden, total = scratch
    many, rows = plan.slabs * plan.rows, plan.rows
    grid = (plan.slabs, rows, WIDE)
    pitch = plan.slabs + 2
    bias_two = jnp.concatenate([bias[1:2, :]] * GROUP, axis=1)

    def first(q):
        value = jnp.dot(packed[q // QH].reshape(many, WIDE), w_in[q % QH], preferred_element_type=F32)
        hidden[pl.ds(q * pitch + 1, plan.slabs)] = jnp.maximum(value.astype(BF), 0).reshape(grid)

    def second(q, left_at, right_at):
        middle = hidden[pl.ds(q * pitch + 1, plan.slabs)]
        left = hidden[pl.ds(left_at, plan.slabs), :, SLAB:WIDE]
        right = hidden[pl.ds(right_at, plan.slabs), :, 0:SLAB]
        window = jnp.concatenate([middle, left, right], axis=2).reshape(many, 2 * WIDE)
        value = jnp.dot(window, w_in[QH:].reshape(2 * WIDE, WIDE), preferred_element_type=F32)
        return jnp.maximum((value + bias_two).astype(BF), 0)

    def onto(layer, q):
        return jnp.dot(layer, w_out[q], preferred_element_type=F32).reshape(plan.slabs, rows, SLAB)

    edge = jnp.zeros((rows, WIDE), BF)
    hidden[(QS - 1) * pitch] = edge
    hidden[pitch - 1] = edge
    ready[0]()
    for q in range(QS):
        first(q)
    ready[1]()

    layer = second(0, (QS - 1) * pitch, pitch + 1)
    total[...] = onto(layer, 0)
    total[0 : plan.slabs - 1] += onto(layer, QS + 1)[1:]

    for q in range(1, QS - 1):
        total[...] += onto(second(q, (q - 1) * pitch + 1, (q + 1) * pitch + 1), q)
    layer = second(QS - 1, (QS - 2) * pitch + 1, 2)
    total[...] += onto(layer, QS - 1)
    total[1 : plan.slabs] += onto(layer, QS)[: plan.slabs - 1]


def waits(fetches):
    return fetches[0].wait, fetches[1].wait


def add_total(plan, now, total, scale=None):
    for t in range(plan.slabs):
        lanes = slice(t * SLAB, (t + 1) * SLAB)
        more = total[t] if scale is None else scale * total[t]
        now[:, lanes] = (now[:, lanes] + more).astype(BF).astype(F32)


def shot_stage(plan, place, tallies, stride, edges, weights, fetches, bias, now, scratch, energy):
    x = now[...]
    row = lax.broadcasted_iota(jnp.int32, (2 * plan.rows, plan.rows), 0)
    col = lax.broadcasted_iota(jnp.int32, (2 * plan.rows, plan.rows), 1)
    line = split_index(col, plan.lines)[1]
    before = (row == col + 1) & (line < plan.lines - 1)
    after = (row == col + plan.rows - 1) & (line > 0)
    moved = jnp.dot((before | after).astype(F32).astype(BF), x.astype(BF), preferred_element_type=F32)
    channels = [moved[: plan.rows], x, moved[plan.rows :]]
    if edges is not None:
        channels[0] += edges[0].astype(F32)
        channels[2] += edges[1].astype(F32)
    pack_inputs(plan, channels, scratch[0])
    network(plan, weights, bias, scratch, waits(fetches))
    add_total(plan, now, scratch[2])
    power = jnp.zeros((plan.rows, SLAB), F32)
    for t in range(plan.slabs):
        piece = now[:, t * SLAB : (t + 1) * SLAB]
        power = power + piece * piece
    member, _ = section_map(plan, place, tallies, stride)
    each = jnp.where(member, jnp.sum(power, axis=1, keepdims=True), 0.0)
    energy[...] = jnp.sum(each, axis=0, keepdims=True)


def station_stage(
    plan, place, tallies, lags, order, pace, energies, mixes, weights, fetches, bias, now, scratch, blend
):
    member, count = section_map(plan, place, tallies, 0)
    totals = energies[...]
    denominator = jnp.maximum(count, 1) * (plan.shots * plan.slabs * SLAB)
    level = jnp.sqrt(totals / denominator.astype(F32) + EPSILON)
    rms = jnp.sum(jnp.where(member, level, 0.0), axis=1, keepdims=True)
    x = (now[...] / rms).astype(BF).astype(F32)
    row = lax.broadcasted_iota(jnp.int32, x.shape, 0)
    channels = [
        shifted(x, plan.lines, row >= plan.lines, 0.0),
        x,
        shifted(x, -plan.lines, row < plan.rows - plan.lines, 0.0),
    ]
    pack_inputs(plan, channels, scratch[0])
    network(plan, weights, bias, scratch, waits(fetches))
    add_total(plan, now, scratch[2], rms)

    fired, misfit = blend
    lane = lax.broadcasted_iota(jnp.int32, (plan.lines, SLAB), 1)
    mixtures = misfit.shape[0]
    per = plan.shots // mixtures
    if plan.whole_lines:
        for n in range(mixes.shape[0]):
            a, b = divmod(n, plan.time_parts)
            share = mixes.shape[2]
            piece = mixes[n, plan.each * plan.block_lines :, :].astype(F32)
            for g in range(mixtures):
                here = slice(a * plan.block_lines, (a + 1) * plan.block_lines)
                misfit[g, here, b * share : (b + 1) * share] = piece[g * plan.block_lines : (g + 1) * plan.block_lines]
    else:
        misfit[...] = mixes[...].astype(F32)
    for s in range(plan.shots):
        lag = lags[s]
        before = jnp.zeros((plan.lines, SLAB), F32)
        for t in range(plan.slabs):
            lanes = slice(t * SLAB, (t + 1) * SLAB)
            turned = pltpu.roll(now[s * plan.lines : (s + 1) * plan.lines, lanes], lag, 1)
            fired[s, :, lanes] = jnp.where(lane < lag, before, turned)
            before = turned
    for g in range(mixtures):
        value = fired[order[g * per]]
        for k in range(1, per):
            value = value + fired[order[g * per + k]]
        misfit[g] = value - misfit[g]
    for s in range(plan.shots):
        lag = lags[s]
        spot = jnp.int32(0)
        for k in range(plan.shots):
            spot = spot + jnp.where(order[k] == s, k, 0)
        which = spot // per
        back = (DMAX - lag) % DMAX
        after = jnp.zeros((plan.lines, SLAB), F32)
        rows = slice(s * plan.lines, (s + 1) * plan.lines)
        for t in range(plan.slabs - 1, -1, -1):
            lanes = slice(t * SLAB, (t + 1) * SLAB)
            turned = pltpu.roll(misfit[which, :, lanes], back, 1)
            pulled = jnp.where(lane < DMAX - lag, turned, after)
            after = turned
            now[rows, lanes] = (now[rows, lanes] - pace * pulled).astype(BF).astype(F32)


def stage_kernel(plan, station_round, with_shot, has_edges, stride, split_in, split_out, *refs):
    refs = list(refs)
    take = lambda n: [refs.pop(0) for _ in range(n)]
    place, tallies, lags, order, paces, source = take(6)
    station = station_round is not None
    if station:
        energies, mixes, *station_weights, station_bias = take(5)
    edges = None
    if with_shot:
        if has_edges:
            (edges,) = take(1)
        *shot_weights, shot_bias = take(3)
    (result,) = take(1)
    if with_shot:
        (energy,) = take(1)
    now, packed, hidden, total = take(4)
    scratch = (packed, hidden, total)
    arrived = refs.pop()
    sets = ([station_weights] if station else []) + ([shot_weights] if with_shot else [])
    held = [[refs.pop(0) for _ in range(2)] for _ in sets]
    fetches = [
        [pltpu.make_async_copy(w, h, arrived.at[2 * n + i]) for i, (w, h) in enumerate(zip(sets[n], held[n]))]
        for n in range(len(sets))
    ]
    for fetch in sum(fetches, []):
        fetch.start()
    if split_in:
        lines = plan.block_lines
        for n in range(source.shape[0]):
            a, b = divmod(n, plan.time_parts)
            share = source.shape[2]
            piece = source[n, 0 : plan.each * lines, :].astype(F32)
            for k in range(plan.each):
                row = k * plan.lines + a * lines
                now[row : row + lines, b * share : (b + 1) * share] = piece[k * lines : (k + 1) * lines]
    else:
        now[...] = source[...].astype(F32)
    if station:
        station_stage(
            plan,
            place,
            tallies,
            lags,
            order,
            paces[station_round],
            energies,
            mixes,
            held[0],
            fetches[0],
            station_bias,
            now,
            scratch,
            refs,
        )
    if with_shot:
        shot_stage(plan, place, tallies, stride, edges, held[-1], fetches[-1], shot_bias, now, scratch, energy)
    if split_out:
        for n, (row, lane, rows, lanes) in enumerate(plan.pieces):
            result[n] = now[row : row + rows, lane : lane + lanes].astype(BF)
    else:
        result[...] = now[...].astype(BF)


SMEM = pl.BlockSpec(memory_space=pltpu.SMEM)
VMEM = pl.BlockSpec(memory_space=pltpu.VMEM)
HBM = pl.BlockSpec(memory_space=pltpu.HBM)


def run_stage(plan, small, source, station=None, shot=None, split_in=False, split_out=False, stride=0, name="stage"):
    operands = [*small, source]
    station_round, has_edges = None, False
    macs = 0
    pass_macs = plan.rows * plan.slabs * QS * WIDE * (WIDE * 3 + SLAB)
    if station is not None:
        station_round, energies, mixes, weights = station
        operands += [energies, mixes, *weights]
        macs += pass_macs
    if shot is not None:
        edges, weights = shot
        has_edges = edges is not None
        operands += ([edges] if has_edges else []) + list(weights)
        macs += pass_macs
    specs = [HBM if getattr(o, "ndim", 0) >= 2 and o.dtype == BF and o.shape[-2] == WIDE else VMEM for o in operands]
    specs[: len(small)] = [SMEM] * len(small)
    fetched = [o for o, spec in zip(operands, specs) if spec is HBM]
    length = plan.slabs * SLAB
    if split_out:
        _, _, rows, lanes = plan.pieces[0]
        shapes = [jax.ShapeDtypeStruct((len(plan.pieces), rows, lanes), BF)]
    else:
        shapes = [jax.ShapeDtypeStruct((plan.rows, length), BF)]
    if shot is not None:
        shapes.append(jax.ShapeDtypeStruct((1, SLAB), F32))
    scratch = [
        pltpu.VMEM((plan.rows, length), F32),
        pltpu.VMEM((2, plan.slabs, plan.rows, WIDE), BF),
        pltpu.VMEM((QS * (plan.slabs + 2), plan.rows, WIDE), BF),
        pltpu.VMEM((plan.slabs, plan.rows, SLAB), F32),
    ]
    scratch += [pltpu.VMEM(w.shape, w.dtype) for w in fetched]
    if station is not None:
        scratch += [
            pltpu.VMEM((plan.shots, plan.lines, length), F32),
            pltpu.VMEM((plan.mixtures, plan.lines, length), F32),
        ]
    scratch += [pltpu.SemaphoreType.DMA((len(fetched),))]
    return pl.pallas_call(
        functools.partial(
            stage_kernel, plan, station_round, shot is not None, has_edges, stride, split_in, split_out
        ),
        out_shape=shapes,
        in_specs=specs,
        out_specs=[VMEM] * len(shapes),
        scratch_shapes=scratch,
        compiler_params=pltpu.CompilerParams(vmem_limit_bytes=VMEM_LIMIT),
        cost_estimate=pl.CostEstimate(flops=2 * macs, bytes_accessed=1 << 20, transcendentals=0),
        name=name,
    )(*operands)


def run_prepare(nets):
    shapes = []
    for _ in range(2):
        shapes += [
            jax.ShapeDtypeStruct((QH + 2, WIDE, WIDE), BF),
            jax.ShapeDtypeStruct((QS + 2, WIDE, SLAB), BF),
        ]
    operands = [jnp.asarray(entry_selector(), BF), jnp.asarray(exit_selector(), BF), *nets]
    scratch = [pltpu.VMEM((SLAB, WIDE), F32), pltpu.VMEM((SLAB, WIDE), F32)]
    scratch += [pltpu.VMEM(o.shape, o.dtype) for o in operands]
    scratch += [pltpu.VMEM(o.shape, o.dtype) for o in shapes]
    scratch += [pltpu.SemaphoreType.DMA((len(operands),)), pltpu.SemaphoreType.DMA((len(shapes),))]
    outs = pl.pallas_call(
        prepare_kernel,
        out_shape=shapes,
        in_specs=[HBM] * len(operands),
        out_specs=[HBM] * len(shapes),
        scratch_shapes=scratch,
        compiler_params=pltpu.CompilerParams(vmem_limit_bytes=VMEM_FULL),
        cost_estimate=pl.CostEstimate(flops=2 * 2 * 8192 * WIDE * SLAB, bytes_accessed=8 << 20, transcendentals=0),
        name="prepare",
    )(*operands)
    return outs[0:2], outs[2:4]


def run_pack(plan, place, traces, mixtures):
    groups, block, _ = mixtures.shape
    width = traces.shape[1]
    return pl.pallas_call(
        functools.partial(pack_kernel, plan),
        out_shape=jax.ShapeDtypeStruct((RPL // plan.each, (plan.each + groups) * plan.block_lines, width), BF),
        in_specs=[SMEM, HBM, HBM],
        out_specs=VMEM,
        scratch_shapes=[
            pltpu.VMEM((block, width), BF),
            pltpu.VMEM((groups * block, width), BF),
            pltpu.SemaphoreType.DMA((groups + 1,)),
        ],
        compiler_params=pltpu.CompilerParams(vmem_limit_bytes=VMEM_FULL),
        cost_estimate=pl.CostEstimate(flops=2 * block * block * width, bytes_accessed=1 << 20, transcendentals=0),
        name="pack",
    )(place, traces, mixtures)


class Plan:
    def __init__(self, **sizes):
        self.__dict__.update(sizes)
        self.rows = self.shots * self.lines


def per_device(
    initial_guess,
    measured_mixtures,
    launch_lags,
    source_launch_order,
    station_portion_tallies,
    source_entry_kernel,
    source_spaced_kernel,
    source_exit_kernel,
    source_inner_offsets,
    station_entry_kernel,
    station_spaced_kernel,
    station_exit_kernel,
    station_inner_offsets,
    learned_pace_factors,
):
    shots_here, block, window = initial_guess.shape
    n_shot, n_line, n_tm = (lax.axis_size(a) for a in ("shot", "line", "tm"))
    at_shot, at_line, at_tm = (lax.axis_index(a) for a in ("shot", "line", "tm"))
    block_lines = block // RPL
    length = window * n_tm
    shots = shots_here * n_shot
    sections = station_portion_tallies.shape[0]
    mixtures = measured_mixtures.shape[0]
    whole_lines = n_shot * n_line * n_tm == RPL
    assert shots_here == 1 and (whole_lines or n_shot == RPL)
    if whole_lines:
        axes = ("line", "tm", "shot")
        lines, blocks = block_lines * n_line, n_line
        quarter = (at_line * n_tm + at_tm) * n_shot
        position = quarter + at_shot
        first_line = 0
    else:
        axes = ("shot", "tm")
        lines = block_lines // n_tm
        blocks, position, quarter = 1, at_shot, at_shot
        first_line = at_tm * lines
    turns = [(s, a, b) for a in range(blocks) for b in range(n_tm) for s in range(n_shot)]
    plan = Plan(
        whole_lines=whole_lines,
        shots=shots,
        lines=lines,
        block_lines=block_lines,
        blocks=blocks,
        sections=sections,
        mixtures=mixtures,
        slabs=length // SLAB,
        each=n_shot,
        time_parts=n_tm,
        pieces=[(s * lines + a * block_lines, b * window, block_lines, window) for s, a, b in turns],
    )

    def placed(at):
        return jnp.stack([jnp.asarray(v, jnp.int32) for v in [at, first_line, at_tm, at_shot]])

    place = placed(position)
    if whole_lines:
        leaving = run_pack(plan, place, initial_guess.reshape(block, window), measured_mixtures)
        arrived = lax.all_to_all(leaving, ("line", "tm"), split_axis=0, concat_axis=0, tiled=True)
    else:
        grid = initial_guess.reshape(n_tm, lines, RPL, window)
        leaving = grid.transpose(2, 0, 1, 3).reshape(RPL * n_tm, lines, window)
        arrived = lax.all_to_all(leaving, axes, split_axis=0, concat_axis=0, tiled=True)

    nets = (
        source_entry_kernel.transpose(1, 0, 2),
        source_spaced_kernel,
        source_exit_kernel,
        source_inner_offsets,
        station_entry_kernel.transpose(1, 0, 2),
        station_spaced_kernel,
        station_exit_kernel,
        station_inner_offsets,
    )
    shot_weights, station_weights = run_prepare(nets)
    shot_weights = (*shot_weights, source_inner_offsets)
    station_weights = (*station_weights, station_inner_offsets)
    small = (place, station_portion_tallies, launch_lags, source_launch_order, learned_pace_factors)
    split = whole_lines and block_lines % 8 == 0
    assert split or not whole_lines
    if whole_lines:
        mixes = source = arrived
    else:
        grid = measured_mixtures.reshape(mixtures, n_tm, lines, RPL, length)
        mixes = lax.dynamic_slice(
            grid, (0, at_tm, 0, position, 0), (mixtures, 1, lines, 1, length)
        ).reshape(mixtures, lines, length)
        source = arrived.reshape(n_shot, n_tm, lines, window).transpose(0, 2, 1, 3).reshape(plan.rows, length)

    def edges_of(current):
        if whole_lines:
            return None
        size = n_line * n_tm
        grid = current.reshape(shots, lines, length)
        up = [(i, i + 1) for i in range(size - 1)]
        down = [(j, i) for i, j in up]
        above = lax.ppermute(grid[:, -1], ("line", "tm"), up)
        below = lax.ppermute(grid[:, 0], ("line", "tm"), down)
        wide = jnp.broadcast_to(jnp.stack([above, below])[:, :, None, :], (2, shots, lines, length))
        return wide.reshape(2, plan.rows, length)

    def shared(energy):
        for axis in ("tm", "line", "shot") if whole_lines else ("tm", "shot"):
            size = lax.axis_size(axis)
            if size <= 4:
                others = [lax.ppermute(energy, axis, [(i, i ^ d) for i in range(size)]) for d in range(1, size)]
                energy = sum(others, energy)
                continue
            step = 1
            while step < size:
                energy = energy + lax.ppermute(energy, axis, [(i, i ^ step) for i in range(size)])
                step *= 2
        return energy

    first = (placed(quarter), *small[1:])
    current, energy = run_stage(
        plan,
        first,
        source,
        shot=(edges_of(source), shot_weights),
        split_in=split,
        stride=1 if whole_lines else 0,
        name="shot_pass",
    )
    if whole_lines:
        grid = current.reshape(n_shot, lines, length)
        current = lax.all_to_all(grid, "shot", split_axis=0, concat_axis=0, tiled=True).reshape(plan.rows, length)
    for i in range(ITERS):
        station = (i, shared(energy), mixes, station_weights)
        if i == ITERS - 1:
            (current,) = run_stage(plan, small, current, station=station, split_out=split, name="station_pass")
        elif whole_lines:
            current, energy = run_stage(
                plan, small, current, station=station, shot=(None, shot_weights), name="station_and_shot_pass"
            )
        else:
            (current,) = run_stage(plan, small, current, station=station, name="station_pass")
            current, energy = run_stage(plan, small, current, shot=(edges_of(current), shot_weights), name="shot_pass")
    if not split:
        current = current.reshape(n_shot, lines, n_tm, window).transpose(0, 2, 1, 3).reshape(-1, lines, window)
    back = lax.all_to_all(current, axes, split_axis=0, concat_axis=0, tiled=True)
    if whole_lines:
        back = back.transpose(1, 0, 2)
    else:
        back = back.reshape(RPL, n_tm, lines, window).transpose(1, 2, 0, 3)
    return back.reshape(shots_here, block, window)


def solution(mesh):
    placed = (P(("group", "shot"), "line", "tm"), P("group", "line", None), P("group"), P("group"), P("group"))
    return jax.shard_map(
        per_device,
        mesh=mesh,
        in_specs=placed + (P(),) * 9,
        out_specs=P(("group", "shot"), "line", "tm"),
        check_vma=False,
    )
```

```python
import functools

import jax
import jax.numpy as jnp
import numpy as np
from jax import lax
from jax.experimental import pallas as pl
from jax.experimental.pallas import tpu as pltpu
from jax.sharding import PartitionSpec as P

RPL = 16
DMAX = 128
ITERS = 2
EPSILON = 1e-05

SLAB = 128
HALF = 64
FEAT = 64
GROUP = 4
WIDE = GROUP * FEAT
QS = SLAB // (2 * GROUP)
QH = QS // 2
assert QH == 8
ONES = 3 * HALF + 6
STEP = 4
VMEM_LIMIT = 53 * 1024 * 1024
VMEM_FULL = 63 * 1024 * 1024

BF = jnp.bfloat16
F32 = jnp.float32


def entry_selector():
    picks = np.zeros((QH, WIDE, GROUP, 4, 8), np.float32)
    for j in range(3):
        picks[:, ONES + j, :, 3, j] = 1
    for q in range(QH):
        for p in range(GROUP):
            for j in range(4):
                i = 2 * (GROUP * q + p) + j - 1
                for c in range(3):
                    if i < 0:
                        lane = 3 * HALF + 2 * c
                    elif i >= HALF:
                        lane = 3 * HALF + 2 * c + 1
                    else:
                        lane = c * HALF + i
                    picks[q, lane, p, c, j] = 1
    return picks.reshape(QH * WIDE, GROUP * 4 * 8)


def exit_selector():
    picks = np.zeros((QS + 2, SLAB, SLAB), np.float32)
    for q in range(QS):
        for p in range(GROUP):
            for j in range(4):
                i = 2 * (GROUP * q + p) + j - 1
                if i < 0:
                    picks[QS + 1, p * 8 + j, SLAB - 1] = 1
                elif i >= SLAB:
                    picks[QS, p * 8 + j, 0] = 1
                else:
                    picks[q, p * 8 + j, i] = 1
    return picks.reshape((QS + 2) * SLAB, SLAB)


def split_bias(bias):
    high = bias.astype(BF).astype(F32)
    middle = (bias - high).astype(BF).astype(F32)
    return high, middle, bias - high - middle


def prepare_kernel(*refs):
    sources, outs = refs[:10], refs[10:14]
    (rhs, cols), held, made = refs[14:16], refs[16:26], refs[26:30]
    done, sent = refs[30:32]
    copies = [pltpu.make_async_copy(src, dst, done.at[i]) for i, (src, dst) in enumerate(zip(sources, held))]
    for copy in copies:
        copy.start()
    for copy in copies:
        copy.wait()
    sel_in, sel_out = held[:2]
    for n in range(2):
        w_in, w_mid, w_out, bias = held[2 + 4 * n : 6 + 4 * n]
        o_in, o_out = made[2 * n : 2 * n + 2]
        leaving = [pltpu.make_async_copy(made[i], outs[i], sent.at[i]) for i in range(2 * n, 2 * n + 2)]
        rhs[...] = jnp.zeros_like(rhs)
        cols[...] = jnp.zeros_like(cols)
        parts = split_bias(bias[0:1, :])
        for p in range(GROUP):
            lanes = slice(p * FEAT, (p + 1) * FEAT)
            for c in range(3):
                rhs[p * 32 + c * 8 : p * 32 + c * 8 + 4, lanes] = w_in[c].astype(F32)
                rhs[p * 32 + 24 + c : p * 32 + 25 + c, lanes] = parts[c]
            cols[p * 8 : p * 8 + 4, lanes] = w_out[...].astype(F32)
        taps = rhs[...].astype(BF)
        for q in range(QH):
            part = sel_in[q * WIDE : (q + 1) * WIDE, :]
            o_in[q] = jnp.dot(part, taps, preferred_element_type=F32).astype(BF)
        back = jnp.transpose(cols[...]).astype(BF)
        for q in range(QS + 2):
            part = sel_out[q * SLAB : (q + 1) * SLAB, :]
            o_out[q] = jnp.dot(back, part, preferred_element_type=F32).astype(BF)
        leaving[1].start()
        o_in[QH:] = jnp.zeros((2, WIDE, WIDE), BF)
        for a, row in [(0, 0), (1, 1), (2, 2), (3, 3), (-2, 4), (-1, 5), (4, 6), (5, 7)]:
            for b in range(GROUP):
                if (a - b) % 2 == 0 and abs(a - b) <= 2:
                    o_in[QH + row // 4, row % 4 * FEAT : (row % 4 + 1) * FEAT, b * FEAT : (b + 1) * FEAT] = w_mid[
                        (a - b) // 2 + 1
                    ]
        leaving[0].start()
    for i in range(4):
        pltpu.make_async_copy(made[i], outs[i], sent.at[i]).wait()


def pack_kernel(plan, place, traces, mixes, packet, held, mixed, done):
    block, window = traces.shape
    groups = mixes.shape[0]
    share = packet.shape[2]
    copies = [pltpu.make_async_copy(traces, held, done.at[0])]
    at = pl.multiple_of(place[2] * share, share)
    for g in range(groups):
        into = mixed.at[g * block : (g + 1) * block, :]
        copies.append(pltpu.make_async_copy(mixes.at[g, :, pl.ds(at, share)], into, done.at[g + 1]))
    for copy in copies:
        copy.start()
    lines, each = plan.block_lines, plan.each
    row = lax.broadcasted_iota(jnp.int32, (block, block), 0)
    col = lax.broadcasted_iota(jnp.int32, (block, block), 1)
    spot, line = split_index(row, lines)
    order = (col == line * RPL + spot).astype(F32).astype(BF)
    rows = packet.shape[0] * groups * lines
    row = lax.broadcasted_iota(jnp.int32, (rows, groups * block), 0)
    col = lax.broadcasted_iota(jnp.int32, (rows, groups * block), 1)
    rest, line = split_index(row, lines)
    to, g = split_index(rest, groups)
    choose = (col == g * block + line * RPL + to * each + place[3]).astype(F32).astype(BF)
    for copy in copies:
        copy.wait()
    top = each * lines
    moved = jnp.dot(order, held[...], preferred_element_type=F32)
    packet[:, 0:top, :] = moved.reshape(packet.shape[0], top, share).astype(BF)
    moved = jnp.dot(choose, mixed[...], preferred_element_type=F32)
    packet[:, top:, :] = moved.reshape(packet.shape[0], groups * lines, share).astype(BF)


def split_index(value, size):
    if size & (size - 1):
        return value // size, value % size
    return value >> (size.bit_length() - 1), value & (size - 1)


def section_map(plan, place, tallies, stride):
    shape = (plan.rows, SLAB)
    lane = lax.broadcasted_iota(jnp.int32, shape, 1)
    apart, line = split_index(lax.broadcasted_iota(jnp.int32, shape, 0), plan.lines)
    block, line = split_index(line + place[1], plan.block_lines)
    spot = line * RPL + place[0] + apart * stride
    low = jnp.zeros(shape, jnp.int32)
    high = jnp.zeros(shape, jnp.int32)
    count = jnp.zeros(shape, jnp.int32)
    start = jnp.int32(0)
    for p in range(plan.sections):
        amount = tallies[p]
        for b in range(plan.blocks):
            here = lane == b * plan.sections + p
            low = jnp.where(here, start, low)
            high = jnp.where(here, start + amount, high)
            count = jnp.where(here, amount, count)
        start = start + amount
    member = (spot >= low) & (spot < high) & (split_index(lane, plan.sections)[0] == block)
    return member, count


def shifted(values, by, ok, edge):
    return jnp.where(ok, pltpu.roll(values, by % values.shape[0], 0), edge)


def pack_inputs(plan, channels, packed):
    lane = lax.broadcasted_iota(jnp.int32, (plan.rows, SLAB), 1)
    low = lane < HALF
    ones = ((lane >= ONES - SLAB) & (lane < ONES - SLAB + 3)).astype(F32)
    slabs = [[x[:, t * SLAB : (t + 1) * SLAB] for t in range(plan.slabs)] for x in channels]
    far = [[pltpu.roll(s, HALF + 1 + 2 * c, 1) for s in slabs[c]] for c in range(3)]
    for t in range(plan.slabs):
        v = [slabs[c][t] for c in range(3)]
        w = [pltpu.roll(s, HALF, 1) for s in v]
        even = jnp.where(low, v[2], ones)
        odd = jnp.where(low, w[2], ones)
        for c in range(3):
            left, right = lane == HALF + 2 * c, lane == HALF + 2 * c + 1
            near = pltpu.roll(v[c], 1 + 2 * c, 1)
            even = jnp.where(right, near, even)
            odd = jnp.where(left, near, odd)
            if t > 0:
                even = jnp.where(left, far[c][t - 1], even)
            if t < plan.slabs - 1:
                odd = jnp.where(right, far[c][t + 1], odd)
        packed[0, t, :, 0:SLAB] = jnp.where(low, v[0], w[1]).astype(BF)
        packed[0, t, :, SLAB:WIDE] = even.astype(BF)
        packed[1, t, :, 0:SLAB] = jnp.where(low, w[0], v[1]).astype(BF)
        packed[1, t, :, SLAB:WIDE] = odd.astype(BF)


def network(plan, weights, bias, scratch, ready=(lambda: None, lambda: None)):
    w_in, w_out = weights
    packed, hidden, total, ends = scratch
    many, rows = plan.slabs * plan.rows, plan.rows
    grid = (plan.slabs, rows, WIDE)
    pitch = plan.slabs + 2
    bias_two = jnp.concatenate([bias[1:2, :]] * GROUP, axis=1)

    def first(q):
        value = jnp.dot(packed[q >> 3].reshape(many, WIDE), w_in[q & 7], preferred_element_type=F32)
        hidden[pl.ds(q * pitch + 1, plan.slabs)] = jnp.maximum(value.astype(BF), 0).reshape(grid)

    def second(q, left_at, right_at):
        middle = hidden[pl.ds(q * pitch + 1, plan.slabs)]
        left = hidden[pl.ds(left_at, plan.slabs), :, SLAB:WIDE]
        right = hidden[pl.ds(right_at, plan.slabs), :, 0:SLAB]
        window = jnp.concatenate([middle, left, right], axis=2).reshape(many, 2 * WIDE)
        value = jnp.dot(window, w_in[QH:].reshape(2 * WIDE, WIDE), preferred_element_type=F32)
        return jnp.maximum((value + bias_two).astype(BF), 0)

    def onto(layer, q):
        return jnp.dot(layer, w_out[q], preferred_element_type=F32).reshape(plan.slabs, rows, SLAB)

    edge = jnp.zeros((rows, WIDE), BF)
    hidden[(QS - 1) * pitch] = edge
    hidden[pitch - 1] = edge
    total[...] = jnp.zeros_like(total)
    ready[0]()

    def first_some(i, _):
        for k in range(STEP):
            first(i * STEP + k)

    lax.fori_loop(0, QS // STEP, first_some, None)
    ready[1]()

    def second_some(i, _):
        for k in range(STEP):
            q = i * STEP + k
            left_at = jnp.where(q == 0, (QS - 1) * pitch, (q - 1) * pitch + 1) if k == 0 else (q - 1) * pitch + 1
            right_at = jnp.where(q == QS - 1, 2, (q + 1) * pitch + 1) if k == STEP - 1 else (q + 1) * pitch + 1
            layer = second(q, left_at, right_at)
            if k == 0:

                @pl.when(i == 0)
                def _():
                    ends[0] = layer

            if k == STEP - 1:

                @pl.when(i == QS // STEP - 1)
                def _():
                    ends[1] = layer

            total[...] += onto(layer, q)

    lax.fori_loop(0, QS // STEP, second_some, None)
    total[0 : plan.slabs - 1] += onto(ends[0], QS + 1)[1:]
    total[1 : plan.slabs] += onto(ends[1], QS)[: plan.slabs - 1]


def waits(fetches):
    return fetches[0].wait, fetches[1].wait


def add_total(plan, now, total, scale=None):
    for t in range(plan.slabs):
        lanes = slice(t * SLAB, (t + 1) * SLAB)
        more = total[t] if scale is None else scale * total[t]
        now[:, lanes] = (now[:, lanes] + more).astype(BF).astype(F32)


def shot_stage(plan, place, tallies, stride, edges, weights, fetches, bias, now, scratch):
    x = now[...]
    line = split_index(lax.broadcasted_iota(jnp.int32, x.shape, 0), plan.lines)[1]
    above = 0.0 if edges is None else edges[0].astype(F32)
    below = 0.0 if edges is None else edges[1].astype(F32)
    channels = [
        shifted(x, 1, line > 0, above),
        x,
        shifted(x, -1, line < plan.lines - 1, below),
    ]
    pack_inputs(plan, channels, scratch[0])
    network(plan, weights, bias, scratch, waits(fetches))
    add_total(plan, now, scratch[2])
    power = jnp.zeros((plan.rows, SLAB), F32)
    for t in range(plan.slabs):
        piece = now[:, t * SLAB : (t + 1) * SLAB]
        power = power + piece * piece
    member, _ = section_map(plan, place, tallies, stride)
    each = jnp.where(member, jnp.sum(power, axis=1, keepdims=True), 0.0)
    return jnp.sum(each, axis=0, keepdims=True)


def station_stage(
    plan, place, tallies, lags, order, pace, energies, mixes, weights, fetches, bias, now, scratch, blend
):
    member, count = section_map(plan, place, tallies, 0)
    totals = energies[...]
    denominator = jnp.maximum(count, 1) * (plan.shots * plan.slabs * SLAB)
    level = jnp.sqrt(totals / denominator.astype(F32) + EPSILON)
    rms = jnp.sum(jnp.where(member, level, 0.0), axis=1, keepdims=True)
    x = (now[...] / rms).astype(BF).astype(F32)
    row = lax.broadcasted_iota(jnp.int32, x.shape, 0)
    channels = [
        shifted(x, plan.lines, row >= plan.lines, 0.0),
        x,
        shifted(x, -plan.lines, row < plan.rows - plan.lines, 0.0),
    ]
    pack_inputs(plan, channels, scratch[0])
    network(plan, weights, bias, scratch, waits(fetches))
    add_total(plan, now, scratch[2], rms)

    fired, misfit = blend
    lane = lax.broadcasted_iota(jnp.int32, (plan.lines, SLAB), 1)
    mixtures = misfit.shape[0]
    per = plan.shots // mixtures
    if plan.whole_lines:
        for n in range(mixes.shape[0]):
            a, b = divmod(n, plan.time_parts)
            share = mixes.shape[2]
            piece = mixes[n, plan.each * plan.block_lines :, :].astype(F32)
            for g in range(mixtures):
                here = slice(a * plan.block_lines, (a + 1) * plan.block_lines)
                misfit[g, here, b * share : (b + 1) * share] = piece[g * plan.block_lines : (g + 1) * plan.block_lines]
    else:
        misfit[...] = mixes[...].astype(F32)
    for s in range(plan.shots):
        lag = lags[s]
        before = jnp.zeros((plan.lines, SLAB), F32)
        for t in range(plan.slabs):
            lanes = slice(t * SLAB, (t + 1) * SLAB)
            turned = pltpu.roll(now[s * plan.lines : (s + 1) * plan.lines, lanes], lag, 1)
            fired[s, :, lanes] = jnp.where(lane < lag, before, turned)
            before = turned
    for g in range(mixtures):
        value = fired[order[g * per]]
        for k in range(1, per):
            value = value + fired[order[g * per + k]]
        misfit[g] = value - misfit[g]
    for s in range(plan.shots):
        lag = lags[s]
        spot = jnp.int32(0)
        for k in range(plan.shots):
            spot = spot + jnp.where(order[k] == s, k, 0)
        which = spot // per
        back = (DMAX - lag) % DMAX
        after = jnp.zeros((plan.lines, SLAB), F32)
        rows = slice(s * plan.lines, (s + 1) * plan.lines)
        for t in range(plan.slabs - 1, -1, -1):
            lanes = slice(t * SLAB, (t + 1) * SLAB)
            turned = pltpu.roll(misfit[which, :, lanes], back, 1)
            pulled = jnp.where(lane < DMAX - lag, turned, after)
            after = turned
            now[rows, lanes] = (now[rows, lanes] - pace * pulled).astype(BF).astype(F32)


def stage_kernel(plan, station_round, with_shot, has_edges, stride, split_in, split_out, *refs):
    refs = list(refs)
    take = lambda n: [refs.pop(0) for _ in range(n)]
    place, tallies, lags, order, paces = take(5)
    sources = take(plan.each if split_in == "parts" else 1)
    source = sources[0]
    station = station_round is not None
    if station:
        energies, mixes, *station_weights, station_bias = take(5)
    edges = None
    if with_shot:
        if has_edges:
            (edges,) = take(1)
        *shot_weights, shot_bias = take(3)
    results = take(plan.each if split_out == "parts" else 1)
    result = results[0]
    if with_shot and split_out != "parts":
        (energy,) = take(1)
    now, packed, hidden, total, ends = take(5)
    scratch = (packed, hidden, total, ends)
    arrived = refs.pop()
    sets = ([station_weights] if station else []) + ([shot_weights] if with_shot else [])
    held = [[refs.pop(0) for _ in range(2)] for _ in sets]
    fetches = [
        [pltpu.make_async_copy(w, h, arrived.at[2 * n + i]) for i, (w, h) in enumerate(zip(sets[n], held[n]))]
        for n in range(len(sets))
    ]
    for fetch in sum(fetches, []):
        fetch.start()
    length = plan.slabs * SLAB
    if split_in == "parts":
        for d, part in enumerate(sources):
            at = pl.multiple_of((place[3] ^ d) * plan.lines, plan.lines)
            now[pl.ds(at, plan.lines), :] = part[:, 0:length].astype(F32)
    elif split_in:
        lines = plan.block_lines
        for n in range(source.shape[0]):
            a, b = divmod(n, plan.time_parts)
            share = source.shape[2]
            piece = source[n, 0 : plan.each * lines, :].astype(F32)
            for k in range(plan.each):
                row = k * plan.lines + a * lines
                now[row : row + lines, b * share : (b + 1) * share] = piece[k * lines : (k + 1) * lines]
    else:
        now[...] = source[...].astype(F32)
    if station:
        station_stage(
            plan,
            place,
            tallies,
            lags,
            order,
            paces[station_round],
            energies,
            mixes,
            held[0],
            fetches[0],
            station_bias,
            now,
            scratch,
            refs,
        )
    if with_shot:
        sums = shot_stage(plan, place, tallies, stride, edges, held[-1], fetches[-1], shot_bias, now, scratch)
    if split_out == "parts":
        row = lax.broadcasted_iota(jnp.int32, (plan.lines, SLAB), 0)
        beside = jnp.zeros((plan.lines, SLAB), F32)
        for i, part in enumerate(split_bias(sums)):
            beside = jnp.where(row == i, part, beside)
        for d, part in enumerate(results):
            at = pl.multiple_of((place[3] ^ d) * plan.lines, plan.lines)
            part[:, 0:length] = now[pl.ds(at, plan.lines), :].astype(BF)
            part[:, length:] = beside.astype(BF)
        return
    if with_shot:
        energy[...] = sums
    if split_out:
        for n, (row, lane, rows, lanes) in enumerate(plan.pieces):
            result[n] = now[row : row + rows, lane : lane + lanes].astype(BF)
    else:
        result[...] = now[...].astype(BF)


SMEM = pl.BlockSpec(memory_space=pltpu.SMEM)
VMEM = pl.BlockSpec(memory_space=pltpu.VMEM)
HBM = pl.BlockSpec(memory_space=pltpu.HBM)


def run_stage(plan, small, source, station=None, shot=None, split_in=False, split_out=False, stride=0, name="stage"):
    operands = [*small, *(source if split_in == "parts" else [source])]
    station_round, has_edges = None, False
    macs = 0
    pass_macs = plan.rows * plan.slabs * QS * WIDE * (WIDE * 3 + SLAB)
    if station is not None:
        station_round, energies, mixes, weights = station
        operands += [energies, mixes, *weights]
        macs += pass_macs
    if shot is not None:
        edges, weights = shot
        has_edges = edges is not None
        operands += ([edges] if has_edges else []) + list(weights)
        macs += pass_macs
    specs = [HBM if getattr(o, "ndim", 0) >= 2 and o.dtype == BF and o.shape[-2] == WIDE else VMEM for o in operands]
    specs[: len(small)] = [SMEM] * len(small)
    fetched = [o for o, spec in zip(operands, specs) if spec is HBM]
    length = plan.slabs * SLAB
    if split_out == "parts":
        shapes = [jax.ShapeDtypeStruct((plan.lines, length + SLAB), BF)] * plan.each
    elif split_out:
        _, _, rows, lanes = plan.pieces[0]
        shapes = [jax.ShapeDtypeStruct((len(plan.pieces), rows, lanes), BF)]
    else:
        shapes = [jax.ShapeDtypeStruct((plan.rows, length), BF)]
    if shot is not None and split_out != "parts":
        shapes.append(jax.ShapeDtypeStruct((1, SLAB), F32))
    scratch = [
        pltpu.VMEM((plan.rows, length), F32),
        pltpu.VMEM((2, plan.slabs, plan.rows, WIDE), BF),
        pltpu.VMEM((QS * (plan.slabs + 2), plan.rows, WIDE), BF),
        pltpu.VMEM((plan.slabs, plan.rows, SLAB), F32),
        pltpu.VMEM((2, plan.slabs * plan.rows, WIDE), BF),
    ]
    scratch += [pltpu.VMEM(w.shape, w.dtype) for w in fetched]
    if station is not None:
        scratch += [
            pltpu.VMEM((plan.shots, plan.lines, length), F32),
            pltpu.VMEM((plan.mixtures, plan.lines, length), F32),
        ]
    scratch += [pltpu.SemaphoreType.DMA((len(fetched),))]
    return pl.pallas_call(
        functools.partial(
            stage_kernel, plan, station_round, shot is not None, has_edges, stride, split_in, split_out
        ),
        out_shape=shapes,
        in_specs=specs,
        out_specs=[VMEM] * len(shapes),
        scratch_shapes=scratch,
        compiler_params=pltpu.CompilerParams(vmem_limit_bytes=VMEM_LIMIT),
        cost_estimate=pl.CostEstimate(flops=2 * macs, bytes_accessed=1 << 20, transcendentals=0),
        name=name,
    )(*operands)


def run_prepare(nets):
    shapes = []
    for _ in range(2):
        shapes += [
            jax.ShapeDtypeStruct((QH + 2, WIDE, WIDE), BF),
            jax.ShapeDtypeStruct((QS + 2, WIDE, SLAB), BF),
        ]
    operands = [jnp.asarray(entry_selector(), BF), jnp.asarray(exit_selector(), BF), *nets]
    scratch = [pltpu.VMEM((SLAB, WIDE), F32), pltpu.VMEM((SLAB, WIDE), F32)]
    scratch += [pltpu.VMEM(o.shape, o.dtype) for o in operands]
    scratch += [pltpu.VMEM(o.shape, o.dtype) for o in shapes]
    scratch += [pltpu.SemaphoreType.DMA((len(operands),)), pltpu.SemaphoreType.DMA((len(shapes),))]
    outs = pl.pallas_call(
        prepare_kernel,
        out_shape=shapes,
        in_specs=[HBM] * len(operands),
        out_specs=[HBM] * len(shapes),
        scratch_shapes=scratch,
        compiler_params=pltpu.CompilerParams(vmem_limit_bytes=VMEM_FULL),
        cost_estimate=pl.CostEstimate(flops=2 * 2 * 8192 * WIDE * SLAB, bytes_accessed=8 << 20, transcendentals=0),
        name="prepare",
    )(*operands)
    return outs[0:2], outs[2:4]


def run_pack(plan, place, traces, mixtures):
    groups, block, _ = mixtures.shape
    width = traces.shape[1]
    return pl.pallas_call(
        functools.partial(pack_kernel, plan),
        out_shape=jax.ShapeDtypeStruct((RPL // plan.each, (plan.each + groups) * plan.block_lines, width), BF),
        in_specs=[SMEM, HBM, HBM],
        out_specs=VMEM,
        scratch_shapes=[
            pltpu.VMEM((block, width), BF),
            pltpu.VMEM((groups * block, width), BF),
            pltpu.SemaphoreType.DMA((groups + 1,)),
        ],
        compiler_params=pltpu.CompilerParams(vmem_limit_bytes=VMEM_FULL),
        cost_estimate=pl.CostEstimate(flops=2 * block * block * width, bytes_accessed=1 << 20, transcendentals=0),
        name="pack",
    )(place, traces, mixtures)


class Plan:
    def __init__(self, **sizes):
        self.__dict__.update(sizes)
        self.rows = self.shots * self.lines


def per_device(
    initial_guess,
    measured_mixtures,
    launch_lags,
    source_launch_order,
    station_portion_tallies,
    source_entry_kernel,
    source_spaced_kernel,
    source_exit_kernel,
    source_inner_offsets,
    station_entry_kernel,
    station_spaced_kernel,
    station_exit_kernel,
    station_inner_offsets,
    learned_pace_factors,
):
    shots_here, block, window = initial_guess.shape
    n_shot, n_line, n_tm = (lax.axis_size(a) for a in ("shot", "line", "tm"))
    at_shot, at_line, at_tm = (lax.axis_index(a) for a in ("shot", "line", "tm"))
    block_lines = block // RPL
    length = window * n_tm
    shots = shots_here * n_shot
    sections = station_portion_tallies.shape[0]
    mixtures = measured_mixtures.shape[0]
    whole_lines = n_shot * n_line * n_tm == RPL
    assert shots_here == 1 and (whole_lines or n_shot == RPL)
    if whole_lines:
        axes = ("line", "tm", "shot")
        lines, blocks = block_lines * n_line, n_line
        quarter = (at_line * n_tm + at_tm) * n_shot
        position = quarter + at_shot
        first_line = 0
    else:
        axes = ("shot", "tm")
        lines = block_lines // n_tm
        blocks, position, quarter = 1, at_shot, at_shot
        first_line = at_tm * lines
    turns = [(s, a, b) for a in range(blocks) for b in range(n_tm) for s in range(n_shot)]
    plan = Plan(
        whole_lines=whole_lines,
        shots=shots,
        lines=lines,
        block_lines=block_lines,
        blocks=blocks,
        sections=sections,
        mixtures=mixtures,
        slabs=length // SLAB,
        each=n_shot,
        time_parts=n_tm,
        pieces=[(s * lines + a * block_lines, b * window, block_lines, window) for s, a, b in turns],
    )

    def placed(at):
        return jnp.stack([jnp.asarray(v, jnp.int32) for v in [at, first_line, at_tm, at_shot]])

    place = placed(position)
    if whole_lines:
        leaving = run_pack(plan, place, initial_guess.reshape(block, window), measured_mixtures)
        arrived = lax.all_to_all(leaving, ("line", "tm"), split_axis=0, concat_axis=0, tiled=True)
    else:
        grid = initial_guess.reshape(n_tm, lines, RPL, window)
        leaving = grid.transpose(2, 0, 1, 3).reshape(RPL * n_tm, lines, window)
        arrived = lax.all_to_all(leaving, axes, split_axis=0, concat_axis=0, tiled=True)

    nets = (
        source_entry_kernel.transpose(1, 0, 2),
        source_spaced_kernel,
        source_exit_kernel,
        source_inner_offsets,
        station_entry_kernel.transpose(1, 0, 2),
        station_spaced_kernel,
        station_exit_kernel,
        station_inner_offsets,
    )
    shot_weights, station_weights = run_prepare(nets)
    shot_weights = (*shot_weights, source_inner_offsets)
    station_weights = (*station_weights, station_inner_offsets)
    small = (place, station_portion_tallies, launch_lags, source_launch_order, learned_pace_factors)
    split = whole_lines and block_lines % 8 == 0
    assert split or not whole_lines
    if whole_lines:
        mixes = source = arrived
    else:
        grid = measured_mixtures.reshape(mixtures, n_tm, lines, RPL, length)
        mixes = lax.dynamic_slice(
            grid, (0, at_tm, 0, position, 0), (mixtures, 1, lines, 1, length)
        ).reshape(mixtures, lines, length)
        source = arrived.reshape(n_shot, n_tm, lines, window).transpose(0, 2, 1, 3).reshape(plan.rows, length)

    def edges_of(current):
        if whole_lines:
            return None
        size = n_line * n_tm
        grid = current.reshape(shots, lines, length)
        up = [(i, i + 1) for i in range(size - 1)]
        down = [(j, i) for i, j in up]
        above = lax.ppermute(grid[:, -1], ("line", "tm"), up)
        below = lax.ppermute(grid[:, 0], ("line", "tm"), down)
        wide = jnp.broadcast_to(jnp.stack([above, below])[:, :, None, :], (2, shots, lines, length))
        return wide.reshape(2, plan.rows, length)

    def summed(value, axis):
        size = lax.axis_size(axis)
        if size <= 4:
            others = [lax.ppermute(value, axis, [(i, i ^ d) for i in range(size)]) for d in range(1, size)]
            return sum(others, value)
        step = 1
        while step < size:
            value = value + lax.ppermute(value, axis, [(i, i ^ step) for i in range(size)])
            step *= 2
        return value

    def shared(energy, along):
        for axis in along:
            energy = summed(energy, axis)
        return energy

    if whole_lines:
        parts = run_stage(
            plan,
            (placed(quarter), *small[1:]),
            source,
            shot=(None, shot_weights),
            split_in=split,
            split_out="parts",
            stride=1,
            name="shot_pass",
        )
        current = [parts[0]]
        for d in range(1, n_shot):
            current.append(lax.ppermute(parts[d], "shot", [(i, i ^ d) for i in range(n_shot)]))
        energy = sum(jnp.sum(p[0:3, length:].astype(F32), axis=0, keepdims=True) for p in current)
        energy = shared(energy, ("tm", "line"))
    else:
        current, energy = run_stage(
            plan, small, source, shot=(edges_of(source), shot_weights), split_in=split, name="shot_pass"
        )
        energy = shared(energy, ("tm", "shot"))
    for i in range(ITERS):
        station = (i, energy, mixes, station_weights)
        form = "parts" if whole_lines and i == 0 else False
        if i == ITERS - 1:
            (current,) = run_stage(
                plan, small, current, station=station, split_in=form, split_out=split, name="station_pass"
            )
        elif whole_lines:
            current, energy = run_stage(
                plan,
                small,
                current,
                station=station,
                shot=(None, shot_weights),
                split_in=form,
                name="station_and_shot_pass",
            )
            energy = shared(energy, ("tm", "line", "shot"))
        else:
            (current,) = run_stage(plan, small, current, station=station, name="station_pass")
            current, energy = run_stage(plan, small, current, shot=(edges_of(current), shot_weights), name="shot_pass")
            energy = shared(energy, ("tm", "shot"))
    if not split:
        current = current.reshape(n_shot, lines, n_tm, window).transpose(0, 2, 1, 3).reshape(-1, lines, window)
    back = lax.all_to_all(current, axes, split_axis=0, concat_axis=0, tiled=True)
    if whole_lines:
        back = back.transpose(1, 0, 2)
    else:
        back = back.reshape(RPL, n_tm, lines, window).transpose(1, 2, 0, 3)
    return back.reshape(shots_here, block, window)


def solution(mesh):
    placed = (P(("group", "shot"), "line", "tm"), P("group", "line", None), P("group"), P("group"), P("group"))
    return jax.shard_map(
        per_device,
        mesh=mesh,
        in_specs=placed + (P(),) * 9,
        out_specs=P(("group", "shot"), "line", "tm"),
        check_vma=False,
    )
```

```python
import functools

import jax
import jax.numpy as jnp
import numpy as np
from jax import lax
from jax.experimental import pallas as pl
from jax.experimental.pallas import tpu as pltpu
from jax.sharding import PartitionSpec as P

RPL = 16
DMAX = 128
ITERS = 2
EPSILON = 1e-05

SLAB = 128
HALF = 64
FEAT = 64
GROUP = 4
WIDE = GROUP * FEAT
QS = SLAB // (2 * GROUP)
QH = QS // 2
assert QH == 8
ONES = 3 * HALF + 6
STEP = 8
VMEM_LIMIT = 53 * 1024 * 1024
VMEM_FULL = 63 * 1024 * 1024

BF = jnp.bfloat16
F32 = jnp.float32


def entry_selector():
    picks = np.zeros((QH, WIDE, GROUP, 4, 8), np.float32)
    for j in range(3):
        picks[:, ONES + j, :, 3, j] = 1
    for q in range(QH):
        for p in range(GROUP):
            for j in range(4):
                i = 2 * (GROUP * q + p) + j - 1
                for c in range(3):
                    if i < 0:
                        lane = 3 * HALF + 2 * c
                    elif i >= HALF:
                        lane = 3 * HALF + 2 * c + 1
                    else:
                        lane = c * HALF + i
                    picks[q, lane, p, c, j] = 1
    return picks.reshape(QH * WIDE, GROUP * 4 * 8)


def exit_selector():
    picks = np.zeros((QS + 2, SLAB, SLAB), np.float32)
    for q in range(QS):
        for p in range(GROUP):
            for j in range(4):
                i = 2 * (GROUP * q + p) + j - 1
                if i < 0:
                    picks[QS + 1, p * 8 + j, SLAB - 1] = 1
                elif i >= SLAB:
                    picks[QS, p * 8 + j, 0] = 1
                else:
                    picks[q, p * 8 + j, i] = 1
    return picks.reshape((QS + 2) * SLAB, SLAB)


def split_bias(bias):
    high = bias.astype(BF).astype(F32)
    middle = (bias - high).astype(BF).astype(F32)
    return high, middle, bias - high - middle


def prepare_kernel(*refs):
    sources, outs = refs[:6], refs[6:8]
    (rhs, cols), held, (o_in, o_out), (done, sent) = refs[8:10], refs[10:16], refs[16:18], refs[18:20]
    copies = [pltpu.make_async_copy(src, dst, done.at[i]) for i, (src, dst) in enumerate(zip(sources, held))]
    leaving = [pltpu.make_async_copy(src, dst, sent.at[i]) for i, (src, dst) in enumerate(zip((o_in, o_out), outs))]
    for copy in copies:
        copy.start()
    rhs[...] = jnp.zeros_like(rhs)
    cols[...] = jnp.zeros_like(cols)
    o_in[QH:] = jnp.zeros((2, WIDE, WIDE), BF)
    for copy in copies:
        copy.wait()
    sel_in, sel_out, w_in, w_mid, w_out, bias = held
    parts = split_bias(bias[0:1, :])
    for p in range(GROUP):
        lanes = slice(p * FEAT, (p + 1) * FEAT)
        for c in range(3):
            rhs[p * 32 + c * 8 : p * 32 + c * 8 + 4, lanes] = w_in[c].astype(F32)
            rhs[p * 32 + 24 + c : p * 32 + 25 + c, lanes] = parts[c]
        cols[p * 8 : p * 8 + 4, lanes] = w_out[...].astype(F32)
    taps = rhs[...].astype(BF)
    for q in range(QH):
        part = sel_in[q * WIDE : (q + 1) * WIDE, :]
        o_in[q] = jnp.dot(part, taps, preferred_element_type=F32).astype(BF)
    for a, row in [(0, 0), (1, 1), (2, 2), (3, 3), (-2, 4), (-1, 5), (4, 6), (5, 7)]:
        for b in range(GROUP):
            if (a - b) % 2 == 0 and abs(a - b) <= 2:
                o_in[QH + row // 4, row % 4 * FEAT : (row % 4 + 1) * FEAT, b * FEAT : (b + 1) * FEAT] = w_mid[
                    (a - b) // 2 + 1
                ]
    leaving[0].start()
    back = jnp.transpose(cols[...]).astype(BF)
    for q in range(QS + 2):
        part = sel_out[q * SLAB : (q + 1) * SLAB, :]
        o_out[q] = jnp.dot(back, part, preferred_element_type=F32).astype(BF)
    leaving[1].start()
    for copy in leaving:
        copy.wait()


def pack_kernel(plan, traces, mixes, packet, held, mixed, done):
    place = places(plan, False)
    block, window = traces.shape
    groups = mixes.shape[0]
    share = packet.shape[2]
    copies = [pltpu.make_async_copy(traces, held, done.at[0])]
    at = pl.multiple_of(place[2] * share, share)
    for g in range(groups):
        into = mixed.at[g * block : (g + 1) * block, :]
        copies.append(pltpu.make_async_copy(mixes.at[g, :, pl.ds(at, share)], into, done.at[g + 1]))
    for copy in copies:
        copy.start()
    lines, each = plan.block_lines, plan.each
    row = lax.broadcasted_iota(jnp.int32, (block, block), 0)
    col = lax.broadcasted_iota(jnp.int32, (block, block), 1)
    spot, line = split_index(row, lines)
    order = (col == line * RPL + spot).astype(F32).astype(BF)
    rows = packet.shape[0] * groups * lines
    row = lax.broadcasted_iota(jnp.int32, (rows, groups * block), 0)
    col = lax.broadcasted_iota(jnp.int32, (rows, groups * block), 1)
    rest, line = split_index(row, lines)
    to, g = split_index(rest, groups)
    choose = (col == g * block + line * RPL + to * each + place[3]).astype(F32).astype(BF)
    for copy in copies:
        copy.wait()
    top = each * lines
    moved = jnp.dot(order, held[...], preferred_element_type=F32)
    packet[:, 0:top, :] = moved.reshape(packet.shape[0], top, share).astype(BF)
    moved = jnp.dot(choose, mixed[...], preferred_element_type=F32)
    packet[:, top:, :] = moved.reshape(packet.shape[0], groups * lines, share).astype(BF)


def places(plan, first):
    at_shot, at_line, at_tm = (lax.axis_index(a) for a in ("shot", "line", "tm"))
    if not plan.whole_lines:
        return at_shot, at_tm * plan.lines, at_tm, at_shot
    quarter = (at_line * plan.time_parts + at_tm) * plan.each
    return quarter if first else quarter + at_shot, 0, at_tm, at_shot


def split_index(value, size):
    if size & (size - 1):
        return value // size, value % size
    return value >> (size.bit_length() - 1), value & (size - 1)


def section_map(plan, place, tallies, stride):
    shape = (plan.rows, SLAB)
    lane = lax.broadcasted_iota(jnp.int32, shape, 1)
    apart, line = split_index(lax.broadcasted_iota(jnp.int32, shape, 0), plan.lines)
    block, line = split_index(line + place[1], plan.block_lines)
    spot = line * RPL + place[0] + apart * stride
    low = jnp.zeros(shape, jnp.int32)
    high = jnp.zeros(shape, jnp.int32)
    count = jnp.zeros(shape, jnp.int32)
    start = jnp.int32(0)
    for p in range(plan.sections):
        amount = tallies[p]
        for b in range(plan.blocks):
            here = lane == b * plan.sections + p
            low = jnp.where(here, start, low)
            high = jnp.where(here, start + amount, high)
            count = jnp.where(here, amount, count)
        start = start + amount
    member = (spot >= low) & (spot < high) & (split_index(lane, plan.sections)[0] == block)
    return member, count


def shifted(values, by, ok, edge):
    return jnp.where(ok, pltpu.roll(values, by % values.shape[0], 0), edge)


def pack_inputs(plan, channels, packed):
    lane = lax.broadcasted_iota(jnp.int32, (plan.rows, SLAB), 1)
    low = lane < HALF
    ones = ((lane >= ONES - SLAB) & (lane < ONES - SLAB + 3)).astype(F32)
    slabs = [[x[:, t * SLAB : (t + 1) * SLAB] for t in range(plan.slabs)] for x in channels]
    far = [[pltpu.roll(s, HALF + 1 + 2 * c, 1) for s in slabs[c]] for c in range(3)]
    for t in range(plan.slabs):
        v = [slabs[c][t] for c in range(3)]
        w = [pltpu.roll(s, HALF, 1) for s in v]
        even = jnp.where(low, v[2], ones)
        odd = jnp.where(low, w[2], ones)
        for c in range(3):
            left, right = lane == HALF + 2 * c, lane == HALF + 2 * c + 1
            near = pltpu.roll(v[c], 1 + 2 * c, 1)
            even = jnp.where(right, near, even)
            odd = jnp.where(left, near, odd)
            if t > 0:
                even = jnp.where(left, far[c][t - 1], even)
            if t < plan.slabs - 1:
                odd = jnp.where(right, far[c][t + 1], odd)
        packed[0, t, :, 0:SLAB] = jnp.where(low, v[0], w[1]).astype(BF)
        packed[0, t, :, SLAB:WIDE] = even.astype(BF)
        packed[1, t, :, 0:SLAB] = jnp.where(low, w[0], v[1]).astype(BF)
        packed[1, t, :, SLAB:WIDE] = odd.astype(BF)


def network(plan, weights, bias, scratch, ready=(lambda: None, lambda: None)):
    w_in, w_out = weights
    packed, hidden, total, ends = scratch
    many, rows = plan.slabs * plan.rows, plan.rows
    grid = (plan.slabs, rows, WIDE)
    pitch = plan.slabs + 2
    bias_two = jnp.concatenate([bias[1:2, :]] * GROUP, axis=1)

    def first(q):
        value = jnp.dot(packed[q >> 3].reshape(many, WIDE), w_in[q & 7], preferred_element_type=F32)
        hidden[pl.ds(q * pitch + 1, plan.slabs)] = jnp.maximum(value.astype(BF), 0).reshape(grid)

    def second(q, left_at, right_at):
        middle = hidden[pl.ds(q * pitch + 1, plan.slabs)]
        left = hidden[pl.ds(left_at, plan.slabs), :, SLAB:WIDE]
        right = hidden[pl.ds(right_at, plan.slabs), :, 0:SLAB]
        window = jnp.concatenate([middle, left, right], axis=2).reshape(many, 2 * WIDE)
        value = jnp.dot(window, w_in[QH:].reshape(2 * WIDE, WIDE), preferred_element_type=F32)
        return jnp.maximum((value + bias_two).astype(BF), 0)

    def onto(layer, q):
        return jnp.dot(layer, w_out[q], preferred_element_type=F32).reshape(plan.slabs, rows, SLAB)

    edge = jnp.zeros((rows, WIDE), BF)
    hidden[(QS - 1) * pitch] = edge
    hidden[pitch - 1] = edge
    total[...] = jnp.zeros_like(total)
    ready[0]()

    def first_some(i, _):
        for k in range(STEP):
            first(i * STEP + k)

    lax.fori_loop(0, QS // STEP, first_some, None)
    ready[1]()

    def second_some(i, _):
        for k in range(STEP):
            q = i * STEP + k
            left_at = jnp.where(q == 0, (QS - 1) * pitch, (q - 1) * pitch + 1) if k == 0 else (q - 1) * pitch + 1
            right_at = jnp.where(q == QS - 1, 2, (q + 1) * pitch + 1) if k == STEP - 1 else (q + 1) * pitch + 1
            layer = second(q, left_at, right_at)
            if k == 0:

                @pl.when(i == 0)
                def _():
                    ends[0] = layer

            if k == STEP - 1:

                @pl.when(i == QS // STEP - 1)
                def _():
                    ends[1] = layer

            total[...] += onto(layer, q)

    lax.fori_loop(0, QS // STEP, second_some, None)
    total[0 : plan.slabs - 1] += onto(ends[0], QS + 1)[1:]
    total[1 : plan.slabs] += onto(ends[1], QS)[: plan.slabs - 1]


def waits(fetches):
    return fetches[0].wait, fetches[1].wait


def add_total(plan, now, total, scale=None):
    for t in range(plan.slabs):
        lanes = slice(t * SLAB, (t + 1) * SLAB)
        more = total[t] if scale is None else scale * total[t]
        now[:, lanes] = (now[:, lanes] + more).astype(BF).astype(F32)


def shot_stage(plan, place, tallies, stride, edges, weights, fetches, bias, now, scratch):
    x = now[...]
    line = split_index(lax.broadcasted_iota(jnp.int32, x.shape, 0), plan.lines)[1]
    above = 0.0 if edges is None else edges[0].astype(F32)
    below = 0.0 if edges is None else edges[1].astype(F32)
    channels = [
        shifted(x, 1, line > 0, above),
        x,
        shifted(x, -1, line < plan.lines - 1, below),
    ]
    pack_inputs(plan, channels, scratch[0])
    network(plan, weights, bias, scratch, waits(fetches))
    add_total(plan, now, scratch[2])
    power = jnp.zeros((plan.rows, SLAB), F32)
    for t in range(plan.slabs):
        piece = now[:, t * SLAB : (t + 1) * SLAB]
        power = power + piece * piece
    member, _ = section_map(plan, place, tallies, stride)
    each = jnp.where(member, jnp.sum(power, axis=1, keepdims=True), 0.0)
    return jnp.sum(each, axis=0, keepdims=True)


def station_stage(
    plan, place, tallies, lags, order, pace, energies, mixes, weights, fetches, bias, now, scratch, blend
):
    member, count = section_map(plan, place, tallies, 0)
    totals = energies[...]
    denominator = jnp.maximum(count, 1) * (plan.shots * plan.slabs * SLAB)
    level = jnp.sqrt(totals / denominator.astype(F32) + EPSILON)
    rms = jnp.sum(jnp.where(member, level, 0.0), axis=1, keepdims=True)
    x = (now[...] / rms).astype(BF).astype(F32)
    row = lax.broadcasted_iota(jnp.int32, x.shape, 0)
    channels = [
        shifted(x, plan.lines, row >= plan.lines, 0.0),
        x,
        shifted(x, -plan.lines, row < plan.rows - plan.lines, 0.0),
    ]
    pack_inputs(plan, channels, scratch[0])
    network(plan, weights, bias, scratch, waits(fetches))
    add_total(plan, now, scratch[2], rms)

    fired, misfit = blend
    lane = lax.broadcasted_iota(jnp.int32, (plan.lines, SLAB), 1)
    mixtures = misfit.shape[0]
    per = plan.shots // mixtures
    if plan.whole_lines:
        for n in range(mixes.shape[0]):
            a, b = divmod(n, plan.time_parts)
            share = mixes.shape[2]
            piece = mixes[n, plan.each * plan.block_lines :, :].astype(F32)
            for g in range(mixtures):
                here = slice(a * plan.block_lines, (a + 1) * plan.block_lines)
                misfit[g, here, b * share : (b + 1) * share] = piece[g * plan.block_lines : (g + 1) * plan.block_lines]
    else:
        misfit[...] = mixes[...].astype(F32)
    for s in range(plan.shots):
        lag = lags[s]
        before = jnp.zeros((plan.lines, SLAB), F32)
        for t in range(plan.slabs):
            lanes = slice(t * SLAB, (t + 1) * SLAB)
            turned = pltpu.roll(now[s * plan.lines : (s + 1) * plan.lines, lanes], lag, 1)
            fired[s, :, lanes] = jnp.where(lane < lag, before, turned)
            before = turned
    for g in range(mixtures):
        value = fired[order[g * per]]
        for k in range(1, per):
            value = value + fired[order[g * per + k]]
        misfit[g] = value - misfit[g]
    for s in range(plan.shots):
        lag = lags[s]
        spot = jnp.int32(0)
        for k in range(plan.shots):
            spot = spot + jnp.where(order[k] == s, k, 0)
        which = spot // per
        back = (DMAX - lag) % DMAX
        after = jnp.zeros((plan.lines, SLAB), F32)
        rows = slice(s * plan.lines, (s + 1) * plan.lines)
        for t in range(plan.slabs - 1, -1, -1):
            lanes = slice(t * SLAB, (t + 1) * SLAB)
            turned = pltpu.roll(misfit[which, :, lanes], back, 1)
            pulled = jnp.where(lane < DMAX - lag, turned, after)
            after = turned
            now[rows, lanes] = (now[rows, lanes] - pace * pulled).astype(BF).astype(F32)


def stage_kernel(plan, station_round, with_shot, has_edges, stride, split_in, split_out, *refs):
    refs = list(refs)
    take = lambda n: [refs.pop(0) for _ in range(n)]
    tallies, lags, order, paces = take(4)
    place = places(plan, stride)
    sources = take(plan.each if split_in == "parts" else 1)
    source = sources[0]
    station = station_round is not None
    if station:
        energies, mixes, *station_weights, station_bias = take(5)
    edges = None
    if with_shot:
        if has_edges:
            (edges,) = take(1)
        *shot_weights, shot_bias = take(3)
    results = take(plan.each if split_out == "parts" else 1)
    result = results[0]
    if with_shot and split_out != "parts":
        (energy,) = take(1)
    now, packed, hidden, total, ends = take(5)
    scratch = (packed, hidden, total, ends)
    arrived = refs.pop()
    sets = ([station_weights] if station else []) + ([shot_weights] if with_shot else [])
    held = [[refs.pop(0) for _ in range(2)] for _ in sets]
    fetches = [
        [pltpu.make_async_copy(w, h, arrived.at[2 * n + i]) for i, (w, h) in enumerate(zip(sets[n], held[n]))]
        for n in range(len(sets))
    ]
    for fetch in sum(fetches, []):
        fetch.start()
    length = plan.slabs * SLAB
    if split_in == "parts":
        for d, part in enumerate(sources):
            at = pl.multiple_of((place[3] ^ d) * plan.lines, plan.lines)
            now[pl.ds(at, plan.lines), :] = part[:, 0:length].astype(F32)
    elif split_in:
        lines = plan.block_lines
        for n in range(source.shape[0]):
            a, b = divmod(n, plan.time_parts)
            share = source.shape[2]
            piece = source[n, 0 : plan.each * lines, :].astype(F32)
            for k in range(plan.each):
                row = k * plan.lines + a * lines
                now[row : row + lines, b * share : (b + 1) * share] = piece[k * lines : (k + 1) * lines]
    else:
        now[...] = source[...].astype(F32)
    if station:
        station_stage(
            plan,
            place,
            tallies,
            lags,
            order,
            paces[station_round],
            energies,
            mixes,
            held[0],
            fetches[0],
            station_bias,
            now,
            scratch,
            refs,
        )
    if with_shot:
        sums = shot_stage(plan, place, tallies, stride, edges, held[-1], fetches[-1], shot_bias, now, scratch)
    if split_out == "parts":
        row = lax.broadcasted_iota(jnp.int32, (plan.lines, SLAB), 0)
        beside = jnp.zeros((plan.lines, SLAB), F32)
        for i, part in enumerate(split_bias(sums)):
            beside = jnp.where(row == i, part, beside)
        for d, part in enumerate(results):
            at = pl.multiple_of((place[3] ^ d) * plan.lines, plan.lines)
            part[:, 0:length] = now[pl.ds(at, plan.lines), :].astype(BF)
            part[:, length:] = beside.astype(BF)
        return
    if with_shot:
        energy[...] = sums
    if split_out:
        for n, (row, lane, rows, lanes) in enumerate(plan.pieces):
            result[n] = now[row : row + rows, lane : lane + lanes].astype(BF)
    else:
        result[...] = now[...].astype(BF)


SMEM = pl.BlockSpec(memory_space=pltpu.SMEM)
VMEM = pl.BlockSpec(memory_space=pltpu.VMEM)
HBM = pl.BlockSpec(memory_space=pltpu.HBM)


def run_stage(plan, small, source, station=None, shot=None, split_in=False, split_out=False, stride=0, name="stage"):
    operands = [*small, *(source if split_in == "parts" else [source])]
    station_round, has_edges = None, False
    macs = 0
    pass_macs = plan.rows * plan.slabs * QS * WIDE * (WIDE * 3 + SLAB)
    if station is not None:
        station_round, energies, mixes, weights = station
        operands += [energies, mixes, *weights]
        macs += pass_macs
    if shot is not None:
        edges, weights = shot
        has_edges = edges is not None
        operands += ([edges] if has_edges else []) + list(weights)
        macs += pass_macs
    specs = [HBM if getattr(o, "ndim", 0) >= 2 and o.dtype == BF and o.shape[-2] == WIDE else VMEM for o in operands]
    specs[: len(small)] = [SMEM] * len(small)
    fetched = [o for o, spec in zip(operands, specs) if spec is HBM]
    length = plan.slabs * SLAB
    if split_out == "parts":
        shapes = [jax.ShapeDtypeStruct((plan.lines, length + SLAB), BF)] * plan.each
    elif split_out:
        _, _, rows, lanes = plan.pieces[0]
        shapes = [jax.ShapeDtypeStruct((len(plan.pieces), rows, lanes), BF)]
    else:
        shapes = [jax.ShapeDtypeStruct((plan.rows, length), BF)]
    if shot is not None and split_out != "parts":
        shapes.append(jax.ShapeDtypeStruct((1, SLAB), F32))
    scratch = [
        pltpu.VMEM((plan.rows, length), F32),
        pltpu.VMEM((2, plan.slabs, plan.rows, WIDE), BF),
        pltpu.VMEM((QS * (plan.slabs + 2), plan.rows, WIDE), BF),
        pltpu.VMEM((plan.slabs, plan.rows, SLAB), F32),
        pltpu.VMEM((2, plan.slabs * plan.rows, WIDE), BF),
    ]
    scratch += [pltpu.VMEM(w.shape, w.dtype) for w in fetched]
    if station is not None:
        scratch += [
            pltpu.VMEM((plan.shots, plan.lines, length), F32),
            pltpu.VMEM((plan.mixtures, plan.lines, length), F32),
        ]
    scratch += [pltpu.SemaphoreType.DMA((len(fetched),))]
    return pl.pallas_call(
        functools.partial(
            stage_kernel, plan, station_round, shot is not None, has_edges, stride, split_in, split_out
        ),
        out_shape=shapes,
        in_specs=specs,
        out_specs=[VMEM] * len(shapes),
        scratch_shapes=scratch,
        compiler_params=pltpu.CompilerParams(vmem_limit_bytes=VMEM_LIMIT),
        cost_estimate=pl.CostEstimate(flops=2 * macs, bytes_accessed=1 << 20, transcendentals=0),
        name=name,
    )(*operands)


def run_prepare(selectors, net, name):
    shapes = [
        jax.ShapeDtypeStruct((QH + 2, WIDE, WIDE), BF),
        jax.ShapeDtypeStruct((QS + 2, WIDE, SLAB), BF),
    ]
    operands = [*selectors, *net]
    scratch = [pltpu.VMEM((SLAB, WIDE), F32), pltpu.VMEM((SLAB, WIDE), F32)]
    scratch += [pltpu.VMEM(o.shape, o.dtype) for o in operands + shapes]
    scratch += [pltpu.SemaphoreType.DMA((len(operands),)), pltpu.SemaphoreType.DMA((len(shapes),))]
    return pl.pallas_call(
        prepare_kernel,
        out_shape=shapes,
        in_specs=[HBM] * len(operands),
        out_specs=[HBM] * len(shapes),
        scratch_shapes=scratch,
        compiler_params=pltpu.CompilerParams(vmem_limit_bytes=VMEM_FULL),
        cost_estimate=pl.CostEstimate(flops=2 * 8192 * WIDE * SLAB, bytes_accessed=4 << 20, transcendentals=0),
        name=name,
    )(*operands)


def run_pack(plan, traces, mixtures):
    groups, block, _ = mixtures.shape
    width = traces.shape[1]
    return pl.pallas_call(
        functools.partial(pack_kernel, plan),
        out_shape=jax.ShapeDtypeStruct((RPL // plan.each, (plan.each + groups) * plan.block_lines, width), BF),
        in_specs=[HBM, HBM],
        out_specs=VMEM,
        scratch_shapes=[
            pltpu.VMEM((block, width), BF),
            pltpu.VMEM((groups * block, width), BF),
            pltpu.SemaphoreType.DMA((groups + 1,)),
        ],
        compiler_params=pltpu.CompilerParams(vmem_limit_bytes=VMEM_FULL),
        cost_estimate=pl.CostEstimate(flops=2 * block * block * width, bytes_accessed=1 << 20, transcendentals=0),
        name="pack",
    )(traces, mixtures)


class Plan:
    def __init__(self, **sizes):
        self.__dict__.update(sizes)
        self.rows = self.shots * self.lines


def per_device(
    initial_guess,
    measured_mixtures,
    launch_lags,
    source_launch_order,
    station_portion_tallies,
    source_entry_kernel,
    source_spaced_kernel,
    source_exit_kernel,
    source_inner_offsets,
    station_entry_kernel,
    station_spaced_kernel,
    station_exit_kernel,
    station_inner_offsets,
    learned_pace_factors,
):
    shots_here, block, window = initial_guess.shape
    n_shot, n_line, n_tm = (lax.axis_size(a) for a in ("shot", "line", "tm"))
    at_shot, at_tm = lax.axis_index("shot"), lax.axis_index("tm")
    block_lines = block // RPL
    length = window * n_tm
    shots = shots_here * n_shot
    sections = station_portion_tallies.shape[0]
    mixtures = measured_mixtures.shape[0]
    whole_lines = n_shot * n_line * n_tm == RPL
    assert shots_here == 1 and (whole_lines or n_shot == RPL)
    if whole_lines:
        axes = ("line", "tm", "shot")
        lines, blocks = block_lines * n_line, n_line
    else:
        axes = ("shot", "tm")
        lines = block_lines // n_tm
        blocks = 1
    turns = [(s, a, b) for a in range(blocks) for b in range(n_tm) for s in range(n_shot)]
    plan = Plan(
        whole_lines=whole_lines,
        shots=shots,
        lines=lines,
        block_lines=block_lines,
        blocks=blocks,
        sections=sections,
        mixtures=mixtures,
        slabs=length // SLAB,
        each=n_shot,
        time_parts=n_tm,
        pieces=[(s * lines + a * block_lines, b * window, block_lines, window) for s, a, b in turns],
    )

    if whole_lines:
        leaving = run_pack(plan, initial_guess.reshape(block, window), measured_mixtures)
        arrived = lax.all_to_all(leaving, ("line", "tm"), split_axis=0, concat_axis=0, tiled=True)
    else:
        grid = initial_guess.reshape(n_tm, lines, RPL, window)
        leaving = grid.transpose(2, 0, 1, 3).reshape(RPL * n_tm, lines, window)
        arrived = lax.all_to_all(leaving, axes, split_axis=0, concat_axis=0, tiled=True)

    selectors = (jnp.asarray(entry_selector(), BF), jnp.asarray(exit_selector(), BF))
    shot_net = (
        source_entry_kernel.transpose(1, 0, 2),
        source_spaced_kernel,
        source_exit_kernel,
        source_inner_offsets,
    )
    station_net = (
        station_entry_kernel.transpose(1, 0, 2),
        station_spaced_kernel,
        station_exit_kernel,
        station_inner_offsets,
    )
    shot_weights = (*run_prepare(selectors, shot_net, "prepare_shot"), source_inner_offsets)
    small = (station_portion_tallies, launch_lags, source_launch_order, learned_pace_factors)
    split = whole_lines and block_lines % 8 == 0
    assert split or not whole_lines
    if whole_lines:
        mixes = source = arrived
    else:
        grid = measured_mixtures.reshape(mixtures, n_tm, lines, RPL, length)
        mixes = lax.dynamic_slice(
            grid, (0, at_tm, 0, at_shot, 0), (mixtures, 1, lines, 1, length)
        ).reshape(mixtures, lines, length)
        source = arrived.reshape(n_shot, n_tm, lines, window).transpose(0, 2, 1, 3).reshape(plan.rows, length)

    def edges_of(current):
        if whole_lines:
            return None
        size = n_line * n_tm
        grid = current.reshape(shots, lines, length)
        up = [(i, i + 1) for i in range(size - 1)]
        down = [(j, i) for i, j in up]
        above = lax.ppermute(grid[:, -1], ("line", "tm"), up)
        below = lax.ppermute(grid[:, 0], ("line", "tm"), down)
        wide = jnp.broadcast_to(jnp.stack([above, below])[:, :, None, :], (2, shots, lines, length))
        return wide.reshape(2, plan.rows, length)

    def summed(value, axis):
        size = lax.axis_size(axis)
        if size <= 4:
            others = [lax.ppermute(value, axis, [(i, i ^ d) for i in range(size)]) for d in range(1, size)]
            return sum(others, value)
        step = 1
        while step < size:
            value = value + lax.ppermute(value, axis, [(i, i ^ step) for i in range(size)])
            step *= 2
        return value

    def shared(energy, along):
        for axis in along:
            energy = summed(energy, axis)
        return energy

    if whole_lines:
        parts = run_stage(
            plan,
            small,
            source,
            shot=(None, shot_weights),
            split_in=split,
            split_out="parts",
            stride=1,
            name="shot_pass",
        )
        station_net, own = lax.optimization_barrier((station_net, parts[0]))
        current = [own]
        for d in range(1, n_shot):
            current.append(lax.ppermute(parts[d], "shot", [(i, i ^ d) for i in range(n_shot)]))
        energy = sum(jnp.sum(p[0:3, length:].astype(F32), axis=0, keepdims=True) for p in current)
        energy = shared(energy, ("tm", "line"))
    else:
        current, energy = run_stage(
            plan, small, source, shot=(edges_of(source), shot_weights), split_in=split, name="shot_pass"
        )
        energy = shared(energy, ("tm", "shot"))
    station_weights = (*run_prepare(selectors, station_net, "prepare_station"), station_inner_offsets)
    for i in range(ITERS):
        station = (i, energy, mixes, station_weights)
        form = "parts" if whole_lines and i == 0 else False
        if i == ITERS - 1:
            (current,) = run_stage(
                plan, small, current, station=station, split_in=form, split_out=split, name="station_pass"
            )
        elif whole_lines:
            current, energy = run_stage(
                plan,
                small,
                current,
                station=station,
                shot=(None, shot_weights),
                split_in=form,
                name="station_and_shot_pass",
            )
            energy = shared(energy, ("tm", "line", "shot"))
        else:
            (current,) = run_stage(plan, small, current, station=station, name="station_pass")
            current, energy = run_stage(plan, small, current, shot=(edges_of(current), shot_weights), name="shot_pass")
            energy = shared(energy, ("tm", "shot"))
    if not split:
        current = current.reshape(n_shot, lines, n_tm, window).transpose(0, 2, 1, 3).reshape(-1, lines, window)
    back = lax.all_to_all(current, axes, split_axis=0, concat_axis=0, tiled=True)
    if whole_lines:
        back = back.transpose(1, 0, 2)
    else:
        back = back.reshape(RPL, n_tm, lines, window).transpose(1, 2, 0, 3)
    return back.reshape(shots_here, block, window)


def solution(mesh):
    placed = (P(("group", "shot"), "line", "tm"), P("group", "line", None), P("group"), P("group"), P("group"))
    return jax.shard_map(
        per_device,
        mesh=mesh,
        in_specs=placed + (P(),) * 9,
        out_specs=P(("group", "shot"), "line", "tm"),
        check_vma=False,
    )
```

```python
import functools

import jax
import jax.numpy as jnp
import numpy as np
from jax import lax
from jax.experimental import pallas as pl
from jax.experimental.pallas import tpu as pltpu
from jax.sharding import PartitionSpec as P

RPL = 16
DMAX = 128
ITERS = 2
EPSILON = 1e-05

SLAB = 128
HALF = 64
FEAT = 64
GROUP = 4
WIDE = GROUP * FEAT
QS = SLAB // (2 * GROUP)
QH = QS // 2
assert QH == 8
ONES = 3 * HALF + 6
VMEM_LIMIT = 53 * 1024 * 1024
VMEM_FULL = 63 * 1024 * 1024

BF = jnp.bfloat16
F32 = jnp.float32


def entry_selector():
    picks = np.zeros((QH, WIDE, GROUP, 4, 8), np.float32)
    for j in range(3):
        picks[:, ONES + j, :, 3, j] = 1
    for q in range(QH):
        for p in range(GROUP):
            for j in range(4):
                i = 2 * (GROUP * q + p) + j - 1
                for c in range(3):
                    if i < 0:
                        lane = 3 * HALF + 2 * c
                    elif i >= HALF:
                        lane = 3 * HALF + 2 * c + 1
                    else:
                        lane = c * HALF + i
                    picks[q, lane, p, c, j] = 1
    return picks.reshape(QH * WIDE, GROUP * 4 * 8)


def exit_selector():
    picks = np.zeros((QS + 2, SLAB, SLAB), np.float32)
    for q in range(QS):
        for p in range(GROUP):
            for j in range(4):
                i = 2 * (GROUP * q + p) + j - 1
                if i < 0:
                    picks[QS + 1, p * 8 + j, SLAB - 1] = 1
                elif i >= SLAB:
                    picks[QS, p * 8 + j, 0] = 1
                else:
                    picks[q, p * 8 + j, i] = 1
    return picks.reshape((QS + 2) * SLAB, SLAB)


def split_bias(bias):
    high = bias.astype(BF).astype(F32)
    middle = (bias - high).astype(BF).astype(F32)
    return high, middle, bias - high - middle


def prepare_kernel(*refs):
    sources, outs = refs[:6], refs[6:8]
    (rhs, cols), held, (o_in, o_out), (done, sent) = refs[8:10], refs[10:16], refs[16:18], refs[18:20]
    copies = [pltpu.make_async_copy(src, dst, done.at[i]) for i, (src, dst) in enumerate(zip(sources, held))]
    leaving = [pltpu.make_async_copy(src, dst, sent.at[i]) for i, (src, dst) in enumerate(zip((o_in, o_out), outs))]
    for copy in copies:
        copy.start()
    rhs[...] = jnp.zeros_like(rhs)
    cols[...] = jnp.zeros_like(cols)
    o_in[QH:] = jnp.zeros((2, WIDE, WIDE), BF)
    for copy in copies:
        copy.wait()
    sel_in, sel_out, w_in, w_mid, w_out, bias = held
    parts = split_bias(bias[0:1, :])
    for p in range(GROUP):
        lanes = slice(p * FEAT, (p + 1) * FEAT)
        for c in range(3):
            rhs[p * 32 + c * 8 : p * 32 + c * 8 + 4, lanes] = w_in[c].astype(F32)
            rhs[p * 32 + 24 + c : p * 32 + 25 + c, lanes] = parts[c]
        cols[p * 8 : p * 8 + 4, lanes] = w_out[...].astype(F32)
    taps = rhs[...].astype(BF)
    for q in range(QH):
        part = sel_in[q * WIDE : (q + 1) * WIDE, :]
        o_in[q] = jnp.dot(part, taps, preferred_element_type=F32).astype(BF)
    for a, row in [(0, 0), (1, 1), (2, 2), (3, 3), (-2, 4), (-1, 5), (4, 6), (5, 7)]:
        for b in range(GROUP):
            if (a - b) % 2 == 0 and abs(a - b) <= 2:
                o_in[QH + row // 4, row % 4 * FEAT : (row % 4 + 1) * FEAT, b * FEAT : (b + 1) * FEAT] = w_mid[
                    (a - b) // 2 + 1
                ]
    leaving[0].start()
    back = jnp.transpose(cols[...]).astype(BF)
    for q in range(QS + 2):
        part = sel_out[q * SLAB : (q + 1) * SLAB, :]
        o_out[q] = jnp.dot(back, part, preferred_element_type=F32).astype(BF)
    leaving[1].start()
    for copy in leaving:
        copy.wait()


def pack_kernel(plan, traces, mixes, *refs):
    count = plan.packets
    packets, (held, mixed, done) = refs[:count], refs[count:]
    _, _, at_tm, at_shot, mine = places(plan, False)
    block, share = traces.shape
    groups = mixes.shape[0]
    copies = [pltpu.make_async_copy(traces, held, done.at[0])]
    at = pl.multiple_of(at_tm * share, share)
    for g in range(groups):
        into = mixed.at[g * block : (g + 1) * block, :]
        copies.append(pltpu.make_async_copy(mixes.at[g, :, pl.ds(at, share)], into, done.at[g + 1]))
    for copy in copies:
        copy.start()
    lines, each = plan.block_lines, plan.each
    row = lax.broadcasted_iota(jnp.int32, (block, block), 0)
    col = lax.broadcasted_iota(jnp.int32, (block, block), 1)
    rest, line = split_index(row, lines)
    d, spot = split_index(rest, each)
    order = (col == line * RPL + (d ^ mine) * each + spot).astype(F32).astype(BF)
    rows = count * groups * lines
    row = lax.broadcasted_iota(jnp.int32, (rows, groups * block), 0)
    col = lax.broadcasted_iota(jnp.int32, (rows, groups * block), 1)
    rest, line = split_index(row, lines)
    d, g = split_index(rest, groups)
    choose = (col == g * block + line * RPL + (d ^ mine) * each + at_shot).astype(F32).astype(BF)
    for copy in copies:
        copy.wait()
    top, rest = each * lines, groups * lines
    moved = jnp.dot(order, held[...], preferred_element_type=F32)
    picked = jnp.dot(choose, mixed[...], preferred_element_type=F32)
    for d, packet in enumerate(packets):
        packet[0:top, :] = moved[d * top : (d + 1) * top].astype(BF)
        packet[top:, :] = picked[d * rest : (d + 1) * rest].astype(BF)


def places(plan, first):
    at_shot, at_line, at_tm = (lax.axis_index(a) for a in ("shot", "line", "tm"))
    if not plan.whole_lines:
        return at_shot, at_tm * plan.lines, at_tm, at_shot, 0
    mine = at_line * plan.time_parts + at_tm
    return mine * plan.each + (0 if first else at_shot), 0, at_tm, at_shot, mine


def split_index(value, size):
    if size & (size - 1):
        return value // size, value % size
    return value >> (size.bit_length() - 1), value & (size - 1)


def section_map(plan, place, tallies, stride):
    shape = (plan.rows, SLAB)
    lane = lax.broadcasted_iota(jnp.int32, shape, 1)
    apart, line = split_index(lax.broadcasted_iota(jnp.int32, shape, 0), plan.lines)
    block, line = split_index(line + place[1], plan.block_lines)
    spot = line * RPL + place[0] + apart * stride
    low = jnp.zeros(shape, jnp.int32)
    high = jnp.zeros(shape, jnp.int32)
    count = jnp.zeros(shape, jnp.int32)
    start = jnp.int32(0)
    for p in range(plan.sections):
        amount = tallies[p]
        for b in range(plan.blocks):
            here = lane == b * plan.sections + p
            low = jnp.where(here, start, low)
            high = jnp.where(here, start + amount, high)
            count = jnp.where(here, amount, count)
        start = start + amount
    member = (spot >= low) & (spot < high) & (split_index(lane, plan.sections)[0] == block)
    return member, count


def shifted(values, by, ok, edge):
    return jnp.where(ok, pltpu.roll(values, by % values.shape[0], 0), edge)


def pack_inputs(plan, channels, packed):
    lane = lax.broadcasted_iota(jnp.int32, (plan.rows, SLAB), 1)
    low = lane < HALF
    ones = ((lane >= ONES - SLAB) & (lane < ONES - SLAB + 3)).astype(F32)
    slabs = [[x[:, t * SLAB : (t + 1) * SLAB] for t in range(plan.slabs)] for x in channels]
    far = [[pltpu.roll(s, HALF + 1 + 2 * c, 1) for s in slabs[c]] for c in range(3)]
    for t in range(plan.slabs):
        v = [slabs[c][t] for c in range(3)]
        w = [pltpu.roll(s, HALF, 1) for s in v]
        even = jnp.where(low, v[2], ones)
        odd = jnp.where(low, w[2], ones)
        for c in range(3):
            left, right = lane == HALF + 2 * c, lane == HALF + 2 * c + 1
            near = pltpu.roll(v[c], 1 + 2 * c, 1)
            even = jnp.where(right, near, even)
            odd = jnp.where(left, near, odd)
            if t > 0:
                even = jnp.where(left, far[c][t - 1], even)
            if t < plan.slabs - 1:
                odd = jnp.where(right, far[c][t + 1], odd)
        packed[0, t, :, 0:SLAB] = jnp.where(low, v[0], w[1]).astype(BF)
        packed[0, t, :, SLAB:WIDE] = even.astype(BF)
        packed[1, t, :, 0:SLAB] = jnp.where(low, w[0], v[1]).astype(BF)
        packed[1, t, :, SLAB:WIDE] = odd.astype(BF)


def network(plan, weights, bias, scratch, ready, steps):
    w_in, w_out = weights
    packed, hidden, total, ends = scratch
    slabs, rows = plan.slabs, plan.rows
    many = slabs * rows
    pitch = slabs + 2
    bias_two = jnp.concatenate([bias[1:2, :]] * GROUP, axis=1)

    def first(q):
        value = jnp.dot(packed[...].reshape(2 * many, WIDE), w_in[q], preferred_element_type=F32)
        value = jnp.maximum(value.astype(BF), 0).reshape(2, slabs, rows, WIDE)
        for h in range(2):
            hidden[pl.ds((q + h * QH) * pitch + 1, slabs)] = value[h]

    def window(q, left_at, right_at):
        middle = hidden[pl.ds(q * pitch + 1, slabs)]
        left = hidden[pl.ds(left_at, slabs), :, SLAB:WIDE]
        right = hidden[pl.ds(right_at, slabs), :, 0:SLAB]
        return jnp.concatenate([middle, left, right], axis=2).reshape(many, 2 * WIDE)

    def second(q):
        left_at = (q - 1) * pitch + 1
        right_at = (q + 2) * pitch + 1
        if isinstance(q, int):
            left_at = (QS - 1) * pitch if q == 0 else left_at
            right_at = 2 if q == QS - 2 else right_at
        else:
            left_at = jnp.where(q == 0, (QS - 1) * pitch, left_at)
            right_at = jnp.where(q == QS - 2, 2, right_at)
        both = jnp.concatenate(
            [window(q, left_at, (q + 1) * pitch + 1), window(q + 1, q * pitch + 1, right_at)], axis=0
        )
        value = jnp.dot(both, w_in[QH:].reshape(2 * WIDE, WIDE), preferred_element_type=F32)
        value = jnp.maximum((value + bias_two).astype(BF), 0)
        return value[:many], value[many:]

    def onto(layer, taps):
        return jnp.dot(layer, taps, preferred_element_type=F32).reshape(slabs, rows, SLAB)

    edge = jnp.zeros((rows, WIDE), BF)
    hidden[(QS - 1) * pitch] = edge
    hidden[pitch - 1] = edge
    total[...] = jnp.zeros_like(total)
    ready[0]()

    def first_some(i):
        for k in range(QH // steps):
            first(i * (QH // steps) + k)

    def second_some(i):
        each = QS // steps
        for k in range(0, each, 2):
            q = i * each + k
            one, two = second(q)
            total[...] += onto(jnp.concatenate([one, two], axis=1), w_out[pl.ds(q, 2)].reshape(2 * WIDE, SLAB))
            if k == 0:
                keep(i == 0, 0, one)
            if k == each - 2:
                keep(i == steps - 1, 1, two)

    def keep(now, at, layer):
        if isinstance(now, bool):
            if now:
                ends[at] = layer
            return

        @pl.when(now)
        def _():
            ends[at] = layer

    def repeat(body):
        if steps == 1:
            body(0)
        else:
            lax.fori_loop(0, steps, lambda i, _: body(i), None)

    repeat(first_some)
    ready[1]()
    repeat(second_some)
    total[0 : slabs - 1] += onto(ends[0], w_out[QS + 1])[1:]
    total[1:slabs] += onto(ends[1], w_out[QS])[: slabs - 1]


def waits(fetches):
    return fetches[0].wait, fetches[1].wait


def add_total(plan, now, total, scale=None):
    for t in range(plan.slabs):
        lanes = slice(t * SLAB, (t + 1) * SLAB)
        more = total[t] if scale is None else scale * total[t]
        now[:, lanes] = (now[:, lanes] + more).astype(BF).astype(F32)


def shot_stage(plan, place, tallies, stride, edges, weights, fetches, bias, now, scratch):
    x = now[...]
    line = split_index(lax.broadcasted_iota(jnp.int32, x.shape, 0), plan.lines)[1]
    above = 0.0 if edges is None else edges[0].astype(F32)
    below = 0.0 if edges is None else edges[1].astype(F32)
    channels = [
        shifted(x, 1, line > 0, above),
        x,
        shifted(x, -1, line < plan.lines - 1, below),
    ]
    pack_inputs(plan, channels, scratch[0])
    network(plan, weights, bias, scratch, waits(fetches), 2)
    add_total(plan, now, scratch[2])
    power = jnp.zeros((plan.rows, SLAB), F32)
    for t in range(plan.slabs):
        piece = now[:, t * SLAB : (t + 1) * SLAB]
        power = power + piece * piece
    member, _ = section_map(plan, place, tallies, stride)
    each = jnp.where(member, jnp.sum(power, axis=1, keepdims=True), 0.0)
    return jnp.sum(each, axis=0, keepdims=True)


def packet_place(plan, place, d, share):
    a, b = split_index(place[4] ^ d, plan.time_parts)
    row = pl.multiple_of(a * plan.block_lines, plan.block_lines)
    return pl.ds(row, plan.block_lines), pl.ds(pl.multiple_of(b * share, share), share)


def station_stage(
    plan, place, tallies, lags, order, pace, energies, mixes, weights, fetches, bias, now, scratch, blend
):
    member, count = section_map(plan, place, tallies, 0)
    totals = energies[...]
    denominator = jnp.maximum(count, 1) * (plan.shots * plan.slabs * SLAB)
    level = jnp.sqrt(totals / denominator.astype(F32) + EPSILON)
    rms = jnp.sum(jnp.where(member, level, 0.0), axis=1, keepdims=True)
    x = (now[...] / rms).astype(BF).astype(F32)
    row = lax.broadcasted_iota(jnp.int32, x.shape, 0)
    channels = [
        shifted(x, plan.lines, row >= plan.lines, 0.0),
        x,
        shifted(x, -plan.lines, row < plan.rows - plan.lines, 0.0),
    ]
    pack_inputs(plan, channels, scratch[0])
    network(plan, weights, bias, scratch, waits(fetches), 1)
    add_total(plan, now, scratch[2], rms)

    fired, misfit = blend
    lane = lax.broadcasted_iota(jnp.int32, (plan.lines, SLAB), 1)
    mixtures = misfit.shape[0]
    per = plan.shots // mixtures
    if plan.whole_lines:
        for d, packet in enumerate(mixes):
            here, lanes = packet_place(plan, place, d, packet.shape[1])
            piece = packet[plan.each * plan.block_lines :, :].astype(F32)
            for g in range(mixtures):
                misfit[g, here, lanes] = piece[g * plan.block_lines : (g + 1) * plan.block_lines]
    else:
        misfit[...] = mixes[0][...].astype(F32)
    for s in range(plan.shots):
        lag = lags[s]
        before = jnp.zeros((plan.lines, SLAB), F32)
        for t in range(plan.slabs):
            lanes = slice(t * SLAB, (t + 1) * SLAB)
            turned = pltpu.roll(now[s * plan.lines : (s + 1) * plan.lines, lanes], lag, 1)
            fired[s, :, lanes] = jnp.where(lane < lag, before, turned)
            before = turned
    for g in range(mixtures):
        value = fired[order[g * per]]
        for k in range(1, per):
            value = value + fired[order[g * per + k]]
        misfit[g] = value - misfit[g]
    for s in range(plan.shots):
        lag = lags[s]
        spot = jnp.int32(0)
        for k in range(plan.shots):
            spot = spot + jnp.where(order[k] == s, k, 0)
        which = spot // per
        back = (DMAX - lag) % DMAX
        after = jnp.zeros((plan.lines, SLAB), F32)
        rows = slice(s * plan.lines, (s + 1) * plan.lines)
        for t in range(plan.slabs - 1, -1, -1):
            lanes = slice(t * SLAB, (t + 1) * SLAB)
            turned = pltpu.roll(misfit[which, :, lanes], back, 1)
            pulled = jnp.where(lane < DMAX - lag, turned, after)
            after = turned
            now[rows, lanes] = (now[rows, lanes] - pace * pulled).astype(BF).astype(F32)


def stage_kernel(plan, station_round, with_shot, has_edges, stride, split_in, split_out, *refs):
    refs = list(refs)
    take = lambda n: [refs.pop(0) for _ in range(n)]
    tallies, lags, order, paces = take(4)
    place = places(plan, stride)
    sources = take({"parts": plan.each, "packets": plan.packets}.get(split_in, 1))
    source = sources[0]
    station = station_round is not None
    if station:
        (energies,) = take(1)
        mixes = take(plan.packets)
        *station_weights, station_bias = take(3)
    edges = None
    if with_shot:
        if has_edges:
            (edges,) = take(1)
        *shot_weights, shot_bias = take(3)
    results = take(plan.each if split_out == "parts" else 1)
    result = results[0]
    if with_shot and split_out != "parts":
        (energy,) = take(1)
    now, packed, hidden, total, ends = take(5)
    scratch = (packed, hidden, total, ends)
    arrived = refs.pop()
    sets = ([station_weights] if station else []) + ([shot_weights] if with_shot else [])
    held = [[refs.pop(0) for _ in range(2)] for _ in sets]
    fetches = [
        [pltpu.make_async_copy(w, h, arrived.at[2 * n + i]) for i, (w, h) in enumerate(zip(sets[n], held[n]))]
        for n in range(len(sets))
    ]
    for fetch in sum(fetches, []):
        fetch.start()
    length = plan.slabs * SLAB
    if split_in == "parts":
        for d, part in enumerate(sources):
            at = pl.multiple_of((place[3] ^ d) * plan.lines, plan.lines)
            now[pl.ds(at, plan.lines), :] = part[:, 0:length].astype(F32)
    elif split_in:
        lines = plan.block_lines
        for d, packet in enumerate(sources):
            here, lanes = packet_place(plan, place, d, packet.shape[1])
            piece = packet[0 : plan.each * lines, :].astype(F32)
            for k in range(plan.each):
                now[pl.ds(k * plan.lines + here.start, lines), lanes] = piece[k * lines : (k + 1) * lines]
    else:
        now[...] = source[...].astype(F32)
    if station:
        station_stage(
            plan,
            place,
            tallies,
            lags,
            order,
            paces[station_round],
            energies,
            mixes,
            held[0],
            fetches[0],
            station_bias,
            now,
            scratch,
            refs,
        )
    if with_shot:
        sums = shot_stage(plan, place, tallies, stride, edges, held[-1], fetches[-1], shot_bias, now, scratch)
    if split_out == "parts":
        row = lax.broadcasted_iota(jnp.int32, (plan.lines, SLAB), 0)
        beside = jnp.zeros((plan.lines, SLAB), F32)
        for i, part in enumerate(split_bias(sums)):
            beside = jnp.where(row == i, part, beside)
        for d, part in enumerate(results):
            at = pl.multiple_of((place[3] ^ d) * plan.lines, plan.lines)
            part[:, 0:length] = now[pl.ds(at, plan.lines), :].astype(BF)
            part[:, length:] = beside.astype(BF)
        return
    if with_shot:
        energy[...] = sums
    if split_out:
        for n, (row, lane, rows, lanes) in enumerate(plan.pieces):
            result[n] = now[row : row + rows, lane : lane + lanes].astype(BF)
    else:
        result[...] = now[...].astype(BF)


SMEM = pl.BlockSpec(memory_space=pltpu.SMEM)
VMEM = pl.BlockSpec(memory_space=pltpu.VMEM)
HBM = pl.BlockSpec(memory_space=pltpu.HBM)


def run_stage(plan, small, source, station=None, shot=None, split_in=False, split_out=False, stride=0, name="stage"):
    operands = [*small, *(source if split_in else [source])]
    station_round, has_edges = None, False
    macs = 0
    pass_macs = plan.rows * plan.slabs * QS * WIDE * (WIDE * 3 + SLAB)
    if station is not None:
        station_round, energies, mixes, weights = station
        operands += [energies, *mixes, *weights]
        macs += pass_macs
    if shot is not None:
        edges, weights = shot
        has_edges = edges is not None
        operands += ([edges] if has_edges else []) + list(weights)
        macs += pass_macs
    specs = [HBM if getattr(o, "ndim", 0) >= 2 and o.dtype == BF and o.shape[-2] == WIDE else VMEM for o in operands]
    specs[: len(small)] = [SMEM] * len(small)
    fetched = [o for o, spec in zip(operands, specs) if spec is HBM]
    length = plan.slabs * SLAB
    if split_out == "parts":
        shapes = [jax.ShapeDtypeStruct((plan.lines, length + SLAB), BF)] * plan.each
    elif split_out:
        _, _, rows, lanes = plan.pieces[0]
        shapes = [jax.ShapeDtypeStruct((len(plan.pieces), rows, lanes), BF)]
    else:
        shapes = [jax.ShapeDtypeStruct((plan.rows, length), BF)]
    if shot is not None and split_out != "parts":
        shapes.append(jax.ShapeDtypeStruct((1, SLAB), F32))
    scratch = [
        pltpu.VMEM((plan.rows, length), F32),
        pltpu.VMEM((2, plan.slabs, plan.rows, WIDE), BF),
        pltpu.VMEM((QS * (plan.slabs + 2), plan.rows, WIDE), BF),
        pltpu.VMEM((plan.slabs, plan.rows, SLAB), F32),
        pltpu.VMEM((2, plan.slabs * plan.rows, WIDE), BF),
    ]
    scratch += [pltpu.VMEM(w.shape, w.dtype) for w in fetched]
    if station is not None:
        scratch += [
            pltpu.VMEM((plan.shots, plan.lines, length), F32),
            pltpu.VMEM((plan.mixtures, plan.lines, length), F32),
        ]
    scratch += [pltpu.SemaphoreType.DMA((len(fetched),))]
    return pl.pallas_call(
        functools.partial(
            stage_kernel, plan, station_round, shot is not None, has_edges, stride, split_in, split_out
        ),
        out_shape=shapes,
        in_specs=specs,
        out_specs=[VMEM] * len(shapes),
        scratch_shapes=scratch,
        compiler_params=pltpu.CompilerParams(vmem_limit_bytes=VMEM_LIMIT),
        cost_estimate=pl.CostEstimate(flops=2 * macs, bytes_accessed=1 << 20, transcendentals=0),
        name=name,
    )(*operands)


def run_prepare(selectors, net, name):
    shapes = [
        jax.ShapeDtypeStruct((QH + 2, WIDE, WIDE), BF),
        jax.ShapeDtypeStruct((QS + 2, WIDE, SLAB), BF),
    ]
    operands = [*selectors, *net]
    scratch = [pltpu.VMEM((SLAB, WIDE), F32), pltpu.VMEM((SLAB, WIDE), F32)]
    scratch += [pltpu.VMEM(o.shape, o.dtype) for o in operands + shapes]
    scratch += [pltpu.SemaphoreType.DMA((len(operands),)), pltpu.SemaphoreType.DMA((len(shapes),))]
    return pl.pallas_call(
        prepare_kernel,
        out_shape=shapes,
        in_specs=[HBM] * len(operands),
        out_specs=[HBM] * len(shapes),
        scratch_shapes=scratch,
        compiler_params=pltpu.CompilerParams(vmem_limit_bytes=VMEM_FULL),
        cost_estimate=pl.CostEstimate(flops=2 * 8192 * WIDE * SLAB, bytes_accessed=4 << 20, transcendentals=0),
        name=name,
    )(*operands)


def run_pack(plan, traces, mixtures):
    groups, block, _ = mixtures.shape
    width = traces.shape[1]
    return pl.pallas_call(
        functools.partial(pack_kernel, plan),
        out_shape=[jax.ShapeDtypeStruct(((plan.each + groups) * plan.block_lines, width), BF)] * plan.packets,
        in_specs=[HBM, HBM],
        out_specs=[VMEM] * plan.packets,
        scratch_shapes=[
            pltpu.VMEM((block, width), BF),
            pltpu.VMEM((groups * block, width), BF),
            pltpu.SemaphoreType.DMA((groups + 1,)),
        ],
        compiler_params=pltpu.CompilerParams(vmem_limit_bytes=VMEM_FULL),
        cost_estimate=pl.CostEstimate(flops=2 * block * block * width, bytes_accessed=1 << 20, transcendentals=0),
        name="pack",
    )(traces, mixtures)


class Plan:
    def __init__(self, **sizes):
        self.__dict__.update(sizes)
        self.rows = self.shots * self.lines


def exchanged(parts, axes):
    size = len(parts)
    return [parts[0]] + [lax.ppermute(parts[d], axes, [(i, i ^ d) for i in range(size)]) for d in range(1, size)]


def per_device(
    initial_guess,
    measured_mixtures,
    launch_lags,
    source_launch_order,
    station_portion_tallies,
    source_entry_kernel,
    source_spaced_kernel,
    source_exit_kernel,
    source_inner_offsets,
    station_entry_kernel,
    station_spaced_kernel,
    station_exit_kernel,
    station_inner_offsets,
    learned_pace_factors,
):
    shots_here, block, window = initial_guess.shape
    n_shot, n_line, n_tm = (lax.axis_size(a) for a in ("shot", "line", "tm"))
    at_shot, at_tm = lax.axis_index("shot"), lax.axis_index("tm")
    block_lines = block // RPL
    length = window * n_tm
    shots = shots_here * n_shot
    sections = station_portion_tallies.shape[0]
    mixtures = measured_mixtures.shape[0]
    whole_lines = n_shot * n_line * n_tm == RPL
    assert shots_here == 1 and (whole_lines or n_shot == RPL)
    if whole_lines:
        axes = ("line", "tm", "shot")
        lines, blocks = block_lines * n_line, n_line
    else:
        axes = ("shot", "tm")
        lines = block_lines // n_tm
        blocks = 1
    turns = [(s, a, b) for a in range(blocks) for b in range(n_tm) for s in range(n_shot)]
    plan = Plan(
        whole_lines=whole_lines,
        shots=shots,
        lines=lines,
        block_lines=block_lines,
        blocks=blocks,
        sections=sections,
        mixtures=mixtures,
        slabs=length // SLAB,
        each=n_shot,
        time_parts=n_tm,
        packets=n_line * n_tm if whole_lines else 1,
        pieces=[(s * lines + a * block_lines, b * window, block_lines, window) for s, a, b in turns],
    )

    if whole_lines:
        assert n_line & (n_line - 1) == 0 and n_tm & (n_tm - 1) == 0 and n_shot & (n_shot - 1) == 0
        arrived = run_pack(plan, initial_guess.reshape(block, window), measured_mixtures)
        arrived = exchanged(arrived, ("line", "tm"))
    else:
        grid = initial_guess.reshape(n_tm, lines, RPL, window)
        leaving = grid.transpose(2, 0, 1, 3).reshape(RPL * n_tm, lines, window)
        arrived = lax.all_to_all(leaving, axes, split_axis=0, concat_axis=0, tiled=True)

    selectors = (jnp.asarray(entry_selector(), BF), jnp.asarray(exit_selector(), BF))
    shot_net = (
        source_entry_kernel.transpose(1, 0, 2),
        source_spaced_kernel,
        source_exit_kernel,
        source_inner_offsets,
    )
    station_net = (
        station_entry_kernel.transpose(1, 0, 2),
        station_spaced_kernel,
        station_exit_kernel,
        station_inner_offsets,
    )
    shot_weights = (*run_prepare(selectors, shot_net, "prepare_shot"), source_inner_offsets)
    small = (station_portion_tallies, launch_lags, source_launch_order, learned_pace_factors)
    split = whole_lines and block_lines % 8 == 0
    assert split or not whole_lines
    if whole_lines:
        mixes = source = arrived
    else:
        grid = measured_mixtures.reshape(mixtures, n_tm, lines, RPL, length)
        mixes = lax.dynamic_slice(grid, (0, at_tm, 0, at_shot, 0), (mixtures, 1, lines, 1, length))
        mixes = [mixes.reshape(mixtures, lines, length)]
        source = arrived.reshape(n_shot, n_tm, lines, window).transpose(0, 2, 1, 3).reshape(plan.rows, length)

    def edges_of(current):
        if whole_lines:
            return None
        size = n_line * n_tm
        grid = current.reshape(shots, lines, length)
        up = [(i, i + 1) for i in range(size - 1)]
        down = [(j, i) for i, j in up]
        above = lax.ppermute(grid[:, -1], ("line", "tm"), up)
        below = lax.ppermute(grid[:, 0], ("line", "tm"), down)
        wide = jnp.broadcast_to(jnp.stack([above, below])[:, :, None, :], (2, shots, lines, length))
        return wide.reshape(2, plan.rows, length)

    def summed(value, axis):
        size = lax.axis_size(axis)
        if size <= 4:
            others = [lax.ppermute(value, axis, [(i, i ^ d) for i in range(size)]) for d in range(1, size)]
            return sum(others, value)
        step = 1
        while step < size:
            value = value + lax.ppermute(value, axis, [(i, i ^ step) for i in range(size)])
            step *= 2
        return value

    def shared(energy, along):
        for axis in along:
            energy = summed(energy, axis)
        return energy

    if whole_lines:
        parts = run_stage(
            plan,
            small,
            source,
            shot=(None, shot_weights),
            split_in="packets",
            split_out="parts",
            stride=1,
            name="shot_pass",
        )
        station_net, own = lax.optimization_barrier((station_net, parts[0]))
        current = exchanged([own, *parts[1:]], "shot")
        station_weights = run_prepare(selectors, station_net, "prepare_station")
        energy = sum(jnp.sum(p[0:3, length:].astype(F32), axis=0, keepdims=True) for p in current)
        station_weights, energy = lax.optimization_barrier((station_weights, energy))
        energy = shared(energy, ("tm", "line"))
    else:
        current, energy = run_stage(
            plan, small, source, shot=(edges_of(source), shot_weights), name="shot_pass"
        )
        energy = shared(energy, ("tm", "shot"))
        station_weights = run_prepare(selectors, station_net, "prepare_station")
    station_weights = (*station_weights, station_inner_offsets)
    for i in range(ITERS):
        station = (i, energy, mixes, station_weights)
        form = "parts" if whole_lines and i == 0 else False
        if i == ITERS - 1:
            (current,) = run_stage(
                plan, small, current, station=station, split_in=form, split_out=split, name="station_pass"
            )
        elif whole_lines:
            current, energy = run_stage(
                plan,
                small,
                current,
                station=station,
                shot=(None, shot_weights),
                split_in=form,
                name="station_and_shot_pass",
            )
            energy = shared(energy, ("tm", "line", "shot"))
        else:
            (current,) = run_stage(plan, small, current, station=station, name="station_pass")
            current, energy = run_stage(plan, small, current, shot=(edges_of(current), shot_weights), name="shot_pass")
            energy = shared(energy, ("tm", "shot"))
    if not split:
        current = current.reshape(n_shot, lines, n_tm, window).transpose(0, 2, 1, 3).reshape(-1, lines, window)
    back = lax.all_to_all(current, axes, split_axis=0, concat_axis=0, tiled=True)
    if whole_lines:
        back = back.transpose(1, 0, 2)
    else:
        back = back.reshape(RPL, n_tm, lines, window).transpose(1, 2, 0, 3)
    return back.reshape(shots_here, block, window)


def solution(mesh):
    placed = (P(("group", "shot"), "line", "tm"), P("group", "line", None), P("group"), P("group"), P("group"))
    return jax.shard_map(
        per_device,
        mesh=mesh,
        in_specs=placed + (P(),) * 9,
        out_specs=P(("group", "shot"), "line", "tm"),
        check_vma=False,
    )
```

```python
import functools

import jax
import jax.numpy as jnp
from jax import lax
from jax.experimental import pallas as pl
from jax.experimental.pallas import tpu as pltpu
from jax.sharding import PartitionSpec as P

RPL = 16
DMAX = 128
ITERS = 2
EPSILON = 1e-05

SLAB = 128
HALF = 64
FEAT = 64
GROUP = 4
WIDE = GROUP * FEAT
QS = SLAB // (2 * GROUP)
QH = QS // 2
assert QH == 8
ONES = 3 * HALF + 6
VMEM_LIMIT = 24 * 1024 * 1024
VMEM_FULL = 63 * 1024 * 1024

BF = jnp.bfloat16
F32 = jnp.float32


def split_bias(bias):
    high = bias.astype(BF).astype(F32)
    middle = (bias - high).astype(BF).astype(F32)
    return high, middle, bias - high - middle


def iota(shape, axis):
    return lax.broadcasted_iota(jnp.int32, shape, axis)


def picks(mask):
    return mask.astype(F32).astype(BF)


def prepare_kernel(bundle, bias, o_in, o_out, rhs, cols):
    rhs[...] = jnp.zeros_like(rhs)
    cols[...] = jnp.zeros_like(cols)
    parts = split_bias(bias[0:1, :])
    exits = bundle[3 * FEAT : 3 * FEAT + 16, :].astype(F32)[0:4]
    for p in range(GROUP):
        lanes = slice(p * FEAT, (p + 1) * FEAT)
        for c in range(3):
            row = 3 * FEAT + 16 * (c + 1)
            rhs[p * 32 + c * 8 : p * 32 + c * 8 + 4, lanes] = bundle[row : row + 16, :].astype(F32)[0:4]
            rhs[p * 32 + 24 + c : p * 32 + 25 + c, lanes] = parts[c]
        cols[p * 8 : p * 8 + 4, lanes] = exits
    taps = rhs[...].astype(BF)
    row, col = iota((WIDE, SLAB), 0), iota((WIDE, SLAB), 1)
    channel, j, target = (col >> 3) & 3, col & 7, 2 * (col >> 5) + (col & 7) - 1
    rest = row - 3 * HALF
    sample = jnp.where(rest < 0, row & (HALF - 1), jnp.where(rest & 1 == 1, HALF, -1))
    same = (jnp.where(rest < 0, row >> 6, rest >> 1) == channel) & (channel < 3) & (j < 4)
    offset = jnp.where(same, sample - target, -SLAB)
    ones = (channel == 3) & (j < 3) & (row == ONES + j)
    for q in range(QH):
        chosen = picks((offset == 2 * GROUP * q) | ones)
        o_in[q] = jnp.dot(chosen, taps, preferred_element_type=F32).astype(BF)
    o_in[QH:] = jnp.zeros((2, WIDE, WIDE), BF)
    for a, at in [(0, 0), (1, 1), (2, 2), (3, 3), (-2, 4), (-1, 5), (4, 6), (5, 7)]:
        for b in range(GROUP):
            if (a - b) % 2 == 0 and abs(a - b) <= 2:
                tap = (a - b) // 2 + 1
                rows, lanes = slice(at % 4 * FEAT, (at % 4 + 1) * FEAT), slice(b * FEAT, (b + 1) * FEAT)
                o_in[QH + at // 4, rows, lanes] = bundle[tap * FEAT : (tap + 1) * FEAT, :]
    row, col = iota((SLAB, SLAB), 0), iota((SLAB, SLAB), 1)
    p, j = row >> 3, row & 7
    offset = jnp.where((p < GROUP) & (j < 4), col - (2 * p + j - 1), -SLAB)
    back = jnp.transpose(cols[...]).astype(BF)
    follows = (p == GROUP - 1) & (j == 3) & (col == 0)
    precedes = (row == 0) & (col == SLAB - 1)
    for q in range(QS + 2):
        chosen = picks(offset == 2 * GROUP * q if q < QS else [follows, precedes][q - QS])
        o_out[q] = jnp.dot(back, chosen, preferred_element_type=F32).astype(BF)


def pack_kernel(plan, traces, mixes, *refs):
    count = plan.packets
    packets, (held, mixed, done) = refs[:count], refs[count:]
    _, _, at_tm, at_shot, mine = places(plan, False)
    block, share = traces.shape
    groups = mixes.shape[0]
    copies = [pltpu.make_async_copy(traces, held, done.at[0])]
    at = pl.multiple_of(at_tm * share, share)
    for g in range(groups):
        into = mixed.at[g * block : (g + 1) * block, :]
        copies.append(pltpu.make_async_copy(mixes.at[g, :, pl.ds(at, share)], into, done.at[g + 1]))
    for copy in copies:
        copy.start()
    lines, each = plan.block_lines, plan.each
    row = lax.broadcasted_iota(jnp.int32, (block, block), 0)
    col = lax.broadcasted_iota(jnp.int32, (block, block), 1)
    rest, line = split_index(row, lines)
    d, spot = split_index(rest, each)
    order = (col == line * RPL + (d ^ mine) * each + spot).astype(F32).astype(BF)
    rows = count * groups * lines
    row = lax.broadcasted_iota(jnp.int32, (rows, groups * block), 0)
    col = lax.broadcasted_iota(jnp.int32, (rows, groups * block), 1)
    rest, line = split_index(row, lines)
    d, g = split_index(rest, groups)
    choose = (col == g * block + line * RPL + (d ^ mine) * each + at_shot).astype(F32).astype(BF)
    for copy in copies:
        copy.wait()
    top, rest = each * lines, groups * lines
    moved = jnp.dot(order, held[...], preferred_element_type=F32)
    picked = jnp.dot(choose, mixed[...], preferred_element_type=F32)
    for d, packet in enumerate(packets):
        packet[0:top, :] = moved[d * top : (d + 1) * top].astype(BF)
        packet[top:, :] = picked[d * rest : (d + 1) * rest].astype(BF)


def places(plan, first):
    at_shot, at_line, at_tm = (lax.axis_index(a) for a in ("shot", "line", "tm"))
    if not plan.whole_lines:
        return at_shot, at_tm * plan.lines, at_tm, at_shot, 0
    mine = at_line * plan.time_parts + at_tm
    return mine * plan.each + (0 if first else at_shot), 0, at_tm, at_shot, mine


def split_index(value, size):
    if size & (size - 1):
        return value // size, value % size
    return value >> (size.bit_length() - 1), value & (size - 1)


def section_map(plan, place, tallies, stride):
    shape = (plan.rows, SLAB)
    lane = lax.broadcasted_iota(jnp.int32, shape, 1)
    apart, line = split_index(lax.broadcasted_iota(jnp.int32, shape, 0), plan.lines)
    block, line = split_index(line + place[1], plan.block_lines)
    spot = line * RPL + place[0] + apart * stride
    low = jnp.zeros(shape, jnp.int32)
    high = jnp.zeros(shape, jnp.int32)
    count = jnp.zeros(shape, jnp.int32)
    start = jnp.int32(0)
    for p in range(plan.sections):
        amount = tallies[p]
        for b in range(plan.blocks):
            here = lane == b * plan.sections + p
            low = jnp.where(here, start, low)
            high = jnp.where(here, start + amount, high)
            count = jnp.where(here, amount, count)
        start = start + amount
    member = (spot >= low) & (spot < high) & (split_index(lane, plan.sections)[0] == block)
    return member, count


def shifted(values, by, ok, edge):
    return jnp.where(ok, pltpu.roll(values, by % values.shape[0], 0), edge)


def pack_inputs(plan, channels, packed):
    lane = lax.broadcasted_iota(jnp.int32, (plan.rows, SLAB), 1)
    low = lane < HALF
    ones = ((lane >= ONES - SLAB) & (lane < ONES - SLAB + 3)).astype(F32)
    slabs = [[x[:, t * SLAB : (t + 1) * SLAB] for t in range(plan.slabs)] for x in channels]
    far = [[pltpu.roll(s, HALF + 1 + 2 * c, 1) for s in slabs[c]] for c in range(3)]
    for t in range(plan.slabs):
        v = [slabs[c][t] for c in range(3)]
        w = [pltpu.roll(s, HALF, 1) for s in v]
        even = jnp.where(low, v[2], ones)
        odd = jnp.where(low, w[2], ones)
        for c in range(3):
            left, right = lane == HALF + 2 * c, lane == HALF + 2 * c + 1
            near = pltpu.roll(v[c], 1 + 2 * c, 1)
            even = jnp.where(right, near, even)
            odd = jnp.where(left, near, odd)
            if t > 0:
                even = jnp.where(left, far[c][t - 1], even)
            if t < plan.slabs - 1:
                odd = jnp.where(right, far[c][t + 1], odd)
        packed[0, t, :, 0:SLAB] = jnp.where(low, v[0], w[1]).astype(BF)
        packed[0, t, :, SLAB:WIDE] = even.astype(BF)
        packed[1, t, :, 0:SLAB] = jnp.where(low, w[0], v[1]).astype(BF)
        packed[1, t, :, SLAB:WIDE] = odd.astype(BF)


def network(plan, weights, bias, scratch, steps):
    w_in, w_out = weights
    packed, hidden, total, ends = scratch
    slabs, rows = plan.slabs, plan.rows
    many = slabs * rows
    pitch = slabs + 2
    bias_two = jnp.concatenate([bias[1:2, :]] * GROUP, axis=1)

    def first(q):
        value = jnp.dot(packed[...].reshape(2 * many, WIDE), w_in[q], preferred_element_type=F32)
        value = jnp.maximum(value.astype(BF), 0).reshape(2, slabs, rows, WIDE)
        for h in range(2):
            hidden[pl.ds((q + h * QH) * pitch + 1, slabs)] = value[h]

    def window(q, left_at, right_at):
        middle = hidden[pl.ds(q * pitch + 1, slabs)]
        left = hidden[pl.ds(left_at, slabs), :, SLAB:WIDE]
        right = hidden[pl.ds(right_at, slabs), :, 0:SLAB]
        return jnp.concatenate([middle, left, right], axis=2).reshape(many, 2 * WIDE)

    def second(q):
        left_at = (q - 1) * pitch + 1
        right_at = (q + 2) * pitch + 1
        if isinstance(q, int):
            left_at = (QS - 1) * pitch if q == 0 else left_at
            right_at = 2 if q == QS - 2 else right_at
        else:
            left_at = jnp.where(q == 0, (QS - 1) * pitch, left_at)
            right_at = jnp.where(q == QS - 2, 2, right_at)
        both = jnp.concatenate(
            [window(q, left_at, (q + 1) * pitch + 1), window(q + 1, q * pitch + 1, right_at)], axis=0
        )
        value = jnp.dot(both, w_in[QH:].reshape(2 * WIDE, WIDE), preferred_element_type=F32)
        value = jnp.maximum((value + bias_two).astype(BF), 0)
        return value[:many], value[many:]

    def onto(layer, taps):
        return jnp.dot(layer, taps, preferred_element_type=F32).reshape(slabs, rows, SLAB)

    edge = jnp.zeros((rows, WIDE), BF)
    hidden[(QS - 1) * pitch] = edge
    hidden[pitch - 1] = edge
    total[...] = jnp.zeros_like(total)

    def first_some(i):
        for k in range(QH // steps):
            first(i * (QH // steps) + k)

    def second_some(i):
        each = QS // steps
        for k in range(0, each, 2):
            q = i * each + k
            one, two = second(q)
            total[...] += onto(jnp.concatenate([one, two], axis=1), w_out[pl.ds(q, 2)].reshape(2 * WIDE, SLAB))
            if k == 0:
                keep(i == 0, 0, one)
            if k == each - 2:
                keep(i == steps - 1, 1, two)

    def keep(now, at, layer):
        if isinstance(now, bool):
            if now:
                ends[at] = layer
            return

        @pl.when(now)
        def _():
            ends[at] = layer

    def repeat(body):
        if steps == 1:
            body(0)
        else:
            lax.fori_loop(0, steps, lambda i, _: body(i), None)

    repeat(first_some)
    repeat(second_some)
    total[0 : slabs - 1] += onto(ends[0], w_out[QS + 1])[1:]
    total[1:slabs] += onto(ends[1], w_out[QS])[: slabs - 1]


def add_total(plan, now, total, scale=None):
    for t in range(plan.slabs):
        lanes = slice(t * SLAB, (t + 1) * SLAB)
        more = total[t] if scale is None else scale * total[t]
        now[:, lanes] = (now[:, lanes] + more).astype(BF).astype(F32)


def shot_stage(plan, place, tallies, stride, edges, weights, bias, now, scratch):
    x = now[...]
    line = split_index(lax.broadcasted_iota(jnp.int32, x.shape, 0), plan.lines)[1]
    above = 0.0 if edges is None else edges[0].astype(F32)
    below = 0.0 if edges is None else edges[1].astype(F32)
    channels = [
        shifted(x, 1, line > 0, above),
        x,
        shifted(x, -1, line < plan.lines - 1, below),
    ]
    pack_inputs(plan, channels, scratch[0])
    network(plan, weights, bias, scratch, 2)
    add_total(plan, now, scratch[2])
    power = jnp.zeros((plan.rows, SLAB), F32)
    for t in range(plan.slabs):
        piece = now[:, t * SLAB : (t + 1) * SLAB]
        power = power + piece * piece
    member, _ = section_map(plan, place, tallies, stride)
    each = jnp.where(member, jnp.sum(power, axis=1, keepdims=True), 0.0)
    return jnp.sum(each, axis=0, keepdims=True)


def packet_place(plan, place, d, share):
    a, b = split_index(place[4] ^ d, plan.time_parts)
    row = pl.multiple_of(a * plan.block_lines, plan.block_lines)
    return pl.ds(row, plan.block_lines), pl.ds(pl.multiple_of(b * share, share), share)


def station_stage(
    plan, place, tallies, lags, order, pace, energies, mixes, weights, bias, now, scratch, blend
):
    member, count = section_map(plan, place, tallies, 0)
    totals = energies[...]
    denominator = jnp.maximum(count, 1) * (plan.shots * plan.slabs * SLAB)
    level = jnp.sqrt(totals / denominator.astype(F32) + EPSILON)
    rms = jnp.sum(jnp.where(member, level, 0.0), axis=1, keepdims=True)
    x = (now[...] / rms).astype(BF).astype(F32)
    row = lax.broadcasted_iota(jnp.int32, x.shape, 0)
    channels = [
        shifted(x, plan.lines, row >= plan.lines, 0.0),
        x,
        shifted(x, -plan.lines, row < plan.rows - plan.lines, 0.0),
    ]
    pack_inputs(plan, channels, scratch[0])
    network(plan, weights, bias, scratch, 1)
    add_total(plan, now, scratch[2], rms)

    fired, misfit = blend
    lane = lax.broadcasted_iota(jnp.int32, (plan.lines, SLAB), 1)
    mixtures = misfit.shape[0]
    per = plan.shots // mixtures
    if plan.whole_lines:
        for d, packet in enumerate(mixes):
            here, lanes = packet_place(plan, place, d, packet.shape[1])
            piece = packet[plan.each * plan.block_lines :, :].astype(F32)
            for g in range(mixtures):
                misfit[g, here, lanes] = piece[g * plan.block_lines : (g + 1) * plan.block_lines]
    else:
        misfit[...] = mixes[0][...].astype(F32)
    for s in range(plan.shots):
        lag = lags[s]
        before = jnp.zeros((plan.lines, SLAB), F32)
        for t in range(plan.slabs):
            lanes = slice(t * SLAB, (t + 1) * SLAB)
            turned = pltpu.roll(now[s * plan.lines : (s + 1) * plan.lines, lanes], lag, 1)
            fired[s, :, lanes] = jnp.where(lane < lag, before, turned)
            before = turned
    for g in range(mixtures):
        value = fired[order[g * per]]
        for k in range(1, per):
            value = value + fired[order[g * per + k]]
        misfit[g] = value - misfit[g]
    for s in range(plan.shots):
        lag = lags[s]
        spot = jnp.int32(0)
        for k in range(plan.shots):
            spot = spot + jnp.where(order[k] == s, k, 0)
        which = spot // per
        back = (DMAX - lag) % DMAX
        after = jnp.zeros((plan.lines, SLAB), F32)
        rows = slice(s * plan.lines, (s + 1) * plan.lines)
        for t in range(plan.slabs - 1, -1, -1):
            lanes = slice(t * SLAB, (t + 1) * SLAB)
            turned = pltpu.roll(misfit[which, :, lanes], back, 1)
            pulled = jnp.where(lane < DMAX - lag, turned, after)
            after = turned
            now[rows, lanes] = (now[rows, lanes] - pace * pulled).astype(BF).astype(F32)


def stage_kernel(plan, station_round, with_shot, has_edges, stride, split_in, split_out, *refs):
    refs = list(refs)
    take = lambda n: [refs.pop(0) for _ in range(n)]
    tallies, lags, order, paces = take(4)
    place = places(plan, stride)
    sources = take({"parts": plan.each, "packets": plan.packets}.get(split_in, 1))
    source = sources[0]
    station = station_round is not None
    if station:
        (energies,) = take(1)
        mixes = take(plan.packets)
        *station_weights, station_bias = take(3)
    edges = None
    if with_shot:
        if has_edges:
            (edges,) = take(1)
        *shot_weights, shot_bias = take(3)
    results = take(plan.each if split_out == "parts" else 1)
    result = results[0]
    if with_shot and split_out != "parts":
        (energy,) = take(1)
    now, packed, hidden, total, ends = take(5)
    scratch = (packed, hidden, total, ends)
    length = plan.slabs * SLAB
    if split_in == "parts":
        for d, part in enumerate(sources):
            at = pl.multiple_of((place[3] ^ d) * plan.lines, plan.lines)
            now[pl.ds(at, plan.lines), :] = part[:, 0:length].astype(F32)
    elif split_in:
        lines = plan.block_lines
        for d, packet in enumerate(sources):
            here, lanes = packet_place(plan, place, d, packet.shape[1])
            piece = packet[0 : plan.each * lines, :].astype(F32)
            for k in range(plan.each):
                now[pl.ds(k * plan.lines + here.start, lines), lanes] = piece[k * lines : (k + 1) * lines]
    else:
        now[...] = source[...].astype(F32)
    if station:
        station_stage(
            plan,
            place,
            tallies,
            lags,
            order,
            paces[station_round],
            energies,
            mixes,
            station_weights,
            station_bias,
            now,
            scratch,
            refs,
        )
    if with_shot:
        sums = shot_stage(plan, place, tallies, stride, edges, shot_weights, shot_bias, now, scratch)
    if split_out == "parts":
        row = lax.broadcasted_iota(jnp.int32, (plan.lines, SLAB), 0)
        beside = jnp.zeros((plan.lines, SLAB), F32)
        for i, part in enumerate(split_bias(sums)):
            beside = jnp.where(row == i, part, beside)
        for d, part in enumerate(results):
            at = pl.multiple_of((place[3] ^ d) * plan.lines, plan.lines)
            part[:, 0:length] = now[pl.ds(at, plan.lines), :].astype(BF)
            part[:, length:] = beside.astype(BF)
        return
    if with_shot:
        energy[...] = sums
    if split_out:
        for n, (row, lane, rows, lanes) in enumerate(plan.pieces):
            result[n] = now[row : row + rows, lane : lane + lanes].astype(BF)
    else:
        result[...] = now[...].astype(BF)


SMEM = pl.BlockSpec(memory_space=pltpu.SMEM)
VMEM = pl.BlockSpec(memory_space=pltpu.VMEM)
HBM = pl.BlockSpec(memory_space=pltpu.HBM)


def run_stage(plan, small, source, station=None, shot=None, split_in=False, split_out=False, stride=0, name="stage"):
    operands = [*small, *(source if split_in else [source])]
    station_round, has_edges = None, False
    macs = 0
    pass_macs = plan.rows * plan.slabs * QS * WIDE * (WIDE * 3 + SLAB)
    if station is not None:
        station_round, energies, mixes, weights = station
        operands += [energies, *mixes, *weights]
        macs += pass_macs
    if shot is not None:
        edges, weights = shot
        has_edges = edges is not None
        operands += ([edges] if has_edges else []) + list(weights)
        macs += pass_macs
    specs = [SMEM] * len(small) + [VMEM] * (len(operands) - len(small))
    length = plan.slabs * SLAB
    if split_out == "parts":
        shapes = [jax.ShapeDtypeStruct((plan.lines, length + SLAB), BF)] * plan.each
    elif split_out:
        _, _, rows, lanes = plan.pieces[0]
        shapes = [jax.ShapeDtypeStruct((len(plan.pieces), rows, lanes), BF)]
    else:
        shapes = [jax.ShapeDtypeStruct((plan.rows, length), BF)]
    if shot is not None and split_out != "parts":
        shapes.append(jax.ShapeDtypeStruct((1, SLAB), F32))
    scratch = [
        pltpu.VMEM((plan.rows, length), F32),
        pltpu.VMEM((2, plan.slabs, plan.rows, WIDE), BF),
        pltpu.VMEM((QS * (plan.slabs + 2), plan.rows, WIDE), BF),
        pltpu.VMEM((plan.slabs, plan.rows, SLAB), F32),
        pltpu.VMEM((2, plan.slabs * plan.rows, WIDE), BF),
    ]
    if station is not None:
        scratch += [
            pltpu.VMEM((plan.shots, plan.lines, length), F32),
            pltpu.VMEM((plan.mixtures, plan.lines, length), F32),
        ]
    return pl.pallas_call(
        functools.partial(
            stage_kernel, plan, station_round, shot is not None, has_edges, stride, split_in, split_out
        ),
        out_shape=shapes,
        in_specs=specs,
        out_specs=[VMEM] * len(shapes),
        scratch_shapes=scratch,
        compiler_params=pltpu.CompilerParams(vmem_limit_bytes=VMEM_LIMIT),
        cost_estimate=pl.CostEstimate(flops=2 * macs, bytes_accessed=1 << 20, transcendentals=0),
        name=name,
    )(*operands)


def bundled(entry, spaced, leave):
    rows = [spaced.reshape(3 * FEAT, FEAT), jnp.pad(leave, ((0, 12), (0, 0)))]
    rows.append(jnp.pad(entry.transpose(1, 0, 2), ((0, 0), (0, 12), (0, 0))).reshape(48, FEAT))
    return jnp.concatenate(rows, axis=0)


def run_prepare(bundle, bias, name):
    return pl.pallas_call(
        prepare_kernel,
        out_shape=[
            jax.ShapeDtypeStruct((QH + 2, WIDE, WIDE), BF),
            jax.ShapeDtypeStruct((QS + 2, WIDE, SLAB), BF),
        ],
        in_specs=[VMEM] * 2,
        out_specs=[VMEM] * 2,
        scratch_shapes=[pltpu.VMEM((SLAB, WIDE), F32), pltpu.VMEM((SLAB, WIDE), F32)],
        compiler_params=pltpu.CompilerParams(vmem_limit_bytes=VMEM_LIMIT),
        cost_estimate=pl.CostEstimate(flops=2 * 8192 * WIDE * SLAB, bytes_accessed=4 << 20, transcendentals=0),
        name=name,
    )(bundle, bias)


def run_pack(plan, traces, mixtures):
    groups, block, _ = mixtures.shape
    width = traces.shape[1]
    return pl.pallas_call(
        functools.partial(pack_kernel, plan),
        out_shape=[jax.ShapeDtypeStruct(((plan.each + groups) * plan.block_lines, width), BF)] * plan.packets,
        in_specs=[HBM, HBM],
        out_specs=[VMEM] * plan.packets,
        scratch_shapes=[
            pltpu.VMEM((block, width), BF),
            pltpu.VMEM((groups * block, width), BF),
            pltpu.SemaphoreType.DMA((groups + 1,)),
        ],
        compiler_params=pltpu.CompilerParams(vmem_limit_bytes=VMEM_FULL),
        cost_estimate=pl.CostEstimate(flops=2 * block * block * width, bytes_accessed=1 << 20, transcendentals=0),
        name="pack",
    )(traces, mixtures)


class Plan:
    def __init__(self, **sizes):
        self.__dict__.update(sizes)
        self.rows = self.shots * self.lines


def exchanged(parts, axes):
    size = len(parts)
    return [parts[0]] + [lax.ppermute(parts[d], axes, [(i, i ^ d) for i in range(size)]) for d in range(1, size)]


def per_device(
    initial_guess,
    measured_mixtures,
    launch_lags,
    source_launch_order,
    station_portion_tallies,
    source_entry_kernel,
    source_spaced_kernel,
    source_exit_kernel,
    source_inner_offsets,
    station_entry_kernel,
    station_spaced_kernel,
    station_exit_kernel,
    station_inner_offsets,
    learned_pace_factors,
):
    shots_here, block, window = initial_guess.shape
    n_shot, n_line, n_tm = (lax.axis_size(a) for a in ("shot", "line", "tm"))
    at_shot, at_tm = lax.axis_index("shot"), lax.axis_index("tm")
    block_lines = block // RPL
    length = window * n_tm
    shots = shots_here * n_shot
    sections = station_portion_tallies.shape[0]
    mixtures = measured_mixtures.shape[0]
    whole_lines = n_shot * n_line * n_tm == RPL
    assert shots_here == 1 and (whole_lines or n_shot == RPL)
    if whole_lines:
        axes = ("line", "tm", "shot")
        lines, blocks = block_lines * n_line, n_line
    else:
        axes = ("shot", "tm")
        lines = block_lines // n_tm
        blocks = 1
    turns = [(s, a, b) for a in range(blocks) for b in range(n_tm) for s in range(n_shot)]
    plan = Plan(
        whole_lines=whole_lines,
        shots=shots,
        lines=lines,
        block_lines=block_lines,
        blocks=blocks,
        sections=sections,
        mixtures=mixtures,
        slabs=length // SLAB,
        each=n_shot,
        time_parts=n_tm,
        packets=n_line * n_tm if whole_lines else 1,
        pieces=[(s * lines + a * block_lines, b * window, block_lines, window) for s, a, b in turns],
    )

    if whole_lines:
        assert n_tm == 2 and n_line & (n_line - 1) == 0 and n_shot & (n_shot - 1) == 0
        arrived = run_pack(plan, initial_guess.reshape(block, window), measured_mixtures)
        arrived = exchanged(arrived, ("line", "tm"))
    else:
        grid = initial_guess.reshape(n_tm, lines, RPL, window)
        leaving = grid.transpose(2, 0, 1, 3).reshape(RPL * n_tm, lines, window)
        arrived = lax.all_to_all(leaving, axes, split_axis=0, concat_axis=0, tiled=True)

    shot_bundle = bundled(source_entry_kernel, source_spaced_kernel, source_exit_kernel)
    station_net = (station_entry_kernel, station_spaced_kernel, station_exit_kernel)
    shot_weights = (*run_prepare(shot_bundle, source_inner_offsets, "prepare_shot"), source_inner_offsets)
    small = (station_portion_tallies, launch_lags, source_launch_order, learned_pace_factors)
    split = whole_lines and block_lines % 8 == 0
    assert split or not whole_lines
    if whole_lines:
        mixes = source = arrived
    else:
        grid = measured_mixtures.reshape(mixtures, n_tm, lines, RPL, length)
        mixes = lax.dynamic_slice(grid, (0, at_tm, 0, at_shot, 0), (mixtures, 1, lines, 1, length))
        mixes = [mixes.reshape(mixtures, lines, length)]
        source = arrived.reshape(n_shot, n_tm, lines, window).transpose(0, 2, 1, 3).reshape(plan.rows, length)

    def edges_of(current):
        if whole_lines:
            return None
        size = n_line * n_tm
        grid = current.reshape(shots, lines, length)
        up = [(i, i + 1) for i in range(size - 1)]
        down = [(j, i) for i, j in up]
        above = lax.ppermute(grid[:, -1], ("line", "tm"), up)
        below = lax.ppermute(grid[:, 0], ("line", "tm"), down)
        wide = jnp.broadcast_to(jnp.stack([above, below])[:, :, None, :], (2, shots, lines, length))
        return wide.reshape(2, plan.rows, length)

    def summed(value, axis):
        size = lax.axis_size(axis)
        if size <= 4:
            others = [lax.ppermute(value, axis, [(i, i ^ d) for i in range(size)]) for d in range(1, size)]
            return sum(others, value)
        step = 1
        while step < size:
            value = value + lax.ppermute(value, axis, [(i, i ^ step) for i in range(size)])
            step *= 2
        return value

    def spread(value):
        value = summed(value, "tm")
        chips = n_line * n_shot
        rounds = chips // 2
        total = jnp.where(at_tm == 0, value, 0.0)
        for d in range(1, rounds + 1):
            pairs = [(2 * c, 2 * (c ^ d)) for c in range(chips)]
            if d + rounds < chips:
                pairs += [(2 * c + 1, 2 * (c ^ (d + rounds)) + 1) for c in range(chips)]
            total = total + lax.ppermute(value, ("shot", "line", "tm"), pairs)
        return summed(total, "tm")

    def shared(energy, along):
        for axis in along:
            energy = summed(energy, axis)
        return energy

    if whole_lines:
        parts = run_stage(
            plan,
            small,
            source,
            shot=(None, shot_weights),
            split_in="packets",
            split_out="parts",
            stride=1,
            name="shot_pass",
        )
        station_net, own = lax.optimization_barrier((station_net, parts[0]))
        current = exchanged([own, *parts[1:]], "shot")
        station_weights = run_prepare(bundled(*station_net), station_inner_offsets, "prepare_station")
        energy = sum(jnp.sum(p[0:3, length:].astype(F32), axis=0, keepdims=True) for p in current)
        station_weights, energy = lax.optimization_barrier((station_weights, energy))
        energy = summed(energy, ("line", "tm"))
    else:
        current, energy = run_stage(
            plan, small, source, shot=(edges_of(source), shot_weights), name="shot_pass"
        )
        energy = shared(energy, ("tm", "shot"))
        station_weights = run_prepare(bundled(*station_net), station_inner_offsets, "prepare_station")
    station_weights = (*station_weights, station_inner_offsets)
    for i in range(ITERS):
        station = (i, energy, mixes, station_weights)
        form = "parts" if whole_lines and i == 0 else False
        if i == ITERS - 1:
            (current,) = run_stage(
                plan, small, current, station=station, split_in=form, split_out=split, name="station_pass"
            )
        elif whole_lines:
            current, energy = run_stage(
                plan,
                small,
                current,
                station=station,
                shot=(None, shot_weights),
                split_in=form,
                name="station_and_shot_pass",
            )
            energy = spread(energy)
        else:
            (current,) = run_stage(plan, small, current, station=station, name="station_pass")
            current, energy = run_stage(plan, small, current, shot=(edges_of(current), shot_weights), name="shot_pass")
            energy = shared(energy, ("tm", "shot"))
    if not split:
        current = current.reshape(n_shot, lines, n_tm, window).transpose(0, 2, 1, 3).reshape(-1, lines, window)
    back = lax.all_to_all(current, axes, split_axis=0, concat_axis=0, tiled=True)
    if whole_lines:
        back = back.transpose(1, 0, 2)
    else:
        back = back.reshape(RPL, n_tm, lines, window).transpose(1, 2, 0, 3)
    return back.reshape(shots_here, block, window)


def solution(mesh):
    placed = (P(("group", "shot"), "line", "tm"), P("group", "line", None), P("group"), P("group"), P("group"))
    return jax.shard_map(
        per_device,
        mesh=mesh,
        in_specs=placed + (P(),) * 9,
        out_specs=P(("group", "shot"), "line", "tm"),
        check_vma=False,
    )
```

```python
import functools

import jax
import jax.numpy as jnp
from jax import lax
from jax.experimental import pallas as pl
from jax.experimental.pallas import tpu as pltpu
from jax.sharding import PartitionSpec as P

RPL = 16
DMAX = 128
ITERS = 2
EPSILON = 1e-05

SLAB = 128
HALF = 64
FEAT = 64
GROUP = 4
WIDE = GROUP * FEAT
QS = SLAB // (2 * GROUP)
QH = QS // 2
assert QH == 8
ONES = 3 * HALF + 6
VMEM_LIMIT = 24 * 1024 * 1024
VMEM_FULL = 63 * 1024 * 1024

BF = jnp.bfloat16
F32 = jnp.float32


def split_bias(bias):
    high = bias.astype(BF).astype(F32)
    middle = (bias - high).astype(BF).astype(F32)
    return high, middle, bias - high - middle


def iota(shape, axis):
    return lax.broadcasted_iota(jnp.int32, shape, axis)


def picks(mask):
    return mask.astype(F32).astype(BF)


def start_of(q):
    return 16 * (q // 2) + 2 * (q % 2)


def prepare_kernel(bundle, bias, o_in, o_out, rhs, cols):
    rhs[...] = jnp.zeros_like(rhs)
    cols[...] = jnp.zeros_like(cols)
    parts = split_bias(bias[0:1, :])
    exits = bundle[3 * FEAT : 3 * FEAT + 16, :].astype(F32)[0:4]
    for p in range(GROUP):
        lanes = slice(p * FEAT, (p + 1) * FEAT)
        for c in range(3):
            row = 3 * FEAT + 16 * (c + 1)
            rhs[p * 32 + c * 8 : p * 32 + c * 8 + 4, lanes] = bundle[row : row + 16, :].astype(F32)[0:4]
            rhs[p * 32 + 24 + c : p * 32 + 25 + c, lanes] = parts[c]
        cols[p * 8 : p * 8 + 4, lanes] = exits
    taps = rhs[...].astype(BF)
    row, col = iota((WIDE, SLAB), 0), iota((WIDE, SLAB), 1)
    channel, j, target = (col >> 3) & 3, col & 7, 4 * (col >> 5) + (col & 7) - 1
    rest = row - 3 * HALF
    sample = jnp.where(rest < 0, row & (HALF - 1), jnp.where(rest & 1 == 1, HALF, -1))
    same = (jnp.where(rest < 0, row >> 6, rest >> 1) == channel) & (channel < 3) & (j < 4)
    offset = jnp.where(same, sample - target, -SLAB)
    ones = (channel == 3) & (j < 3) & (row == ONES + j)
    for q in range(QH):
        chosen = picks((offset == start_of(q)) | ones)
        o_in[q] = jnp.dot(chosen, taps, preferred_element_type=F32).astype(BF)
    o_in[QH:] = jnp.zeros((2, WIDE, WIDE), BF)
    for a, at in [(0, 0), (1, 1), (2, 2), (3, 3), (4, 4), (-1, 5)]:
        for b in range(GROUP):
            if abs(a - b) <= 1:
                tap = a - b + 1
                rows, lanes = slice(at % 4 * FEAT, (at % 4 + 1) * FEAT), slice(b * FEAT, (b + 1) * FEAT)
                o_in[QH + at // 4, rows, lanes] = bundle[tap * FEAT : (tap + 1) * FEAT, :]
    row, col = iota((SLAB, SLAB), 0), iota((SLAB, SLAB), 1)
    p, j = row >> 3, row & 7
    offset = jnp.where((p < GROUP) & (j < 4), col - (4 * p + j - 1), -SLAB)
    back = jnp.transpose(cols[...]).astype(BF)
    follows = (p == GROUP - 1) & (j == 3) & (col == 0)
    precedes = (row == 0) & (col == SLAB - 1)
    for q in range(QS + 2):
        chosen = picks(offset == start_of(q) if q < QS else [follows, precedes][q - QS])
        o_out[q] = jnp.dot(back, chosen, preferred_element_type=F32).astype(BF)


def pack_kernel(plan, traces, mixes, *refs):
    count = plan.packets
    packets, (held, mixed, done) = refs[:count], refs[count:]
    _, _, at_tm, at_shot, mine = places(plan, False)
    block, share = traces.shape
    groups = mixes.shape[0]
    copies = [pltpu.make_async_copy(traces, held, done.at[0])]
    at = pl.multiple_of(at_tm * share, share)
    for g in range(groups):
        into = mixed.at[g * block : (g + 1) * block, :]
        copies.append(pltpu.make_async_copy(mixes.at[g, :, pl.ds(at, share)], into, done.at[g + 1]))
    for copy in copies:
        copy.start()
    lines, each = plan.block_lines, plan.each
    row = lax.broadcasted_iota(jnp.int32, (block, block), 0)
    col = lax.broadcasted_iota(jnp.int32, (block, block), 1)
    rest, line = split_index(row, lines)
    d, spot = split_index(rest, each)
    order = (col == line * RPL + (d ^ mine) * each + spot).astype(F32).astype(BF)
    rows = count * groups * lines
    row = lax.broadcasted_iota(jnp.int32, (rows, groups * block), 0)
    col = lax.broadcasted_iota(jnp.int32, (rows, groups * block), 1)
    rest, line = split_index(row, lines)
    d, g = split_index(rest, groups)
    choose = (col == g * block + line * RPL + (d ^ mine) * each + at_shot).astype(F32).astype(BF)
    for copy in copies:
        copy.wait()
    top, rest = each * lines, groups * lines
    moved = jnp.dot(order, held[...], preferred_element_type=F32)
    picked = jnp.dot(choose, mixed[...], preferred_element_type=F32)
    for d, packet in enumerate(packets):
        packet[0:top, :] = moved[d * top : (d + 1) * top].astype(BF)
        packet[top:, :] = picked[d * rest : (d + 1) * rest].astype(BF)


def places(plan, first):
    at_shot, at_line, at_tm = (lax.axis_index(a) for a in ("shot", "line", "tm"))
    if not plan.whole_lines:
        return at_shot, at_tm * plan.lines, at_tm, at_shot, 0
    mine = at_line * plan.time_parts + at_tm
    return mine * plan.each + (0 if first else at_shot), 0, at_tm, at_shot, mine


def split_index(value, size):
    if size & (size - 1):
        return value // size, value % size
    return value >> (size.bit_length() - 1), value & (size - 1)


def section_map(plan, place, tallies, stride):
    shape = (plan.rows, SLAB)
    lane = lax.broadcasted_iota(jnp.int32, shape, 1)
    apart, line = split_index(lax.broadcasted_iota(jnp.int32, shape, 0), plan.lines)
    block, line = split_index(line + place[1], plan.block_lines)
    spot = line * RPL + place[0] + apart * stride
    low = jnp.zeros(shape, jnp.int32)
    high = jnp.zeros(shape, jnp.int32)
    count = jnp.zeros(shape, jnp.int32)
    start = jnp.int32(0)
    for p in range(plan.sections):
        amount = tallies[p]
        for b in range(plan.blocks):
            here = lane == b * plan.sections + p
            low = jnp.where(here, start, low)
            high = jnp.where(here, start + amount, high)
            count = jnp.where(here, amount, count)
        start = start + amount
    member = (spot >= low) & (spot < high) & (split_index(lane, plan.sections)[0] == block)
    return member, count


def shifted(values, by, ok, edge):
    return jnp.where(ok, pltpu.roll(values, by % values.shape[0], 0), edge)


def pack_inputs(plan, channels, packed):
    lane = lax.broadcasted_iota(jnp.int32, (plan.rows, SLAB), 1)
    low = lane < HALF
    ones = ((lane >= ONES - SLAB) & (lane < ONES - SLAB + 3)).astype(F32)
    slabs = [[x[:, t * SLAB : (t + 1) * SLAB] for t in range(plan.slabs)] for x in channels]
    far = [[pltpu.roll(s, HALF + 1 + 2 * c, 1) for s in slabs[c]] for c in range(3)]
    for t in range(plan.slabs):
        v = [slabs[c][t] for c in range(3)]
        w = [pltpu.roll(s, HALF, 1) for s in v]
        even = jnp.where(low, v[2], ones)
        odd = jnp.where(low, w[2], ones)
        for c in range(3):
            left, right = lane == HALF + 2 * c, lane == HALF + 2 * c + 1
            near = pltpu.roll(v[c], 1 + 2 * c, 1)
            even = jnp.where(right, near, even)
            odd = jnp.where(left, near, odd)
            if t > 0:
                even = jnp.where(left, far[c][t - 1], even)
            if t < plan.slabs - 1:
                odd = jnp.where(right, far[c][t + 1], odd)
        packed[0, t, :, 0:SLAB] = jnp.where(low, v[0], w[1]).astype(BF)
        packed[0, t, :, SLAB:WIDE] = even.astype(BF)
        packed[1, t, :, 0:SLAB] = jnp.where(low, w[0], v[1]).astype(BF)
        packed[1, t, :, SLAB:WIDE] = odd.astype(BF)


def network(plan, weights, bias, scratch, steps):
    w_in, w_out = weights
    packed, hidden, total, ends = scratch
    slabs, rows = plan.slabs, plan.rows
    many = slabs * rows
    pitch = slabs + 2
    bias_two = jnp.concatenate([bias[1:2, :]] * GROUP, axis=1)

    def first(q):
        value = jnp.dot(packed[...].reshape(2 * many, WIDE), w_in[q], preferred_element_type=F32)
        value = jnp.maximum(value.astype(BF), 0).reshape(2, slabs, rows, WIDE)
        for h in range(2):
            hidden[pl.ds((q + h * QH) * pitch + 1, slabs)] = value[h]

    lane = iota((slabs, rows, SLAB), 2)

    def window(q):
        if isinstance(q, int):
            left_at = (q - 2) * pitch + 1 if q >= 2 else (q + QS - 2) * pitch
            right_at = (q + 2) * pitch + 1 if q < QS - 2 else (q + 2 - QS) * pitch + 2
        else:
            left_at = jnp.where(q >= 2, (q - 2) * pitch + 1, (q + QS - 2) * pitch)
            right_at = jnp.where(q < QS - 2, (q + 2) * pitch + 1, (q + 2 - QS) * pitch + 2)
        middle = hidden[pl.ds(q * pitch + 1, slabs)]
        left = hidden[pl.ds(left_at, slabs), :, SLAB:WIDE]
        right = hidden[pl.ds(right_at, slabs), :, 0:SLAB]
        beside = jnp.where(lane < FEAT, right, left)
        return jnp.concatenate([middle, beside], axis=2).reshape(many, WIDE + SLAB)

    def second(q):
        both = jnp.concatenate([window(q), window(q + 1)], axis=0)
        taps = w_in[QH:].reshape(2 * WIDE, WIDE)[0 : WIDE + SLAB]
        value = jnp.dot(both, taps, preferred_element_type=F32)
        value = jnp.maximum((value + bias_two).astype(BF), 0)
        return value[:many], value[many:]

    def onto(layer, taps):
        return jnp.dot(layer, taps, preferred_element_type=F32).reshape(slabs, rows, SLAB)

    edge = jnp.zeros((rows, WIDE), BF)
    for k in range(2):
        hidden[(QS - 2 + k) * pitch] = edge
        hidden[(k + 1) * pitch - 1] = edge
    total[...] = jnp.zeros_like(total)

    def first_some(i):
        for k in range(QH // steps):
            first(i * (QH // steps) + k)

    def second_some(i):
        each = QS // steps
        for k in range(0, each, 2):
            q = i * each + k
            one, two = second(q)
            total[...] += onto(jnp.concatenate([one, two], axis=1), w_out[pl.ds(q, 2)].reshape(2 * WIDE, SLAB))
            if k == 0:
                keep(i == 0, 0, one)
            if k == each - 2:
                keep(i == steps - 1, 1, two)

    def keep(now, at, layer):
        if isinstance(now, bool):
            if now:
                ends[at] = layer
            return

        @pl.when(now)
        def _():
            ends[at] = layer

    def repeat(body):
        if steps == 1:
            body(0)
        else:
            lax.fori_loop(0, steps, lambda i, _: body(i), None)

    repeat(first_some)
    repeat(second_some)
    total[0 : slabs - 1] += onto(ends[0], w_out[QS + 1])[1:]
    total[1:slabs] += onto(ends[1], w_out[QS])[: slabs - 1]


def add_total(plan, now, total, scale=None):
    for t in range(plan.slabs):
        lanes = slice(t * SLAB, (t + 1) * SLAB)
        more = total[t] if scale is None else scale * total[t]
        now[:, lanes] = (now[:, lanes] + more).astype(BF).astype(F32)


def shot_stage(plan, place, tallies, stride, edges, weights, bias, now, scratch):
    x = now[...]
    line = split_index(lax.broadcasted_iota(jnp.int32, x.shape, 0), plan.lines)[1]
    above = 0.0 if edges is None else edges[0].astype(F32)
    below = 0.0 if edges is None else edges[1].astype(F32)
    channels = [
        shifted(x, 1, line > 0, above),
        x,
        shifted(x, -1, line < plan.lines - 1, below),
    ]
    pack_inputs(plan, channels, scratch[0])
    network(plan, weights, bias, scratch, 2)
    add_total(plan, now, scratch[2])
    power = jnp.zeros((plan.rows, SLAB), F32)
    for t in range(plan.slabs):
        piece = now[:, t * SLAB : (t + 1) * SLAB]
        power = power + piece * piece
    member, _ = section_map(plan, place, tallies, stride)
    each = jnp.where(member, jnp.sum(power, axis=1, keepdims=True), 0.0)
    return jnp.sum(each, axis=0, keepdims=True)


def packet_place(plan, place, d, share):
    a, b = split_index(place[4] ^ d, plan.time_parts)
    row = pl.multiple_of(a * plan.block_lines, plan.block_lines)
    return pl.ds(row, plan.block_lines), pl.ds(pl.multiple_of(b * share, share), share)


def station_stage(
    plan, place, tallies, lags, order, pace, energies, mixes, weights, bias, now, scratch, blend
):
    member, count = section_map(plan, place, tallies, 0)
    totals = energies[...]
    denominator = jnp.maximum(count, 1) * (plan.shots * plan.slabs * SLAB)
    level = jnp.sqrt(totals / denominator.astype(F32) + EPSILON)
    rms = jnp.sum(jnp.where(member, level, 0.0), axis=1, keepdims=True)
    x = (now[...] / rms).astype(BF).astype(F32)
    row = lax.broadcasted_iota(jnp.int32, x.shape, 0)
    channels = [
        shifted(x, plan.lines, row >= plan.lines, 0.0),
        x,
        shifted(x, -plan.lines, row < plan.rows - plan.lines, 0.0),
    ]
    pack_inputs(plan, channels, scratch[0])
    network(plan, weights, bias, scratch, 1)
    add_total(plan, now, scratch[2], rms)

    fired, misfit = blend
    lane = lax.broadcasted_iota(jnp.int32, (plan.lines, SLAB), 1)
    mixtures = misfit.shape[0]
    per = plan.shots // mixtures
    if plan.whole_lines:
        for d, packet in enumerate(mixes):
            here, lanes = packet_place(plan, place, d, packet.shape[1])
            piece = packet[plan.each * plan.block_lines :, :].astype(F32)
            for g in range(mixtures):
                misfit[g, here, lanes] = piece[g * plan.block_lines : (g + 1) * plan.block_lines]
    else:
        misfit[...] = mixes[0][...].astype(F32)
    for s in range(plan.shots):
        lag = lags[s]
        before = jnp.zeros((plan.lines, SLAB), F32)
        for t in range(plan.slabs):
            lanes = slice(t * SLAB, (t + 1) * SLAB)
            turned = pltpu.roll(now[s * plan.lines : (s + 1) * plan.lines, lanes], lag, 1)
            fired[s, :, lanes] = jnp.where(lane < lag, before, turned)
            before = turned
    for g in range(mixtures):
        value = fired[order[g * per]]
        for k in range(1, per):
            value = value + fired[order[g * per + k]]
        misfit[g] = value - misfit[g]
    for s in range(plan.shots):
        lag = lags[s]
        spot = jnp.int32(0)
        for k in range(plan.shots):
            spot = spot + jnp.where(order[k] == s, k, 0)
        which = spot // per
        back = (DMAX - lag) % DMAX
        after = jnp.zeros((plan.lines, SLAB), F32)
        rows = slice(s * plan.lines, (s + 1) * plan.lines)
        for t in range(plan.slabs - 1, -1, -1):
            lanes = slice(t * SLAB, (t + 1) * SLAB)
            turned = pltpu.roll(misfit[which, :, lanes], back, 1)
            pulled = jnp.where(lane < DMAX - lag, turned, after)
            after = turned
            now[rows, lanes] = (now[rows, lanes] - pace * pulled).astype(BF).astype(F32)


def stage_kernel(plan, station_round, with_shot, has_edges, stride, split_in, split_out, *refs):
    refs = list(refs)
    take = lambda n: [refs.pop(0) for _ in range(n)]
    tallies, lags, order, paces = take(4)
    place = places(plan, stride)
    sources = take({"parts": plan.each, "packets": plan.packets}.get(split_in, 1))
    source = sources[0]
    station = station_round is not None
    if station:
        (energies,) = take(1)
        mixes = take(plan.packets)
        *station_weights, station_bias = take(3)
    edges = None
    if with_shot:
        if has_edges:
            (edges,) = take(1)
        *shot_weights, shot_bias = take(3)
    results = take(plan.each if split_out == "parts" else 1)
    result = results[0]
    if with_shot and split_out != "parts":
        (energy,) = take(1)
    now, packed, hidden, total, ends = take(5)
    scratch = (packed, hidden, total, ends)
    length = plan.slabs * SLAB
    if split_in == "parts":
        for d, part in enumerate(sources):
            at = pl.multiple_of((place[3] ^ d) * plan.lines, plan.lines)
            now[pl.ds(at, plan.lines), :] = part[:, 0:length].astype(F32)
    elif split_in:
        lines = plan.block_lines
        for d, packet in enumerate(sources):
            here, lanes = packet_place(plan, place, d, packet.shape[1])
            piece = packet[0 : plan.each * lines, :].astype(F32)
            for k in range(plan.each):
                now[pl.ds(k * plan.lines + here.start, lines), lanes] = piece[k * lines : (k + 1) * lines]
    else:
        now[...] = source[...].astype(F32)
    if station:
        station_stage(
            plan,
            place,
            tallies,
            lags,
            order,
            paces[station_round],
            energies,
            mixes,
            station_weights,
            station_bias,
            now,
            scratch,
            refs,
        )
    if with_shot:
        sums = shot_stage(plan, place, tallies, stride, edges, shot_weights, shot_bias, now, scratch)
    if split_out == "parts":
        row = lax.broadcasted_iota(jnp.int32, (plan.lines, SLAB), 0)
        beside = jnp.zeros((plan.lines, SLAB), F32)
        for i, part in enumerate(split_bias(sums)):
            beside = jnp.where(row == i, part, beside)
        for d, part in enumerate(results):
            at = pl.multiple_of((place[3] ^ d) * plan.lines, plan.lines)
            part[:, 0:length] = now[pl.ds(at, plan.lines), :].astype(BF)
            part[:, length:] = beside.astype(BF)
        return
    if with_shot:
        energy[...] = sums
    if split_out:
        for n, (row, lane, rows, lanes) in enumerate(plan.pieces):
            result[n] = now[row : row + rows, lane : lane + lanes].astype(BF)
    else:
        result[...] = now[...].astype(BF)


SMEM = pl.BlockSpec(memory_space=pltpu.SMEM)
VMEM = pl.BlockSpec(memory_space=pltpu.VMEM)
HBM = pl.BlockSpec(memory_space=pltpu.HBM)


def run_stage(plan, small, source, station=None, shot=None, split_in=False, split_out=False, stride=0, name="stage"):
    operands = [*small, *(source if split_in else [source])]
    station_round, has_edges = None, False
    macs = 0
    pass_macs = plan.rows * plan.slabs * QS * WIDE * (WIDE * 3 + SLAB)
    if station is not None:
        station_round, energies, mixes, weights = station
        operands += [energies, *mixes, *weights]
        macs += pass_macs
    if shot is not None:
        edges, weights = shot
        has_edges = edges is not None
        operands += ([edges] if has_edges else []) + list(weights)
        macs += pass_macs
    specs = [SMEM] * len(small) + [VMEM] * (len(operands) - len(small))
    length = plan.slabs * SLAB
    if split_out == "parts":
        shapes = [jax.ShapeDtypeStruct((plan.lines, length + SLAB), BF)] * plan.each
    elif split_out:
        _, _, rows, lanes = plan.pieces[0]
        shapes = [jax.ShapeDtypeStruct((len(plan.pieces), rows, lanes), BF)]
    else:
        shapes = [jax.ShapeDtypeStruct((plan.rows, length), BF)]
    if shot is not None and split_out != "parts":
        shapes.append(jax.ShapeDtypeStruct((1, SLAB), F32))
    scratch = [
        pltpu.VMEM((plan.rows, length), F32),
        pltpu.VMEM((2, plan.slabs, plan.rows, WIDE), BF),
        pltpu.VMEM((QS * (plan.slabs + 2), plan.rows, WIDE), BF),
        pltpu.VMEM((plan.slabs, plan.rows, SLAB), F32),
        pltpu.VMEM((2, plan.slabs * plan.rows, WIDE), BF),
    ]
    if station is not None:
        scratch += [
            pltpu.VMEM((plan.shots, plan.lines, length), F32),
            pltpu.VMEM((plan.mixtures, plan.lines, length), F32),
        ]
    return pl.pallas_call(
        functools.partial(
            stage_kernel, plan, station_round, shot is not None, has_edges, stride, split_in, split_out
        ),
        out_shape=shapes,
        in_specs=specs,
        out_specs=[VMEM] * len(shapes),
        scratch_shapes=scratch,
        compiler_params=pltpu.CompilerParams(vmem_limit_bytes=VMEM_LIMIT),
        cost_estimate=pl.CostEstimate(flops=2 * macs, bytes_accessed=1 << 20, transcendentals=0),
        name=name,
    )(*operands)


def bundled(entry, spaced, leave):
    rows = [spaced.reshape(3 * FEAT, FEAT), jnp.pad(leave, ((0, 12), (0, 0)))]
    rows.append(jnp.pad(entry.transpose(1, 0, 2), ((0, 0), (0, 12), (0, 0))).reshape(48, FEAT))
    return jnp.concatenate(rows, axis=0)


def run_prepare(bundle, bias, name):
    return pl.pallas_call(
        prepare_kernel,
        out_shape=[
            jax.ShapeDtypeStruct((QH + 2, WIDE, WIDE), BF),
            jax.ShapeDtypeStruct((QS + 2, WIDE, SLAB), BF),
        ],
        in_specs=[VMEM] * 2,
        out_specs=[VMEM] * 2,
        scratch_shapes=[pltpu.VMEM((SLAB, WIDE), F32), pltpu.VMEM((SLAB, WIDE), F32)],
        compiler_params=pltpu.CompilerParams(vmem_limit_bytes=VMEM_LIMIT),
        cost_estimate=pl.CostEstimate(flops=2 * 8192 * WIDE * SLAB, bytes_accessed=4 << 20, transcendentals=0),
        name=name,
    )(bundle, bias)


def run_pack(plan, traces, mixtures):
    groups, block, _ = mixtures.shape
    width = traces.shape[1]
    return pl.pallas_call(
        functools.partial(pack_kernel, plan),
        out_shape=[jax.ShapeDtypeStruct(((plan.each + groups) * plan.block_lines, width), BF)] * plan.packets,
        in_specs=[HBM, HBM],
        out_specs=[VMEM] * plan.packets,
        scratch_shapes=[
            pltpu.VMEM((block, width), BF),
            pltpu.VMEM((groups * block, width), BF),
            pltpu.SemaphoreType.DMA((groups + 1,)),
        ],
        compiler_params=pltpu.CompilerParams(vmem_limit_bytes=VMEM_FULL),
        cost_estimate=pl.CostEstimate(flops=2 * block * block * width, bytes_accessed=1 << 20, transcendentals=0),
        name="pack",
    )(traces, mixtures)


class Plan:
    def __init__(self, **sizes):
        self.__dict__.update(sizes)
        self.rows = self.shots * self.lines


def exchanged(parts, axes):
    size = len(parts)
    return [parts[0]] + [lax.ppermute(parts[d], axes, [(i, i ^ d) for i in range(size)]) for d in range(1, size)]


def per_device(
    initial_guess,
    measured_mixtures,
    launch_lags,
    source_launch_order,
    station_portion_tallies,
    source_entry_kernel,
    source_spaced_kernel,
    source_exit_kernel,
    source_inner_offsets,
    station_entry_kernel,
    station_spaced_kernel,
    station_exit_kernel,
    station_inner_offsets,
    learned_pace_factors,
):
    shots_here, block, window = initial_guess.shape
    n_shot, n_line, n_tm = (lax.axis_size(a) for a in ("shot", "line", "tm"))
    at_shot, at_tm = lax.axis_index("shot"), lax.axis_index("tm")
    block_lines = block // RPL
    length = window * n_tm
    shots = shots_here * n_shot
    sections = station_portion_tallies.shape[0]
    mixtures = measured_mixtures.shape[0]
    whole_lines = n_shot * n_line * n_tm == RPL
    assert shots_here == 1 and (whole_lines or n_shot == RPL)
    if whole_lines:
        axes = ("line", "tm", "shot")
        lines, blocks = block_lines * n_line, n_line
    else:
        axes = ("shot", "tm")
        lines = block_lines // n_tm
        blocks = 1
    turns = [(s, a, b) for a in range(blocks) for b in range(n_tm) for s in range(n_shot)]
    plan = Plan(
        whole_lines=whole_lines,
        shots=shots,
        lines=lines,
        block_lines=block_lines,
        blocks=blocks,
        sections=sections,
        mixtures=mixtures,
        slabs=length // SLAB,
        each=n_shot,
        time_parts=n_tm,
        packets=n_line * n_tm if whole_lines else 1,
        pieces=[(s * lines + a * block_lines, b * window, block_lines, window) for s, a, b in turns],
    )

    if whole_lines:
        assert n_tm == 2 and n_line & (n_line - 1) == 0 and n_shot & (n_shot - 1) == 0
        arrived = run_pack(plan, initial_guess.reshape(block, window), measured_mixtures)
        arrived = exchanged(arrived, ("line", "tm"))
    else:
        grid = initial_guess.reshape(n_tm, lines, RPL, window)
        leaving = grid.transpose(2, 0, 1, 3).reshape(RPL * n_tm, lines, window)
        arrived = lax.all_to_all(leaving, axes, split_axis=0, concat_axis=0, tiled=True)

    shot_bundle = bundled(source_entry_kernel, source_spaced_kernel, source_exit_kernel)
    station_net = (station_entry_kernel, station_spaced_kernel, station_exit_kernel)
    shot_weights = (*run_prepare(shot_bundle, source_inner_offsets, "prepare_shot"), source_inner_offsets)
    small = (station_portion_tallies, launch_lags, source_launch_order, learned_pace_factors)
    split = whole_lines and block_lines % 8 == 0
    assert split or not whole_lines
    if whole_lines:
        mixes = source = arrived
    else:
        grid = measured_mixtures.reshape(mixtures, n_tm, lines, RPL, length)
        mixes = lax.dynamic_slice(grid, (0, at_tm, 0, at_shot, 0), (mixtures, 1, lines, 1, length))
        mixes = [mixes.reshape(mixtures, lines, length)]
        source = arrived.reshape(n_shot, n_tm, lines, window).transpose(0, 2, 1, 3).reshape(plan.rows, length)

    def edges_of(current):
        if whole_lines:
            return None
        size = n_line * n_tm
        grid = current.reshape(shots, lines, length)
        up = [(i, i + 1) for i in range(size - 1)]
        down = [(j, i) for i, j in up]
        above = lax.ppermute(grid[:, -1], ("line", "tm"), up)
        below = lax.ppermute(grid[:, 0], ("line", "tm"), down)
        wide = jnp.broadcast_to(jnp.stack([above, below])[:, :, None, :], (2, shots, lines, length))
        return wide.reshape(2, plan.rows, length)

    def summed(value, axis):
        size = lax.axis_size(axis)
        if size <= 4:
            others = [lax.ppermute(value, axis, [(i, i ^ d) for i in range(size)]) for d in range(1, size)]
            return sum(others, value)
        step = 1
        while step < size:
            value = value + lax.ppermute(value, axis, [(i, i ^ step) for i in range(size)])
            step *= 2
        return value

    def shared(energy, along):
        for axis in along:
            energy = summed(energy, axis)
        return energy

    if whole_lines:
        parts = run_stage(
            plan,
            small,
            source,
            shot=(None, shot_weights),
            split_in="packets",
            split_out="parts",
            stride=1,
            name="shot_pass",
        )
        station_net, own = lax.optimization_barrier((station_net, parts[0]))
        current = exchanged([own, *parts[1:]], "shot")
        bundle = bundled(*station_net)
        station_weights = run_prepare(bundle, station_inner_offsets, "prepare_station")
        energy = sum(jnp.sum(p[0:3, length:].astype(F32), axis=0, keepdims=True) for p in current)
        station_weights, energy = lax.optimization_barrier((station_weights, energy))
        energy = summed(energy, ("line", "tm"))
    else:
        current, energy = run_stage(
            plan, small, source, shot=(edges_of(source), shot_weights), name="shot_pass"
        )
        energy = shared(energy, ("tm", "shot"))
        station_weights = run_prepare(bundled(*station_net), station_inner_offsets, "prepare_station")
    station_weights = (*station_weights, station_inner_offsets)
    for i in range(ITERS):
        station = (i, energy, mixes, station_weights)
        form = "parts" if whole_lines and i == 0 else False
        if i == ITERS - 1:
            (current,) = run_stage(
                plan, small, current, station=station, split_in=form, split_out=split, name="station_pass"
            )
        elif whole_lines:
            current, energy = run_stage(
                plan,
                small,
                current,
                station=station,
                shot=(None, shot_weights),
                split_in=form,
                name="station_and_shot_pass",
            )
            fresh, energy = lax.optimization_barrier((bundle, energy))
            station_weights = (*run_prepare(fresh, station_inner_offsets, "prepare_station"), station_inner_offsets)
            energy = summed(summed(energy, ("line", "tm")), "shot")
        else:
            (current,) = run_stage(plan, small, current, station=station, name="station_pass")
            current, energy = run_stage(plan, small, current, shot=(edges_of(current), shot_weights), name="shot_pass")
            energy = shared(energy, ("tm", "shot"))
    if not split:
        current = current.reshape(n_shot, lines, n_tm, window).transpose(0, 2, 1, 3).reshape(-1, lines, window)
    back = lax.all_to_all(current, axes, split_axis=0, concat_axis=0, tiled=True)
    if whole_lines:
        back = back.transpose(1, 0, 2)
    else:
        back = back.reshape(RPL, n_tm, lines, window).transpose(1, 2, 0, 3)
    return back.reshape(shots_here, block, window)


def solution(mesh):
    placed = (P(("group", "shot"), "line", "tm"), P("group", "line", None), P("group"), P("group"), P("group"))
    return jax.shard_map(
        per_device,
        mesh=mesh,
        in_specs=placed + (P(),) * 9,
        out_specs=P(("group", "shot"), "line", "tm"),
        check_vma=False,
    )
```

```python
import functools

import jax
import jax.numpy as jnp
from jax import lax
from jax.experimental import pallas as pl
from jax.experimental.pallas import tpu as pltpu
from jax.sharding import PartitionSpec as P

RPL = 16
DMAX = 128
ITERS = 2
EPSILON = 1e-05

SLAB = 128
HALF = 64
FEAT = 64
GROUP = 4
WIDE = GROUP * FEAT
QS = SLAB // (2 * GROUP)
QH = QS // 2
assert QH == 8
ONES = 3 * HALF + 6
VMEM_LIMIT = 24 * 1024 * 1024
VMEM_FULL = 63 * 1024 * 1024

BF = jnp.bfloat16
F32 = jnp.float32


def split_bias(bias):
    high = bias.astype(BF).astype(F32)
    middle = (bias - high).astype(BF).astype(F32)
    return high, middle, bias - high - middle


def iota(shape, axis):
    return lax.broadcasted_iota(jnp.int32, shape, axis)


def picks(mask):
    return mask.astype(F32).astype(BF)


def start_of(q):
    return 16 * (q // 2) + 2 * (q % 2)


def prepare_kernel(bundle, bias, o_in, o_out, rhs, cols):
    rhs[...] = jnp.zeros_like(rhs)
    cols[...] = jnp.zeros_like(cols)
    parts = split_bias(bias[0:1, :])
    exits = bundle[3 * FEAT : 3 * FEAT + 16, :].astype(F32)[0:4]
    for p in range(GROUP):
        lanes = slice(p * FEAT, (p + 1) * FEAT)
        for c in range(3):
            row = 3 * FEAT + 16 * (c + 1)
            rhs[p * 32 + c * 8 : p * 32 + c * 8 + 4, lanes] = bundle[row : row + 16, :].astype(F32)[0:4]
            rhs[p * 32 + 24 + c : p * 32 + 25 + c, lanes] = parts[c]
        cols[p * 8 : p * 8 + 4, lanes] = exits
    taps = rhs[...].astype(BF)
    row, col = iota((WIDE, SLAB), 0), iota((WIDE, SLAB), 1)
    channel, j, target = (col >> 3) & 3, col & 7, 4 * (col >> 5) + (col & 7) - 1
    rest = row - 3 * HALF
    sample = jnp.where(rest < 0, row & (HALF - 1), jnp.where(rest & 1 == 1, HALF, -1))
    same = (jnp.where(rest < 0, row >> 6, rest >> 1) == channel) & (channel < 3) & (j < 4)
    offset = jnp.where(same, sample - target, -SLAB)
    ones = (channel == 3) & (j < 3) & (row == ONES + j)
    for q in range(QH):
        chosen = picks((offset == start_of(q)) | ones)
        o_in[q] = jnp.dot(chosen, taps, preferred_element_type=F32).astype(BF)
    o_in[QH:] = jnp.zeros((2, WIDE, WIDE), BF)
    for a, at in [(0, 0), (1, 1), (2, 2), (3, 3), (4, 4), (-1, 5)]:
        for b in range(GROUP):
            if abs(a - b) <= 1:
                tap = a - b + 1
                rows, lanes = slice(at % 4 * FEAT, (at % 4 + 1) * FEAT), slice(b * FEAT, (b + 1) * FEAT)
                o_in[QH + at // 4, rows, lanes] = bundle[tap * FEAT : (tap + 1) * FEAT, :]
    row = iota((16, FEAT), 0)
    below = jnp.zeros((16, FEAT), F32)
    for i, part in enumerate(split_bias(bias[1:2, :])):
        below = jnp.where(row == i, part, below)
    for b in range(GROUP):
        o_in[QH + 1, SLAB : SLAB + 16, b * FEAT : (b + 1) * FEAT] = below.astype(BF)
    row, col = iota((SLAB, SLAB), 0), iota((SLAB, SLAB), 1)
    p, j = row >> 3, row & 7
    offset = jnp.where((p < GROUP) & (j < 4), col - (4 * p + j - 1), -SLAB)
    back = jnp.transpose(cols[...]).astype(BF)
    follows = (p == GROUP - 1) & (j == 3) & (col == 0)
    precedes = (row == 0) & (col == SLAB - 1)
    for q in range(QS + 2):
        chosen = picks(offset == start_of(q) if q < QS else [follows, precedes][q - QS])
        o_out[q] = jnp.dot(back, chosen, preferred_element_type=F32).astype(BF)


def pack_kernel(plan, traces, mixes, *refs):
    count = plan.packets
    packets, (held, mixed, done) = refs[:count], refs[count:]
    _, _, at_tm, at_shot, mine = places(plan, False)
    block, share = traces.shape
    groups = mixes.shape[0]
    copies = [pltpu.make_async_copy(traces, held, done.at[0])]
    at = pl.multiple_of(at_tm * share, share)
    for g in range(groups):
        into = mixed.at[g * block : (g + 1) * block, :]
        copies.append(pltpu.make_async_copy(mixes.at[g, :, pl.ds(at, share)], into, done.at[g + 1]))
    for copy in copies:
        copy.start()
    lines, each = plan.block_lines, plan.each
    row = lax.broadcasted_iota(jnp.int32, (block, block), 0)
    col = lax.broadcasted_iota(jnp.int32, (block, block), 1)
    rest, line = split_index(row, lines)
    d, spot = split_index(rest, each)
    order = (col == line * RPL + (d ^ mine) * each + spot).astype(F32).astype(BF)
    rows = count * groups * lines
    row = lax.broadcasted_iota(jnp.int32, (rows, groups * block), 0)
    col = lax.broadcasted_iota(jnp.int32, (rows, groups * block), 1)
    rest, line = split_index(row, lines)
    d, g = split_index(rest, groups)
    choose = (col == g * block + line * RPL + (d ^ mine) * each + at_shot).astype(F32).astype(BF)
    for copy in copies:
        copy.wait()
    top, rest = each * lines, groups * lines
    moved = jnp.dot(order, held[...], preferred_element_type=F32)
    picked = jnp.dot(choose, mixed[...], preferred_element_type=F32)
    for d, packet in enumerate(packets):
        packet[0:top, :] = moved[d * top : (d + 1) * top].astype(BF)
        packet[top:, :] = picked[d * rest : (d + 1) * rest].astype(BF)


def places(plan, first):
    at_shot, at_line, at_tm = (lax.axis_index(a) for a in ("shot", "line", "tm"))
    if not plan.whole_lines:
        return at_shot, at_tm * plan.lines, at_tm, at_shot, 0
    mine = at_line * plan.time_parts + at_tm
    return mine * plan.each + (0 if first else at_shot), 0, at_tm, at_shot, mine


def split_index(value, size):
    if size & (size - 1):
        return value // size, value % size
    return value >> (size.bit_length() - 1), value & (size - 1)


def section_map(plan, place, tallies, stride):
    shape = (plan.rows, SLAB)
    lane = lax.broadcasted_iota(jnp.int32, shape, 1)
    apart, line = split_index(lax.broadcasted_iota(jnp.int32, shape, 0), plan.lines)
    block, line = split_index(line + place[1], plan.block_lines)
    spot = line * RPL + place[0] + apart * stride
    low = jnp.zeros(shape, jnp.int32)
    high = jnp.zeros(shape, jnp.int32)
    count = jnp.zeros(shape, jnp.int32)
    start = jnp.int32(0)
    for p in range(plan.sections):
        amount = tallies[p]
        for b in range(plan.blocks):
            here = lane == b * plan.sections + p
            low = jnp.where(here, start, low)
            high = jnp.where(here, start + amount, high)
            count = jnp.where(here, amount, count)
        start = start + amount
    member = (spot >= low) & (spot < high) & (split_index(lane, plan.sections)[0] == block)
    return member, count


def shifted(values, by, ok, edge):
    return jnp.where(ok, pltpu.roll(values, by % values.shape[0], 0), edge)


def pack_inputs(plan, channels, packed):
    lane = lax.broadcasted_iota(jnp.int32, (plan.rows, SLAB), 1)
    low = lane < HALF
    ones = ((lane >= ONES - SLAB) & (lane < ONES - SLAB + 3)).astype(F32)
    slabs = [[x[:, t * SLAB : (t + 1) * SLAB] for t in range(plan.slabs)] for x in channels]
    far = [[pltpu.roll(s, HALF + 1 + 2 * c, 1) for s in slabs[c]] for c in range(3)]
    for t in range(plan.slabs):
        v = [slabs[c][t] for c in range(3)]
        w = [pltpu.roll(s, HALF, 1) for s in v]
        even = jnp.where(low, v[2], ones)
        odd = jnp.where(low, w[2], ones)
        for c in range(3):
            left, right = lane == HALF + 2 * c, lane == HALF + 2 * c + 1
            near = pltpu.roll(v[c], 1 + 2 * c, 1)
            even = jnp.where(right, near, even)
            odd = jnp.where(left, near, odd)
            if t > 0:
                even = jnp.where(left, far[c][t - 1], even)
            if t < plan.slabs - 1:
                odd = jnp.where(right, far[c][t + 1], odd)
        packed[0, t, :, 0:SLAB] = jnp.where(low, v[0], w[1]).astype(BF)
        packed[0, t, :, SLAB:WIDE] = even.astype(BF)
        packed[1, t, :, 0:SLAB] = jnp.where(low, w[0], v[1]).astype(BF)
        packed[1, t, :, SLAB:WIDE] = odd.astype(BF)


def network(plan, weights, scratch, regions):
    w_in, w_out = weights
    packed, hidden, total, ends = scratch
    slabs, rows = plan.slabs, plan.rows
    many = slabs * rows
    pitch = slabs + 2

    def first(q):
        value = jnp.dot(packed[...].reshape(2 * many, WIDE), w_in[q], preferred_element_type=F32)
        value = jnp.maximum(value.astype(BF), 0).reshape(2, slabs, rows, WIDE)
        for h in range(2):
            hidden[pl.ds((q + h * QH) * pitch + 1, slabs)] = value[h]

    lane = iota((slabs, rows, SLAB), 2)
    ones = picks(lane < 3)

    def window(q):
        if isinstance(q, int):
            left_at = (q - 2) * pitch + 1 if q >= 2 else (q + QS - 2) * pitch
            right_at = (q + 2) * pitch + 1 if q < QS - 2 else (q + 2 - QS) * pitch + 2
        else:
            left_at = jnp.where(q >= 2, (q - 2) * pitch + 1, (q + QS - 2) * pitch)
            right_at = jnp.where(q < QS - 2, (q + 2) * pitch + 1, (q + 2 - QS) * pitch + 2)
        middle = hidden[pl.ds(q * pitch + 1, slabs)]
        left = hidden[pl.ds(left_at, slabs), :, SLAB:WIDE]
        right = hidden[pl.ds(right_at, slabs), :, 0:SLAB]
        beside = jnp.where(lane < FEAT, right, left)
        return jnp.concatenate([middle, beside, ones], axis=2).reshape(many, 2 * WIDE)

    def second(q):
        both = jnp.concatenate([window(q), window(q + 1)], axis=0)
        value = jnp.dot(both, w_in[QH:].reshape(2 * WIDE, WIDE), preferred_element_type=F32)
        value = jnp.maximum(value.astype(BF), 0)
        return value[:many], value[many:]

    def onto(layer, taps):
        return jnp.dot(layer, taps, preferred_element_type=F32).reshape(slabs, rows, SLAB)

    edge = jnp.zeros((rows, WIDE), BF)
    for k in range(2):
        hidden[(QS - 2 + k) * pitch] = edge
        hidden[(k + 1) * pitch - 1] = edge
    total[...] = jnp.zeros_like(total)

    @regions
    def _():
        for q in range(QH):
            first(q)

    @regions
    def _():
        for q in range(0, QS, 2):
            one, two = second(q)
            total[...] += onto(jnp.concatenate([one, two], axis=1), w_out[q : q + 2].reshape(2 * WIDE, SLAB))
            if q == 0:
                ends[0] = one
            if q == QS - 2:
                ends[1] = two

    total[0 : slabs - 1] += onto(ends[0], w_out[QS + 1])[1:]
    total[1:slabs] += onto(ends[1], w_out[QS])[: slabs - 1]


def inline(body):
    body()


def add_total(plan, now, total, scale=None):
    for t in range(plan.slabs):
        lanes = slice(t * SLAB, (t + 1) * SLAB)
        more = total[t] if scale is None else scale * total[t]
        now[:, lanes] = (now[:, lanes] + more).astype(BF).astype(F32)


def shot_stage(plan, place, tallies, stride, edges, weights, now, scratch):
    apart = pl.when(place[0] >= 0)

    @apart
    def _():
        x = now[...]
        line = split_index(iota(x.shape, 0), plan.lines)[1]
        above = 0.0 if edges is None else edges[0].astype(F32)
        below = 0.0 if edges is None else edges[1].astype(F32)
        channels = [
            shifted(x, 1, line > 0, above),
            x,
            shifted(x, -1, line < plan.lines - 1, below),
        ]
        pack_inputs(plan, channels, scratch[0])

    network(plan, weights, scratch, apart)
    add_total(plan, now, scratch[2])
    power = jnp.zeros((plan.rows, SLAB), F32)
    for t in range(plan.slabs):
        piece = now[:, t * SLAB : (t + 1) * SLAB]
        power = power + piece * piece
    member, _ = section_map(plan, place, tallies, stride)
    each = jnp.where(member, jnp.sum(power, axis=1, keepdims=True), 0.0)
    return jnp.sum(each, axis=0, keepdims=True)


def packet_place(plan, place, d, share):
    a, b = split_index(place[4] ^ d, plan.time_parts)
    row = pl.multiple_of(a * plan.block_lines, plan.block_lines)
    return pl.ds(row, plan.block_lines), pl.ds(pl.multiple_of(b * share, share), share)


def station_stage(
    plan, place, tallies, lags, order, pace, energies, mixes, weights, now, scratch, blend
):
    member, count = section_map(plan, place, tallies, 0)
    totals = energies[...]
    denominator = jnp.maximum(count, 1) * (plan.shots * plan.slabs * SLAB)
    level = jnp.sqrt(totals / denominator.astype(F32) + EPSILON)
    rms = jnp.sum(jnp.where(member, level, 0.0), axis=1, keepdims=True)
    x = (now[...] / rms).astype(BF).astype(F32)
    row = lax.broadcasted_iota(jnp.int32, x.shape, 0)
    channels = [
        shifted(x, plan.lines, row >= plan.lines, 0.0),
        x,
        shifted(x, -plan.lines, row < plan.rows - plan.lines, 0.0),
    ]
    pack_inputs(plan, channels, scratch[0])
    network(plan, weights, scratch, inline)
    add_total(plan, now, scratch[2], rms)

    fired, misfit = blend
    lane = lax.broadcasted_iota(jnp.int32, (plan.lines, SLAB), 1)
    mixtures = misfit.shape[0]
    per = plan.shots // mixtures
    if plan.whole_lines:
        for d, packet in enumerate(mixes):
            here, lanes = packet_place(plan, place, d, packet.shape[1])
            piece = packet[plan.each * plan.block_lines :, :].astype(F32)
            for g in range(mixtures):
                misfit[g, here, lanes] = piece[g * plan.block_lines : (g + 1) * plan.block_lines]
    else:
        misfit[...] = mixes[0][...].astype(F32)
    for s in range(plan.shots):
        lag = lags[s]
        before = jnp.zeros((plan.lines, SLAB), F32)
        for t in range(plan.slabs):
            lanes = slice(t * SLAB, (t + 1) * SLAB)
            turned = pltpu.roll(now[s * plan.lines : (s + 1) * plan.lines, lanes], lag, 1)
            fired[s, :, lanes] = jnp.where(lane < lag, before, turned)
            before = turned
    for g in range(mixtures):
        value = fired[order[g * per]]
        for k in range(1, per):
            value = value + fired[order[g * per + k]]
        misfit[g] = value - misfit[g]
    for s in range(plan.shots):
        lag = lags[s]
        spot = jnp.int32(0)
        for k in range(plan.shots):
            spot = spot + jnp.where(order[k] == s, k, 0)
        which = spot // per
        back = (DMAX - lag) % DMAX
        after = jnp.zeros((plan.lines, SLAB), F32)
        rows = slice(s * plan.lines, (s + 1) * plan.lines)
        for t in range(plan.slabs - 1, -1, -1):
            lanes = slice(t * SLAB, (t + 1) * SLAB)
            turned = pltpu.roll(misfit[which, :, lanes], back, 1)
            pulled = jnp.where(lane < DMAX - lag, turned, after)
            after = turned
            now[rows, lanes] = (now[rows, lanes] - pace * pulled).astype(BF).astype(F32)


def stage_kernel(plan, station_round, with_shot, has_edges, stride, split_in, split_out, *refs):
    refs = list(refs)
    take = lambda n: [refs.pop(0) for _ in range(n)]
    tallies, lags, order, paces = take(4)
    place = places(plan, stride)
    sources = take({"parts": plan.each, "packets": plan.packets}.get(split_in, 1))
    source = sources[0]
    station = station_round is not None
    if station:
        (energies,) = take(1)
        mixes = take(plan.packets)
        station_weights = take(2)
    edges = None
    if with_shot:
        if has_edges:
            (edges,) = take(1)
        shot_weights = take(2)
    results = take(plan.each if split_out == "parts" else 1)
    result = results[0]
    if with_shot and split_out != "parts":
        (energy,) = take(1)
    now, packed, hidden, total, ends = take(5)
    scratch = (packed, hidden, total, ends)
    length = plan.slabs * SLAB
    if split_in == "parts":
        for d, part in enumerate(sources):
            at = pl.multiple_of((place[3] ^ d) * plan.lines, plan.lines)
            now[pl.ds(at, plan.lines), :] = part[:, 0:length].astype(F32)
    elif split_in:
        lines = plan.block_lines
        for d, packet in enumerate(sources):
            here, lanes = packet_place(plan, place, d, packet.shape[1])
            piece = packet[0 : plan.each * lines, :].astype(F32)
            for k in range(plan.each):
                now[pl.ds(k * plan.lines + here.start, lines), lanes] = piece[k * lines : (k + 1) * lines]
    else:
        now[...] = source[...].astype(F32)
    if station:
        station_stage(
            plan,
            place,
            tallies,
            lags,
            order,
            paces[station_round],
            energies,
            mixes,
            station_weights,
            now,
            scratch,
            refs,
        )
    if with_shot:
        sums = shot_stage(plan, place, tallies, stride, edges, shot_weights, now, scratch)
    if split_out == "parts":
        row = lax.broadcasted_iota(jnp.int32, (plan.lines, SLAB), 0)
        beside = jnp.zeros((plan.lines, SLAB), F32)
        for i, part in enumerate(split_bias(sums)):
            beside = jnp.where(row == i, part, beside)
        for d, part in enumerate(results):
            at = pl.multiple_of((place[3] ^ d) * plan.lines, plan.lines)
            part[:, 0:length] = now[pl.ds(at, plan.lines), :].astype(BF)
            part[:, length:] = beside.astype(BF)
        return
    if with_shot:
        energy[...] = sums
    if split_out:
        for n, (row, lane, rows, lanes) in enumerate(plan.pieces):
            result[n] = now[row : row + rows, lane : lane + lanes].astype(BF)
    else:
        result[...] = now[...].astype(BF)


SMEM = pl.BlockSpec(memory_space=pltpu.SMEM)
VMEM = pl.BlockSpec(memory_space=pltpu.VMEM)
HBM = pl.BlockSpec(memory_space=pltpu.HBM)


def run_stage(plan, small, source, station=None, shot=None, split_in=False, split_out=False, stride=0, name="stage"):
    operands = [*small, *(source if split_in else [source])]
    station_round, has_edges = None, False
    macs = 0
    pass_macs = plan.rows * plan.slabs * QS * WIDE * (WIDE * 3 + SLAB)
    if station is not None:
        station_round, energies, mixes, weights = station
        operands += [energies, *mixes, *weights]
        macs += pass_macs
    if shot is not None:
        edges, weights = shot
        has_edges = edges is not None
        operands += ([edges] if has_edges else []) + list(weights)
        macs += pass_macs
    specs = [SMEM] * len(small) + [VMEM] * (len(operands) - len(small))
    length = plan.slabs * SLAB
    if split_out == "parts":
        shapes = [jax.ShapeDtypeStruct((plan.lines, length + SLAB), BF)] * plan.each
    elif split_out:
        _, _, rows, lanes = plan.pieces[0]
        shapes = [jax.ShapeDtypeStruct((len(plan.pieces), rows, lanes), BF)]
    else:
        shapes = [jax.ShapeDtypeStruct((plan.rows, length), BF)]
    if shot is not None and split_out != "parts":
        shapes.append(jax.ShapeDtypeStruct((1, SLAB), F32))
    scratch = [
        pltpu.VMEM((plan.rows, length), F32),
        pltpu.VMEM((2, plan.slabs, plan.rows, WIDE), BF),
        pltpu.VMEM((QS * (plan.slabs + 2), plan.rows, WIDE), BF),
        pltpu.VMEM((plan.slabs, plan.rows, SLAB), F32),
        pltpu.VMEM((2, plan.slabs * plan.rows, WIDE), BF),
    ]
    if station is not None:
        scratch += [
            pltpu.VMEM((plan.shots, plan.lines, length), F32),
            pltpu.VMEM((plan.mixtures, plan.lines, length), F32),
        ]
    return pl.pallas_call(
        functools.partial(
            stage_kernel, plan, station_round, shot is not None, has_edges, stride, split_in, split_out
        ),
        out_shape=shapes,
        in_specs=specs,
        out_specs=[VMEM] * len(shapes),
        scratch_shapes=scratch,
        compiler_params=pltpu.CompilerParams(vmem_limit_bytes=VMEM_LIMIT),
        cost_estimate=pl.CostEstimate(flops=2 * macs, bytes_accessed=1 << 20, transcendentals=0),
        name=name,
    )(*operands)


def bundled(entry, spaced, leave):
    rows = [spaced.reshape(3 * FEAT, FEAT), jnp.pad(leave, ((0, 12), (0, 0)))]
    rows.append(jnp.pad(entry.transpose(1, 0, 2), ((0, 0), (0, 12), (0, 0))).reshape(48, FEAT))
    return jnp.concatenate(rows, axis=0)


def run_prepare(bundle, bias, name):
    return pl.pallas_call(
        prepare_kernel,
        out_shape=[
            jax.ShapeDtypeStruct((QH + 2, WIDE, WIDE), BF),
            jax.ShapeDtypeStruct((QS + 2, WIDE, SLAB), BF),
        ],
        in_specs=[VMEM] * 2,
        out_specs=[VMEM] * 2,
        scratch_shapes=[pltpu.VMEM((SLAB, WIDE), F32), pltpu.VMEM((SLAB, WIDE), F32)],
        compiler_params=pltpu.CompilerParams(vmem_limit_bytes=VMEM_LIMIT),
        cost_estimate=pl.CostEstimate(flops=2 * 8192 * WIDE * SLAB, bytes_accessed=4 << 20, transcendentals=0),
        name=name,
    )(bundle, bias)


def run_pack(plan, traces, mixtures):
    groups, block, _ = mixtures.shape
    width = traces.shape[1]
    return pl.pallas_call(
        functools.partial(pack_kernel, plan),
        out_shape=[jax.ShapeDtypeStruct(((plan.each + groups) * plan.block_lines, width), BF)] * plan.packets,
        in_specs=[HBM, HBM],
        out_specs=[VMEM] * plan.packets,
        scratch_shapes=[
            pltpu.VMEM((block, width), BF),
            pltpu.VMEM((groups * block, width), BF),
            pltpu.SemaphoreType.DMA((groups + 1,)),
        ],
        compiler_params=pltpu.CompilerParams(vmem_limit_bytes=VMEM_FULL),
        cost_estimate=pl.CostEstimate(flops=2 * block * block * width, bytes_accessed=1 << 20, transcendentals=0),
        name="pack",
    )(traces, mixtures)


class Plan:
    def __init__(self, **sizes):
        self.__dict__.update(sizes)
        self.rows = self.shots * self.lines


def exchanged(parts, axes):
    size = len(parts)
    return [parts[0]] + [lax.ppermute(parts[d], axes, [(i, i ^ d) for i in range(size)]) for d in range(1, size)]


def per_device(
    initial_guess,
    measured_mixtures,
    launch_lags,
    source_launch_order,
    station_portion_tallies,
    source_entry_kernel,
    source_spaced_kernel,
    source_exit_kernel,
    source_inner_offsets,
    station_entry_kernel,
    station_spaced_kernel,
    station_exit_kernel,
    station_inner_offsets,
    learned_pace_factors,
):
    shots_here, block, window = initial_guess.shape
    n_shot, n_line, n_tm = (lax.axis_size(a) for a in ("shot", "line", "tm"))
    at_shot, at_tm = lax.axis_index("shot"), lax.axis_index("tm")
    block_lines = block // RPL
    length = window * n_tm
    shots = shots_here * n_shot
    sections = station_portion_tallies.shape[0]
    mixtures = measured_mixtures.shape[0]
    whole_lines = n_shot * n_line * n_tm == RPL
    assert shots_here == 1 and (whole_lines or n_shot == RPL)
    if whole_lines:
        axes = ("line", "tm", "shot")
        lines, blocks = block_lines * n_line, n_line
    else:
        axes = ("shot", "tm")
        lines = block_lines // n_tm
        blocks = 1
    turns = [(s, a, b) for a in range(blocks) for b in range(n_tm) for s in range(n_shot)]
    plan = Plan(
        whole_lines=whole_lines,
        shots=shots,
        lines=lines,
        block_lines=block_lines,
        blocks=blocks,
        sections=sections,
        mixtures=mixtures,
        slabs=length // SLAB,
        each=n_shot,
        time_parts=n_tm,
        packets=n_line * n_tm if whole_lines else 1,
        pieces=[(s * lines + a * block_lines, b * window, block_lines, window) for s, a, b in turns],
    )

    if whole_lines:
        assert n_tm == 2 and n_line & (n_line - 1) == 0 and n_shot & (n_shot - 1) == 0
        arrived = run_pack(plan, initial_guess.reshape(block, window), measured_mixtures)
        arrived = exchanged(arrived, ("line", "tm"))
    else:
        grid = initial_guess.reshape(n_tm, lines, RPL, window)
        leaving = grid.transpose(2, 0, 1, 3).reshape(RPL * n_tm, lines, window)
        arrived = lax.all_to_all(leaving, axes, split_axis=0, concat_axis=0, tiled=True)

    shot_bundle = bundled(source_entry_kernel, source_spaced_kernel, source_exit_kernel)
    station_net = (station_entry_kernel, station_spaced_kernel, station_exit_kernel)
    shot_weights = run_prepare(shot_bundle, source_inner_offsets, "prepare_shot")
    small = (station_portion_tallies, launch_lags, source_launch_order, learned_pace_factors)
    split = whole_lines and block_lines % 8 == 0
    assert split or not whole_lines
    if whole_lines:
        mixes = source = arrived
    else:
        grid = measured_mixtures.reshape(mixtures, n_tm, lines, RPL, length)
        mixes = lax.dynamic_slice(grid, (0, at_tm, 0, at_shot, 0), (mixtures, 1, lines, 1, length))
        mixes = [mixes.reshape(mixtures, lines, length)]
        source = arrived.reshape(n_shot, n_tm, lines, window).transpose(0, 2, 1, 3).reshape(plan.rows, length)

    def edges_of(current):
        if whole_lines:
            return None
        size = n_line * n_tm
        grid = current.reshape(shots, lines, length)
        up = [(i, i + 1) for i in range(size - 1)]
        down = [(j, i) for i, j in up]
        above = lax.ppermute(grid[:, -1], ("line", "tm"), up)
        below = lax.ppermute(grid[:, 0], ("line", "tm"), down)
        wide = jnp.broadcast_to(jnp.stack([above, below])[:, :, None, :], (2, shots, lines, length))
        return wide.reshape(2, plan.rows, length)

    def summed(value, axis):
        size = lax.axis_size(axis)
        if size <= 4:
            others = [lax.ppermute(value, axis, [(i, i ^ d) for i in range(size)]) for d in range(1, size)]
            return sum(others, value)
        step = 1
        while step < size:
            value = value + lax.ppermute(value, axis, [(i, i ^ step) for i in range(size)])
            step *= 2
        return value

    def shared(energy, along):
        for axis in along:
            energy = summed(energy, axis)
        return energy

    if whole_lines:
        parts = run_stage(
            plan,
            small,
            source,
            shot=(None, shot_weights),
            split_in="packets",
            split_out="parts",
            stride=1,
            name="shot_pass",
        )
        station_net, own = lax.optimization_barrier((station_net, parts[0]))
        current = exchanged([own, *parts[1:]], "shot")
        bundle = bundled(*station_net)
        station_weights = run_prepare(bundle, station_inner_offsets, "prepare_station")
        energy = sum(jnp.sum(p[0:3, length:].astype(F32), axis=0, keepdims=True) for p in current)
        station_weights, energy = lax.optimization_barrier((station_weights, energy))
        energy = summed(energy, ("line", "tm"))
    else:
        current, energy = run_stage(
            plan, small, source, shot=(edges_of(source), shot_weights), name="shot_pass"
        )
        energy = shared(energy, ("tm", "shot"))
        station_weights = run_prepare(bundled(*station_net), station_inner_offsets, "prepare_station")
    for i in range(ITERS):
        station = (i, energy, mixes, station_weights)
        form = "parts" if whole_lines and i == 0 else False
        if i == ITERS - 1:
            (current,) = run_stage(
                plan, small, current, station=station, split_in=form, split_out=split, name="station_pass"
            )
        elif whole_lines:
            current, energy = run_stage(
                plan,
                small,
                current,
                station=station,
                shot=(None, shot_weights),
                split_in=form,
                name="station_and_shot_pass",
            )
            fresh, energy = lax.optimization_barrier((bundle, energy))
            station_weights = run_prepare(fresh, station_inner_offsets, "prepare_station")
            energy = summed(summed(energy, ("line", "tm")), "shot")
        else:
            (current,) = run_stage(plan, small, current, station=station, name="station_pass")
            current, energy = run_stage(plan, small, current, shot=(edges_of(current), shot_weights), name="shot_pass")
            energy = shared(energy, ("tm", "shot"))
    if not split:
        current = current.reshape(n_shot, lines, n_tm, window).transpose(0, 2, 1, 3).reshape(-1, lines, window)
    back = lax.all_to_all(current, axes, split_axis=0, concat_axis=0, tiled=True)
    if whole_lines:
        back = back.transpose(1, 0, 2)
    else:
        back = back.reshape(RPL, n_tm, lines, window).transpose(1, 2, 0, 3)
    return back.reshape(shots_here, block, window)


def solution(mesh):
    placed = (P(("group", "shot"), "line", "tm"), P("group", "line", None), P("group"), P("group"), P("group"))
    return jax.shard_map(
        per_device,
        mesh=mesh,
        in_specs=placed + (P(),) * 9,
        out_specs=P(("group", "shot"), "line", "tm"),
        check_vma=False,
    )
```

```python
import functools

import jax
import jax.numpy as jnp
from jax import lax
from jax.experimental import pallas as pl
from jax.experimental.pallas import tpu as pltpu
from jax.sharding import PartitionSpec as P

RPL = 16
DMAX = 128
ITERS = 2
EPSILON = 1e-05

SLAB = 128
HALF = 64
FEAT = 64
GROUP = 4
WIDE = GROUP * FEAT
QS = SLAB // (2 * GROUP)
QH = QS // 2
assert QH == 8
ONES = 3 * HALF + 6
VMEM_LIMIT = 24 * 1024 * 1024
VMEM_FULL = 63 * 1024 * 1024

BF = jnp.bfloat16
F32 = jnp.float32


def split_bias(bias):
    high = bias.astype(BF).astype(F32)
    middle = (bias - high).astype(BF).astype(F32)
    return high, middle, bias - high - middle


def iota(shape, axis):
    return lax.broadcasted_iota(jnp.int32, shape, axis)


def picks(mask):
    return mask.astype(F32).astype(BF)


def start_of(q):
    return 16 * (q // 2) + 2 * (q % 2)


def prepare_kernel(bundle, bias, o_in, o_out, rhs, cols):
    rhs[...] = jnp.zeros_like(rhs)
    cols[...] = jnp.zeros_like(cols)
    parts = split_bias(bias[0:1, :])
    exits = bundle[3 * FEAT : 3 * FEAT + 16, :].astype(F32)[0:4]
    for p in range(GROUP):
        lanes = slice(p * FEAT, (p + 1) * FEAT)
        for c in range(3):
            row = 3 * FEAT + 16 * (c + 1)
            rhs[p * 32 + c * 8 : p * 32 + c * 8 + 4, lanes] = bundle[row : row + 16, :].astype(F32)[0:4]
            rhs[p * 32 + 24 + c : p * 32 + 25 + c, lanes] = parts[c]
        cols[p * 8 : p * 8 + 4, lanes] = exits
    taps = rhs[...].astype(BF)
    row, col = iota((WIDE, SLAB), 0), iota((WIDE, SLAB), 1)
    channel, j, target = (col >> 3) & 3, col & 7, 4 * (col >> 5) + (col & 7) - 1
    rest = row - 3 * HALF
    sample = jnp.where(rest < 0, row & (HALF - 1), jnp.where(rest & 1 == 1, HALF, -1))
    same = (jnp.where(rest < 0, row >> 6, rest >> 1) == channel) & (channel < 3) & (j < 4)
    offset = jnp.where(same, sample - target, -SLAB)
    ones = (channel == 3) & (j < 3) & (row == ONES + j)
    for q in range(QH):
        chosen = picks((offset == start_of(q)) | ones)
        o_in[q] = jnp.dot(chosen, taps, preferred_element_type=F32).astype(BF)
    o_in[QH:] = jnp.zeros((2, WIDE, WIDE), BF)
    for a, at in [(0, 0), (1, 1), (2, 2), (3, 3), (4, 4), (-1, 5)]:
        for b in range(GROUP):
            if abs(a - b) <= 1:
                tap = a - b + 1
                rows, lanes = slice(at % 4 * FEAT, (at % 4 + 1) * FEAT), slice(b * FEAT, (b + 1) * FEAT)
                o_in[QH + at // 4, rows, lanes] = bundle[tap * FEAT : (tap + 1) * FEAT, :]
    row = iota((16, FEAT), 0)
    below = jnp.zeros((16, FEAT), F32)
    for i, part in enumerate(split_bias(bias[1:2, :])):
        below = jnp.where(row == i, part, below)
    for b in range(GROUP):
        o_in[QH + 1, SLAB : SLAB + 16, b * FEAT : (b + 1) * FEAT] = below.astype(BF)
    row, col = iota((SLAB, SLAB), 0), iota((SLAB, SLAB), 1)
    p, j = row >> 3, row & 7
    offset = jnp.where((p < GROUP) & (j < 4), col - (4 * p + j - 1), -SLAB)
    back = jnp.transpose(cols[...]).astype(BF)
    follows = (p == GROUP - 1) & (j == 3) & (col == 0)
    precedes = (row == 0) & (col == SLAB - 1)
    for q in range(QS + 2):
        chosen = picks(offset == start_of(q) if q < QS else [follows, precedes][q - QS])
        o_out[q] = jnp.dot(back, chosen, preferred_element_type=F32).astype(BF)


def pack_kernel(plan, traces, mixes, *refs):
    count = plan.packets
    packets, (held, mixed, done) = refs[:count], refs[count:]
    _, _, at_tm, at_shot, mine = places(plan, False)
    block, share = traces.shape
    groups = mixes.shape[0]
    copies = [pltpu.make_async_copy(traces, held, done.at[0])]
    at = pl.multiple_of(at_tm * share, share)
    for g in range(groups):
        into = mixed.at[g * block : (g + 1) * block, :]
        copies.append(pltpu.make_async_copy(mixes.at[g, :, pl.ds(at, share)], into, done.at[g + 1]))
    for copy in copies:
        copy.start()
    lines, each = plan.block_lines, plan.each
    row = lax.broadcasted_iota(jnp.int32, (block, block), 0)
    col = lax.broadcasted_iota(jnp.int32, (block, block), 1)
    rest, line = split_index(row, lines)
    d, spot = split_index(rest, each)
    order = (col == line * RPL + (d ^ mine) * each + spot).astype(F32).astype(BF)
    rows = count * groups * lines
    row = lax.broadcasted_iota(jnp.int32, (rows, groups * block), 0)
    col = lax.broadcasted_iota(jnp.int32, (rows, groups * block), 1)
    rest, line = split_index(row, lines)
    d, g = split_index(rest, groups)
    choose = (col == g * block + line * RPL + (d ^ mine) * each + at_shot).astype(F32).astype(BF)
    for copy in copies:
        copy.wait()
    top, rest = each * lines, groups * lines
    moved = jnp.dot(order, held[...], preferred_element_type=F32)
    picked = jnp.dot(choose, mixed[...], preferred_element_type=F32)
    for d, packet in enumerate(packets):
        packet[0:top, :] = moved[d * top : (d + 1) * top].astype(BF)
        packet[top:, :] = picked[d * rest : (d + 1) * rest].astype(BF)


def places(plan, first):
    at_shot, at_line, at_tm = (lax.axis_index(a) for a in ("shot", "line", "tm"))
    if not plan.whole_lines:
        return at_shot, at_tm * plan.lines, at_tm, at_shot, 0
    mine = at_line * plan.time_parts + at_tm
    return mine * plan.each + (0 if first else at_shot), 0, at_tm, at_shot, mine


def split_index(value, size):
    if size & (size - 1):
        return value // size, value % size
    return value >> (size.bit_length() - 1), value & (size - 1)


def section_map(plan, place, tallies, stride):
    shape = (plan.rows, SLAB)
    lane = lax.broadcasted_iota(jnp.int32, shape, 1)
    apart, line = split_index(lax.broadcasted_iota(jnp.int32, shape, 0), plan.lines)
    block, line = split_index(line + place[1], plan.block_lines)
    spot = line * RPL + place[0] + apart * stride
    low = jnp.zeros(shape, jnp.int32)
    high = jnp.zeros(shape, jnp.int32)
    count = jnp.zeros(shape, jnp.int32)
    start = jnp.int32(0)
    for p in range(plan.sections):
        amount = tallies[p]
        for b in range(plan.blocks):
            here = lane == b * plan.sections + p
            low = jnp.where(here, start, low)
            high = jnp.where(here, start + amount, high)
            count = jnp.where(here, amount, count)
        start = start + amount
    member = (spot >= low) & (spot < high) & (split_index(lane, plan.sections)[0] == block)
    return member, count


def shifted(values, by, ok, edge):
    return jnp.where(ok, pltpu.roll(values, by % values.shape[0], 0), edge)


def pack_inputs(plan, channels, packed):
    lane = lax.broadcasted_iota(jnp.int32, (plan.rows, SLAB), 1)
    low = lane < HALF
    ones = ((lane >= ONES - SLAB) & (lane < ONES - SLAB + 3)).astype(F32)
    slabs = [[x[:, t * SLAB : (t + 1) * SLAB] for t in range(plan.slabs)] for x in channels]
    far = [[pltpu.roll(s, HALF + 1 + 2 * c, 1) for s in slabs[c]] for c in range(3)]
    for t in range(plan.slabs):
        v = [slabs[c][t] for c in range(3)]
        w = [pltpu.roll(s, HALF, 1) for s in v]
        even = jnp.where(low, v[2], ones)
        odd = jnp.where(low, w[2], ones)
        for c in range(3):
            left, right = lane == HALF + 2 * c, lane == HALF + 2 * c + 1
            near = pltpu.roll(v[c], 1 + 2 * c, 1)
            even = jnp.where(right, near, even)
            odd = jnp.where(left, near, odd)
            if t > 0:
                even = jnp.where(left, far[c][t - 1], even)
            if t < plan.slabs - 1:
                odd = jnp.where(right, far[c][t + 1], odd)
        packed[0, t, :, 0:SLAB] = jnp.where(low, v[0], w[1]).astype(BF)
        packed[0, t, :, SLAB:WIDE] = even.astype(BF)
        packed[1, t, :, 0:SLAB] = jnp.where(low, w[0], v[1]).astype(BF)
        packed[1, t, :, SLAB:WIDE] = odd.astype(BF)


def network(plan, weights, scratch, regions):
    w_in, w_out = weights
    packed, hidden, total, ends = scratch
    slabs, rows = plan.slabs, plan.rows
    many = slabs * rows
    pitch = slabs + 2

    def first(q):
        taps = jnp.concatenate([w_in[q], w_in[q + 1]], axis=1)
        value = jnp.dot(packed[...].reshape(2 * many, WIDE), taps, preferred_element_type=F32)
        value = jnp.maximum(value.astype(BF), 0).reshape(2, slabs, rows, 2 * WIDE)
        for h in range(2):
            for k in range(2):
                at = pl.ds((q + k + h * QH) * pitch + 1, slabs)
                hidden[at] = value[h, :, :, k * WIDE : (k + 1) * WIDE]

    lane = iota((slabs, rows, SLAB), 2)
    ones = picks(lane < 3)

    def window(q):
        if isinstance(q, int):
            left_at = (q - 2) * pitch + 1 if q >= 2 else (q + QS - 2) * pitch
            right_at = (q + 2) * pitch + 1 if q < QS - 2 else (q + 2 - QS) * pitch + 2
        else:
            left_at = jnp.where(q >= 2, (q - 2) * pitch + 1, (q + QS - 2) * pitch)
            right_at = jnp.where(q < QS - 2, (q + 2) * pitch + 1, (q + 2 - QS) * pitch + 2)
        middle = hidden[pl.ds(q * pitch + 1, slabs)]
        left = hidden[pl.ds(left_at, slabs), :, SLAB:WIDE]
        right = hidden[pl.ds(right_at, slabs), :, 0:SLAB]
        beside = jnp.where(lane < FEAT, right, left)
        return jnp.concatenate([middle, beside, ones], axis=2).reshape(many, 2 * WIDE)

    def second(q):
        both = jnp.concatenate([window(q), window(q + 1)], axis=0)
        value = jnp.dot(both, w_in[QH:].reshape(2 * WIDE, WIDE), preferred_element_type=F32)
        value = jnp.maximum(value.astype(BF), 0)
        return value[:many], value[many:]

    def onto(layer, taps):
        return jnp.dot(layer, taps, preferred_element_type=F32).reshape(slabs, rows, SLAB)

    edge = jnp.zeros((rows, WIDE), BF)
    for k in range(2):
        hidden[(QS - 2 + k) * pitch] = edge
        hidden[(k + 1) * pitch - 1] = edge
    total[...] = jnp.zeros_like(total)

    @regions
    def _():
        for q in range(0, QH, 2):
            first(q)

    @regions
    def _():
        for q in range(0, QS, 2):
            one, two = second(q)
            total[...] += onto(jnp.concatenate([one, two], axis=1), w_out[q : q + 2].reshape(2 * WIDE, SLAB))
            if q == 0:
                ends[0] = one
            if q == QS - 2:
                ends[1] = two

    total[0 : slabs - 1] += onto(ends[0], w_out[QS + 1])[1:]
    total[1:slabs] += onto(ends[1], w_out[QS])[: slabs - 1]


def add_total(plan, now, total, scale=None):
    for t in range(plan.slabs):
        lanes = slice(t * SLAB, (t + 1) * SLAB)
        more = total[t] if scale is None else scale * total[t]
        now[:, lanes] = (now[:, lanes] + more).astype(BF).astype(F32)


def shot_stage(plan, place, tallies, stride, edges, weights, now, scratch):
    apart = pl.when(place[0] >= 0)

    @apart
    def _():
        x = now[...]
        line = split_index(iota(x.shape, 0), plan.lines)[1]
        above = 0.0 if edges is None else edges[0].astype(F32)
        below = 0.0 if edges is None else edges[1].astype(F32)
        channels = [
            shifted(x, 1, line > 0, above),
            x,
            shifted(x, -1, line < plan.lines - 1, below),
        ]
        pack_inputs(plan, channels, scratch[0])

    network(plan, weights, scratch, apart)
    add_total(plan, now, scratch[2])
    power = jnp.zeros((plan.rows, SLAB), F32)
    for t in range(plan.slabs):
        piece = now[:, t * SLAB : (t + 1) * SLAB]
        power = power + piece * piece
    member, _ = section_map(plan, place, tallies, stride)
    each = jnp.where(member, jnp.sum(power, axis=1, keepdims=True), 0.0)
    return jnp.sum(each, axis=0, keepdims=True)


def packet_place(plan, place, d, share):
    a, b = split_index(place[4] ^ d, plan.time_parts)
    row = pl.multiple_of(a * plan.block_lines, plan.block_lines)
    return pl.ds(row, plan.block_lines), pl.ds(pl.multiple_of(b * share, share), share)


def station_stage(
    plan, place, tallies, lags, order, pace, energies, mixes, weights, now, scratch, blend
):
    fired, misfit, scale = blend
    apart = pl.when(place[0] >= 0)

    @apart
    def _():
        member, count = section_map(plan, place, tallies, 0)
        denominator = jnp.maximum(count, 1) * (plan.shots * plan.slabs * SLAB)
        level = jnp.sqrt(energies[...] / denominator.astype(F32) + EPSILON)
        rms = jnp.sum(jnp.where(member, level, 0.0), axis=1, keepdims=True)
        scale[...] = jnp.broadcast_to(rms, scale.shape)
        x = (now[...] / rms).astype(BF).astype(F32)
        row = iota(x.shape, 0)
        channels = [
            shifted(x, plan.lines, row >= plan.lines, 0.0),
            x,
            shifted(x, -plan.lines, row < plan.rows - plan.lines, 0.0),
        ]
        pack_inputs(plan, channels, scratch[0])

    network(plan, weights, scratch, apart)
    add_total(plan, now, scratch[2], scale[...])
    lane = lax.broadcasted_iota(jnp.int32, (plan.lines, SLAB), 1)
    mixtures = misfit.shape[0]
    per = plan.shots // mixtures
    if plan.whole_lines:
        for d, packet in enumerate(mixes):
            here, lanes = packet_place(plan, place, d, packet.shape[1])
            piece = packet[plan.each * plan.block_lines :, :].astype(F32)
            for g in range(mixtures):
                misfit[g, here, lanes] = piece[g * plan.block_lines : (g + 1) * plan.block_lines]
    else:
        misfit[...] = mixes[0][...].astype(F32)
    for s in range(plan.shots):
        lag = lags[s]
        before = jnp.zeros((plan.lines, SLAB), F32)
        for t in range(plan.slabs):
            lanes = slice(t * SLAB, (t + 1) * SLAB)
            turned = pltpu.roll(now[s * plan.lines : (s + 1) * plan.lines, lanes], lag, 1)
            fired[s, :, lanes] = jnp.where(lane < lag, before, turned)
            before = turned
    for g in range(mixtures):
        value = fired[order[g * per]]
        for k in range(1, per):
            value = value + fired[order[g * per + k]]
        misfit[g] = value - misfit[g]
    for s in range(plan.shots):
        lag = lags[s]
        spot = jnp.int32(0)
        for k in range(plan.shots):
            spot = spot + jnp.where(order[k] == s, k, 0)
        which = spot // per
        back = (DMAX - lag) % DMAX
        after = jnp.zeros((plan.lines, SLAB), F32)
        rows = slice(s * plan.lines, (s + 1) * plan.lines)
        for t in range(plan.slabs - 1, -1, -1):
            lanes = slice(t * SLAB, (t + 1) * SLAB)
            turned = pltpu.roll(misfit[which, :, lanes], back, 1)
            pulled = jnp.where(lane < DMAX - lag, turned, after)
            after = turned
            now[rows, lanes] = (now[rows, lanes] - pace * pulled).astype(BF).astype(F32)


def stage_kernel(plan, station_round, with_shot, has_edges, stride, split_in, split_out, *refs):
    refs = list(refs)
    take = lambda n: [refs.pop(0) for _ in range(n)]
    tallies, lags, order, paces = take(4)
    place = places(plan, stride)
    sources = take({"parts": plan.each, "packets": plan.packets}.get(split_in, 1))
    source = sources[0]
    station = station_round is not None
    if station:
        (energies,) = take(1)
        mixes = take(plan.packets)
        station_weights = take(2)
    edges = None
    if with_shot:
        if has_edges:
            (edges,) = take(1)
        shot_weights = take(2)
    results = take(plan.each if split_out == "parts" else 1)
    result = results[0]
    if with_shot and split_out != "parts":
        (energy,) = take(1)
    now, packed, hidden, total, ends = take(5)
    scratch = (packed, hidden, total, ends)
    length = plan.slabs * SLAB
    if split_in == "parts":
        for d, part in enumerate(sources):
            at = pl.multiple_of((place[3] ^ d) * plan.lines, plan.lines)
            now[pl.ds(at, plan.lines), :] = part[:, 0:length].astype(F32)
    elif split_in:
        lines = plan.block_lines
        for d, packet in enumerate(sources):
            here, lanes = packet_place(plan, place, d, packet.shape[1])
            piece = packet[0 : plan.each * lines, :].astype(F32)
            for k in range(plan.each):
                now[pl.ds(k * plan.lines + here.start, lines), lanes] = piece[k * lines : (k + 1) * lines]
    else:
        now[...] = source[...].astype(F32)
    if station:
        station_stage(
            plan,
            place,
            tallies,
            lags,
            order,
            paces[station_round],
            energies,
            mixes,
            station_weights,
            now,
            scratch,
            refs,
        )
    if with_shot:
        sums = shot_stage(plan, place, tallies, stride, edges, shot_weights, now, scratch)
    if split_out == "parts":
        row = lax.broadcasted_iota(jnp.int32, (plan.lines, SLAB), 0)
        beside = jnp.zeros((plan.lines, SLAB), F32)
        for i, part in enumerate(split_bias(sums)):
            beside = jnp.where(row == i, part, beside)
        for d, part in enumerate(results):
            at = pl.multiple_of((place[3] ^ d) * plan.lines, plan.lines)
            part[:, 0:length] = now[pl.ds(at, plan.lines), :].astype(BF)
            part[:, length:] = beside.astype(BF)
        return
    if with_shot:
        energy[...] = sums
    if split_out:
        for n, (row, lane, rows, lanes) in enumerate(plan.pieces):
            result[n] = now[row : row + rows, lane : lane + lanes].astype(BF)
    else:
        result[...] = now[...].astype(BF)


SMEM = pl.BlockSpec(memory_space=pltpu.SMEM)
VMEM = pl.BlockSpec(memory_space=pltpu.VMEM)
HBM = pl.BlockSpec(memory_space=pltpu.HBM)


def run_stage(plan, small, source, station=None, shot=None, split_in=False, split_out=False, stride=0, name="stage"):
    operands = [*small, *(source if split_in else [source])]
    station_round, has_edges = None, False
    macs = 0
    pass_macs = plan.rows * plan.slabs * QS * WIDE * (WIDE * 3 + SLAB)
    if station is not None:
        station_round, energies, mixes, weights = station
        operands += [energies, *mixes, *weights]
        macs += pass_macs
    if shot is not None:
        edges, weights = shot
        has_edges = edges is not None
        operands += ([edges] if has_edges else []) + list(weights)
        macs += pass_macs
    specs = [SMEM] * len(small) + [VMEM] * (len(operands) - len(small))
    length = plan.slabs * SLAB
    if split_out == "parts":
        shapes = [jax.ShapeDtypeStruct((plan.lines, length + SLAB), BF)] * plan.each
    elif split_out:
        _, _, rows, lanes = plan.pieces[0]
        shapes = [jax.ShapeDtypeStruct((len(plan.pieces), rows, lanes), BF)]
    else:
        shapes = [jax.ShapeDtypeStruct((plan.rows, length), BF)]
    if shot is not None and split_out != "parts":
        shapes.append(jax.ShapeDtypeStruct((1, SLAB), F32))
    scratch = [
        pltpu.VMEM((plan.rows, length), F32),
        pltpu.VMEM((2, plan.slabs, plan.rows, WIDE), BF),
        pltpu.VMEM((QS * (plan.slabs + 2), plan.rows, WIDE), BF),
        pltpu.VMEM((plan.slabs, plan.rows, SLAB), F32),
        pltpu.VMEM((2, plan.slabs * plan.rows, WIDE), BF),
    ]
    if station is not None:
        scratch += [
            pltpu.VMEM((plan.shots, plan.lines, length), F32),
            pltpu.VMEM((plan.mixtures, plan.lines, length), F32),
            pltpu.VMEM((plan.rows, SLAB), F32),
        ]
    return pl.pallas_call(
        functools.partial(
            stage_kernel, plan, station_round, shot is not None, has_edges, stride, split_in, split_out
        ),
        out_shape=shapes,
        in_specs=specs,
        out_specs=[VMEM] * len(shapes),
        scratch_shapes=scratch,
        compiler_params=pltpu.CompilerParams(vmem_limit_bytes=VMEM_LIMIT),
        cost_estimate=pl.CostEstimate(flops=2 * macs, bytes_accessed=1 << 20, transcendentals=0),
        name=name,
    )(*operands)


def bundled(entry, spaced, leave):
    rows = [spaced.reshape(3 * FEAT, FEAT), jnp.pad(leave, ((0, 12), (0, 0)))]
    rows.append(jnp.pad(entry.transpose(1, 0, 2), ((0, 0), (0, 12), (0, 0))).reshape(48, FEAT))
    return jnp.concatenate(rows, axis=0)


def run_prepare(bundle, bias, name):
    return pl.pallas_call(
        prepare_kernel,
        out_shape=[
            jax.ShapeDtypeStruct((QH + 2, WIDE, WIDE), BF),
            jax.ShapeDtypeStruct((QS + 2, WIDE, SLAB), BF),
        ],
        in_specs=[VMEM] * 2,
        out_specs=[VMEM] * 2,
        scratch_shapes=[pltpu.VMEM((SLAB, WIDE), F32), pltpu.VMEM((SLAB, WIDE), F32)],
        compiler_params=pltpu.CompilerParams(vmem_limit_bytes=VMEM_LIMIT),
        cost_estimate=pl.CostEstimate(flops=2 * 8192 * WIDE * SLAB, bytes_accessed=4 << 20, transcendentals=0),
        name=name,
    )(bundle, bias)


def run_pack(plan, traces, mixtures):
    groups, block, _ = mixtures.shape
    width = traces.shape[1]
    return pl.pallas_call(
        functools.partial(pack_kernel, plan),
        out_shape=[jax.ShapeDtypeStruct(((plan.each + groups) * plan.block_lines, width), BF)] * plan.packets,
        in_specs=[HBM, HBM],
        out_specs=[VMEM] * plan.packets,
        scratch_shapes=[
            pltpu.VMEM((block, width), BF),
            pltpu.VMEM((groups * block, width), BF),
            pltpu.SemaphoreType.DMA((groups + 1,)),
        ],
        compiler_params=pltpu.CompilerParams(vmem_limit_bytes=VMEM_FULL),
        cost_estimate=pl.CostEstimate(flops=2 * block * block * width, bytes_accessed=1 << 20, transcendentals=0),
        name="pack",
    )(traces, mixtures)


class Plan:
    def __init__(self, **sizes):
        self.__dict__.update(sizes)
        self.rows = self.shots * self.lines


def exchanged(parts, axes):
    size = len(parts)
    return [parts[0]] + [lax.ppermute(parts[d], axes, [(i, i ^ d) for i in range(size)]) for d in range(1, size)]


def per_device(
    initial_guess,
    measured_mixtures,
    launch_lags,
    source_launch_order,
    station_portion_tallies,
    source_entry_kernel,
    source_spaced_kernel,
    source_exit_kernel,
    source_inner_offsets,
    station_entry_kernel,
    station_spaced_kernel,
    station_exit_kernel,
    station_inner_offsets,
    learned_pace_factors,
):
    shots_here, block, window = initial_guess.shape
    n_shot, n_line, n_tm = (lax.axis_size(a) for a in ("shot", "line", "tm"))
    at_shot, at_tm = lax.axis_index("shot"), lax.axis_index("tm")
    block_lines = block // RPL
    length = window * n_tm
    shots = shots_here * n_shot
    sections = station_portion_tallies.shape[0]
    mixtures = measured_mixtures.shape[0]
    whole_lines = n_shot * n_line * n_tm == RPL
    assert shots_here == 1 and (whole_lines or n_shot == RPL)
    if whole_lines:
        axes = ("line", "tm", "shot")
        lines, blocks = block_lines * n_line, n_line
    else:
        axes = ("shot", "tm")
        lines = block_lines // n_tm
        blocks = 1
    turns = [(s, a, b) for a in range(blocks) for b in range(n_tm) for s in range(n_shot)]
    plan = Plan(
        whole_lines=whole_lines,
        shots=shots,
        lines=lines,
        block_lines=block_lines,
        blocks=blocks,
        sections=sections,
        mixtures=mixtures,
        slabs=length // SLAB,
        each=n_shot,
        time_parts=n_tm,
        packets=n_line * n_tm if whole_lines else 1,
        pieces=[(s * lines + a * block_lines, b * window, block_lines, window) for s, a, b in turns],
    )

    if whole_lines:
        assert n_tm == 2 and n_line & (n_line - 1) == 0 and n_shot & (n_shot - 1) == 0
        arrived = run_pack(plan, initial_guess.reshape(block, window), measured_mixtures)
        arrived = exchanged(arrived, ("line", "tm"))
    else:
        grid = initial_guess.reshape(n_tm, lines, RPL, window)
        leaving = grid.transpose(2, 0, 1, 3).reshape(RPL * n_tm, lines, window)
        arrived = lax.all_to_all(leaving, axes, split_axis=0, concat_axis=0, tiled=True)

    shot_bundle = bundled(source_entry_kernel, source_spaced_kernel, source_exit_kernel)
    station_net = (station_entry_kernel, station_spaced_kernel, station_exit_kernel)
    shot_weights = run_prepare(shot_bundle, source_inner_offsets, "prepare_shot")
    small = (station_portion_tallies, launch_lags, source_launch_order, learned_pace_factors)
    split = whole_lines and block_lines % 8 == 0
    assert split or not whole_lines
    if whole_lines:
        mixes = source = arrived
    else:
        grid = measured_mixtures.reshape(mixtures, n_tm, lines, RPL, length)
        mixes = lax.dynamic_slice(grid, (0, at_tm, 0, at_shot, 0), (mixtures, 1, lines, 1, length))
        mixes = [mixes.reshape(mixtures, lines, length)]
        source = arrived.reshape(n_shot, n_tm, lines, window).transpose(0, 2, 1, 3).reshape(plan.rows, length)

    def edges_of(current):
        if whole_lines:
            return None
        size = n_line * n_tm
        grid = current.reshape(shots, lines, length)
        up = [(i, i + 1) for i in range(size - 1)]
        down = [(j, i) for i, j in up]
        above = lax.ppermute(grid[:, -1], ("line", "tm"), up)
        below = lax.ppermute(grid[:, 0], ("line", "tm"), down)
        wide = jnp.broadcast_to(jnp.stack([above, below])[:, :, None, :], (2, shots, lines, length))
        return wide.reshape(2, plan.rows, length)

    def summed(value, axis):
        size = lax.axis_size(axis)
        if size <= 4:
            others = [lax.ppermute(value, axis, [(i, i ^ d) for i in range(size)]) for d in range(1, size)]
            return sum(others, value)
        step = 1
        while step < size:
            value = value + lax.ppermute(value, axis, [(i, i ^ step) for i in range(size)])
            step *= 2
        return value

    def shared(energy, along):
        for axis in along:
            energy = summed(energy, axis)
        return energy

    if whole_lines:
        parts = run_stage(
            plan,
            small,
            source,
            shot=(None, shot_weights),
            split_in="packets",
            split_out="parts",
            stride=1,
            name="shot_pass",
        )
        station_net, own = lax.optimization_barrier((station_net, parts[0]))
        current = exchanged([own, *parts[1:]], "shot")
        bundle = bundled(*station_net)
        station_weights = run_prepare(bundle, station_inner_offsets, "prepare_station")
        energy = sum(jnp.sum(p[0:3, length:].astype(F32), axis=0, keepdims=True) for p in current)
        station_weights, energy = lax.optimization_barrier((station_weights, energy))
        energy = summed(energy, ("line", "tm"))
    else:
        current, energy = run_stage(
            plan, small, source, shot=(edges_of(source), shot_weights), name="shot_pass"
        )
        energy = shared(energy, ("tm", "shot"))
        station_weights = run_prepare(bundled(*station_net), station_inner_offsets, "prepare_station")
    for i in range(ITERS):
        station = (i, energy, mixes, station_weights)
        form = "parts" if whole_lines and i == 0 else False
        if i == ITERS - 1:
            (current,) = run_stage(
                plan, small, current, station=station, split_in=form, split_out=split, name="station_pass"
            )
        elif whole_lines:
            current, energy = run_stage(
                plan,
                small,
                current,
                station=station,
                shot=(None, shot_weights),
                split_in=form,
                name="station_and_shot_pass",
            )
            fresh, energy = lax.optimization_barrier((bundle, energy))
            station_weights = run_prepare(fresh, station_inner_offsets, "prepare_station")
            energy = summed(summed(energy, ("line", "tm")), "shot")
        else:
            (current,) = run_stage(plan, small, current, station=station, name="station_pass")
            current, energy = run_stage(plan, small, current, shot=(edges_of(current), shot_weights), name="shot_pass")
            energy = shared(energy, ("tm", "shot"))
    if not split:
        current = current.reshape(n_shot, lines, n_tm, window).transpose(0, 2, 1, 3).reshape(-1, lines, window)
    back = lax.all_to_all(current, axes, split_axis=0, concat_axis=0, tiled=True)
    if whole_lines:
        back = back.transpose(1, 0, 2)
    else:
        back = back.reshape(RPL, n_tm, lines, window).transpose(1, 2, 0, 3)
    return back.reshape(shots_here, block, window)


def solution(mesh):
    placed = (P(("group", "shot"), "line", "tm"), P("group", "line", None), P("group"), P("group"), P("group"))
    return jax.shard_map(
        per_device,
        mesh=mesh,
        in_specs=placed + (P(),) * 9,
        out_specs=P(("group", "shot"), "line", "tm"),
        check_vma=False,
    )
```

```python
import functools

import jax
import jax.numpy as jnp
from jax import lax
from jax.experimental import pallas as pl
from jax.experimental.pallas import tpu as pltpu
from jax.sharding import PartitionSpec as P

RPL = 16
DMAX = 128
ITERS = 2
EPSILON = 1e-05

SLAB = 128
HALF = 64
FEAT = 64
GROUP = 4
WIDE = GROUP * FEAT
QS = SLAB // (2 * GROUP)
QH = QS // 2
assert QH == 8
ONES = 3 * HALF + 6
VMEM_LIMIT = 24 * 1024 * 1024
VMEM_FULL = 63 * 1024 * 1024

BF = jnp.bfloat16
F32 = jnp.float32


def split_bias(bias):
    high = bias.astype(BF).astype(F32)
    middle = (bias - high).astype(BF).astype(F32)
    return high, middle, bias - high - middle


def iota(shape, axis):
    return lax.broadcasted_iota(jnp.int32, shape, axis)


def picks(mask):
    return mask.astype(F32).astype(BF)


def start_of(q):
    return 16 * (q // 2) + 2 * (q % 2)


def prepare_kernel(bundle, bias, o_in, o_out, rhs, cols):
    rhs[...] = jnp.zeros_like(rhs)
    cols[...] = jnp.zeros_like(cols)
    parts = split_bias(bias[0:1, :])
    exits = bundle[3 * FEAT : 3 * FEAT + 16, :].astype(F32)[0:4]
    for p in range(GROUP):
        lanes = slice(p * FEAT, (p + 1) * FEAT)
        for c in range(3):
            row = 3 * FEAT + 16 * (c + 1)
            rhs[p * 32 + c * 8 : p * 32 + c * 8 + 4, lanes] = bundle[row : row + 16, :].astype(F32)[0:4]
            rhs[p * 32 + 24 + c : p * 32 + 25 + c, lanes] = parts[c]
        cols[p * 8 : p * 8 + 4, lanes] = exits
    taps = rhs[...].astype(BF)
    row, col = iota((WIDE, SLAB), 0), iota((WIDE, SLAB), 1)
    channel, j, target = (col >> 3) & 3, col & 7, 4 * (col >> 5) + (col & 7) - 1
    rest = row - 3 * HALF
    sample = jnp.where(rest < 0, row & (HALF - 1), jnp.where(rest & 1 == 1, HALF, -1))
    same = (jnp.where(rest < 0, row >> 6, rest >> 1) == channel) & (channel < 3) & (j < 4)
    offset = jnp.where(same, sample - target, -SLAB)
    ones = (channel == 3) & (j < 3) & (row == ONES + j)
    for q in range(QH):
        chosen = picks((offset == start_of(q)) | ones)
        o_in[q] = jnp.dot(chosen, taps, preferred_element_type=F32).astype(BF)
    o_in[QH:] = jnp.zeros((2, WIDE, WIDE), BF)
    for a, at in [(0, 0), (1, 1), (2, 2), (3, 3), (4, 4), (-1, 5)]:
        for b in range(GROUP):
            if abs(a - b) <= 1:
                tap = a - b + 1
                rows, lanes = slice(at % 4 * FEAT, (at % 4 + 1) * FEAT), slice(b * FEAT, (b + 1) * FEAT)
                o_in[QH + at // 4, rows, lanes] = bundle[tap * FEAT : (tap + 1) * FEAT, :]
    row = iota((16, FEAT), 0)
    below = jnp.zeros((16, FEAT), F32)
    for i, part in enumerate(split_bias(bias[1:2, :])):
        below = jnp.where(row == i, part, below)
    for b in range(GROUP):
        o_in[QH + 1, SLAB : SLAB + 16, b * FEAT : (b + 1) * FEAT] = below.astype(BF)
    row, col = iota((SLAB, SLAB), 0), iota((SLAB, SLAB), 1)
    p, j = row >> 3, row & 7
    offset = jnp.where((p < GROUP) & (j < 4), col - (4 * p + j - 1), -SLAB)
    back = jnp.transpose(cols[...]).astype(BF)
    follows = (p == GROUP - 1) & (j == 3) & (col == 0)
    precedes = (row == 0) & (col == SLAB - 1)
    for q in range(QS + 2):
        chosen = picks(offset == start_of(q) if q < QS else [follows, precedes][q - QS])
        o_out[q] = jnp.dot(back, chosen, preferred_element_type=F32).astype(BF)


def pack_kernel(plan, traces, *refs):
    outs, held, done = refs[:4], refs[4], refs[5]
    _, _, at_tm, _, at_line = places(plan, True)
    block = traces.shape[0]
    copy = pltpu.make_async_copy(traces, held, done)
    copy.start()
    lines = plan.lines
    half = block // 2
    row, col = iota((block, block), 0), iota((block, block), 1)
    spot, line = split_index(row, lines)
    d, spot = split_index(spot, half // lines)
    order = picks(col == line * RPL + (at_tm ^ d) * (half // lines) + spot)
    row, col = iota((32, block), 0), iota((32, block), 1)
    d, spot = split_index(row, 16)
    sent = jnp.where(at_line == 0, lines - 1, 0)
    outer = picks((col == sent * RPL + (at_tm ^ d) * (half // lines) + spot) & (spot < half // lines))
    copy.wait()
    moved = jnp.dot(order, held[...], preferred_element_type=F32).astype(BF)
    edge = jnp.dot(outer, held[...], preferred_element_type=F32).astype(BF)
    outs[0][...] = moved[:half]
    outs[1][...] = moved[half:]
    outs[2][...] = edge[:16]
    outs[3][...] = edge[16:]


def places(plan, first):
    at_shot, at_line, at_tm = (lax.axis_index(a) for a in ("shot", "line", "tm"))
    if not plan.paired:
        return at_shot, at_tm * plan.lines, at_tm, at_shot, at_line
    return at_tm * (RPL // 2) + (0 if first else at_shot * plan.per), 0, at_tm, at_shot, at_line


def split_index(value, size):
    if size & (size - 1):
        return value // size, value % size
    return value >> (size.bit_length() - 1), value & (size - 1)


def section_map(plan, place, tallies, first):
    shape = (plan.rows, SLAB)
    lane = lax.broadcasted_iota(jnp.int32, shape, 1)
    apart, line = split_index(iota(shape, 0), plan.lines)
    if not first:
        apart = split_index(apart, plan.per)[1]
    spot = (line + place[1]) * RPL + place[0] + apart
    low = jnp.zeros(shape, jnp.int32)
    high = jnp.zeros(shape, jnp.int32)
    count = jnp.zeros(shape, jnp.int32)
    start = jnp.int32(0)
    for p in range(plan.sections):
        amount = tallies[p]
        here = lane == p
        low = jnp.where(here, start, low)
        high = jnp.where(here, start + amount, high)
        count = jnp.where(here, amount, count)
        start = start + amount
    member = (spot >= low) & (spot < high)
    return member, count


def shifted(values, by, ok, edge):
    return jnp.where(ok, pltpu.roll(values, by % values.shape[0], 0), edge)


def pack_inputs(plan, channels, packed):
    lane = lax.broadcasted_iota(jnp.int32, (plan.rows, SLAB), 1)
    low = lane < HALF
    ones = ((lane >= ONES - SLAB) & (lane < ONES - SLAB + 3)).astype(F32)
    slabs = [[x[:, t * SLAB : (t + 1) * SLAB] for t in range(plan.slabs)] for x in channels]
    far = [[pltpu.roll(s, HALF + 1 + 2 * c, 1) for s in slabs[c]] for c in range(3)]
    for t in range(plan.slabs):
        v = [slabs[c][t] for c in range(3)]
        w = [pltpu.roll(s, HALF, 1) for s in v]
        even = jnp.where(low, v[2], ones)
        odd = jnp.where(low, w[2], ones)
        for c in range(3):
            left, right = lane == HALF + 2 * c, lane == HALF + 2 * c + 1
            near = pltpu.roll(v[c], 1 + 2 * c, 1)
            even = jnp.where(right, near, even)
            odd = jnp.where(left, near, odd)
            if t > 0:
                even = jnp.where(left, far[c][t - 1], even)
            if t < plan.slabs - 1:
                odd = jnp.where(right, far[c][t + 1], odd)
        packed[0, t, :, 0:SLAB] = jnp.where(low, v[0], w[1]).astype(BF)
        packed[0, t, :, SLAB:WIDE] = even.astype(BF)
        packed[1, t, :, 0:SLAB] = jnp.where(low, w[0], v[1]).astype(BF)
        packed[1, t, :, SLAB:WIDE] = odd.astype(BF)


def network(plan, weights, scratch, regions):
    w_in, w_out = weights
    packed, hidden, total, ends = scratch
    slabs, rows = plan.slabs, plan.rows
    many = slabs * rows
    pitch = slabs + 2

    def first(q):
        taps = jnp.concatenate([w_in[q], w_in[q + 1]], axis=1)
        value = jnp.dot(packed[...].reshape(2 * many, WIDE), taps, preferred_element_type=F32)
        value = jnp.maximum(value.astype(BF), 0).reshape(2, slabs, rows, 2 * WIDE)
        for h in range(2):
            for k in range(2):
                at = pl.ds((q + k + h * QH) * pitch + 1, slabs)
                hidden[at] = value[h, :, :, k * WIDE : (k + 1) * WIDE]

    lane = iota((slabs, rows, SLAB), 2)
    ones = picks(lane < 3)

    def window(q):
        if isinstance(q, int):
            left_at = (q - 2) * pitch + 1 if q >= 2 else (q + QS - 2) * pitch
            right_at = (q + 2) * pitch + 1 if q < QS - 2 else (q + 2 - QS) * pitch + 2
        else:
            left_at = jnp.where(q >= 2, (q - 2) * pitch + 1, (q + QS - 2) * pitch)
            right_at = jnp.where(q < QS - 2, (q + 2) * pitch + 1, (q + 2 - QS) * pitch + 2)
        middle = hidden[pl.ds(q * pitch + 1, slabs)]
        left = hidden[pl.ds(left_at, slabs), :, SLAB:WIDE]
        right = hidden[pl.ds(right_at, slabs), :, 0:SLAB]
        beside = jnp.where(lane < FEAT, right, left)
        return jnp.concatenate([middle, beside, ones], axis=2).reshape(many, 2 * WIDE)

    def second(q):
        both = jnp.concatenate([window(q), window(q + 1)], axis=0)
        value = jnp.dot(both, w_in[QH:].reshape(2 * WIDE, WIDE), preferred_element_type=F32)
        value = jnp.maximum(value.astype(BF), 0)
        return value[:many], value[many:]

    def onto(layer, taps):
        return jnp.dot(layer, taps, preferred_element_type=F32).reshape(slabs, rows, SLAB)

    edge = jnp.zeros((rows, WIDE), BF)
    for k in range(2):
        hidden[(QS - 2 + k) * pitch] = edge
        hidden[(k + 1) * pitch - 1] = edge
    total[...] = jnp.zeros_like(total)

    @regions
    def _():
        for q in range(0, QH, 2):
            first(q)

    @regions
    def _():
        for q in range(0, QS, 2):
            one, two = second(q)
            total[...] += onto(jnp.concatenate([one, two], axis=1), w_out[q : q + 2].reshape(2 * WIDE, SLAB))
            if q == 0:
                ends[0] = one
            if q == QS - 2:
                ends[1] = two

    total[0 : slabs - 1] += onto(ends[0], w_out[QS + 1])[1:]
    total[1:slabs] += onto(ends[1], w_out[QS])[: slabs - 1]


def add_total(plan, now, total, scale=None):
    for t in range(plan.slabs):
        lanes = slice(t * SLAB, (t + 1) * SLAB)
        more = total[t] if scale is None else scale * total[t]
        now[:, lanes] = (now[:, lanes] + more).astype(BF).astype(F32)


def shot_stage(plan, place, tallies, first, edges, weights, now, scratch):
    apart = pl.when(place[0] >= 0)

    @apart
    def _():
        x = now[...]
        line = split_index(iota(x.shape, 0), plan.lines)[1]
        if plan.paired:
            wide = [jnp.broadcast_to(edges[g : g + 1, :], (plan.lines, x.shape[1])) for g in range(plan.groups)]
            wide = jnp.concatenate(wide, axis=0)
            above = jnp.where(place[4] == 1, wide, 0.0)
            below = jnp.where(place[4] == 1, 0.0, wide)
        else:
            above, below = edges[0].astype(F32), edges[1].astype(F32)
        channels = [
            shifted(x, 1, line > 0, above),
            x,
            shifted(x, -1, line < plan.lines - 1, below),
        ]
        pack_inputs(plan, channels, scratch[0])

    network(plan, weights, scratch, apart)
    add_total(plan, now, scratch[2])
    power = jnp.zeros((plan.rows, SLAB), F32)
    for t in range(plan.slabs):
        piece = now[:, t * SLAB : (t + 1) * SLAB]
        power = power + piece * piece
    member, _ = section_map(plan, place, tallies, first)
    each = jnp.where(member, jnp.sum(power, axis=1, keepdims=True), 0.0)
    return jnp.sum(each, axis=0, keepdims=True)


def station_stage(
    plan, place, tallies, lags, order, pace, energies, mixes, fetches, weights, now, scratch, blend
):
    fired, misfit, scale = blend
    apart = pl.when(place[0] >= 0)

    @apart
    def _():
        member, count = section_map(plan, place, tallies, False)
        denominator = jnp.maximum(count, 1) * (plan.shots * plan.slabs * SLAB)
        level = jnp.sqrt(energies[...] / denominator.astype(F32) + EPSILON)
        rms = jnp.sum(jnp.where(member, level, 0.0), axis=1, keepdims=True)
        scale[...] = jnp.broadcast_to(rms, scale.shape)
        x = (now[...] / rms).astype(BF).astype(F32)
        row = iota(x.shape, 0)
        channels = [
            shifted(x, plan.span, row >= plan.span, 0.0),
            x,
            shifted(x, -plan.span, row < plan.rows - plan.span, 0.0),
        ]
        pack_inputs(plan, channels, scratch[0])

    network(plan, weights, scratch, apart)
    add_total(plan, now, scratch[2], scale[...])
    lane = lax.broadcasted_iota(jnp.int32, (plan.span, SLAB), 1)
    mixtures = misfit.shape[0]
    per = plan.shots // mixtures
    if plan.paired:
        row, col = iota((plan.span, mixes.shape[1]), 0), iota((plan.span, mixes.shape[1]), 1)
        spot, line = split_index(row, plan.lines)
        choose = picks(col == line * RPL + place[0] + spot)
        for g in range(mixtures):
            fetches[g].wait()
            misfit[g] = jnp.dot(choose, mixes[g], preferred_element_type=F32)
    else:
        misfit[...] = mixes[...].astype(F32)
    for s in range(plan.shots):
        lag = lags[s]
        before = jnp.zeros((plan.span, SLAB), F32)
        for t in range(plan.slabs):
            lanes = slice(t * SLAB, (t + 1) * SLAB)
            turned = pltpu.roll(now[s * plan.span : (s + 1) * plan.span, lanes], lag, 1)
            fired[s, :, lanes] = jnp.where(lane < lag, before, turned)
            before = turned
    for g in range(mixtures):
        value = fired[order[g * per]]
        for k in range(1, per):
            value = value + fired[order[g * per + k]]
        misfit[g] = value - misfit[g]
    for s in range(plan.shots):
        lag = lags[s]
        spot = jnp.int32(0)
        for k in range(plan.shots):
            spot = spot + jnp.where(order[k] == s, k, 0)
        which = spot // per
        back = (DMAX - lag) % DMAX
        after = jnp.zeros((plan.span, SLAB), F32)
        rows = slice(s * plan.span, (s + 1) * plan.span)
        for t in range(plan.slabs - 1, -1, -1):
            lanes = slice(t * SLAB, (t + 1) * SLAB)
            turned = pltpu.roll(misfit[which, :, lanes], back, 1)
            pulled = jnp.where(lane < DMAX - lag, turned, after)
            after = turned
            now[rows, lanes] = (now[rows, lanes] - pace * pulled).astype(BF).astype(F32)


def stage_kernel(plan, station_round, with_shot, first, split_in, split_out, *refs):
    refs = list(refs)
    take = lambda n: [refs.pop(0) for _ in range(n)]
    tallies, lags, order, paces = take(4)
    place = places(plan, first)
    sources = take(4 if split_in else 1)
    station = station_round is not None
    if station:
        energies, mixes = take(2)
        station_weights = take(2)
    if with_shot:
        edges = take(0 if first else 1)
        shot_weights = take(2)
    results = take({"parts": plan.each, "edge": 2}.get(split_out, 1))
    if with_shot and split_out != "parts":
        (energy,) = take(1)
    now, packed, hidden, total, ends, rim = take(6)
    scratch = (packed, hidden, total, ends)
    length = plan.slabs * SLAB
    fetches = []
    if station and plan.paired:
        done, held = refs.pop(), refs.pop()
        fetches = [pltpu.make_async_copy(mixes.at[g], held.at[g], done.at[g]) for g in range(plan.mixtures)]
        for fetch in fetches:
            fetch.start()
        mixes = held
    if split_in == "parts":
        for d, part in enumerate(sources):
            at = pl.multiple_of((place[3] ^ d) * plan.span, plan.span)
            now[pl.ds(at, plan.span), :] = part[:, 0:length].astype(F32)
    elif split_in:
        share = length // plan.time_parts
        for d in range(2):
            lanes = pl.ds(pl.multiple_of((place[2] ^ d) * share, share), share)
            now[:, lanes] = sources[d][...].astype(F32)
            rim[:, lanes] = sources[2 + d][...].astype(F32)
    else:
        now[...] = sources[0][...].astype(F32)
    if station:
        station_stage(
            plan,
            place,
            tallies,
            lags,
            order,
            paces[station_round],
            energies,
            mixes,
            fetches,
            station_weights,
            now,
            scratch,
            refs,
        )
    if with_shot:
        if plan.paired and not first:
            rim[...] = edges[0][...].astype(F32)
        outer = rim if plan.paired else edges[0]
        sums = shot_stage(plan, place, tallies, first, outer, shot_weights, now, scratch)
    if split_out == "parts":
        row = iota((plan.span, SLAB), 0)
        beside = jnp.zeros((plan.span, SLAB), F32)
        for i, part in enumerate(split_bias(sums)):
            beside = jnp.where(row == i, part, beside)
        for d, part in enumerate(results):
            at = pl.multiple_of((place[3] ^ d) * plan.span, plan.span)
            part[:, 0:length] = now[pl.ds(at, plan.span), :].astype(BF)
            part[:, length:] = beside.astype(BF)
        return
    if with_shot:
        energy[...] = sums
    if split_out == "final":
        share = length // plan.time_parts
        for n in range(results[0].shape[0]):
            b, k = divmod(n, plan.each)
            results[0][n] = now[k * plan.span : (k + 1) * plan.span, b * share : (b + 1) * share].astype(BF)
        return
    results[0][...] = now[...].astype(BF)
    if split_out == "edge":
        row, col = iota((16, plan.rows), 0), iota((16, plan.rows), 1)
        sent = jnp.where(place[4] == 0, plan.lines - 1, 0)
        choose = picks(col == row * plan.lines + sent)
        results[1][...] = jnp.dot(choose, now[...].astype(BF), preferred_element_type=F32).astype(BF)


SMEM = pl.BlockSpec(memory_space=pltpu.SMEM)
VMEM = pl.BlockSpec(memory_space=pltpu.VMEM)
HBM = pl.BlockSpec(memory_space=pltpu.HBM)


def run_stage(plan, small, source, station=None, shot=None, first=False, split_in=None, split_out=None, name="stage"):
    operands = [*small, *source]
    specs = [SMEM] * len(small) + [VMEM] * len(source)
    station_round = None
    macs = 0
    pass_macs = plan.rows * plan.slabs * QS * WIDE * (WIDE * 3 + SLAB)
    if station is not None:
        station_round, energies, mixes, weights = station
        operands += [energies, mixes, *weights]
        specs += [VMEM, HBM if plan.paired else VMEM, VMEM, VMEM]
        macs += pass_macs
    if shot is not None:
        edges, weights = shot
        operands += [*edges, *weights]
        specs += [VMEM] * (len(edges) + 2)
        macs += pass_macs
    length = plan.slabs * SLAB
    if split_out == "parts":
        shapes = [jax.ShapeDtypeStruct((plan.span, length + SLAB), BF)] * plan.each
    elif split_out == "final":
        shapes = [jax.ShapeDtypeStruct((plan.each * plan.time_parts, plan.span, length // plan.time_parts), BF)]
    else:
        shapes = [jax.ShapeDtypeStruct((plan.rows, length), BF)]
        if split_out == "edge":
            shapes.append(jax.ShapeDtypeStruct((16, length), BF))
    if shot is not None and split_out != "parts":
        shapes.append(jax.ShapeDtypeStruct((1, SLAB), F32))
    scratch = [
        pltpu.VMEM((plan.rows, length), F32),
        pltpu.VMEM((2, plan.slabs, plan.rows, WIDE), BF),
        pltpu.VMEM((QS * (plan.slabs + 2), plan.rows, WIDE), BF),
        pltpu.VMEM((plan.slabs, plan.rows, SLAB), F32),
        pltpu.VMEM((2, plan.slabs * plan.rows, WIDE), BF),
        pltpu.VMEM((16, length), F32),
    ]
    if station is not None:
        scratch += [
            pltpu.VMEM((plan.shots, plan.span, length), F32),
            pltpu.VMEM((plan.mixtures, plan.span, length), F32),
            pltpu.VMEM((plan.rows, SLAB), F32),
        ]
        if plan.paired:
            scratch += [pltpu.VMEM(mixes.shape, BF), pltpu.SemaphoreType.DMA((plan.mixtures,))]
    return pl.pallas_call(
        functools.partial(stage_kernel, plan, station_round, shot is not None, first, split_in, split_out),
        out_shape=shapes,
        in_specs=specs,
        out_specs=[VMEM] * len(shapes),
        scratch_shapes=scratch,
        compiler_params=pltpu.CompilerParams(vmem_limit_bytes=VMEM_LIMIT),
        cost_estimate=pl.CostEstimate(flops=2 * macs, bytes_accessed=1 << 20, transcendentals=0),
        name=name,
    )(*operands)


def bundled(entry, spaced, leave):
    rows = [spaced.reshape(3 * FEAT, FEAT), jnp.pad(leave, ((0, 12), (0, 0)))]
    rows.append(jnp.pad(entry.transpose(1, 0, 2), ((0, 0), (0, 12), (0, 0))).reshape(48, FEAT))
    return jnp.concatenate(rows, axis=0)


def run_prepare(bundle, bias, name):
    return pl.pallas_call(
        prepare_kernel,
        out_shape=[
            jax.ShapeDtypeStruct((QH + 2, WIDE, WIDE), BF),
            jax.ShapeDtypeStruct((QS + 2, WIDE, SLAB), BF),
        ],
        in_specs=[VMEM] * 2,
        out_specs=[VMEM] * 2,
        scratch_shapes=[pltpu.VMEM((SLAB, WIDE), F32), pltpu.VMEM((SLAB, WIDE), F32)],
        compiler_params=pltpu.CompilerParams(vmem_limit_bytes=VMEM_LIMIT),
        cost_estimate=pl.CostEstimate(flops=2 * 8192 * WIDE * SLAB, bytes_accessed=4 << 20, transcendentals=0),
        name=name,
    )(bundle, bias)


def run_pack(plan, traces):
    block, width = traces.shape
    return pl.pallas_call(
        functools.partial(pack_kernel, plan),
        out_shape=[jax.ShapeDtypeStruct((rows, width), BF) for rows in (block // 2, block // 2, 16, 16)],
        in_specs=[HBM],
        out_specs=[VMEM] * 4,
        scratch_shapes=[pltpu.VMEM((block, width), BF), pltpu.SemaphoreType.DMA],
        compiler_params=pltpu.CompilerParams(vmem_limit_bytes=VMEM_FULL),
        cost_estimate=pl.CostEstimate(flops=2 * block * block * width, bytes_accessed=1 << 20, transcendentals=0),
        name="pack",
    )(traces)


class Plan:
    def __init__(self, **sizes):
        self.__dict__.update(sizes)
        self.span = self.lines * self.per
        self.rows = self.shots * self.span
        self.groups = self.rows // self.lines


def exchanged(parts, axes):
    size = len(parts)
    return [parts[0]] + [lax.ppermute(parts[d], axes, [(i, i ^ d) for i in range(size)]) for d in range(1, size)]


def per_device(
    initial_guess,
    measured_mixtures,
    launch_lags,
    source_launch_order,
    station_portion_tallies,
    source_entry_kernel,
    source_spaced_kernel,
    source_exit_kernel,
    source_inner_offsets,
    station_entry_kernel,
    station_spaced_kernel,
    station_exit_kernel,
    station_inner_offsets,
    learned_pace_factors,
):
    shots_here, block, window = initial_guess.shape
    n_shot, n_line, n_tm = (lax.axis_size(a) for a in ("shot", "line", "tm"))
    at_shot, at_tm = lax.axis_index("shot"), lax.axis_index("tm")
    block_lines = block // RPL
    length = window * n_tm
    shots = shots_here * n_shot
    sections = station_portion_tallies.shape[0]
    mixtures = measured_mixtures.shape[0]
    paired = n_shot * n_line * n_tm == RPL and n_line == 2 and n_tm == 2 and block_lines == 8
    assert shots_here == 1 and (paired or n_shot == RPL)
    plan = Plan(
        paired=paired,
        shots=shots,
        lines=block_lines if paired else block_lines // n_tm,
        per=RPL // (n_shot * n_tm) if paired else 1,
        sections=sections,
        mixtures=mixtures,
        slabs=length // SLAB,
        each=n_shot,
        time_parts=n_tm,
    )
    lines = plan.lines

    if paired:
        source = exchanged(run_pack(plan, initial_guess.reshape(block, window)), ("line", "tm"))
        mixes = measured_mixtures
    else:
        grid = initial_guess.reshape(n_tm, lines, RPL, window)
        leaving = grid.transpose(2, 0, 1, 3).reshape(RPL * n_tm, lines, window)
        arrived = lax.all_to_all(leaving, ("shot", "tm"), split_axis=0, concat_axis=0, tiled=True)
        source = arrived.reshape(n_shot, n_tm, lines, window).transpose(0, 2, 1, 3).reshape(plan.rows, length)
        grid = measured_mixtures.reshape(mixtures, n_tm, lines, RPL, length)
        mixes = lax.dynamic_slice(grid, (0, at_tm, 0, at_shot, 0), (mixtures, 1, lines, 1, length))
        mixes = mixes.reshape(mixtures, lines, length)

    shot_bundle = bundled(source_entry_kernel, source_spaced_kernel, source_exit_kernel)
    station_net = (station_entry_kernel, station_spaced_kernel, station_exit_kernel)
    shot_weights = run_prepare(shot_bundle, source_inner_offsets, "prepare_shot")
    small = (station_portion_tallies, launch_lags, source_launch_order, learned_pace_factors)
    def edges_of(current):
        size = n_line * n_tm
        grid = current.reshape(shots, lines, length)
        up = [(i, i + 1) for i in range(size - 1)]
        down = [(j, i) for i, j in up]
        above = lax.ppermute(grid[:, -1], ("line", "tm"), up)
        below = lax.ppermute(grid[:, 0], ("line", "tm"), down)
        wide = jnp.broadcast_to(jnp.stack([above, below])[:, :, None, :], (2, shots, lines, length))
        return wide.reshape(2, plan.rows, length)

    def summed(value, axis):
        size = lax.axis_size(axis)
        if size <= 4:
            others = [lax.ppermute(value, axis, [(i, i ^ d) for i in range(size)]) for d in range(1, size)]
            return sum(others, value)
        step = 1
        while step < size:
            value = value + lax.ppermute(value, axis, [(i, i ^ step) for i in range(size)])
            step *= 2
        return value

    def shared(energy, along):
        for axis in along:
            energy = summed(energy, axis)
        return energy

    if paired:
        parts = run_stage(
            plan,
            small,
            source,
            shot=([], shot_weights),
            first=True,
            split_in="packets",
            split_out="parts",
            name="shot_pass",
        )
        station_net, own = lax.optimization_barrier((station_net, parts[0]))
        current = exchanged([own, *parts[1:]], "shot")
        bundle = bundled(*station_net)
        station_weights = run_prepare(bundle, station_inner_offsets, "prepare_station")
        energy = sum(jnp.sum(p[0:3, length:].astype(F32), axis=0, keepdims=True) for p in current)
        station_weights, energy = lax.optimization_barrier((station_weights, energy))
        energy = summed(energy, "tm")
    else:
        current, energy = run_stage(plan, small, [source], shot=([edges_of(source)], shot_weights), name="shot_pass")
        energy = shared(energy, ("tm", "shot"))
        station_weights = run_prepare(bundled(*station_net), station_inner_offsets, "prepare_station")
    for i in range(ITERS):
        station = (i, energy, mixes, station_weights)
        form = {"split_in": "parts"} if paired and i == 0 else {}
        came = current if form else [current]
        if i == ITERS - 1:
            form["split_out"] = "final" if paired else None
            (current,) = run_stage(plan, small, came, station=station, name="station_pass", **form)
        elif paired:
            current, edge = run_stage(
                plan, small, came, station=station, name="station_pass", split_out="edge", **form
            )
            edge = lax.ppermute(edge, "line", [(0, 1), (1, 0)])
            current, energy = run_stage(plan, small, [current], shot=([edge], shot_weights), name="shot_pass")
            fresh, energy = lax.optimization_barrier((bundle, energy))
            station_weights = run_prepare(fresh, station_inner_offsets, "prepare_station")
            energy = shared(energy, ("tm", "shot"))
        else:
            (current,) = run_stage(plan, small, came, station=station, name="station_pass")
            edges = [edges_of(current)]
            current, energy = run_stage(plan, small, [current], shot=(edges, shot_weights), name="shot_pass")
            energy = shared(energy, ("tm", "shot"))
    if paired:
        back = lax.all_to_all(current, ("tm", "shot"), split_axis=0, concat_axis=0, tiled=True)
        back = back.reshape(RPL, lines, window).transpose(1, 0, 2)
    else:
        current = current.reshape(n_shot, lines, n_tm, window).transpose(0, 2, 1, 3).reshape(-1, lines, window)
        back = lax.all_to_all(current, ("shot", "tm"), split_axis=0, concat_axis=0, tiled=True)
        back = back.reshape(RPL, n_tm, lines, window).transpose(1, 2, 0, 3)
    return back.reshape(shots_here, block, window)


def solution(mesh):
    placed = (P(("group", "shot"), "line", "tm"), P("group", "line", None), P("group"), P("group"), P("group"))
    return jax.shard_map(
        per_device,
        mesh=mesh,
        in_specs=placed + (P(),) * 9,
        out_specs=P(("group", "shot"), "line", "tm"),
        check_vma=False,
    )
```

```python
import functools

import jax
import jax.numpy as jnp
from jax import lax
from jax.experimental import pallas as pl
from jax.experimental.pallas import tpu as pltpu
from jax.sharding import PartitionSpec as P

RPL = 16
DMAX = 128
ITERS = 2
EPSILON = 1e-05

SLAB = 128
HALF = 64
FEAT = 64
GROUP = 4
WIDE = GROUP * FEAT
QS = SLAB // (2 * GROUP)
QH = QS // 2
assert QH == 8
ONES = 3 * HALF + 6
VMEM_LIMIT = 24 * 1024 * 1024
VMEM_FULL = 63 * 1024 * 1024

BF = jnp.bfloat16
F32 = jnp.float32


def split_bias(bias):
    high = bias.astype(BF).astype(F32)
    middle = (bias - high).astype(BF).astype(F32)
    return high, middle, bias - high - middle


def iota(shape, axis):
    return lax.broadcasted_iota(jnp.int32, shape, axis)


def picks(mask):
    return mask.astype(F32).astype(BF)


def start_of(q):
    return 16 * (q // 2) + 2 * (q % 2)


def prepare_kernel(bundle, o_in, o_out, rhs, cols):
    rhs[...] = jnp.zeros_like(rhs)
    cols[...] = jnp.zeros_like(cols)
    base = 3 * FEAT
    bias = bundle[base + 16 : base + 24, :]
    parts = split_bias(bias[0:1, :])
    exits = bundle[base : base + 4, :]
    for p in range(GROUP):
        lanes = slice(p * FEAT, (p + 1) * FEAT)
        for c in range(3):
            row = base + 4 * (c + 1)
            rhs[p * 32 + c * 8 : p * 32 + c * 8 + 4, lanes] = bundle[row : row + 4, :]
            rhs[p * 32 + 24 + c : p * 32 + 25 + c, lanes] = parts[c]
        cols[p * 8 : p * 8 + 4, lanes] = exits
    taps = rhs[...].astype(BF)
    row, col = iota((WIDE, SLAB), 0), iota((WIDE, SLAB), 1)
    channel, j, target = (col >> 3) & 3, col & 7, 4 * (col >> 5) + (col & 7) - 1
    rest = row - 3 * HALF
    sample = jnp.where(rest < 0, row & (HALF - 1), jnp.where(rest & 1 == 1, HALF, -1))
    same = (jnp.where(rest < 0, row >> 6, rest >> 1) == channel) & (channel < 3) & (j < 4)
    offset = jnp.where(same, sample - target, -SLAB)
    ones = (channel == 3) & (j < 3) & (row == ONES + j)
    for q in range(QH):
        chosen = picks((offset == start_of(q)) | ones)
        o_in[q] = jnp.dot(chosen, taps, preferred_element_type=F32).astype(BF)
    o_in[QH:] = jnp.zeros((2, WIDE, WIDE), BF)
    for a, at in [(0, 0), (1, 1), (2, 2), (3, 3), (4, 4), (-1, 5)]:
        for b in range(GROUP):
            if abs(a - b) <= 1:
                tap = a - b + 1
                rows, lanes = slice(at % 4 * FEAT, (at % 4 + 1) * FEAT), slice(b * FEAT, (b + 1) * FEAT)
                o_in[QH + at // 4, rows, lanes] = bundle[tap * FEAT : (tap + 1) * FEAT, :].astype(BF)
    row = iota((16, FEAT), 0)
    below = jnp.zeros((16, FEAT), F32)
    for i, part in enumerate(split_bias(bias[1:2, :])):
        below = jnp.where(row == i, part, below)
    for b in range(GROUP):
        o_in[QH + 1, SLAB : SLAB + 16, b * FEAT : (b + 1) * FEAT] = below.astype(BF)
    row, col = iota((SLAB, SLAB), 0), iota((SLAB, SLAB), 1)
    p, j = row >> 3, row & 7
    offset = jnp.where((p < GROUP) & (j < 4), col - (4 * p + j - 1), -SLAB)
    back = jnp.transpose(cols[...]).astype(BF)
    follows = (p == GROUP - 1) & (j == 3) & (col == 0)
    precedes = (row == 0) & (col == SLAB - 1)
    for q in range(QS + 2):
        chosen = picks(offset == start_of(q) if q < QS else [follows, precedes][q - QS])
        o_out[q] = jnp.dot(back, chosen, preferred_element_type=F32).astype(BF)


def pack_kernel(plan, *refs):
    sources, outs, fetched, done = refs[:9], refs[9:15], refs[15:24], refs[24]
    held = fetched[0]
    _, _, at_tm, _, at_line = places(plan, True)
    block = held.shape[0]
    copies = [pltpu.make_async_copy(src, dst, done.at[i]) for i, (src, dst) in enumerate(zip(sources, fetched))]
    for copy in copies:
        copy.start()
    lines = plan.lines
    half = block // 2
    row, col = iota((block, block), 0), iota((block, block), 1)
    spot, line = split_index(row, lines)
    d, spot = split_index(spot, half // lines)
    order = picks(col == line * RPL + (at_tm ^ d) * (half // lines) + spot)
    row, col = iota((32, block), 0), iota((32, block), 1)
    d, spot = split_index(row, 16)
    sent = jnp.where(at_line == 0, lines - 1, 0)
    outer = picks((col == sent * RPL + (at_tm ^ d) * (half // lines) + spot) & (spot < half // lines))
    for copy in copies:
        copy.wait()
    moved = jnp.dot(order, held[...], preferred_element_type=F32).astype(BF)
    edge = jnp.dot(outer, held[...], preferred_element_type=F32).astype(BF)
    outs[0][...] = moved[:half]
    outs[1][...] = moved[half:]
    outs[2][...] = edge[:16]
    outs[3][...] = edge[16:]
    for n, bundle in enumerate(outs[4:6]):
        entry, spaced, leave, bias = fetched[1 + 4 * n : 5 + 4 * n]
        for j in range(3):
            bundle[j * FEAT : (j + 1) * FEAT, :] = spaced[j].astype(F32)
            row = 3 * FEAT + 4 * (j + 1)
            bundle[row : row + 4, :] = entry[j].astype(F32)
        bundle[3 * FEAT : 3 * FEAT + 4, :] = leave[...].astype(F32)
        bundle[3 * FEAT + 16 : 3 * FEAT + 24, :] = jnp.zeros((8, FEAT), F32)
        bundle[3 * FEAT + 16 : 3 * FEAT + 18, :] = bias[...]


def pick_kernel(plan, mixes, picked):
    base = places(plan, False)[0]
    row, col = iota((plan.span, mixes.shape[1]), 0), iota((plan.span, mixes.shape[1]), 1)
    spot, line = split_index(row, plan.lines)
    choose = picks(col == line * RPL + base + spot)
    for g in range(plan.mixtures):
        picked[g] = jnp.dot(choose, mixes[g], preferred_element_type=F32).astype(BF)


def places(plan, first):
    at_shot, at_line, at_tm = (lax.axis_index(a) for a in ("shot", "line", "tm"))
    if not plan.paired:
        return at_shot, at_tm * plan.lines, at_tm, at_shot, at_line
    return at_tm * (RPL // 2) + (0 if first else at_shot * plan.per), 0, at_tm, at_shot, at_line


def split_index(value, size):
    if size & (size - 1):
        return value // size, value % size
    return value >> (size.bit_length() - 1), value & (size - 1)


def section_map(plan, place, tallies, first):
    shape = (plan.rows, SLAB)
    lane = lax.broadcasted_iota(jnp.int32, shape, 1)
    apart, line = split_index(iota(shape, 0), plan.lines)
    if not first:
        apart = split_index(apart, plan.per)[1]
    spot = (line + place[1]) * RPL + place[0] + apart
    low = jnp.zeros(shape, jnp.int32)
    high = jnp.zeros(shape, jnp.int32)
    count = jnp.zeros(shape, jnp.int32)
    start = jnp.int32(0)
    for p in range(plan.sections):
        amount = tallies[p]
        here = lane == p
        low = jnp.where(here, start, low)
        high = jnp.where(here, start + amount, high)
        count = jnp.where(here, amount, count)
        start = start + amount
    member = (spot >= low) & (spot < high)
    return member, count


def shifted(values, by, ok, edge):
    return jnp.where(ok, pltpu.roll(values, by % values.shape[0], 0), edge)


def pack_inputs(plan, channels, packed):
    lane = lax.broadcasted_iota(jnp.int32, (plan.rows, SLAB), 1)
    low = lane < HALF
    ones = ((lane >= ONES - SLAB) & (lane < ONES - SLAB + 3)).astype(F32)
    slabs = [[x[:, t * SLAB : (t + 1) * SLAB] for t in range(plan.slabs)] for x in channels]
    far = [[pltpu.roll(s, HALF + 1 + 2 * c, 1) for s in slabs[c]] for c in range(3)]
    for t in range(plan.slabs):
        v = [slabs[c][t] for c in range(3)]
        w = [pltpu.roll(s, HALF, 1) for s in v]
        even = jnp.where(low, v[2], ones)
        odd = jnp.where(low, w[2], ones)
        for c in range(3):
            left, right = lane == HALF + 2 * c, lane == HALF + 2 * c + 1
            near = pltpu.roll(v[c], 1 + 2 * c, 1)
            even = jnp.where(right, near, even)
            odd = jnp.where(left, near, odd)
            if t > 0:
                even = jnp.where(left, far[c][t - 1], even)
            if t < plan.slabs - 1:
                odd = jnp.where(right, far[c][t + 1], odd)
        packed[0, t, :, 0:SLAB] = jnp.where(low, v[0], w[1]).astype(BF)
        packed[0, t, :, SLAB:WIDE] = even.astype(BF)
        packed[1, t, :, 0:SLAB] = jnp.where(low, w[0], v[1]).astype(BF)
        packed[1, t, :, SLAB:WIDE] = odd.astype(BF)


def network(plan, weights, scratch, regions):
    w_in, w_out = weights
    packed, hidden, total, ends = scratch
    slabs, rows = plan.slabs, plan.rows
    many = slabs * rows
    pitch = slabs + 2

    def first(q):
        taps = jnp.concatenate([w_in[q], w_in[q + 1]], axis=1)
        value = jnp.dot(packed[...].reshape(2 * many, WIDE), taps, preferred_element_type=F32)
        value = jnp.maximum(value.astype(BF), 0).reshape(2, slabs, rows, 2 * WIDE)
        for h in range(2):
            for k in range(2):
                at = pl.ds((q + k + h * QH) * pitch + 1, slabs)
                hidden[at] = value[h, :, :, k * WIDE : (k + 1) * WIDE]

    lane = iota((slabs, rows, SLAB), 2)
    ones = picks(lane < 3)

    def window(q):
        if isinstance(q, int):
            left_at = (q - 2) * pitch + 1 if q >= 2 else (q + QS - 2) * pitch
            right_at = (q + 2) * pitch + 1 if q < QS - 2 else (q + 2 - QS) * pitch + 2
        else:
            left_at = jnp.where(q >= 2, (q - 2) * pitch + 1, (q + QS - 2) * pitch)
            right_at = jnp.where(q < QS - 2, (q + 2) * pitch + 1, (q + 2 - QS) * pitch + 2)
        middle = hidden[pl.ds(q * pitch + 1, slabs)]
        left = hidden[pl.ds(left_at, slabs), :, SLAB:WIDE]
        right = hidden[pl.ds(right_at, slabs), :, 0:SLAB]
        beside = jnp.where(lane < FEAT, right, left)
        return jnp.concatenate([middle, beside, ones], axis=2).reshape(many, 2 * WIDE)

    def second(q):
        both = jnp.concatenate([window(q), window(q + 1)], axis=0)
        value = jnp.dot(both, w_in[QH:].reshape(2 * WIDE, WIDE), preferred_element_type=F32)
        value = jnp.maximum(value.astype(BF), 0)
        return value[:many], value[many:]

    def onto(layer, taps):
        return jnp.dot(layer, taps, preferred_element_type=F32).reshape(slabs, rows, SLAB)

    edge = jnp.zeros((rows, WIDE), BF)
    for k in range(2):
        hidden[(QS - 2 + k) * pitch] = edge
        hidden[(k + 1) * pitch - 1] = edge
    total[...] = jnp.zeros_like(total)

    @regions
    def _():
        for q in range(0, QH, 2):
            first(q)

    @regions
    def _():
        for q in range(0, QS, 2):
            one, two = second(q)
            total[...] += onto(jnp.concatenate([one, two], axis=1), w_out[q : q + 2].reshape(2 * WIDE, SLAB))
            if q == 0:
                ends[0] = one
            if q == QS - 2:
                ends[1] = two

    total[0 : slabs - 1] += onto(ends[0], w_out[QS + 1])[1:]
    total[1:slabs] += onto(ends[1], w_out[QS])[: slabs - 1]


def add_total(plan, now, total, scale=None):
    for t in range(plan.slabs):
        lanes = slice(t * SLAB, (t + 1) * SLAB)
        more = total[t] if scale is None else scale * total[t]
        now[:, lanes] = (now[:, lanes] + more).astype(BF).astype(F32)


def shot_stage(plan, place, tallies, first, edges, weights, now, scratch):
    apart = pl.when(place[0] >= 0)

    @apart
    def _():
        x = now[...]
        line = split_index(iota(x.shape, 0), plan.lines)[1]
        if plan.paired:
            wide = [jnp.broadcast_to(edges[g : g + 1, :], (plan.lines, x.shape[1])) for g in range(plan.groups)]
            wide = jnp.concatenate(wide, axis=0)
            above = jnp.where(place[4] == 1, wide, 0.0)
            below = jnp.where(place[4] == 1, 0.0, wide)
        else:
            above, below = edges[0].astype(F32), edges[1].astype(F32)
        channels = [
            shifted(x, 1, line > 0, above),
            x,
            shifted(x, -1, line < plan.lines - 1, below),
        ]
        pack_inputs(plan, channels, scratch[0])

    network(plan, weights, scratch, apart)
    add_total(plan, now, scratch[2])
    power = jnp.zeros((plan.rows, SLAB), F32)
    for t in range(plan.slabs):
        piece = now[:, t * SLAB : (t + 1) * SLAB]
        power = power + piece * piece
    member, _ = section_map(plan, place, tallies, first)
    each = jnp.where(member, jnp.sum(power, axis=1, keepdims=True), 0.0)
    return jnp.sum(each, axis=0, keepdims=True)


def station_stage(
    plan, place, tallies, lags, order, pace, energies, mixes, weights, now, scratch, blend
):
    fired, misfit, scale = blend
    apart = lambda body: body()

    @apart
    def _():
        member, count = section_map(plan, place, tallies, False)
        denominator = jnp.maximum(count, 1) * (plan.shots * plan.slabs * SLAB)
        level = jnp.sqrt(energies[...] / denominator.astype(F32) + EPSILON)
        rms = jnp.sum(jnp.where(member, level, 0.0), axis=1, keepdims=True)
        scale[...] = jnp.broadcast_to(rms, scale.shape)
        x = (now[...] / rms).astype(BF).astype(F32)
        row = iota(x.shape, 0)
        channels = [
            shifted(x, plan.span, row >= plan.span, 0.0),
            x,
            shifted(x, -plan.span, row < plan.rows - plan.span, 0.0),
        ]
        pack_inputs(plan, channels, scratch[0])

    network(plan, weights, scratch, apart)
    add_total(plan, now, scratch[2], scale[...])
    lane = lax.broadcasted_iota(jnp.int32, (plan.span, SLAB), 1)
    mixtures = misfit.shape[0]
    per = plan.shots // mixtures
    misfit[...] = mixes[...].astype(F32)
    for s in range(plan.shots):
        lag = lags[s]
        before = jnp.zeros((plan.span, SLAB), F32)
        for t in range(plan.slabs):
            lanes = slice(t * SLAB, (t + 1) * SLAB)
            turned = pltpu.roll(now[s * plan.span : (s + 1) * plan.span, lanes], lag, 1)
            fired[s, :, lanes] = jnp.where(lane < lag, before, turned)
            before = turned
    for g in range(mixtures):
        value = fired[order[g * per]]
        for k in range(1, per):
            value = value + fired[order[g * per + k]]
        misfit[g] = value - misfit[g]
    for s in range(plan.shots):
        lag = lags[s]
        spot = jnp.int32(0)
        for k in range(plan.shots):
            spot = spot + jnp.where(order[k] == s, k, 0)
        which = spot // per
        back = (DMAX - lag) % DMAX
        after = jnp.zeros((plan.span, SLAB), F32)
        rows = slice(s * plan.span, (s + 1) * plan.span)
        for t in range(plan.slabs - 1, -1, -1):
            lanes = slice(t * SLAB, (t + 1) * SLAB)
            turned = pltpu.roll(misfit[which, :, lanes], back, 1)
            pulled = jnp.where(lane < DMAX - lag, turned, after)
            after = turned
            now[rows, lanes] = (now[rows, lanes] - pace * pulled).astype(BF).astype(F32)


def stage_kernel(plan, station_round, with_shot, first, split_in, split_out, *refs):
    refs = list(refs)
    take = lambda n: [refs.pop(0) for _ in range(n)]
    tallies, lags, order, paces = take(4)
    place = places(plan, first)
    sources = take(4 if split_in else 1)
    station = station_round is not None
    if station:
        energies, mixes = take(2)
        station_weights = take(2)
    if with_shot:
        edges = take(0 if first else 1)
        shot_weights = take(2)
    results = take({"parts": plan.each, "edge": 2}.get(split_out, 1))
    if with_shot and split_out != "parts":
        (energy,) = take(1)
    now, packed, hidden, total, ends, rim = take(6)
    scratch = (packed, hidden, total, ends)
    length = plan.slabs * SLAB
    if split_in == "parts":
        for d, part in enumerate(sources):
            at = pl.multiple_of((place[3] ^ d) * plan.span, plan.span)
            now[pl.ds(at, plan.span), :] = part[:, 0:length].astype(F32)
    elif split_in:
        share = length // plan.time_parts
        for d in range(2):
            lanes = pl.ds(pl.multiple_of((place[2] ^ d) * share, share), share)
            now[:, lanes] = sources[d][...].astype(F32)
            rim[:, lanes] = sources[2 + d][...].astype(F32)
    else:
        now[...] = sources[0][...].astype(F32)
    if station:
        station_stage(
            plan,
            place,
            tallies,
            lags,
            order,
            paces[station_round],
            energies,
            mixes,
            station_weights,
            now,
            scratch,
            refs,
        )
    if with_shot:
        if plan.paired and not first:
            rim[...] = edges[0][...].astype(F32)
        outer = rim if plan.paired else edges[0]
        sums = shot_stage(plan, place, tallies, first, outer, shot_weights, now, scratch)
    if split_out == "parts":
        row = iota((plan.span, SLAB), 0)
        beside = jnp.zeros((plan.span, SLAB), F32)
        for i, part in enumerate(split_bias(sums)):
            beside = jnp.where(row == i, part, beside)
        for d, part in enumerate(results):
            at = pl.multiple_of((place[3] ^ d) * plan.span, plan.span)
            part[:, 0:length] = now[pl.ds(at, plan.span), :].astype(BF)
            part[:, length:] = beside.astype(BF)
        return
    if with_shot:
        energy[...] = sums
    if split_out == "final":
        share = length // plan.time_parts
        for n in range(results[0].shape[0]):
            b, k = divmod(n, plan.each)
            results[0][n] = now[k * plan.span : (k + 1) * plan.span, b * share : (b + 1) * share].astype(BF)
        return
    results[0][...] = now[...].astype(BF)
    if split_out == "edge":
        row, col = iota((16, plan.rows), 0), iota((16, plan.rows), 1)
        sent = jnp.where(place[4] == 0, plan.lines - 1, 0)
        choose = picks(col == row * plan.lines + sent)
        results[1][...] = jnp.dot(choose, now[...].astype(BF), preferred_element_type=F32).astype(BF)


SMEM = pl.BlockSpec(memory_space=pltpu.SMEM)
VMEM = pl.BlockSpec(memory_space=pltpu.VMEM)
HBM = pl.BlockSpec(memory_space=pltpu.HBM)


def run_stage(plan, small, source, station=None, shot=None, first=False, split_in=None, split_out=None, name="stage"):
    operands = [*small, *source]
    specs = [SMEM] * len(small) + [VMEM] * len(source)
    station_round = None
    macs = 0
    pass_macs = plan.rows * plan.slabs * QS * WIDE * (WIDE * 3 + SLAB)
    if station is not None:
        station_round, energies, mixes, weights = station
        operands += [energies, mixes, *weights]
        specs += [VMEM] * 4
        macs += pass_macs
    if shot is not None:
        edges, weights = shot
        operands += [*edges, *weights]
        specs += [VMEM] * (len(edges) + 2)
        macs += pass_macs
    length = plan.slabs * SLAB
    if split_out == "parts":
        shapes = [jax.ShapeDtypeStruct((plan.span, length + SLAB), BF)] * plan.each
    elif split_out == "final":
        shapes = [jax.ShapeDtypeStruct((plan.each * plan.time_parts, plan.span, length // plan.time_parts), BF)]
    else:
        shapes = [jax.ShapeDtypeStruct((plan.rows, length), BF)]
        if split_out == "edge":
            shapes.append(jax.ShapeDtypeStruct((16, length), BF))
    if shot is not None and split_out != "parts":
        shapes.append(jax.ShapeDtypeStruct((1, SLAB), F32))
    scratch = [
        pltpu.VMEM((plan.rows, length), F32),
        pltpu.VMEM((2, plan.slabs, plan.rows, WIDE), BF),
        pltpu.VMEM((QS * (plan.slabs + 2), plan.rows, WIDE), BF),
        pltpu.VMEM((plan.slabs, plan.rows, SLAB), F32),
        pltpu.VMEM((2, plan.slabs * plan.rows, WIDE), BF),
        pltpu.VMEM((16, length), F32),
    ]
    if station is not None:
        scratch += [
            pltpu.VMEM((plan.shots, plan.span, length), F32),
            pltpu.VMEM((plan.mixtures, plan.span, length), F32),
            pltpu.VMEM((plan.rows, SLAB), F32),
        ]
    return pl.pallas_call(
        functools.partial(stage_kernel, plan, station_round, shot is not None, first, split_in, split_out),
        out_shape=shapes,
        in_specs=specs,
        out_specs=[VMEM] * len(shapes),
        scratch_shapes=scratch,
        compiler_params=pltpu.CompilerParams(vmem_limit_bytes=VMEM_LIMIT),
        cost_estimate=pl.CostEstimate(flops=2 * macs, bytes_accessed=1 << 20, transcendentals=0),
        name=name,
    )(*operands)


def bundled(entry, spaced, leave, bias):
    rows = [spaced.reshape(3 * FEAT, FEAT), leave, entry.transpose(1, 0, 2).reshape(12, FEAT), bias]
    return jnp.concatenate([r.astype(F32) for r in rows] + [jnp.zeros((6, FEAT), F32)], axis=0)


def run_prepare(bundle, name):
    return pl.pallas_call(
        prepare_kernel,
        out_shape=[
            jax.ShapeDtypeStruct((QH + 2, WIDE, WIDE), BF),
            jax.ShapeDtypeStruct((QS + 2, WIDE, SLAB), BF),
        ],
        in_specs=[VMEM],
        out_specs=[VMEM] * 2,
        scratch_shapes=[pltpu.VMEM((SLAB, WIDE), F32), pltpu.VMEM((SLAB, WIDE), F32)],
        compiler_params=pltpu.CompilerParams(vmem_limit_bytes=VMEM_LIMIT),
        cost_estimate=pl.CostEstimate(flops=2 * 8192 * WIDE * SLAB, bytes_accessed=4 << 20, transcendentals=0),
        name=name,
    )(bundle)


def run_pack(plan, traces, *nets):
    block, width = traces.shape
    operands = [traces]
    for entry, spaced, leave, bias in nets:
        operands += [entry.transpose(1, 0, 2), spaced, leave, bias]
    shapes = [jax.ShapeDtypeStruct((rows, width), BF) for rows in (block // 2, block // 2, 16, 16)]
    shapes += [jax.ShapeDtypeStruct((3 * FEAT + 24, FEAT), F32)] * len(nets)
    return pl.pallas_call(
        functools.partial(pack_kernel, plan),
        out_shape=shapes,
        in_specs=[HBM] * len(operands),
        out_specs=[VMEM] * len(shapes),
        scratch_shapes=[*(pltpu.VMEM(o.shape, o.dtype) for o in operands), pltpu.SemaphoreType.DMA((len(operands),))],
        compiler_params=pltpu.CompilerParams(vmem_limit_bytes=VMEM_FULL),
        cost_estimate=pl.CostEstimate(flops=2 * block * block * width, bytes_accessed=1 << 20, transcendentals=0),
        name="pack",
    )(*operands)


def run_pick(plan, mixes):
    return pl.pallas_call(
        functools.partial(pick_kernel, plan),
        out_shape=jax.ShapeDtypeStruct((plan.mixtures, plan.span, mixes.shape[2]), BF),
        in_specs=[VMEM],
        out_specs=VMEM,
        compiler_params=pltpu.CompilerParams(vmem_limit_bytes=VMEM_LIMIT),
        cost_estimate=pl.CostEstimate(flops=1 << 24, bytes_accessed=1 << 20, transcendentals=0),
        name="pick",
    )(mixes)


class Plan:
    def __init__(self, **sizes):
        self.__dict__.update(sizes)
        self.span = self.lines * self.per
        self.rows = self.shots * self.span
        self.groups = self.rows // self.lines


def exchanged(parts, axes):
    size = len(parts)
    came = [lax.ppermute(parts[d], axes, [(i, i ^ d) for i in range(size)]) for d in range(size - 1, 0, -1)]
    return [parts[0]] + came[::-1]


def per_device(
    initial_guess,
    measured_mixtures,
    launch_lags,
    source_launch_order,
    station_portion_tallies,
    source_entry_kernel,
    source_spaced_kernel,
    source_exit_kernel,
    source_inner_offsets,
    station_entry_kernel,
    station_spaced_kernel,
    station_exit_kernel,
    station_inner_offsets,
    learned_pace_factors,
):
    shots_here, block, window = initial_guess.shape
    n_shot, n_line, n_tm = (lax.axis_size(a) for a in ("shot", "line", "tm"))
    at_shot, at_tm = lax.axis_index("shot"), lax.axis_index("tm")
    block_lines = block // RPL
    length = window * n_tm
    shots = shots_here * n_shot
    sections = station_portion_tallies.shape[0]
    mixtures = measured_mixtures.shape[0]
    paired = n_shot * n_line * n_tm == RPL and n_line == 2 and n_tm == 2 and block_lines == 8
    assert shots_here == 1 and (paired or n_shot == RPL)
    plan = Plan(
        paired=paired,
        shots=shots,
        lines=block_lines if paired else block_lines // n_tm,
        per=RPL // (n_shot * n_tm) if paired else 1,
        sections=sections,
        mixtures=mixtures,
        slabs=length // SLAB,
        each=n_shot,
        time_parts=n_tm,
    )
    lines = plan.lines

    shot_net = (source_entry_kernel, source_spaced_kernel, source_exit_kernel, source_inner_offsets)
    station_net = (station_entry_kernel, station_spaced_kernel, station_exit_kernel, station_inner_offsets)
    if paired:
        *source, shot_net, station_net = run_pack(plan, initial_guess.reshape(block, window), shot_net, station_net)
        source = exchanged(source, ("line", "tm"))
        mixes = measured_mixtures
    else:
        grid = initial_guess.reshape(n_tm, lines, RPL, window)
        leaving = grid.transpose(2, 0, 1, 3).reshape(RPL * n_tm, lines, window)
        arrived = lax.all_to_all(leaving, ("shot", "tm"), split_axis=0, concat_axis=0, tiled=True)
        source = arrived.reshape(n_shot, n_tm, lines, window).transpose(0, 2, 1, 3).reshape(plan.rows, length)
        grid = measured_mixtures.reshape(mixtures, n_tm, lines, RPL, length)
        mixes = lax.dynamic_slice(grid, (0, at_tm, 0, at_shot, 0), (mixtures, 1, lines, 1, length))
        mixes = mixes.reshape(mixtures, lines, length)
        shot_net, station_net = bundled(*shot_net), bundled(*station_net)

    shot_weights = run_prepare(shot_net, "prepare_shot")
    small = (station_portion_tallies, launch_lags, source_launch_order, learned_pace_factors)
    def edges_of(current):
        size = n_line * n_tm
        grid = current.reshape(shots, lines, length)
        up = [(i, i + 1) for i in range(size - 1)]
        down = [(j, i) for i, j in up]
        above = lax.ppermute(grid[:, -1], ("line", "tm"), up)
        below = lax.ppermute(grid[:, 0], ("line", "tm"), down)
        wide = jnp.broadcast_to(jnp.stack([above, below])[:, :, None, :], (2, shots, lines, length))
        return wide.reshape(2, plan.rows, length)

    def summed(value, axis):
        size = lax.axis_size(axis)
        if size <= 4:
            others = [lax.ppermute(value, axis, [(i, i ^ d) for i in range(size)]) for d in range(1, size)]
            return sum(others, value)
        step = 1
        while step < size:
            value = value + lax.ppermute(value, axis, [(i, i ^ step) for i in range(size)])
            step *= 2
        return value

    def shared(energy, along):
        for axis in along:
            energy = summed(energy, axis)
        return energy

    if paired:
        parts = run_stage(
            plan,
            small,
            source,
            shot=([], shot_weights),
            first=True,
            split_in="packets",
            split_out="parts",
            name="shot_pass",
        )
        station_net, mixes, own = lax.optimization_barrier((station_net, mixes, parts[0]))
        current = exchanged([own, *parts[1:]], "shot")
        station_weights = run_prepare(station_net, "prepare_station")
        energy = sum(jnp.sum(p[0:3, length:].astype(F32), axis=0, keepdims=True) for p in current)
        mixes = run_pick(plan, mixes)
        station_weights, mixes, energy = lax.optimization_barrier((station_weights, mixes, energy))
        energy = summed(energy, "tm")
    else:
        current, energy = run_stage(plan, small, [source], shot=([edges_of(source)], shot_weights), name="shot_pass")
        energy = shared(energy, ("tm", "shot"))
        station_weights = run_prepare(station_net, "prepare_station")
    for i in range(ITERS):
        station = (i, energy, mixes, station_weights)
        form = {"split_in": "parts"} if paired and i == 0 else {}
        came = current if form else [current]
        if i == ITERS - 1:
            form["split_out"] = "final" if paired else None
            (current,) = run_stage(plan, small, came, station=station, name="station_pass", **form)
        elif paired:
            current, edge = run_stage(
                plan, small, came, station=station, name="station_pass", split_out="edge", **form
            )
            edge = lax.ppermute(edge, "line", [(0, 1), (1, 0)])
            current, energy = run_stage(plan, small, [current], shot=([edge], shot_weights), name="shot_pass")
            fresh, energy = lax.optimization_barrier((station_net, energy))
            station_weights = run_prepare(fresh, "prepare_station")
            energy = shared(energy, ("tm", "shot"))
        else:
            (current,) = run_stage(plan, small, came, station=station, name="station_pass")
            edges = [edges_of(current)]
            current, energy = run_stage(plan, small, [current], shot=(edges, shot_weights), name="shot_pass")
            energy = shared(energy, ("tm", "shot"))
    if paired:
        back = lax.all_to_all(current, ("tm", "shot"), split_axis=0, concat_axis=0, tiled=True)
        back = back.reshape(RPL, lines, window).transpose(1, 0, 2)
    else:
        current = current.reshape(n_shot, lines, n_tm, window).transpose(0, 2, 1, 3).reshape(-1, lines, window)
        back = lax.all_to_all(current, ("shot", "tm"), split_axis=0, concat_axis=0, tiled=True)
        back = back.reshape(RPL, n_tm, lines, window).transpose(1, 2, 0, 3)
    return back.reshape(shots_here, block, window)


def solution(mesh):
    placed = (P(("group", "shot"), "line", "tm"), P("group", "line", None), P("group"), P("group"), P("group"))
    return jax.shard_map(
        per_device,
        mesh=mesh,
        in_specs=placed + (P(),) * 9,
        out_specs=P(("group", "shot"), "line", "tm"),
        check_vma=False,
    )
```

```python
import functools

import jax
import jax.numpy as jnp
from jax import lax
from jax.experimental import pallas as pl
from jax.experimental.pallas import tpu as pltpu
from jax.sharding import PartitionSpec as P

RPL = 16
DMAX = 128
ITERS = 2
EPSILON = 1e-05

SLAB = 128
HALF = 64
FEAT = 64
GROUP = 4
WIDE = GROUP * FEAT
QS = SLAB // (2 * GROUP)
QH = QS // 2
assert QH == 8
ONES = 3 * HALF + 6
VMEM_LIMIT = 24 * 1024 * 1024
VMEM_FULL = 63 * 1024 * 1024

BF = jnp.bfloat16
F32 = jnp.float32


def split_bias(bias):
    high = bias.astype(BF).astype(F32)
    middle = (bias - high).astype(BF).astype(F32)
    return high, middle, bias - high - middle


def iota(shape, axis):
    return lax.broadcasted_iota(jnp.int32, shape, axis)


def picks(mask):
    return mask.astype(F32).astype(BF)


def start_of(q):
    return 16 * (q // 2) + 2 * (q % 2)


def prepare_kernel(bundle, o_in, o_out, rhs, cols):
    rhs[...] = jnp.zeros_like(rhs)
    cols[...] = jnp.zeros_like(cols)
    base = 3 * FEAT
    bias = bundle[base + 16 : base + 24, :]
    parts = split_bias(bias[0:1, :])
    exits = bundle[base : base + 4, :]
    for p in range(GROUP):
        lanes = slice(p * FEAT, (p + 1) * FEAT)
        for c in range(3):
            row = base + 4 * (c + 1)
            rhs[p * 32 + c * 8 : p * 32 + c * 8 + 4, lanes] = bundle[row : row + 4, :]
            rhs[p * 32 + 24 + c : p * 32 + 25 + c, lanes] = parts[c]
        cols[p * 8 : p * 8 + 4, lanes] = exits
    taps = rhs[...].astype(BF)
    row, col = iota((WIDE, SLAB), 0), iota((WIDE, SLAB), 1)
    channel, j, target = (col >> 3) & 3, col & 7, 4 * (col >> 5) + (col & 7) - 1
    rest = row - 3 * HALF
    sample = jnp.where(rest < 0, row & (HALF - 1), jnp.where(rest & 1 == 1, HALF, -1))
    same = (jnp.where(rest < 0, row >> 6, rest >> 1) == channel) & (channel < 3) & (j < 4)
    offset = jnp.where(same, sample - target, -SLAB)
    ones = (channel == 3) & (j < 3) & (row == ONES + j)
    for q in range(QH):
        chosen = picks((offset == start_of(q)) | ones)
        o_in[q] = jnp.dot(chosen, taps, preferred_element_type=F32).astype(BF)
    o_in[QH:] = jnp.zeros((2, WIDE, WIDE), BF)
    for a, at in [(0, 0), (1, 1), (2, 2), (3, 3), (4, 4), (-1, 5)]:
        for b in range(GROUP):
            if abs(a - b) <= 1:
                tap = a - b + 1
                rows, lanes = slice(at % 4 * FEAT, (at % 4 + 1) * FEAT), slice(b * FEAT, (b + 1) * FEAT)
                o_in[QH + at // 4, rows, lanes] = bundle[tap * FEAT : (tap + 1) * FEAT, :].astype(BF)
    row = iota((16, FEAT), 0)
    below = jnp.zeros((16, FEAT), F32)
    for i, part in enumerate(split_bias(bias[1:2, :])):
        below = jnp.where(row == i, part, below)
    for b in range(GROUP):
        o_in[QH + 1, SLAB : SLAB + 16, b * FEAT : (b + 1) * FEAT] = below.astype(BF)
    row, col = iota((SLAB, SLAB), 0), iota((SLAB, SLAB), 1)
    p, j = row >> 3, row & 7
    offset = jnp.where((p < GROUP) & (j < 4), col - (4 * p + j - 1), -SLAB)
    back = jnp.transpose(cols[...]).astype(BF)
    follows = (p == GROUP - 1) & (j == 3) & (col == 0)
    precedes = (row == 0) & (col == SLAB - 1)
    for q in range(QS + 2):
        chosen = picks(offset == start_of(q) if q < QS else [follows, precedes][q - QS])
        o_out[q] = jnp.dot(back, chosen, preferred_element_type=F32).astype(BF)


def pack_kernel(plan, *refs):
    sources, outs, fetched, done = refs[:9], refs[9:15], refs[15:24], refs[24]
    held = fetched[0]
    _, _, at_tm, _, at_line = places(plan, True)
    block = held.shape[0]
    copies = [pltpu.make_async_copy(src, dst, done.at[i]) for i, (src, dst) in enumerate(zip(sources, fetched))]
    for copy in copies:
        copy.start()
    lines = plan.lines
    half = block // 2
    row, col = iota((block, block), 0), iota((block, block), 1)
    spot, line = split_index(row, lines)
    d, spot = split_index(spot, half // lines)
    order = picks(col == line * RPL + (at_tm ^ d) * (half // lines) + spot)
    row, col = iota((32, block), 0), iota((32, block), 1)
    d, spot = split_index(row, 16)
    sent = jnp.where(at_line == 0, lines - 1, 0)
    outer = picks((col == sent * RPL + (at_tm ^ d) * (half // lines) + spot) & (spot < half // lines))
    for copy in copies:
        copy.wait()
    moved = jnp.dot(order, held[...], preferred_element_type=F32).astype(BF)
    edge = jnp.dot(outer, held[...], preferred_element_type=F32).astype(BF)
    outs[0][...] = moved[:half]
    outs[1][...] = moved[half:]
    outs[2][...] = edge[:16]
    outs[3][...] = edge[16:]
    for n, bundle in enumerate(outs[4:6]):
        entry, spaced, leave, bias = fetched[1 + 4 * n : 5 + 4 * n]
        for j in range(3):
            bundle[j * FEAT : (j + 1) * FEAT, :] = spaced[j].astype(F32)
            row = 3 * FEAT + 4 * (j + 1)
            bundle[row : row + 4, :] = entry[j].astype(F32)
        bundle[3 * FEAT : 3 * FEAT + 4, :] = leave[...].astype(F32)
        bundle[3 * FEAT + 16 : 3 * FEAT + 24, :] = jnp.zeros((8, FEAT), F32)
        bundle[3 * FEAT + 16 : 3 * FEAT + 18, :] = bias[...]


def pick_kernel(plan, mixes, picked):
    base = places(plan, False)[0]
    row, col = iota((plan.span, mixes.shape[1]), 0), iota((plan.span, mixes.shape[1]), 1)
    spot, line = split_index(row, plan.lines)
    choose = picks(col == line * RPL + base + spot)
    for g in range(plan.mixtures):
        picked[g] = jnp.dot(choose, mixes[g], preferred_element_type=F32).astype(BF)


def places(plan, first):
    at_shot, at_line, at_tm = (lax.axis_index(a) for a in ("shot", "line", "tm"))
    if not plan.paired:
        return at_shot, at_tm * plan.lines, at_tm, at_shot, at_line
    return at_tm * (RPL // 2) + (0 if first else at_shot * plan.per), 0, at_tm, at_shot, at_line


def split_index(value, size):
    if size & (size - 1):
        return value // size, value % size
    return value >> (size.bit_length() - 1), value & (size - 1)


def section_map(plan, place, tallies, first):
    shape = (plan.rows, SLAB)
    lane = lax.broadcasted_iota(jnp.int32, shape, 1)
    apart, line = split_index(iota(shape, 0), plan.lines)
    if not first:
        apart = split_index(apart, plan.per)[1]
    spot = (line + place[1]) * RPL + place[0] + apart
    low = jnp.zeros(shape, jnp.int32)
    high = jnp.zeros(shape, jnp.int32)
    count = jnp.zeros(shape, jnp.int32)
    start = jnp.int32(0)
    for p in range(plan.sections):
        amount = tallies[p]
        here = lane == p
        low = jnp.where(here, start, low)
        high = jnp.where(here, start + amount, high)
        count = jnp.where(here, amount, count)
        start = start + amount
    member = (spot >= low) & (spot < high)
    return member, count


def shifted(values, by, ok, edge):
    return jnp.where(ok, pltpu.roll(values, by % values.shape[0], 0), edge)


def pack_inputs(plan, channels, packed):
    lane = lax.broadcasted_iota(jnp.int32, (plan.rows, SLAB), 1)
    low = lane < HALF
    ones = ((lane >= ONES - SLAB) & (lane < ONES - SLAB + 3)).astype(F32)
    slabs = [[x[:, t * SLAB : (t + 1) * SLAB] for t in range(plan.slabs)] for x in channels]
    far = [[pltpu.roll(s, HALF + 1 + 2 * c, 1) for s in slabs[c]] for c in range(3)]
    for t in range(plan.slabs):
        v = [slabs[c][t] for c in range(3)]
        w = [pltpu.roll(s, HALF, 1) for s in v]
        even = jnp.where(low, v[2], ones)
        odd = jnp.where(low, w[2], ones)
        for c in range(3):
            left, right = lane == HALF + 2 * c, lane == HALF + 2 * c + 1
            near = pltpu.roll(v[c], 1 + 2 * c, 1)
            even = jnp.where(right, near, even)
            odd = jnp.where(left, near, odd)
            if t > 0:
                even = jnp.where(left, far[c][t - 1], even)
            if t < plan.slabs - 1:
                odd = jnp.where(right, far[c][t + 1], odd)
        packed[0, t, :, 0:SLAB] = jnp.where(low, v[0], w[1]).astype(BF)
        packed[0, t, :, SLAB:WIDE] = even.astype(BF)
        packed[1, t, :, 0:SLAB] = jnp.where(low, w[0], v[1]).astype(BF)
        packed[1, t, :, SLAB:WIDE] = odd.astype(BF)


def network(plan, weights, scratch, regions):
    w_in, w_out = weights
    packed, hidden, total, ends = scratch
    slabs, rows = plan.slabs, plan.rows
    many = slabs * rows
    pitch = slabs + 2

    def first(q):
        taps = jnp.concatenate([w_in[q], w_in[q + 1]], axis=1)
        value = jnp.dot(packed[...].reshape(2 * many, WIDE), taps, preferred_element_type=F32)
        value = jnp.maximum(value.astype(BF), 0).reshape(2, slabs, rows, 2 * WIDE)
        for h in range(2):
            for k in range(2):
                at = pl.ds((q + k + h * QH) * pitch + 1, slabs)
                hidden[at] = value[h, :, :, k * WIDE : (k + 1) * WIDE]

    lane = iota((slabs, rows, SLAB), 2)
    ones = picks(lane < 3)

    def window(q):
        if isinstance(q, int):
            left_at = (q - 2) * pitch + 1 if q >= 2 else (q + QS - 2) * pitch
            right_at = (q + 2) * pitch + 1 if q < QS - 2 else (q + 2 - QS) * pitch + 2
        else:
            left_at = jnp.where(q >= 2, (q - 2) * pitch + 1, (q + QS - 2) * pitch)
            right_at = jnp.where(q < QS - 2, (q + 2) * pitch + 1, (q + 2 - QS) * pitch + 2)
        middle = hidden[pl.ds(q * pitch + 1, slabs)]
        left = hidden[pl.ds(left_at, slabs), :, SLAB:WIDE]
        right = hidden[pl.ds(right_at, slabs), :, 0:SLAB]
        beside = jnp.where(lane < FEAT, right, left)
        return jnp.concatenate([middle, beside, ones], axis=2).reshape(many, 2 * WIDE)

    def second(q):
        both = jnp.concatenate([window(q), window(q + 1)], axis=0)
        value = jnp.dot(both, w_in[QH:].reshape(2 * WIDE, WIDE), preferred_element_type=F32)
        value = jnp.maximum(value.astype(BF), 0)
        return value[:many], value[many:]

    def onto(layer, taps):
        return jnp.dot(layer, taps, preferred_element_type=F32).reshape(slabs, rows, SLAB)

    edge = jnp.zeros((rows, WIDE), BF)
    for k in range(2):
        hidden[(QS - 2 + k) * pitch] = edge
        hidden[(k + 1) * pitch - 1] = edge
    total[...] = jnp.zeros_like(total)

    @regions
    def _():
        for q in range(0, QH, 2):
            first(q)

    @regions
    def _():
        for q in range(0, QS, 2):
            one, two = second(q)
            total[...] += onto(jnp.concatenate([one, two], axis=1), w_out[q : q + 2].reshape(2 * WIDE, SLAB))
            if q == 0:
                ends[0] = one
            if q == QS - 2:
                ends[1] = two

    total[0 : slabs - 1] += onto(ends[0], w_out[QS + 1])[1:]
    total[1:slabs] += onto(ends[1], w_out[QS])[: slabs - 1]


def add_total(plan, now, total, scale=None):
    for t in range(plan.slabs):
        lanes = slice(t * SLAB, (t + 1) * SLAB)
        more = total[t] if scale is None else scale * total[t]
        now[:, lanes] = (now[:, lanes] + more).astype(BF).astype(F32)


def shot_stage(plan, place, tallies, first, edges, weights, now, scratch):
    apart = pl.when(place[0] >= 0)

    @apart
    def _():
        x = now[...]
        line = split_index(iota(x.shape, 0), plan.lines)[1]
        if plan.paired:
            wide = [jnp.broadcast_to(edges[g : g + 1, :], (plan.lines, x.shape[1])) for g in range(plan.groups)]
            wide = jnp.concatenate(wide, axis=0)
            above = jnp.where(place[4] == 1, wide, 0.0)
            below = jnp.where(place[4] == 1, 0.0, wide)
        else:
            above, below = edges[0].astype(F32), edges[1].astype(F32)
        channels = [
            shifted(x, 1, line > 0, above),
            x,
            shifted(x, -1, line < plan.lines - 1, below),
        ]
        pack_inputs(plan, channels, scratch[0])

    network(plan, weights, scratch, apart)
    add_total(plan, now, scratch[2])
    power = jnp.zeros((plan.rows, SLAB), F32)
    for t in range(plan.slabs):
        piece = now[:, t * SLAB : (t + 1) * SLAB]
        power = power + piece * piece
    member, _ = section_map(plan, place, tallies, first)
    each = jnp.where(member, jnp.sum(power, axis=1, keepdims=True), 0.0)
    return jnp.sum(each, axis=0, keepdims=True)


def station_stage(
    plan, place, tallies, lags, order, pace, energies, mixes, weights, now, scratch, blend
):
    fired, misfit, scale = blend
    apart = lambda body: body()

    @apart
    def _():
        member, count = section_map(plan, place, tallies, False)
        denominator = jnp.maximum(count, 1) * (plan.shots * plan.slabs * SLAB)
        level = jnp.sqrt(energies[...] / denominator.astype(F32) + EPSILON)
        rms = jnp.sum(jnp.where(member, level, 0.0), axis=1, keepdims=True)
        scale[...] = jnp.broadcast_to(rms, scale.shape)
        x = (now[...] / rms).astype(BF).astype(F32)
        row = iota(x.shape, 0)
        channels = [
            shifted(x, plan.span, row >= plan.span, 0.0),
            x,
            shifted(x, -plan.span, row < plan.rows - plan.span, 0.0),
        ]
        pack_inputs(plan, channels, scratch[0])

    network(plan, weights, scratch, apart)
    add_total(plan, now, scratch[2], scale[...])
    lane = lax.broadcasted_iota(jnp.int32, (plan.span, SLAB), 1)
    mixtures = misfit.shape[0]
    per = plan.shots // mixtures
    misfit[...] = mixes[...].astype(F32)
    for s in range(plan.shots):
        lag = lags[s]
        before = jnp.zeros((plan.span, SLAB), F32)
        for t in range(plan.slabs):
            lanes = slice(t * SLAB, (t + 1) * SLAB)
            turned = pltpu.roll(now[s * plan.span : (s + 1) * plan.span, lanes], lag, 1)
            fired[s, :, lanes] = jnp.where(lane < lag, before, turned)
            before = turned
    for g in range(mixtures):
        value = fired[order[g * per]]
        for k in range(1, per):
            value = value + fired[order[g * per + k]]
        misfit[g] = value - misfit[g]
    for s in range(plan.shots):
        lag = lags[s]
        spot = jnp.int32(0)
        for k in range(plan.shots):
            spot = spot + jnp.where(order[k] == s, k, 0)
        which = spot // per
        back = (DMAX - lag) % DMAX
        after = jnp.zeros((plan.span, SLAB), F32)
        rows = slice(s * plan.span, (s + 1) * plan.span)
        for t in range(plan.slabs - 1, -1, -1):
            lanes = slice(t * SLAB, (t + 1) * SLAB)
            turned = pltpu.roll(misfit[which, :, lanes], back, 1)
            pulled = jnp.where(lane < DMAX - lag, turned, after)
            after = turned
            now[rows, lanes] = (now[rows, lanes] - pace * pulled).astype(BF).astype(F32)


def stage_kernel(plan, station_round, with_shot, first, split_in, split_out, *refs):
    refs = list(refs)
    take = lambda n: [refs.pop(0) for _ in range(n)]
    tallies, lags, order, paces = take(4)
    place = places(plan, first)
    sources = take(4 if split_in else 1)
    station = station_round is not None
    if station:
        energies, mixes = take(2)
        station_weights = take(2)
    if with_shot:
        edges = take(0 if first else 1)
        shot_weights = take(2)
    results = take({"parts": plan.each, "edge": 2}.get(split_out, 1))
    if with_shot and split_out != "parts":
        (energy,) = take(1)
    now, packed, hidden, total, ends, rim = take(6)
    scratch = (packed, hidden, total, ends)
    length = plan.slabs * SLAB
    if split_in == "parts":
        for d, part in enumerate(sources):
            at = pl.multiple_of((place[3] ^ d) * plan.span, plan.span)
            now[pl.ds(at, plan.span), :] = part[:, 0:length].astype(F32)
    elif split_in:
        share = length // plan.time_parts
        for d in range(2):
            lanes = pl.ds(pl.multiple_of((place[2] ^ d) * share, share), share)
            now[:, lanes] = sources[d][...].astype(F32)
            rim[:, lanes] = sources[2 + d][...].astype(F32)
    else:
        now[...] = sources[0][...].astype(F32)
    if station:
        station_stage(
            plan,
            place,
            tallies,
            lags,
            order,
            paces[station_round],
            energies,
            mixes,
            station_weights,
            now,
            scratch,
            refs,
        )
    if with_shot:
        if plan.paired and not first:
            rim[0 : plan.groups, :] = edges[0][...].astype(F32)
        outer = rim if plan.paired else edges[0]
        sums = shot_stage(plan, place, tallies, first, outer, shot_weights, now, scratch)
    if split_out == "parts":
        row = iota((plan.span, SLAB), 0)
        beside = jnp.zeros((plan.span, SLAB), F32)
        for i, part in enumerate(split_bias(sums)):
            beside = jnp.where(row == i, part, beside)
        for d, part in enumerate(results):
            at = pl.multiple_of((place[3] ^ d) * plan.span, plan.span)
            part[:, 0:length] = now[pl.ds(at, plan.span), :].astype(BF)
            part[:, length:] = beside.astype(BF)
        return
    if with_shot:
        energy[...] = sums
    if split_out == "final":
        share = length // plan.time_parts
        for n in range(results[0].shape[0]):
            b, k = divmod(n, plan.each)
            results[0][n] = now[k * plan.span : (k + 1) * plan.span, b * share : (b + 1) * share].astype(BF)
        return
    results[0][...] = now[...].astype(BF)
    if split_out == "edge":
        row, col = iota((16, plan.rows), 0), iota((16, plan.rows), 1)
        sent = jnp.where(place[4] == 0, plan.lines - 1, 0)
        choose = picks(col == row * plan.lines + sent)
        sent = jnp.dot(choose, now[...].astype(BF), preferred_element_type=F32)
        results[1][...] = sent[: plan.groups].astype(BF)


SMEM = pl.BlockSpec(memory_space=pltpu.SMEM)
VMEM = pl.BlockSpec(memory_space=pltpu.VMEM)
HBM = pl.BlockSpec(memory_space=pltpu.HBM)


def run_stage(plan, small, source, station=None, shot=None, first=False, split_in=None, split_out=None, name="stage"):
    operands = [*small, *source]
    specs = [SMEM] * len(small) + [VMEM] * len(source)
    station_round = None
    macs = 0
    pass_macs = plan.rows * plan.slabs * QS * WIDE * (WIDE * 3 + SLAB)
    if station is not None:
        station_round, energies, mixes, weights = station
        operands += [energies, mixes, *weights]
        specs += [VMEM] * 4
        macs += pass_macs
    if shot is not None:
        edges, weights = shot
        operands += [*edges, *weights]
        specs += [VMEM] * (len(edges) + 2)
        macs += pass_macs
    length = plan.slabs * SLAB
    if split_out == "parts":
        shapes = [jax.ShapeDtypeStruct((plan.span, length + SLAB), BF)] * plan.each
    elif split_out == "final":
        shapes = [jax.ShapeDtypeStruct((plan.each * plan.time_parts, plan.span, length // plan.time_parts), BF)]
    else:
        shapes = [jax.ShapeDtypeStruct((plan.rows, length), BF)]
        if split_out == "edge":
            shapes.append(jax.ShapeDtypeStruct((plan.groups, length), BF))
    if shot is not None and split_out != "parts":
        shapes.append(jax.ShapeDtypeStruct((1, SLAB), F32))
    scratch = [
        pltpu.VMEM((plan.rows, length), F32),
        pltpu.VMEM((2, plan.slabs, plan.rows, WIDE), BF),
        pltpu.VMEM((QS * (plan.slabs + 2), plan.rows, WIDE), BF),
        pltpu.VMEM((plan.slabs, plan.rows, SLAB), F32),
        pltpu.VMEM((2, plan.slabs * plan.rows, WIDE), BF),
        pltpu.VMEM((16, length), F32),
    ]
    if station is not None:
        scratch += [
            pltpu.VMEM((plan.shots, plan.span, length), F32),
            pltpu.VMEM((plan.mixtures, plan.span, length), F32),
            pltpu.VMEM((plan.rows, SLAB), F32),
        ]
    return pl.pallas_call(
        functools.partial(stage_kernel, plan, station_round, shot is not None, first, split_in, split_out),
        out_shape=shapes,
        in_specs=specs,
        out_specs=[VMEM] * len(shapes),
        scratch_shapes=scratch,
        compiler_params=pltpu.CompilerParams(vmem_limit_bytes=VMEM_LIMIT),
        cost_estimate=pl.CostEstimate(flops=2 * macs, bytes_accessed=1 << 20, transcendentals=0),
        name=name,
    )(*operands)


def bundled(entry, spaced, leave, bias):
    rows = [spaced.reshape(3 * FEAT, FEAT), leave, entry.transpose(1, 0, 2).reshape(12, FEAT), bias]
    return jnp.concatenate([r.astype(F32) for r in rows] + [jnp.zeros((6, FEAT), F32)], axis=0)


def run_prepare(bundle, name):
    return pl.pallas_call(
        prepare_kernel,
        out_shape=[
            jax.ShapeDtypeStruct((QH + 2, WIDE, WIDE), BF),
            jax.ShapeDtypeStruct((QS + 2, WIDE, SLAB), BF),
        ],
        in_specs=[VMEM],
        out_specs=[VMEM] * 2,
        scratch_shapes=[pltpu.VMEM((SLAB, WIDE), F32), pltpu.VMEM((SLAB, WIDE), F32)],
        compiler_params=pltpu.CompilerParams(vmem_limit_bytes=VMEM_LIMIT),
        cost_estimate=pl.CostEstimate(flops=2 * 8192 * WIDE * SLAB, bytes_accessed=4 << 20, transcendentals=0),
        name=name,
    )(bundle)


def run_pack(plan, traces, *nets):
    block, width = traces.shape
    operands = [traces]
    for entry, spaced, leave, bias in nets:
        operands += [entry.transpose(1, 0, 2), spaced, leave, bias]
    shapes = [jax.ShapeDtypeStruct((rows, width), BF) for rows in (block // 2, block // 2, 16, 16)]
    shapes += [jax.ShapeDtypeStruct((3 * FEAT + 24, FEAT), F32)] * len(nets)
    return pl.pallas_call(
        functools.partial(pack_kernel, plan),
        out_shape=shapes,
        in_specs=[HBM] * len(operands),
        out_specs=[VMEM] * len(shapes),
        scratch_shapes=[*(pltpu.VMEM(o.shape, o.dtype) for o in operands), pltpu.SemaphoreType.DMA((len(operands),))],
        compiler_params=pltpu.CompilerParams(vmem_limit_bytes=VMEM_FULL),
        cost_estimate=pl.CostEstimate(flops=2 * block * block * width, bytes_accessed=1 << 20, transcendentals=0),
        name="pack",
    )(*operands)


def run_pick(plan, mixes):
    return pl.pallas_call(
        functools.partial(pick_kernel, plan),
        out_shape=jax.ShapeDtypeStruct((plan.mixtures, plan.span, mixes.shape[2]), BF),
        in_specs=[VMEM],
        out_specs=VMEM,
        compiler_params=pltpu.CompilerParams(vmem_limit_bytes=VMEM_LIMIT),
        cost_estimate=pl.CostEstimate(flops=1 << 24, bytes_accessed=1 << 20, transcendentals=0),
        name="pick",
    )(mixes)


class Plan:
    def __init__(self, **sizes):
        self.__dict__.update(sizes)
        self.span = self.lines * self.per
        self.rows = self.shots * self.span
        self.groups = self.rows // self.lines


def exchanged(parts, axes, direct=True):
    size = len(parts)
    came = [parts[0]]
    for d in range(1, size):
        steps = [d] if direct else [1 << k for k in reversed(range(size.bit_length())) if d >> k & 1]
        part = parts[d]
        for step in steps:
            part = lax.ppermute(part, axes, [(i, i ^ step) for i in range(size)])
        came.append(part)
    return came


def per_device(
    initial_guess,
    measured_mixtures,
    launch_lags,
    source_launch_order,
    station_portion_tallies,
    source_entry_kernel,
    source_spaced_kernel,
    source_exit_kernel,
    source_inner_offsets,
    station_entry_kernel,
    station_spaced_kernel,
    station_exit_kernel,
    station_inner_offsets,
    learned_pace_factors,
):
    shots_here, block, window = initial_guess.shape
    n_shot, n_line, n_tm = (lax.axis_size(a) for a in ("shot", "line", "tm"))
    at_shot, at_tm = lax.axis_index("shot"), lax.axis_index("tm")
    block_lines = block // RPL
    length = window * n_tm
    shots = shots_here * n_shot
    sections = station_portion_tallies.shape[0]
    mixtures = measured_mixtures.shape[0]
    paired = n_shot * n_line * n_tm == RPL and n_line == 2 and n_tm == 2 and block_lines == 8
    assert shots_here == 1 and (paired or n_shot == RPL)
    plan = Plan(
        paired=paired,
        shots=shots,
        lines=block_lines if paired else block_lines // n_tm,
        per=RPL // (n_shot * n_tm) if paired else 1,
        sections=sections,
        mixtures=mixtures,
        slabs=length // SLAB,
        each=n_shot,
        time_parts=n_tm,
    )
    lines = plan.lines

    shot_net = (source_entry_kernel, source_spaced_kernel, source_exit_kernel, source_inner_offsets)
    station_net = (station_entry_kernel, station_spaced_kernel, station_exit_kernel, station_inner_offsets)
    if paired:
        *source, shot_net, station_net = run_pack(plan, initial_guess.reshape(block, window), shot_net, station_net)
        source = exchanged(source, ("line", "tm"))
        mixes = measured_mixtures
    else:
        grid = initial_guess.reshape(n_tm, lines, RPL, window)
        leaving = grid.transpose(2, 0, 1, 3).reshape(RPL * n_tm, lines, window)
        arrived = lax.all_to_all(leaving, ("shot", "tm"), split_axis=0, concat_axis=0, tiled=True)
        source = arrived.reshape(n_shot, n_tm, lines, window).transpose(0, 2, 1, 3).reshape(plan.rows, length)
        grid = measured_mixtures.reshape(mixtures, n_tm, lines, RPL, length)
        mixes = lax.dynamic_slice(grid, (0, at_tm, 0, at_shot, 0), (mixtures, 1, lines, 1, length))
        mixes = mixes.reshape(mixtures, lines, length)
        shot_net, station_net = bundled(*shot_net), bundled(*station_net)

    shot_weights = run_prepare(shot_net, "prepare_shot")
    small = (station_portion_tallies, launch_lags, source_launch_order, learned_pace_factors)
    def edges_of(current):
        size = n_line * n_tm
        grid = current.reshape(shots, lines, length)
        up = [(i, i + 1) for i in range(size - 1)]
        down = [(j, i) for i, j in up]
        above = lax.ppermute(grid[:, -1], ("line", "tm"), up)
        below = lax.ppermute(grid[:, 0], ("line", "tm"), down)
        wide = jnp.broadcast_to(jnp.stack([above, below])[:, :, None, :], (2, shots, lines, length))
        return wide.reshape(2, plan.rows, length)

    def summed(value, axis):
        size = lax.axis_size(axis)
        if size <= 4:
            others = [lax.ppermute(value, axis, [(i, i ^ d) for i in range(size)]) for d in range(1, size)]
            return sum(others, value)
        step = 1
        while step < size:
            value = value + lax.ppermute(value, axis, [(i, i ^ step) for i in range(size)])
            step *= 2
        return value

    def shared(energy, along):
        for axis in along:
            energy = summed(energy, axis)
        return energy

    if paired:
        parts = run_stage(
            plan,
            small,
            source,
            shot=([], shot_weights),
            first=True,
            split_in="packets",
            split_out="parts",
            name="shot_pass",
        )
        station_net, mixes, own = lax.optimization_barrier((station_net, mixes, parts[0]))
        mixes, *others = lax.optimization_barrier((run_pick(plan, mixes), *parts[1:-1]))
        current = exchanged([own, *others, parts[-1]], "shot", direct=False)
        station_weights = run_prepare(station_net, "prepare_station")
        energy = sum(jnp.sum(p[0:3, length:].astype(F32), axis=0, keepdims=True) for p in current)
        station_weights, energy = lax.optimization_barrier((station_weights, energy))
        energy = summed(energy, "tm")
    else:
        current, energy = run_stage(plan, small, [source], shot=([edges_of(source)], shot_weights), name="shot_pass")
        energy = shared(energy, ("tm", "shot"))
        station_weights = run_prepare(station_net, "prepare_station")
    for i in range(ITERS):
        station = (i, energy, mixes, station_weights)
        form = {"split_in": "parts"} if paired and i == 0 else {}
        came = current if form else [current]
        if i == ITERS - 1:
            form["split_out"] = "final" if paired else None
            (current,) = run_stage(plan, small, came, station=station, name="station_pass", **form)
        elif paired:
            current, edge = run_stage(
                plan, small, came, station=station, name="station_pass", split_out="edge", **form
            )
            edge = lax.ppermute(edge, "line", [(0, 1), (1, 0)])
            current, energy = run_stage(plan, small, [current], shot=([edge], shot_weights), name="shot_pass")
            fresh, energy = lax.optimization_barrier((station_net, energy))
            station_weights = run_prepare(fresh, "prepare_station")
            energy = shared(energy, ("tm", "shot"))
        else:
            (current,) = run_stage(plan, small, came, station=station, name="station_pass")
            edges = [edges_of(current)]
            current, energy = run_stage(plan, small, [current], shot=(edges, shot_weights), name="shot_pass")
            energy = shared(energy, ("tm", "shot"))
    if paired:
        back = lax.all_to_all(current, ("tm", "shot"), split_axis=0, concat_axis=0, tiled=True)
        back = back.reshape(RPL, lines, window).transpose(1, 0, 2)
    else:
        current = current.reshape(n_shot, lines, n_tm, window).transpose(0, 2, 1, 3).reshape(-1, lines, window)
        back = lax.all_to_all(current, ("shot", "tm"), split_axis=0, concat_axis=0, tiled=True)
        back = back.reshape(RPL, n_tm, lines, window).transpose(1, 2, 0, 3)
    return back.reshape(shots_here, block, window)


def solution(mesh):
    placed = (P(("group", "shot"), "line", "tm"), P("group", "line", None), P("group"), P("group"), P("group"))
    return jax.shard_map(
        per_device,
        mesh=mesh,
        in_specs=placed + (P(),) * 9,
        out_specs=P(("group", "shot"), "line", "tm"),
        check_vma=False,
    )
```

```python
import functools

import jax
import jax.numpy as jnp
from jax import lax
from jax.experimental import pallas as pl
from jax.experimental.pallas import tpu as pltpu
from jax.sharding import PartitionSpec as P

RPL = 16
DMAX = 128
ITERS = 2
EPSILON = 1e-05

SLAB = 128
HALF = 64
FEAT = 64
GROUP = 4
WIDE = GROUP * FEAT
QS = SLAB // (2 * GROUP)
QH = QS // 2
assert QH == 8
ONES = 3 * HALF + 6
VMEM_LIMIT = 24 * 1024 * 1024
VMEM_FULL = 63 * 1024 * 1024

BF = jnp.bfloat16
F32 = jnp.float32


def split_bias(bias):
    high = bias.astype(BF).astype(F32)
    middle = (bias - high).astype(BF).astype(F32)
    return high, middle, bias - high - middle


def iota(shape, axis):
    return lax.broadcasted_iota(jnp.int32, shape, axis)


def picks(mask):
    return mask.astype(F32).astype(BF)


def start_of(q):
    return 16 * (q // 2) + 2 * (q % 2)


def prepare_kernel(bundle, o_in, o_out, rhs, cols):
    rhs[...] = jnp.zeros_like(rhs)
    cols[...] = jnp.zeros_like(cols)
    base = 3 * FEAT
    bias = bundle[base + 16 : base + 24, :]
    parts = split_bias(bias[0:1, :])
    exits = bundle[base : base + 4, :]
    for p in range(GROUP):
        lanes = slice(p * FEAT, (p + 1) * FEAT)
        for c in range(3):
            row = base + 4 * (c + 1)
            rhs[p * 32 + c * 8 : p * 32 + c * 8 + 4, lanes] = bundle[row : row + 4, :]
            rhs[p * 32 + 24 + c : p * 32 + 25 + c, lanes] = parts[c]
        cols[p * 8 : p * 8 + 4, lanes] = exits
    taps = rhs[...].astype(BF)
    row, col = iota((WIDE, SLAB), 0), iota((WIDE, SLAB), 1)
    channel, j, target = (col >> 3) & 3, col & 7, 4 * (col >> 5) + (col & 7) - 1
    rest = row - 3 * HALF
    sample = jnp.where(rest < 0, row & (HALF - 1), jnp.where(rest & 1 == 1, HALF, -1))
    same = (jnp.where(rest < 0, row >> 6, rest >> 1) == channel) & (channel < 3) & (j < 4)
    offset = jnp.where(same, sample - target, -SLAB)
    ones = (channel == 3) & (j < 3) & (row == ONES + j)
    for q in range(QH):
        chosen = picks((offset == start_of(q)) | ones)
        o_in[q] = jnp.dot(chosen, taps, preferred_element_type=F32).astype(BF)
    o_in[QH:] = jnp.zeros((2, WIDE, WIDE), BF)
    for a, at in [(0, 0), (1, 1), (2, 2), (3, 3), (4, 4), (-1, 5)]:
        for b in range(GROUP):
            if abs(a - b) <= 1:
                tap = a - b + 1
                rows, lanes = slice(at % 4 * FEAT, (at % 4 + 1) * FEAT), slice(b * FEAT, (b + 1) * FEAT)
                o_in[QH + at // 4, rows, lanes] = bundle[tap * FEAT : (tap + 1) * FEAT, :].astype(BF)
    row = iota((16, FEAT), 0)
    below = jnp.zeros((16, FEAT), F32)
    for i, part in enumerate(split_bias(bias[1:2, :])):
        below = jnp.where(row == i, part, below)
    for b in range(GROUP):
        o_in[QH + 1, SLAB : SLAB + 16, b * FEAT : (b + 1) * FEAT] = below.astype(BF)
    row, col = iota((SLAB, SLAB), 0), iota((SLAB, SLAB), 1)
    p, j = row >> 3, row & 7
    offset = jnp.where((p < GROUP) & (j < 4), col - (4 * p + j - 1), -SLAB)
    back = jnp.transpose(cols[...]).astype(BF)
    follows = (p == GROUP - 1) & (j == 3) & (col == 0)
    precedes = (row == 0) & (col == SLAB - 1)
    for q in range(QS + 2):
        chosen = picks(offset == start_of(q) if q < QS else [follows, precedes][q - QS])
        o_out[q] = jnp.dot(back, chosen, preferred_element_type=F32).astype(BF)


def pack_kernel(plan, *refs):
    sources, outs, fetched, done = refs[:9], refs[9:15], refs[15:24], refs[24]
    held = fetched[0]
    _, _, at_tm, _, at_line = places(plan, True)
    block = held.shape[0]
    copies = [pltpu.make_async_copy(src, dst, done.at[i]) for i, (src, dst) in enumerate(zip(sources, fetched))]
    for copy in copies:
        copy.start()
    lines = plan.lines
    half = block // 2
    row, col = iota((block, block), 0), iota((block, block), 1)
    spot, line = split_index(row, lines)
    d, spot = split_index(spot, half // lines)
    order = picks(col == line * RPL + (at_tm ^ d) * (half // lines) + spot)
    row, col = iota((32, block), 0), iota((32, block), 1)
    d, spot = split_index(row, 16)
    sent = jnp.where(at_line == 0, lines - 1, 0)
    outer = picks((col == sent * RPL + (at_tm ^ d) * (half // lines) + spot) & (spot < half // lines))
    for copy in copies:
        copy.wait()
    moved = jnp.dot(order, held[...], preferred_element_type=F32).astype(BF)
    edge = jnp.dot(outer, held[...], preferred_element_type=F32).astype(BF)
    outs[0][...] = moved[:half]
    outs[1][...] = moved[half:]
    outs[2][...] = edge[:16]
    outs[3][...] = edge[16:]
    for n, bundle in enumerate(outs[4:6]):
        entry, spaced, leave, bias = fetched[1 + 4 * n : 5 + 4 * n]
        for j in range(3):
            bundle[j * FEAT : (j + 1) * FEAT, :] = spaced[j].astype(F32)
            row = 3 * FEAT + 4 * (j + 1)
            bundle[row : row + 4, :] = entry[j].astype(F32)
        bundle[3 * FEAT : 3 * FEAT + 4, :] = leave[...].astype(F32)
        bundle[3 * FEAT + 16 : 3 * FEAT + 24, :] = jnp.zeros((8, FEAT), F32)
        bundle[3 * FEAT + 16 : 3 * FEAT + 18, :] = bias[...]


def pick_kernel(plan, mixes, picked):
    base = places(plan, False)[0]
    row, col = iota((plan.span, mixes.shape[1]), 0), iota((plan.span, mixes.shape[1]), 1)
    spot, line = split_index(row, plan.lines)
    choose = picks(col == line * RPL + base + spot)
    for g in range(plan.mixtures):
        picked[g] = jnp.dot(choose, mixes[g], preferred_element_type=F32).astype(BF)


def places(plan, first):
    at_shot, at_line, at_tm = (lax.axis_index(a) for a in ("shot", "line", "tm"))
    if not plan.paired:
        return at_shot, at_tm * plan.lines, at_tm, at_shot, at_line
    return at_tm * (RPL // 2) + (0 if first else at_shot * plan.per), 0, at_tm, at_shot, at_line


def split_index(value, size):
    if size & (size - 1):
        return value // size, value % size
    return value >> (size.bit_length() - 1), value & (size - 1)


def section_map(plan, place, tallies, first):
    shape = (plan.rows, SLAB)
    lane = lax.broadcasted_iota(jnp.int32, shape, 1)
    apart, line = split_index(iota(shape, 0), plan.lines)
    if not first:
        apart = split_index(apart, plan.per)[1]
    spot = (line + place[1]) * RPL + place[0] + apart
    low = jnp.zeros(shape, jnp.int32)
    high = jnp.zeros(shape, jnp.int32)
    count = jnp.zeros(shape, jnp.int32)
    start = jnp.int32(0)
    for p in range(plan.sections):
        amount = tallies[p]
        here = lane == p
        low = jnp.where(here, start, low)
        high = jnp.where(here, start + amount, high)
        count = jnp.where(here, amount, count)
        start = start + amount
    member = (spot >= low) & (spot < high)
    return member, count


def shifted(values, by, ok, edge):
    return jnp.where(ok, pltpu.roll(values, by % values.shape[0], 0), edge)


def pack_inputs(plan, channels, packed):
    lane = lax.broadcasted_iota(jnp.int32, (plan.rows, SLAB), 1)
    low = lane < HALF
    ones = ((lane >= ONES - SLAB) & (lane < ONES - SLAB + 3)).astype(F32)
    slabs = [[x[:, t * SLAB : (t + 1) * SLAB] for t in range(plan.slabs)] for x in channels]
    far = [[pltpu.roll(s, HALF + 1 + 2 * c, 1) for s in slabs[c]] for c in range(3)]
    for t in range(plan.slabs):
        v = [slabs[c][t] for c in range(3)]
        w = [pltpu.roll(s, HALF, 1) for s in v]
        even = jnp.where(low, v[2], ones)
        odd = jnp.where(low, w[2], ones)
        for c in range(3):
            left, right = lane == HALF + 2 * c, lane == HALF + 2 * c + 1
            near = pltpu.roll(v[c], 1 + 2 * c, 1)
            even = jnp.where(right, near, even)
            odd = jnp.where(left, near, odd)
            if t > 0:
                even = jnp.where(left, far[c][t - 1], even)
            if t < plan.slabs - 1:
                odd = jnp.where(right, far[c][t + 1], odd)
        packed[0, t, :, 0:SLAB] = jnp.where(low, v[0], w[1]).astype(BF)
        packed[0, t, :, SLAB:WIDE] = even.astype(BF)
        packed[1, t, :, 0:SLAB] = jnp.where(low, w[0], v[1]).astype(BF)
        packed[1, t, :, SLAB:WIDE] = odd.astype(BF)


def network(plan, weights, scratch, regions):
    w_in, w_out = weights
    packed, hidden, total, ends = scratch
    slabs, rows = plan.slabs, plan.rows
    many = slabs * rows
    pitch = slabs + 2

    def first(q):
        taps = jnp.concatenate([w_in[q], w_in[q + 1]], axis=1)
        value = jnp.dot(packed[...].reshape(2 * many, WIDE), taps, preferred_element_type=F32)
        value = jnp.maximum(value.astype(BF), 0).reshape(2, slabs, rows, 2 * WIDE)
        for h in range(2):
            for k in range(2):
                at = pl.ds((q + k + h * QH) * pitch + 1, slabs)
                hidden[at] = value[h, :, :, k * WIDE : (k + 1) * WIDE]

    lane = iota((slabs, rows, SLAB), 2)
    ones = picks(lane < 3)

    def window(q):
        if isinstance(q, int):
            left_at = (q - 2) * pitch + 1 if q >= 2 else (q + QS - 2) * pitch
            right_at = (q + 2) * pitch + 1 if q < QS - 2 else (q + 2 - QS) * pitch + 2
        else:
            left_at = jnp.where(q >= 2, (q - 2) * pitch + 1, (q + QS - 2) * pitch)
            right_at = jnp.where(q < QS - 2, (q + 2) * pitch + 1, (q + 2 - QS) * pitch + 2)
        middle = hidden[pl.ds(q * pitch + 1, slabs)]
        left = hidden[pl.ds(left_at, slabs), :, SLAB:WIDE]
        right = hidden[pl.ds(right_at, slabs), :, 0:SLAB]
        beside = jnp.where(lane < FEAT, right, left)
        return jnp.concatenate([middle, beside, ones], axis=2).reshape(many, 2 * WIDE)

    def second(q):
        both = jnp.concatenate([window(q), window(q + 1)], axis=0)
        value = jnp.dot(both, w_in[QH:].reshape(2 * WIDE, WIDE), preferred_element_type=F32)
        value = jnp.maximum(value.astype(BF), 0)
        return value[:many], value[many:]

    def onto(layer, taps):
        return jnp.dot(layer, taps, preferred_element_type=F32).reshape(slabs, rows, SLAB)

    edge = jnp.zeros((rows, WIDE), BF)
    for k in range(2):
        hidden[(QS - 2 + k) * pitch] = edge
        hidden[(k + 1) * pitch - 1] = edge
    total[...] = jnp.zeros_like(total)

    @regions
    def _():
        for q in range(0, QH, 2):
            first(q)

    @regions
    def _():
        for q in range(0, QS, 2):
            one, two = second(q)
            total[...] += onto(jnp.concatenate([one, two], axis=1), w_out[q : q + 2].reshape(2 * WIDE, SLAB))
            if q == 0:
                ends[0] = one
            if q == QS - 2:
                ends[1] = two

    total[0 : slabs - 1] += onto(ends[0], w_out[QS + 1])[1:]
    total[1:slabs] += onto(ends[1], w_out[QS])[: slabs - 1]


def add_total(plan, now, total, scale=None):
    for t in range(plan.slabs):
        lanes = slice(t * SLAB, (t + 1) * SLAB)
        more = total[t] if scale is None else scale * total[t]
        now[:, lanes] = (now[:, lanes] + more).astype(BF).astype(F32)


def shot_stage(plan, place, tallies, first, edges, weights, now, scratch):
    apart = pl.when(place[0] >= 0)

    @apart
    def _():
        x = now[...]
        line = split_index(iota(x.shape, 0), plan.lines)[1]
        if plan.paired:
            wide = [jnp.broadcast_to(edges[g : g + 1, :], (plan.lines, x.shape[1])) for g in range(plan.groups)]
            wide = jnp.concatenate(wide, axis=0)
            above = jnp.where(place[4] == 1, wide, 0.0)
            below = jnp.where(place[4] == 1, 0.0, wide)
        else:
            above, below = edges[0].astype(F32), edges[1].astype(F32)
        channels = [
            shifted(x, 1, line > 0, above),
            x,
            shifted(x, -1, line < plan.lines - 1, below),
        ]
        pack_inputs(plan, channels, scratch[0])

    network(plan, weights, scratch, apart)
    add_total(plan, now, scratch[2])
    power = jnp.zeros((plan.rows, SLAB), F32)
    for t in range(plan.slabs):
        piece = now[:, t * SLAB : (t + 1) * SLAB]
        power = power + piece * piece
    member, _ = section_map(plan, place, tallies, first)
    each = jnp.where(member, jnp.sum(power, axis=1, keepdims=True), 0.0)
    return jnp.sum(each, axis=0, keepdims=True)


def station_stage(
    plan, place, tallies, lags, order, pace, energies, mixes, weights, now, scratch, blend
):
    fired, misfit, scale = blend
    apart = lambda body: body()

    @apart
    def _():
        member, count = section_map(plan, place, tallies, False)
        denominator = jnp.maximum(count, 1) * (plan.shots * plan.slabs * SLAB)
        level = jnp.sqrt(energies[...] / denominator.astype(F32) + EPSILON)
        rms = jnp.sum(jnp.where(member, level, 0.0), axis=1, keepdims=True)
        scale[...] = jnp.broadcast_to(rms, scale.shape)
        x = (now[...] / rms).astype(BF).astype(F32)
        row = iota(x.shape, 0)
        channels = [
            shifted(x, plan.span, row >= plan.span, 0.0),
            x,
            shifted(x, -plan.span, row < plan.rows - plan.span, 0.0),
        ]
        pack_inputs(plan, channels, scratch[0])

    network(plan, weights, scratch, apart)
    add_total(plan, now, scratch[2], scale[...])
    lane = lax.broadcasted_iota(jnp.int32, (plan.span, SLAB), 1)
    mixtures = misfit.shape[0]
    per = plan.shots // mixtures
    misfit[...] = mixes[...].astype(F32)
    for s in range(plan.shots):
        lag = lags[s]
        before = jnp.zeros((plan.span, SLAB), F32)
        for t in range(plan.slabs):
            lanes = slice(t * SLAB, (t + 1) * SLAB)
            turned = pltpu.roll(now[s * plan.span : (s + 1) * plan.span, lanes], lag, 1)
            fired[s, :, lanes] = jnp.where(lane < lag, before, turned)
            before = turned
    for g in range(mixtures):
        value = fired[order[g * per]]
        for k in range(1, per):
            value = value + fired[order[g * per + k]]
        misfit[g] = value - misfit[g]
    for s in range(plan.shots):
        lag = lags[s]
        spot = jnp.int32(0)
        for k in range(plan.shots):
            spot = spot + jnp.where(order[k] == s, k, 0)
        which = spot // per
        back = (DMAX - lag) % DMAX
        after = jnp.zeros((plan.span, SLAB), F32)
        rows = slice(s * plan.span, (s + 1) * plan.span)
        for t in range(plan.slabs - 1, -1, -1):
            lanes = slice(t * SLAB, (t + 1) * SLAB)
            turned = pltpu.roll(misfit[which, :, lanes], back, 1)
            pulled = jnp.where(lane < DMAX - lag, turned, after)
            after = turned
            now[rows, lanes] = (now[rows, lanes] - pace * pulled).astype(BF).astype(F32)


def stage_kernel(plan, station_round, with_shot, first, split_in, split_out, *refs):
    refs = list(refs)
    take = lambda n: [refs.pop(0) for _ in range(n)]
    tallies, lags, order, paces = take(4)
    place = places(plan, first)
    sources = take(4 if split_in else 1)
    station = station_round is not None
    if station:
        energies, mixes = take(2)
        station_weights = take(2)
    if with_shot:
        edges = take(0 if first else 1)
        shot_weights = take(2)
    results = take({"parts": plan.each, "edge": 2}.get(split_out, 1))
    if with_shot and split_out != "parts":
        (energy,) = take(1)
    now, packed, hidden, total, ends, rim = take(6)
    scratch = (packed, hidden, total, ends)
    length = plan.slabs * SLAB
    if split_in == "parts":
        for d, part in enumerate(sources):
            at = pl.multiple_of((place[3] ^ d) * plan.span, plan.span)
            now[pl.ds(at, plan.span), :] = part[:, 0:length].astype(F32)
    elif split_in:
        share = length // plan.time_parts
        for d in range(2):
            lanes = pl.ds(pl.multiple_of((place[2] ^ d) * share, share), share)
            now[:, lanes] = sources[d][...].astype(F32)
            rim[:, lanes] = sources[2 + d][...].astype(F32)
    else:
        now[...] = sources[0][...].astype(F32)
    if station:
        station_stage(
            plan,
            place,
            tallies,
            lags,
            order,
            paces[station_round],
            energies,
            mixes,
            station_weights,
            now,
            scratch,
            refs,
        )
    if with_shot:
        if plan.paired and not first:
            rim[0 : plan.groups, :] = edges[0][...].astype(F32)
        outer = rim if plan.paired else edges[0]
        sums = shot_stage(plan, place, tallies, first, outer, shot_weights, now, scratch)
    if split_out == "parts":
        row = iota((plan.span, SLAB), 0)
        beside = jnp.zeros((plan.span, SLAB), F32)
        for i, part in enumerate(split_bias(sums)):
            beside = jnp.where(row == i, part, beside)
        for d, part in enumerate(results):
            at = pl.multiple_of((place[3] ^ d) * plan.span, plan.span)
            part[:, 0:length] = now[pl.ds(at, plan.span), :].astype(BF)
            part[:, length:] = beside.astype(BF)
        return
    if with_shot:
        energy[...] = sums
    if split_out == "final":
        share = length // plan.time_parts
        for n in range(results[0].shape[0]):
            b, k = divmod(n, plan.each)
            results[0][n] = now[k * plan.span : (k + 1) * plan.span, b * share : (b + 1) * share].astype(BF)
        return
    results[0][...] = now[...].astype(BF)
    if split_out == "edge":
        row, col = iota((16, plan.rows), 0), iota((16, plan.rows), 1)
        sent = jnp.where(place[4] == 0, plan.lines - 1, 0)
        choose = picks(col == row * plan.lines + sent)
        sent = jnp.dot(choose, now[...].astype(BF), preferred_element_type=F32)
        results[1][...] = sent[: plan.groups].astype(BF)


SMEM = pl.BlockSpec(memory_space=pltpu.SMEM)
VMEM = pl.BlockSpec(memory_space=pltpu.VMEM)
HBM = pl.BlockSpec(memory_space=pltpu.HBM)


def run_stage(plan, small, source, station=None, shot=None, first=False, split_in=None, split_out=None, name="stage"):
    operands = [*small, *source]
    specs = [SMEM] * len(small) + [VMEM] * len(source)
    station_round = None
    macs = 0
    pass_macs = plan.rows * plan.slabs * QS * WIDE * (WIDE * 3 + SLAB)
    if station is not None:
        station_round, energies, mixes, weights = station
        operands += [energies, mixes, *weights]
        specs += [VMEM] * 4
        macs += pass_macs
    if shot is not None:
        edges, weights = shot
        operands += [*edges, *weights]
        specs += [VMEM] * (len(edges) + 2)
        macs += pass_macs
    length = plan.slabs * SLAB
    if split_out == "parts":
        shapes = [jax.ShapeDtypeStruct((plan.span, length + SLAB), BF)] * plan.each
    elif split_out == "final":
        shapes = [jax.ShapeDtypeStruct((plan.each * plan.time_parts, plan.span, length // plan.time_parts), BF)]
    else:
        shapes = [jax.ShapeDtypeStruct((plan.rows, length), BF)]
        if split_out == "edge":
            shapes.append(jax.ShapeDtypeStruct((plan.groups, length), BF))
    if shot is not None and split_out != "parts":
        shapes.append(jax.ShapeDtypeStruct((1, SLAB), F32))
    scratch = [
        pltpu.VMEM((plan.rows, length), F32),
        pltpu.VMEM((2, plan.slabs, plan.rows, WIDE), BF),
        pltpu.VMEM((QS * (plan.slabs + 2), plan.rows, WIDE), BF),
        pltpu.VMEM((plan.slabs, plan.rows, SLAB), F32),
        pltpu.VMEM((2, plan.slabs * plan.rows, WIDE), BF),
        pltpu.VMEM((16, length), F32),
    ]
    if station is not None:
        scratch += [
            pltpu.VMEM((plan.shots, plan.span, length), F32),
            pltpu.VMEM((plan.mixtures, plan.span, length), F32),
            pltpu.VMEM((plan.rows, SLAB), F32),
        ]
    return pl.pallas_call(
        functools.partial(stage_kernel, plan, station_round, shot is not None, first, split_in, split_out),
        out_shape=shapes,
        in_specs=specs,
        out_specs=[VMEM] * len(shapes),
        scratch_shapes=scratch,
        compiler_params=pltpu.CompilerParams(vmem_limit_bytes=VMEM_LIMIT),
        cost_estimate=pl.CostEstimate(flops=2 * macs, bytes_accessed=1 << 20, transcendentals=0),
        name=name,
    )(*operands)


def bundled(entry, spaced, leave, bias):
    rows = [spaced.reshape(3 * FEAT, FEAT), leave, entry.transpose(1, 0, 2).reshape(12, FEAT), bias]
    return jnp.concatenate([r.astype(F32) for r in rows] + [jnp.zeros((6, FEAT), F32)], axis=0)


def run_prepare(bundle, name):
    return pl.pallas_call(
        prepare_kernel,
        out_shape=[
            jax.ShapeDtypeStruct((QH + 2, WIDE, WIDE), BF),
            jax.ShapeDtypeStruct((QS + 2, WIDE, SLAB), BF),
        ],
        in_specs=[VMEM],
        out_specs=[VMEM] * 2,
        scratch_shapes=[pltpu.VMEM((SLAB, WIDE), F32), pltpu.VMEM((SLAB, WIDE), F32)],
        compiler_params=pltpu.CompilerParams(vmem_limit_bytes=VMEM_LIMIT),
        cost_estimate=pl.CostEstimate(flops=2 * 8192 * WIDE * SLAB, bytes_accessed=4 << 20, transcendentals=0),
        name=name,
    )(bundle)


def run_pack(plan, traces, *nets):
    block, width = traces.shape
    operands = [traces]
    for entry, spaced, leave, bias in nets:
        operands += [entry.transpose(1, 0, 2), spaced, leave, bias]
    shapes = [jax.ShapeDtypeStruct((rows, width), BF) for rows in (block // 2, block // 2, 16, 16)]
    shapes += [jax.ShapeDtypeStruct((3 * FEAT + 24, FEAT), F32)] * len(nets)
    return pl.pallas_call(
        functools.partial(pack_kernel, plan),
        out_shape=shapes,
        in_specs=[HBM] * len(operands),
        out_specs=[VMEM] * len(shapes),
        scratch_shapes=[*(pltpu.VMEM(o.shape, o.dtype) for o in operands), pltpu.SemaphoreType.DMA((len(operands),))],
        compiler_params=pltpu.CompilerParams(vmem_limit_bytes=VMEM_FULL),
        cost_estimate=pl.CostEstimate(flops=2 * block * block * width, bytes_accessed=1 << 20, transcendentals=0),
        name="pack",
    )(*operands)


def run_pick(plan, mixes):
    return pl.pallas_call(
        functools.partial(pick_kernel, plan),
        out_shape=jax.ShapeDtypeStruct((plan.mixtures, plan.span, mixes.shape[2]), BF),
        in_specs=[VMEM],
        out_specs=VMEM,
        compiler_params=pltpu.CompilerParams(vmem_limit_bytes=VMEM_LIMIT),
        cost_estimate=pl.CostEstimate(flops=1 << 24, bytes_accessed=1 << 20, transcendentals=0),
        name="pick",
    )(mixes)


class Plan:
    def __init__(self, **sizes):
        self.__dict__.update(sizes)
        self.span = self.lines * self.per
        self.rows = self.shots * self.span
        self.groups = self.rows // self.lines


def exchanged(parts, axes):
    size = len(parts)
    return [parts[0]] + [lax.ppermute(parts[d], axes, [(i, i ^ d) for i in range(size)]) for d in range(1, size)]


def per_device(
    initial_guess,
    measured_mixtures,
    launch_lags,
    source_launch_order,
    station_portion_tallies,
    source_entry_kernel,
    source_spaced_kernel,
    source_exit_kernel,
    source_inner_offsets,
    station_entry_kernel,
    station_spaced_kernel,
    station_exit_kernel,
    station_inner_offsets,
    learned_pace_factors,
):
    shots_here, block, window = initial_guess.shape
    n_shot, n_line, n_tm = (lax.axis_size(a) for a in ("shot", "line", "tm"))
    at_shot, at_tm = lax.axis_index("shot"), lax.axis_index("tm")
    block_lines = block // RPL
    length = window * n_tm
    shots = shots_here * n_shot
    sections = station_portion_tallies.shape[0]
    mixtures = measured_mixtures.shape[0]
    paired = n_shot * n_line * n_tm == RPL and n_line == 2 and n_tm == 2 and block_lines == 8
    assert shots_here == 1 and (paired or n_shot == RPL)
    plan = Plan(
        paired=paired,
        shots=shots,
        lines=block_lines if paired else block_lines // n_tm,
        per=RPL // (n_shot * n_tm) if paired else 1,
        sections=sections,
        mixtures=mixtures,
        slabs=length // SLAB,
        each=n_shot,
        time_parts=n_tm,
    )
    lines = plan.lines

    shot_net = (source_entry_kernel, source_spaced_kernel, source_exit_kernel, source_inner_offsets)
    station_net = (station_entry_kernel, station_spaced_kernel, station_exit_kernel, station_inner_offsets)
    if paired:
        *source, shot_net, station_net = run_pack(plan, initial_guess.reshape(block, window), shot_net, station_net)
        source = exchanged(source, ("line", "tm"))
        mixes = measured_mixtures
    else:
        grid = initial_guess.reshape(n_tm, lines, RPL, window)
        leaving = grid.transpose(2, 0, 1, 3).reshape(RPL * n_tm, lines, window)
        arrived = lax.all_to_all(leaving, ("shot", "tm"), split_axis=0, concat_axis=0, tiled=True)
        source = arrived.reshape(n_shot, n_tm, lines, window).transpose(0, 2, 1, 3).reshape(plan.rows, length)
        grid = measured_mixtures.reshape(mixtures, n_tm, lines, RPL, length)
        mixes = lax.dynamic_slice(grid, (0, at_tm, 0, at_shot, 0), (mixtures, 1, lines, 1, length))
        mixes = mixes.reshape(mixtures, lines, length)
        shot_net, station_net = bundled(*shot_net), bundled(*station_net)

    shot_weights = run_prepare(shot_net, "prepare_shot")
    small = (station_portion_tallies, launch_lags, source_launch_order, learned_pace_factors)
    def edges_of(current):
        size = n_line * n_tm
        grid = current.reshape(shots, lines, length)
        up = [(i, i + 1) for i in range(size - 1)]
        down = [(j, i) for i, j in up]
        above = lax.ppermute(grid[:, -1], ("line", "tm"), up)
        below = lax.ppermute(grid[:, 0], ("line", "tm"), down)
        wide = jnp.broadcast_to(jnp.stack([above, below])[:, :, None, :], (2, shots, lines, length))
        return wide.reshape(2, plan.rows, length)

    def summed(value, axis):
        size = lax.axis_size(axis)
        if size <= 4:
            others = [lax.ppermute(value, axis, [(i, i ^ d) for i in range(size)]) for d in range(1, size)]
            return sum(others, value)
        step = 1
        while step < size:
            value = value + lax.ppermute(value, axis, [(i, i ^ step) for i in range(size)])
            step *= 2
        return value

    def shared(energy, along):
        for axis in along:
            energy = summed(energy, axis)
        return energy

    if paired:
        parts = run_stage(
            plan,
            small,
            source,
            shot=([], shot_weights),
            first=True,
            split_in="packets",
            split_out="parts",
            name="shot_pass",
        )
        station_net, mixes, own = lax.optimization_barrier((station_net, mixes, parts[0]))
        mixes, middle = lax.optimization_barrier((run_pick(plan, mixes), parts[2:-1]))
        station_weights = run_prepare(station_net, "prepare_station")
        station_weights, nearest = lax.optimization_barrier((station_weights, parts[1]))
        current = exchanged([own, nearest, *middle, parts[-1]], "shot")
        energy = sum(jnp.sum(p[0:3, length:].astype(F32), axis=0, keepdims=True) for p in current)
        energy = summed(energy, "tm")
    else:
        current, energy = run_stage(plan, small, [source], shot=([edges_of(source)], shot_weights), name="shot_pass")
        energy = shared(energy, ("tm", "shot"))
        station_weights = run_prepare(station_net, "prepare_station")
    for i in range(ITERS):
        station = (i, energy, mixes, station_weights)
        form = {"split_in": "parts"} if paired and i == 0 else {}
        came = current if form else [current]
        if i == ITERS - 1:
            form["split_out"] = "final" if paired else None
            (current,) = run_stage(plan, small, came, station=station, name="station_pass", **form)
        elif paired:
            current, edge = run_stage(
                plan, small, came, station=station, name="station_pass", split_out="edge", **form
            )
            edge = lax.ppermute(edge, "line", [(0, 1), (1, 0)])
            current, energy = run_stage(plan, small, [current], shot=([edge], shot_weights), name="shot_pass")
            fresh, energy = lax.optimization_barrier((station_net, energy))
            station_weights = run_prepare(fresh, "prepare_station")
            energy = shared(energy, ("tm", "shot"))
        else:
            (current,) = run_stage(plan, small, came, station=station, name="station_pass")
            edges = [edges_of(current)]
            current, energy = run_stage(plan, small, [current], shot=(edges, shot_weights), name="shot_pass")
            energy = shared(energy, ("tm", "shot"))
    if paired:
        back = lax.all_to_all(current, ("tm", "shot"), split_axis=0, concat_axis=0, tiled=True)
        back = back.reshape(RPL, lines, window).transpose(1, 0, 2)
    else:
        current = current.reshape(n_shot, lines, n_tm, window).transpose(0, 2, 1, 3).reshape(-1, lines, window)
        back = lax.all_to_all(current, ("shot", "tm"), split_axis=0, concat_axis=0, tiled=True)
        back = back.reshape(RPL, n_tm, lines, window).transpose(1, 2, 0, 3)
    return back.reshape(shots_here, block, window)


def solution(mesh):
    placed = (P(("group", "shot"), "line", "tm"), P("group", "line", None), P("group"), P("group"), P("group"))
    return jax.shard_map(
        per_device,
        mesh=mesh,
        in_specs=placed + (P(),) * 9,
        out_specs=P(("group", "shot"), "line", "tm"),
        check_vma=False,
    )
```

```python
import functools

import jax
import jax.numpy as jnp
from jax import lax
from jax.experimental import pallas as pl
from jax.experimental.pallas import tpu as pltpu
from jax.sharding import PartitionSpec as P

RPL = 16
DMAX = 128
ITERS = 2
EPSILON = 1e-05

SLAB = 128
HALF = 64
FEAT = 64
GROUP = 4
WIDE = GROUP * FEAT
QS = SLAB // (2 * GROUP)
QH = QS // 2
assert QH == 8
ONES = 3 * HALF + 6
VMEM_LIMIT = 24 * 1024 * 1024
VMEM_FULL = 63 * 1024 * 1024

BF = jnp.bfloat16
F32 = jnp.float32


def split_bias(bias):
    high = bias.astype(BF).astype(F32)
    middle = (bias - high).astype(BF).astype(F32)
    return high, middle, bias - high - middle


def iota(shape, axis):
    return lax.broadcasted_iota(jnp.int32, shape, axis)


def picks(mask):
    return mask.astype(F32).astype(BF)


def start_of(q):
    return 16 * (q // 2) + 2 * (q % 2)


def prepare_kernel(bundle, o_in, o_out, rhs, cols):
    rhs[...] = jnp.zeros_like(rhs)
    cols[...] = jnp.zeros_like(cols)
    base = 3 * FEAT
    bias = bundle[base + 16 : base + 24, :]
    parts = split_bias(bias[0:1, :])
    exits = bundle[base : base + 4, :]
    for p in range(GROUP):
        lanes = slice(p * FEAT, (p + 1) * FEAT)
        for c in range(3):
            row = base + 4 * (c + 1)
            rhs[p * 32 + c * 8 : p * 32 + c * 8 + 4, lanes] = bundle[row : row + 4, :]
            rhs[p * 32 + 24 + c : p * 32 + 25 + c, lanes] = parts[c]
        cols[p * 8 : p * 8 + 4, lanes] = exits
    taps = rhs[...].astype(BF)
    row, col = iota((WIDE, SLAB), 0), iota((WIDE, SLAB), 1)
    channel, j, target = (col >> 3) & 3, col & 7, 4 * (col >> 5) + (col & 7) - 1
    rest = row - 3 * HALF
    sample = jnp.where(rest < 0, row & (HALF - 1), jnp.where(rest & 1 == 1, HALF, -1))
    same = (jnp.where(rest < 0, row >> 6, rest >> 1) == channel) & (channel < 3) & (j < 4)
    offset = jnp.where(same, sample - target, -SLAB)
    ones = (channel == 3) & (j < 3) & (row == ONES + j)
    for q in range(QH):
        chosen = picks((offset == start_of(q)) | ones)
        o_in[q] = jnp.dot(chosen, taps, preferred_element_type=F32).astype(BF)
    o_in[QH:] = jnp.zeros((2, WIDE, WIDE), BF)
    for a, at in [(0, 0), (1, 1), (2, 2), (3, 3), (4, 4), (-1, 5)]:
        for b in range(GROUP):
            if abs(a - b) <= 1:
                tap = a - b + 1
                rows, lanes = slice(at % 4 * FEAT, (at % 4 + 1) * FEAT), slice(b * FEAT, (b + 1) * FEAT)
                o_in[QH + at // 4, rows, lanes] = bundle[tap * FEAT : (tap + 1) * FEAT, :].astype(BF)
    row = iota((16, FEAT), 0)
    below = jnp.zeros((16, FEAT), F32)
    for i, part in enumerate(split_bias(bias[1:2, :])):
        below = jnp.where(row == i, part, below)
    for b in range(GROUP):
        o_in[QH + 1, SLAB : SLAB + 16, b * FEAT : (b + 1) * FEAT] = below.astype(BF)
    row, col = iota((SLAB, SLAB), 0), iota((SLAB, SLAB), 1)
    p, j = row >> 3, row & 7
    offset = jnp.where((p < GROUP) & (j < 4), col - (4 * p + j - 1), -SLAB)
    back = jnp.transpose(cols[...]).astype(BF)
    follows = (p == GROUP - 1) & (j == 3) & (col == 0)
    precedes = (row == 0) & (col == SLAB - 1)
    for q in range(QS + 2):
        chosen = picks(offset == start_of(q) if q < QS else [follows, precedes][q - QS])
        o_out[q] = jnp.dot(back, chosen, preferred_element_type=F32).astype(BF)


def pack_kernel(plan, *refs):
    sources, outs, fetched, done = refs[:9], refs[9:15], refs[15:24], refs[24]
    held = fetched[0]
    _, _, at_tm, _, at_line = places(plan, True)
    block = held.shape[0]
    copies = [pltpu.make_async_copy(src, dst, done.at[i]) for i, (src, dst) in enumerate(zip(sources, fetched))]
    for copy in copies:
        copy.start()
    lines = plan.lines
    half = block // 2
    row, col = iota((block, block), 0), iota((block, block), 1)
    spot, line = split_index(row, lines)
    d, spot = split_index(spot, half // lines)
    order = picks(col == line * RPL + (at_tm ^ d) * (half // lines) + spot)
    row, col = iota((32, block), 0), iota((32, block), 1)
    d, spot = split_index(row, 16)
    sent = jnp.where(at_line == 0, lines - 1, 0)
    outer = picks((col == sent * RPL + (at_tm ^ d) * (half // lines) + spot) & (spot < half // lines))
    for copy in copies:
        copy.wait()
    moved = jnp.dot(order, held[...], preferred_element_type=F32).astype(BF)
    edge = jnp.dot(outer, held[...], preferred_element_type=F32).astype(BF)
    outs[0][...] = moved[:half]
    outs[1][...] = moved[half:]
    outs[2][...] = edge[:16]
    outs[3][...] = edge[16:]
    for n, bundle in enumerate(outs[4:6]):
        entry, spaced, leave, bias = fetched[1 + 4 * n : 5 + 4 * n]
        for j in range(3):
            bundle[j * FEAT : (j + 1) * FEAT, :] = spaced[j].astype(F32)
            row = 3 * FEAT + 4 * (j + 1)
            bundle[row : row + 4, :] = entry[j].astype(F32)
        bundle[3 * FEAT : 3 * FEAT + 4, :] = leave[...].astype(F32)
        bundle[3 * FEAT + 16 : 3 * FEAT + 24, :] = jnp.zeros((8, FEAT), F32)
        bundle[3 * FEAT + 16 : 3 * FEAT + 18, :] = bias[...]


def pick_kernel(plan, mixes, picked):
    base = places(plan, False)[0]
    row, col = iota((plan.span, mixes.shape[1]), 0), iota((plan.span, mixes.shape[1]), 1)
    spot, line = split_index(row, plan.lines)
    choose = picks(col == line * RPL + base + spot)
    for g in range(plan.mixtures):
        picked[g] = jnp.dot(choose, mixes[g], preferred_element_type=F32).astype(BF)


def places(plan, first):
    at_shot, at_line, at_tm = (lax.axis_index(a) for a in ("shot", "line", "tm"))
    if not plan.paired:
        return at_shot, at_tm * plan.lines, at_tm, at_shot, at_line
    return at_tm * (RPL // 2) + (0 if first else at_shot * plan.per), 0, at_tm, at_shot, at_line


def split_index(value, size):
    if size & (size - 1):
        return value // size, value % size
    return value >> (size.bit_length() - 1), value & (size - 1)


def section_map(plan, place, tallies, first):
    shape = (plan.rows, SLAB)
    lane = lax.broadcasted_iota(jnp.int32, shape, 1)
    apart, line = split_index(iota(shape, 0), plan.lines)
    if not first:
        apart = split_index(apart, plan.per)[1]
    spot = (line + place[1]) * RPL + place[0] + apart
    low = jnp.zeros(shape, jnp.int32)
    high = jnp.zeros(shape, jnp.int32)
    count = jnp.zeros(shape, jnp.int32)
    start = jnp.int32(0)
    for p in range(plan.sections):
        amount = tallies[p]
        here = lane == p
        low = jnp.where(here, start, low)
        high = jnp.where(here, start + amount, high)
        count = jnp.where(here, amount, count)
        start = start + amount
    member = (spot >= low) & (spot < high)
    return member, count


def shifted(values, by, ok, edge):
    return jnp.where(ok, pltpu.roll(values, by % values.shape[0], 0), edge)


def pack_inputs(plan, channels, packed):
    lane = lax.broadcasted_iota(jnp.int32, (plan.rows, SLAB), 1)
    low = lane < HALF
    ones = ((lane >= ONES - SLAB) & (lane < ONES - SLAB + 3)).astype(F32)
    slabs = [[x[:, t * SLAB : (t + 1) * SLAB] for t in range(plan.slabs)] for x in channels]
    far = [[pltpu.roll(s, HALF + 1 + 2 * c, 1) for s in slabs[c]] for c in range(3)]
    for t in range(plan.slabs):
        v = [slabs[c][t] for c in range(3)]
        w = [pltpu.roll(s, HALF, 1) for s in v]
        even = jnp.where(low, v[2], ones)
        odd = jnp.where(low, w[2], ones)
        for c in range(3):
            left, right = lane == HALF + 2 * c, lane == HALF + 2 * c + 1
            near = pltpu.roll(v[c], 1 + 2 * c, 1)
            even = jnp.where(right, near, even)
            odd = jnp.where(left, near, odd)
            if t > 0:
                even = jnp.where(left, far[c][t - 1], even)
            if t < plan.slabs - 1:
                odd = jnp.where(right, far[c][t + 1], odd)
        packed[0, t, :, 0:SLAB] = jnp.where(low, v[0], w[1]).astype(BF)
        packed[0, t, :, SLAB:WIDE] = even.astype(BF)
        packed[1, t, :, 0:SLAB] = jnp.where(low, w[0], v[1]).astype(BF)
        packed[1, t, :, SLAB:WIDE] = odd.astype(BF)


def network(plan, weights, scratch, regions):
    w_in, w_out = weights
    packed, hidden, total, ends = scratch
    slabs, rows = plan.slabs, plan.rows
    many = slabs * rows
    pitch = slabs + 2

    def first(q):
        taps = jnp.concatenate([w_in[q], w_in[q + 1]], axis=1)
        value = jnp.dot(packed[...].reshape(2 * many, WIDE), taps, preferred_element_type=F32)
        value = jnp.maximum(value.astype(BF), 0).reshape(2, slabs, rows, 2 * WIDE)
        for h in range(2):
            for k in range(2):
                at = pl.ds((q + k + h * QH) * pitch + 1, slabs)
                hidden[at] = value[h, :, :, k * WIDE : (k + 1) * WIDE]

    lane = iota((slabs, rows, SLAB), 2)
    ones = picks(lane < 3)

    def window(q):
        if isinstance(q, int):
            left_at = (q - 2) * pitch + 1 if q >= 2 else (q + QS - 2) * pitch
            right_at = (q + 2) * pitch + 1 if q < QS - 2 else (q + 2 - QS) * pitch + 2
        else:
            left_at = jnp.where(q >= 2, (q - 2) * pitch + 1, (q + QS - 2) * pitch)
            right_at = jnp.where(q < QS - 2, (q + 2) * pitch + 1, (q + 2 - QS) * pitch + 2)
        middle = hidden[pl.ds(q * pitch + 1, slabs)]
        left = hidden[pl.ds(left_at, slabs), :, SLAB:WIDE]
        right = hidden[pl.ds(right_at, slabs), :, 0:SLAB]
        beside = jnp.where(lane < FEAT, right, left)
        return jnp.concatenate([middle, beside, ones], axis=2).reshape(many, 2 * WIDE)

    def second(q):
        both = jnp.concatenate([window(q), window(q + 1)], axis=0)
        value = jnp.dot(both, w_in[QH:].reshape(2 * WIDE, WIDE), preferred_element_type=F32)
        value = jnp.maximum(value.astype(BF), 0)
        return value[:many], value[many:]

    def onto(layer, taps):
        return jnp.dot(layer, taps, preferred_element_type=F32).reshape(slabs, rows, SLAB)

    edge = jnp.zeros((rows, WIDE), BF)
    for k in range(2):
        hidden[(QS - 2 + k) * pitch] = edge
        hidden[(k + 1) * pitch - 1] = edge

    @regions
    def _():
        for q in range(0, QH, 2):
            first(q)

    @regions
    def _():
        for q in range(0, QS, 2):
            one, two = second(q)
            value = onto(jnp.concatenate([one, two], axis=1), w_out[q : q + 2].reshape(2 * WIDE, SLAB))
            total[...] = value if q == 0 else total[...] + value
            if q == 0:
                ends[0] = one
            if q == QS - 2:
                ends[1] = two

    total[0 : slabs - 1] += onto(ends[0], w_out[QS + 1])[1:]
    total[1:slabs] += onto(ends[1], w_out[QS])[: slabs - 1]


def add_total(plan, now, total, scale=None):
    for t in range(plan.slabs):
        lanes = slice(t * SLAB, (t + 1) * SLAB)
        more = total[t] if scale is None else scale * total[t]
        value = (now[:, lanes] + more).astype(BF).astype(F32)
        now[:, lanes] = value
        power = value * value if t == 0 else power + value * value
    return power


def shot_stage(plan, place, tallies, first, edges, weights, now, scratch):
    apart = pl.when(place[0] >= 0)

    @apart
    def _():
        x = now[...]
        line = split_index(iota(x.shape, 0), plan.lines)[1]
        if plan.paired:
            wide = [jnp.broadcast_to(edges[g : g + 1, :], (plan.lines, x.shape[1])) for g in range(plan.groups)]
            wide = jnp.concatenate(wide, axis=0)
            above = jnp.where(place[4] == 1, wide, 0.0)
            below = jnp.where(place[4] == 1, 0.0, wide)
        else:
            above, below = edges[0].astype(F32), edges[1].astype(F32)
        channels = [
            shifted(x, 1, line > 0, above),
            x,
            shifted(x, -1, line < plan.lines - 1, below),
        ]
        pack_inputs(plan, channels, scratch[0])

    network(plan, weights, scratch, lambda body: body())
    power = add_total(plan, now, scratch[2])
    member, _ = section_map(plan, place, tallies, first)
    each = jnp.where(member, jnp.sum(power, axis=1, keepdims=True), 0.0)
    return jnp.sum(each, axis=0, keepdims=True)


def station_stage(
    plan, place, tallies, lags, order, pace, energies, mixes, weights, now, scratch, blend
):
    fired, misfit, scale = blend
    apart = lambda body: body()

    @apart
    def _():
        member, count = section_map(plan, place, tallies, False)
        denominator = jnp.maximum(count, 1) * (plan.shots * plan.slabs * SLAB)
        level = jnp.sqrt(energies[...] / denominator.astype(F32) + EPSILON)
        rms = jnp.sum(jnp.where(member, level, 0.0), axis=1, keepdims=True)
        scale[...] = jnp.broadcast_to(rms, scale.shape)
        x = (now[...] / rms).astype(BF).astype(F32)
        row = iota(x.shape, 0)
        channels = [
            shifted(x, plan.span, row >= plan.span, 0.0),
            x,
            shifted(x, -plan.span, row < plan.rows - plan.span, 0.0),
        ]
        pack_inputs(plan, channels, scratch[0])

    network(plan, weights, scratch, apart)
    add_total(plan, now, scratch[2], scale[...])
    lane = lax.broadcasted_iota(jnp.int32, (plan.span, SLAB), 1)
    mixtures = misfit.shape[0]
    per = plan.shots // mixtures
    misfit[...] = mixes[...].astype(F32)
    for s in range(plan.shots):
        lag = lags[s]
        before = jnp.zeros((plan.span, SLAB), F32)
        for t in range(plan.slabs):
            lanes = slice(t * SLAB, (t + 1) * SLAB)
            turned = pltpu.roll(now[s * plan.span : (s + 1) * plan.span, lanes], lag, 1)
            fired[s, :, lanes] = jnp.where(lane < lag, before, turned)
            before = turned
    for g in range(mixtures):
        value = fired[order[g * per]]
        for k in range(1, per):
            value = value + fired[order[g * per + k]]
        misfit[g] = value - misfit[g]
    for s in range(plan.shots):
        lag = lags[s]
        spot = jnp.int32(0)
        for k in range(plan.shots):
            spot = spot + jnp.where(order[k] == s, k, 0)
        which = spot // per
        back = (DMAX - lag) % DMAX
        after = jnp.zeros((plan.span, SLAB), F32)
        rows = slice(s * plan.span, (s + 1) * plan.span)
        for t in range(plan.slabs - 1, -1, -1):
            lanes = slice(t * SLAB, (t + 1) * SLAB)
            turned = pltpu.roll(misfit[which, :, lanes], back, 1)
            pulled = jnp.where(lane < DMAX - lag, turned, after)
            after = turned
            now[rows, lanes] = (now[rows, lanes] - pace * pulled).astype(BF).astype(F32)


def stage_kernel(plan, station_round, with_shot, first, split_in, split_out, *refs):
    refs = list(refs)
    take = lambda n: [refs.pop(0) for _ in range(n)]
    tallies, lags, order, paces = take(4)
    place = places(plan, first)
    sources = take(4 if split_in else 1)
    station = station_round is not None
    if station:
        energies, mixes = take(2)
        station_weights = take(2)
    if with_shot:
        edges = take(0 if first else 1)
        shot_weights = take(2)
    results = take({"parts": plan.each, "edge": 2}.get(split_out, 1))
    if with_shot and split_out != "parts":
        (energy,) = take(1)
    now, packed, hidden, total, ends, rim = take(6)
    scratch = (packed, hidden, total, ends)
    length = plan.slabs * SLAB
    if split_in == "parts":
        for d, part in enumerate(sources):
            at = pl.multiple_of((place[3] ^ d) * plan.span, plan.span)
            now[pl.ds(at, plan.span), :] = part[:, 0:length].astype(F32)
    elif split_in:
        share = length // plan.time_parts
        for d in range(2):
            lanes = pl.ds(pl.multiple_of((place[2] ^ d) * share, share), share)
            now[:, lanes] = sources[d][...].astype(F32)
            rim[:, lanes] = sources[2 + d][...].astype(F32)
    else:
        now[...] = sources[0][...].astype(F32)
    if station:
        station_stage(
            plan,
            place,
            tallies,
            lags,
            order,
            paces[station_round],
            energies,
            mixes,
            station_weights,
            now,
            scratch,
            refs,
        )
    if with_shot:
        if plan.paired and not first:
            rim[0 : plan.groups, :] = edges[0][...].astype(F32)
        outer = rim if plan.paired else edges[0]
        sums = shot_stage(plan, place, tallies, first, outer, shot_weights, now, scratch)
    if split_out == "parts":
        row = iota((plan.span, SLAB), 0)
        beside = jnp.zeros((plan.span, SLAB), F32)
        for i, part in enumerate(split_bias(sums)):
            beside = jnp.where(row == i, part, beside)
        for d, part in enumerate(results):
            at = pl.multiple_of((place[3] ^ d) * plan.span, plan.span)
            part[:, 0:length] = now[pl.ds(at, plan.span), :].astype(BF)
            part[:, length:] = beside.astype(BF)
        return
    if with_shot:
        energy[...] = sums
    if split_out == "final":
        share = length // plan.time_parts
        for n in range(results[0].shape[0]):
            b, k = divmod(n, plan.each)
            results[0][n] = now[k * plan.span : (k + 1) * plan.span, b * share : (b + 1) * share].astype(BF)
        return
    results[0][...] = now[...].astype(BF)
    if split_out == "edge":
        row, col = iota((16, plan.rows), 0), iota((16, plan.rows), 1)
        sent = jnp.where(place[4] == 0, plan.lines - 1, 0)
        choose = picks(col == row * plan.lines + sent)
        sent = jnp.dot(choose, now[...].astype(BF), preferred_element_type=F32)
        results[1][...] = sent[: plan.groups].astype(BF)


SMEM = pl.BlockSpec(memory_space=pltpu.SMEM)
VMEM = pl.BlockSpec(memory_space=pltpu.VMEM)
HBM = pl.BlockSpec(memory_space=pltpu.HBM)


def run_stage(plan, small, source, station=None, shot=None, first=False, split_in=None, split_out=None, name="stage"):
    operands = [*small, *source]
    specs = [SMEM] * len(small) + [VMEM] * len(source)
    station_round = None
    macs = 0
    pass_macs = plan.rows * plan.slabs * QS * WIDE * (WIDE * 3 + SLAB)
    if station is not None:
        station_round, energies, mixes, weights = station
        operands += [energies, mixes, *weights]
        specs += [VMEM] * 4
        macs += pass_macs
    if shot is not None:
        edges, weights = shot
        operands += [*edges, *weights]
        specs += [VMEM] * (len(edges) + 2)
        macs += pass_macs
    length = plan.slabs * SLAB
    if split_out == "parts":
        shapes = [jax.ShapeDtypeStruct((plan.span, length + SLAB), BF)] * plan.each
    elif split_out == "final":
        shapes = [jax.ShapeDtypeStruct((plan.each * plan.time_parts, plan.span, length // plan.time_parts), BF)]
    else:
        shapes = [jax.ShapeDtypeStruct((plan.rows, length), BF)]
        if split_out == "edge":
            shapes.append(jax.ShapeDtypeStruct((plan.groups, length), BF))
    if shot is not None and split_out != "parts":
        shapes.append(jax.ShapeDtypeStruct((1, SLAB), F32))
    scratch = [
        pltpu.VMEM((plan.rows, length), F32),
        pltpu.VMEM((2, plan.slabs, plan.rows, WIDE), BF),
        pltpu.VMEM((QS * (plan.slabs + 2), plan.rows, WIDE), BF),
        pltpu.VMEM((plan.slabs, plan.rows, SLAB), F32),
        pltpu.VMEM((2, plan.slabs * plan.rows, WIDE), BF),
        pltpu.VMEM((16, length), F32),
    ]
    if station is not None:
        scratch += [
            pltpu.VMEM((plan.shots, plan.span, length), F32),
            pltpu.VMEM((plan.mixtures, plan.span, length), F32),
            pltpu.VMEM((plan.rows, SLAB), F32),
        ]
    return pl.pallas_call(
        functools.partial(stage_kernel, plan, station_round, shot is not None, first, split_in, split_out),
        out_shape=shapes,
        in_specs=specs,
        out_specs=[VMEM] * len(shapes),
        scratch_shapes=scratch,
        compiler_params=pltpu.CompilerParams(vmem_limit_bytes=VMEM_LIMIT),
        cost_estimate=pl.CostEstimate(flops=2 * macs, bytes_accessed=1 << 20, transcendentals=0),
        name=name,
    )(*operands)


def bundled(entry, spaced, leave, bias):
    rows = [spaced.reshape(3 * FEAT, FEAT), leave, entry.transpose(1, 0, 2).reshape(12, FEAT), bias]
    return jnp.concatenate([r.astype(F32) for r in rows] + [jnp.zeros((6, FEAT), F32)], axis=0)


def run_prepare(bundle, name):
    return pl.pallas_call(
        prepare_kernel,
        out_shape=[
            jax.ShapeDtypeStruct((QH + 2, WIDE, WIDE), BF),
            jax.ShapeDtypeStruct((QS + 2, WIDE, SLAB), BF),
        ],
        in_specs=[VMEM],
        out_specs=[VMEM] * 2,
        scratch_shapes=[pltpu.VMEM((SLAB, WIDE), F32), pltpu.VMEM((SLAB, WIDE), F32)],
        compiler_params=pltpu.CompilerParams(vmem_limit_bytes=VMEM_LIMIT),
        cost_estimate=pl.CostEstimate(flops=2 * 8192 * WIDE * SLAB, bytes_accessed=4 << 20, transcendentals=0),
        name=name,
    )(bundle)


def run_pack(plan, traces, *nets):
    block, width = traces.shape
    operands = [traces]
    for entry, spaced, leave, bias in nets:
        operands += [entry.transpose(1, 0, 2), spaced, leave, bias]
    shapes = [jax.ShapeDtypeStruct((rows, width), BF) for rows in (block // 2, block // 2, 16, 16)]
    shapes += [jax.ShapeDtypeStruct((3 * FEAT + 24, FEAT), F32)] * len(nets)
    return pl.pallas_call(
        functools.partial(pack_kernel, plan),
        out_shape=shapes,
        in_specs=[HBM] * len(operands),
        out_specs=[VMEM] * len(shapes),
        scratch_shapes=[*(pltpu.VMEM(o.shape, o.dtype) for o in operands), pltpu.SemaphoreType.DMA((len(operands),))],
        compiler_params=pltpu.CompilerParams(vmem_limit_bytes=VMEM_FULL),
        cost_estimate=pl.CostEstimate(flops=2 * block * block * width, bytes_accessed=1 << 20, transcendentals=0),
        name="pack",
    )(*operands)


def run_pick(plan, mixes):
    return pl.pallas_call(
        functools.partial(pick_kernel, plan),
        out_shape=jax.ShapeDtypeStruct((plan.mixtures, plan.span, mixes.shape[2]), BF),
        in_specs=[VMEM],
        out_specs=VMEM,
        compiler_params=pltpu.CompilerParams(vmem_limit_bytes=VMEM_LIMIT),
        cost_estimate=pl.CostEstimate(flops=1 << 24, bytes_accessed=1 << 20, transcendentals=0),
        name="pick",
    )(mixes)


class Plan:
    def __init__(self, **sizes):
        self.__dict__.update(sizes)
        self.span = self.lines * self.per
        self.rows = self.shots * self.span
        self.groups = self.rows // self.lines


def exchanged(parts, axes):
    size = len(parts)
    return [parts[0]] + [lax.ppermute(parts[d], axes, [(i, i ^ d) for i in range(size)]) for d in range(1, size)]


def per_device(
    initial_guess,
    measured_mixtures,
    launch_lags,
    source_launch_order,
    station_portion_tallies,
    source_entry_kernel,
    source_spaced_kernel,
    source_exit_kernel,
    source_inner_offsets,
    station_entry_kernel,
    station_spaced_kernel,
    station_exit_kernel,
    station_inner_offsets,
    learned_pace_factors,
):
    shots_here, block, window = initial_guess.shape
    n_shot, n_line, n_tm = (lax.axis_size(a) for a in ("shot", "line", "tm"))
    at_shot, at_tm = lax.axis_index("shot"), lax.axis_index("tm")
    block_lines = block // RPL
    length = window * n_tm
    shots = shots_here * n_shot
    sections = station_portion_tallies.shape[0]
    mixtures = measured_mixtures.shape[0]
    paired = n_shot * n_line * n_tm == RPL and n_line == 2 and n_tm == 2 and block_lines == 8
    assert shots_here == 1 and (paired or n_shot == RPL)
    plan = Plan(
        paired=paired,
        shots=shots,
        lines=block_lines if paired else block_lines // n_tm,
        per=RPL // (n_shot * n_tm) if paired else 1,
        sections=sections,
        mixtures=mixtures,
        slabs=length // SLAB,
        each=n_shot,
        time_parts=n_tm,
    )
    lines = plan.lines

    shot_net = (source_entry_kernel, source_spaced_kernel, source_exit_kernel, source_inner_offsets)
    station_net = (station_entry_kernel, station_spaced_kernel, station_exit_kernel, station_inner_offsets)
    if paired:
        *source, shot_net, station_net = run_pack(plan, initial_guess.reshape(block, window), shot_net, station_net)
        source = exchanged(source, ("line", "tm"))
        mixes = measured_mixtures
    else:
        grid = initial_guess.reshape(n_tm, lines, RPL, window)
        leaving = grid.transpose(2, 0, 1, 3).reshape(RPL * n_tm, lines, window)
        arrived = lax.all_to_all(leaving, ("shot", "tm"), split_axis=0, concat_axis=0, tiled=True)
        source = arrived.reshape(n_shot, n_tm, lines, window).transpose(0, 2, 1, 3).reshape(plan.rows, length)
        grid = measured_mixtures.reshape(mixtures, n_tm, lines, RPL, length)
        mixes = lax.dynamic_slice(grid, (0, at_tm, 0, at_shot, 0), (mixtures, 1, lines, 1, length))
        mixes = mixes.reshape(mixtures, lines, length)
        shot_net, station_net = bundled(*shot_net), bundled(*station_net)

    shot_weights = run_prepare(shot_net, "prepare_shot")
    small = (station_portion_tallies, launch_lags, source_launch_order, learned_pace_factors)
    def edges_of(current):
        size = n_line * n_tm
        grid = current.reshape(shots, lines, length)
        up = [(i, i + 1) for i in range(size - 1)]
        down = [(j, i) for i, j in up]
        above = lax.ppermute(grid[:, -1], ("line", "tm"), up)
        below = lax.ppermute(grid[:, 0], ("line", "tm"), down)
        wide = jnp.broadcast_to(jnp.stack([above, below])[:, :, None, :], (2, shots, lines, length))
        return wide.reshape(2, plan.rows, length)

    def summed(value, axis):
        size = lax.axis_size(axis)
        if size <= 4:
            others = [lax.ppermute(value, axis, [(i, i ^ d) for i in range(size)]) for d in range(1, size)]
            return sum(others, value)
        step = 1
        while step < size:
            value = value + lax.ppermute(value, axis, [(i, i ^ step) for i in range(size)])
            step *= 2
        return value

    def shared(energy, along):
        for axis in along:
            energy = summed(energy, axis)
        return energy

    if paired:
        parts = run_stage(
            plan,
            small,
            source,
            shot=([], shot_weights),
            first=True,
            split_in="packets",
            split_out="parts",
            name="shot_pass",
        )
        station_net, mixes, own = lax.optimization_barrier((station_net, mixes, parts[0]))
        mixes, middle = lax.optimization_barrier((run_pick(plan, mixes), parts[2:-1]))
        station_weights = run_prepare(station_net, "prepare_station")
        station_weights, nearest = lax.optimization_barrier((station_weights, parts[1]))
        current = exchanged([own, nearest, *middle, parts[-1]], "shot")
        energy = sum(jnp.sum(p[0:3, length:].astype(F32), axis=0, keepdims=True) for p in current)
        energy = summed(energy, "tm")
    else:
        current, energy = run_stage(plan, small, [source], shot=([edges_of(source)], shot_weights), name="shot_pass")
        energy = shared(energy, ("tm", "shot"))
        station_weights = run_prepare(station_net, "prepare_station")
    for i in range(ITERS):
        station = (i, energy, mixes, station_weights)
        form = {"split_in": "parts"} if paired and i == 0 else {}
        came = current if form else [current]
        if i == ITERS - 1:
            form["split_out"] = "final" if paired else None
            (current,) = run_stage(plan, small, came, station=station, name="station_pass", **form)
        elif paired:
            current, edge = run_stage(
                plan, small, came, station=station, name="station_pass", split_out="edge", **form
            )
            edge = lax.ppermute(edge, "line", [(0, 1), (1, 0)])
            current, energy = run_stage(plan, small, [current], shot=([edge], shot_weights), name="shot_pass")
            fresh, energy = lax.optimization_barrier((station_net, energy))
            station_weights = run_prepare(fresh, "prepare_station")
            energy = shared(energy, ("tm", "shot"))
        else:
            (current,) = run_stage(plan, small, came, station=station, name="station_pass")
            edges = [edges_of(current)]
            current, energy = run_stage(plan, small, [current], shot=(edges, shot_weights), name="shot_pass")
            energy = shared(energy, ("tm", "shot"))
    if paired:
        back = lax.all_to_all(current, ("tm", "shot"), split_axis=0, concat_axis=0, tiled=True)
        back = back.reshape(RPL, lines, window).transpose(1, 0, 2)
    else:
        current = current.reshape(n_shot, lines, n_tm, window).transpose(0, 2, 1, 3).reshape(-1, lines, window)
        back = lax.all_to_all(current, ("shot", "tm"), split_axis=0, concat_axis=0, tiled=True)
        back = back.reshape(RPL, n_tm, lines, window).transpose(1, 2, 0, 3)
    return back.reshape(shots_here, block, window)


def solution(mesh):
    placed = (P(("group", "shot"), "line", "tm"), P("group", "line", None), P("group"), P("group"), P("group"))
    return jax.shard_map(
        per_device,
        mesh=mesh,
        in_specs=placed + (P(),) * 9,
        out_specs=P(("group", "shot"), "line", "tm"),
        check_vma=False,
    )
```

```python
import functools

import jax
import jax.numpy as jnp
from jax import lax
from jax.experimental import pallas as pl
from jax.experimental.pallas import tpu as pltpu
from jax.sharding import PartitionSpec as P

RPL = 16
DMAX = 128
ITERS = 2
EPSILON = 1e-05

SLAB = 128
HALF = 64
FEAT = 64
GROUP = 4
WIDE = GROUP * FEAT
QS = SLAB // (2 * GROUP)
QH = QS // 2
assert QH == 8
ONES = 3 * HALF + 6
VMEM_LIMIT = 24 * 1024 * 1024
VMEM_FULL = 63 * 1024 * 1024

BF = jnp.bfloat16
F32 = jnp.float32


def split_bias(bias):
    high = bias.astype(BF).astype(F32)
    middle = (bias - high).astype(BF).astype(F32)
    return high, middle, bias - high - middle


def iota(shape, axis):
    return lax.broadcasted_iota(jnp.int32, shape, axis)


def picks(mask):
    return mask.astype(F32).astype(BF)


def start_of(q):
    return 16 * (q // 2) + 2 * (q % 2)


def prepare_kernel(bundle, o_in, o_out, rhs, cols):
    rhs[...] = jnp.zeros_like(rhs)
    cols[...] = jnp.zeros_like(cols)
    base = 3 * FEAT
    bias = bundle[base + 16 : base + 24, :]
    parts = split_bias(bias[0:1, :])
    exits = bundle[base : base + 4, :]
    for p in range(GROUP):
        lanes = slice(p * FEAT, (p + 1) * FEAT)
        for c in range(3):
            row = base + 4 * (c + 1)
            rhs[p * 32 + c * 8 : p * 32 + c * 8 + 4, lanes] = bundle[row : row + 4, :]
            rhs[p * 32 + 24 + c : p * 32 + 25 + c, lanes] = parts[c]
        cols[p * 8 : p * 8 + 4, lanes] = exits
    taps = rhs[...].astype(BF)
    row, col = iota((WIDE, SLAB), 0), iota((WIDE, SLAB), 1)
    channel, j, target = (col >> 3) & 3, col & 7, 4 * (col >> 5) + (col & 7) - 1
    rest = row - 3 * HALF
    sample = jnp.where(rest < 0, row & (HALF - 1), jnp.where(rest & 1 == 1, HALF, -1))
    same = (jnp.where(rest < 0, row >> 6, rest >> 1) == channel) & (channel < 3) & (j < 4)
    offset = jnp.where(same, sample - target, -SLAB)
    ones = (channel == 3) & (j < 3) & (row == ONES + j)
    for q in range(QH):
        chosen = picks((offset == start_of(q)) | ones)
        o_in[q] = jnp.dot(chosen, taps, preferred_element_type=F32).astype(BF)
    o_in[QH:] = jnp.zeros((2, WIDE, WIDE), BF)
    for a, at in [(0, 0), (1, 1), (2, 2), (3, 3), (4, 4), (-1, 5)]:
        for b in range(GROUP):
            if abs(a - b) <= 1:
                tap = a - b + 1
                rows, lanes = slice(at % 4 * FEAT, (at % 4 + 1) * FEAT), slice(b * FEAT, (b + 1) * FEAT)
                o_in[QH + at // 4, rows, lanes] = bundle[tap * FEAT : (tap + 1) * FEAT, :].astype(BF)
    row = iota((16, FEAT), 0)
    below = jnp.zeros((16, FEAT), F32)
    for i, part in enumerate(split_bias(bias[1:2, :])):
        below = jnp.where(row == i, part, below)
    for b in range(GROUP):
        o_in[QH + 1, SLAB : SLAB + 16, b * FEAT : (b + 1) * FEAT] = below.astype(BF)
    row, col = iota((SLAB, SLAB), 0), iota((SLAB, SLAB), 1)
    p, j = row >> 3, row & 7
    offset = jnp.where((p < GROUP) & (j < 4), col - (4 * p + j - 1), -SLAB)
    back = jnp.transpose(cols[...]).astype(BF)
    follows = (p == GROUP - 1) & (j == 3) & (col == 0)
    precedes = (row == 0) & (col == SLAB - 1)
    for q in range(QS + 2):
        chosen = picks(offset == start_of(q) if q < QS else [follows, precedes][q - QS])
        o_out[q] = jnp.dot(back, chosen, preferred_element_type=F32).astype(BF)


def pack_kernel(plan, *refs):
    sources, outs, fetched, done = refs[:9], refs[9:15], refs[15:24], refs[24]
    held = fetched[0]
    _, _, at_tm, _, at_line = places(plan, True)
    block = held.shape[0]
    copies = [pltpu.make_async_copy(src, dst, done.at[i]) for i, (src, dst) in enumerate(zip(sources, fetched))]
    for copy in copies:
        copy.start()
    lines = plan.lines
    half = block // 2
    row, col = iota((block, block), 0), iota((block, block), 1)
    spot, line = split_index(row, lines)
    d, spot = split_index(spot, half // lines)
    order = picks(col == line * RPL + (at_tm ^ d) * (half // lines) + spot)
    row, col = iota((32, block), 0), iota((32, block), 1)
    d, spot = split_index(row, 16)
    sent = jnp.where(at_line == 0, lines - 1, 0)
    outer = picks((col == sent * RPL + (at_tm ^ d) * (half // lines) + spot) & (spot < half // lines))
    for copy in copies:
        copy.wait()
    moved = jnp.dot(order, held[...], preferred_element_type=F32).astype(BF)
    edge = jnp.dot(outer, held[...], preferred_element_type=F32).astype(BF)
    outs[0][...] = moved[:half]
    outs[1][...] = moved[half:]
    outs[2][...] = edge[:16]
    outs[3][...] = edge[16:]
    for n, bundle in enumerate(outs[4:6]):
        entry, spaced, leave, bias = fetched[1 + 4 * n : 5 + 4 * n]
        for j in range(3):
            bundle[j * FEAT : (j + 1) * FEAT, :] = spaced[j].astype(F32)
            row = 3 * FEAT + 4 * (j + 1)
            bundle[row : row + 4, :] = entry[j].astype(F32)
        bundle[3 * FEAT : 3 * FEAT + 4, :] = leave[...].astype(F32)
        bundle[3 * FEAT + 16 : 3 * FEAT + 24, :] = jnp.zeros((8, FEAT), F32)
        bundle[3 * FEAT + 16 : 3 * FEAT + 18, :] = bias[...]


def pick_kernel(plan, mixes, picked):
    base = places(plan, False)[0]
    row, col = iota((plan.span, mixes.shape[1]), 0), iota((plan.span, mixes.shape[1]), 1)
    spot, line = split_index(row, plan.lines)
    choose = picks(col == line * RPL + base + spot)
    for g in range(plan.mixtures):
        picked[g] = jnp.dot(choose, mixes[g], preferred_element_type=F32).astype(BF)


def places(plan, first):
    at_shot, at_line, at_tm = (lax.axis_index(a) for a in ("shot", "line", "tm"))
    if not plan.paired:
        return at_shot, at_tm * plan.lines, at_tm, at_shot, at_line
    return at_tm * (RPL // 2) + (0 if first else at_shot * plan.per), 0, at_tm, at_shot, at_line


def split_index(value, size):
    if size & (size - 1):
        return value // size, value % size
    return value >> (size.bit_length() - 1), value & (size - 1)


def section_map(plan, place, tallies, first):
    shape = (plan.rows, SLAB)
    lane = lax.broadcasted_iota(jnp.int32, shape, 1)
    apart, line = split_index(iota(shape, 0), plan.lines)
    if not first:
        apart = split_index(apart, plan.per)[1]
    spot = (line + place[1]) * RPL + place[0] + apart
    low = jnp.zeros(shape, jnp.int32)
    high = jnp.zeros(shape, jnp.int32)
    count = jnp.zeros(shape, jnp.int32)
    start = jnp.int32(0)
    for p in range(plan.sections):
        amount = tallies[p]
        here = lane == p
        low = jnp.where(here, start, low)
        high = jnp.where(here, start + amount, high)
        count = jnp.where(here, amount, count)
        start = start + amount
    member = (spot >= low) & (spot < high)
    return member, count


def shifted(values, by, ok, edge):
    return jnp.where(ok, pltpu.roll(values, by % values.shape[0], 0), edge)


def pack_inputs(plan, channels, packed):
    lane = lax.broadcasted_iota(jnp.int32, (plan.rows, SLAB), 1)
    low = lane < HALF
    ones = ((lane >= ONES - SLAB) & (lane < ONES - SLAB + 3)).astype(F32)
    slabs = [[x[:, t * SLAB : (t + 1) * SLAB] for t in range(plan.slabs)] for x in channels]
    far = [[pltpu.roll(s, HALF + 1 + 2 * c, 1) for s in slabs[c]] for c in range(3)]
    for t in range(plan.slabs):
        v = [slabs[c][t] for c in range(3)]
        w = [pltpu.roll(s, HALF, 1) for s in v]
        even = jnp.where(low, v[2], ones)
        odd = jnp.where(low, w[2], ones)
        for c in range(3):
            left, right = lane == HALF + 2 * c, lane == HALF + 2 * c + 1
            near = pltpu.roll(v[c], 1 + 2 * c, 1)
            even = jnp.where(right, near, even)
            odd = jnp.where(left, near, odd)
            if t > 0:
                even = jnp.where(left, far[c][t - 1], even)
            if t < plan.slabs - 1:
                odd = jnp.where(right, far[c][t + 1], odd)
        packed[0, t, :, 0:SLAB] = jnp.where(low, v[0], w[1]).astype(BF)
        packed[0, t, :, SLAB:WIDE] = even.astype(BF)
        packed[1, t, :, 0:SLAB] = jnp.where(low, w[0], v[1]).astype(BF)
        packed[1, t, :, SLAB:WIDE] = odd.astype(BF)


def network(plan, weights, scratch, regions):
    w_in, w_out = weights
    packed, hidden, total, ends = scratch
    slabs, rows = plan.slabs, plan.rows
    many = slabs * rows
    pitch = slabs + 2

    def first(q):
        taps = jnp.concatenate([w_in[q], w_in[q + 1]], axis=1)
        value = jnp.dot(packed[...].reshape(2 * many, WIDE), taps, preferred_element_type=F32)
        value = jnp.maximum(value.astype(BF), 0).reshape(2, slabs, rows, 2 * WIDE)
        for h in range(2):
            for k in range(2):
                at = pl.ds((q + k + h * QH) * pitch + 1, slabs)
                hidden[at] = value[h, :, :, k * WIDE : (k + 1) * WIDE]

    lane = iota((slabs, rows, SLAB), 2)
    ones = picks(lane < 3)

    def window(q):
        if isinstance(q, int):
            left_at = (q - 2) * pitch + 1 if q >= 2 else (q + QS - 2) * pitch
            right_at = (q + 2) * pitch + 1 if q < QS - 2 else (q + 2 - QS) * pitch + 2
        else:
            left_at = jnp.where(q >= 2, (q - 2) * pitch + 1, (q + QS - 2) * pitch)
            right_at = jnp.where(q < QS - 2, (q + 2) * pitch + 1, (q + 2 - QS) * pitch + 2)
        middle = hidden[pl.ds(q * pitch + 1, slabs)]
        left = hidden[pl.ds(left_at, slabs), :, SLAB:WIDE]
        right = hidden[pl.ds(right_at, slabs), :, 0:SLAB]
        beside = jnp.where(lane < FEAT, right, left)
        return jnp.concatenate([middle, beside, ones], axis=2).reshape(many, 2 * WIDE)

    def second(q):
        both = jnp.concatenate([window(q), window(q + 1)], axis=0)
        value = jnp.dot(both, w_in[QH:].reshape(2 * WIDE, WIDE), preferred_element_type=F32)
        value = jnp.maximum(value.astype(BF), 0)
        return value[:many], value[many:]

    def onto(layer, taps):
        return jnp.dot(layer, taps, preferred_element_type=F32).reshape(slabs, rows, SLAB)

    edge = jnp.zeros((rows, WIDE), BF)
    for k in range(2):
        hidden[(QS - 2 + k) * pitch] = edge
        hidden[(k + 1) * pitch - 1] = edge

    @regions[0]
    def _():
        for q in range(0, QH, 2):
            first(q)

    @regions[1]
    def _():
        for q in range(0, QS, 2):
            one, two = second(q)
            value = onto(jnp.concatenate([one, two], axis=1), w_out[q : q + 2].reshape(2 * WIDE, SLAB))
            total[...] = value if q == 0 else total[...] + value
            if q == 0:
                ends[0] = one
            if q == QS - 2:
                ends[1] = two

    total[0 : slabs - 1] += onto(ends[0], w_out[QS + 1])[1:]
    total[1:slabs] += onto(ends[1], w_out[QS])[: slabs - 1]


def add_total(plan, now, total, scale=None):
    for t in range(plan.slabs):
        lanes = slice(t * SLAB, (t + 1) * SLAB)
        more = total[t] if scale is None else scale * total[t]
        value = (now[:, lanes] + more).astype(BF).astype(F32)
        now[:, lanes] = value
        power = value * value if t == 0 else power + value * value
    return power


def shot_stage(plan, place, tallies, first, edges, weights, now, scratch):
    apart = pl.when(place[0] >= 0)

    @apart
    def _():
        x = now[...]
        line = split_index(iota(x.shape, 0), plan.lines)[1]
        if plan.paired:
            wide = [jnp.broadcast_to(edges[g : g + 1, :], (plan.lines, x.shape[1])) for g in range(plan.groups)]
            wide = jnp.concatenate(wide, axis=0)
            above = jnp.where(place[4] == 1, wide, 0.0)
            below = jnp.where(place[4] == 1, 0.0, wide)
        else:
            above, below = edges[0].astype(F32), edges[1].astype(F32)
        channels = [
            shifted(x, 1, line > 0, above),
            x,
            shifted(x, -1, line < plan.lines - 1, below),
        ]
        pack_inputs(plan, channels, scratch[0])

    network(plan, weights, scratch, (apart, apart))
    power = add_total(plan, now, scratch[2])
    member, _ = section_map(plan, place, tallies, first)
    each = jnp.where(member, jnp.sum(power, axis=1, keepdims=True), 0.0)
    return jnp.sum(each, axis=0, keepdims=True)


def station_stage(
    plan, place, tallies, lags, order, pace, energies, mixes, weights, now, scratch, blend
):
    fired, misfit, scale = blend
    apart = pl.when(place[0] >= 0)
    inline = lambda body: body()

    @inline
    def _():
        member, count = section_map(plan, place, tallies, False)
        denominator = jnp.maximum(count, 1) * (plan.shots * plan.slabs * SLAB)
        level = jnp.sqrt(energies[...] / denominator.astype(F32) + EPSILON)
        rms = jnp.sum(jnp.where(member, level, 0.0), axis=1, keepdims=True)
        scale[...] = jnp.broadcast_to(rms, scale.shape)
        x = (now[...] / rms).astype(BF).astype(F32)
        row = iota(x.shape, 0)
        channels = [
            shifted(x, plan.span, row >= plan.span, 0.0),
            x,
            shifted(x, -plan.span, row < plan.rows - plan.span, 0.0),
        ]
        pack_inputs(plan, channels, scratch[0])

    network(plan, weights, scratch, (inline, apart))
    add_total(plan, now, scratch[2], scale[...])
    lane = lax.broadcasted_iota(jnp.int32, (plan.span, SLAB), 1)
    mixtures = misfit.shape[0]
    per = plan.shots // mixtures
    misfit[...] = mixes[...].astype(F32)
    for s in range(plan.shots):
        lag = lags[s]
        before = jnp.zeros((plan.span, SLAB), F32)
        for t in range(plan.slabs):
            lanes = slice(t * SLAB, (t + 1) * SLAB)
            turned = pltpu.roll(now[s * plan.span : (s + 1) * plan.span, lanes], lag, 1)
            fired[s, :, lanes] = jnp.where(lane < lag, before, turned)
            before = turned
    for g in range(mixtures):
        value = fired[order[g * per]]
        for k in range(1, per):
            value = value + fired[order[g * per + k]]
        misfit[g] = value - misfit[g]
    for s in range(plan.shots):
        lag = lags[s]
        spot = jnp.int32(0)
        for k in range(plan.shots):
            spot = spot + jnp.where(order[k] == s, k, 0)
        which = spot // per
        back = (DMAX - lag) % DMAX
        after = jnp.zeros((plan.span, SLAB), F32)
        rows = slice(s * plan.span, (s + 1) * plan.span)
        for t in range(plan.slabs - 1, -1, -1):
            lanes = slice(t * SLAB, (t + 1) * SLAB)
            turned = pltpu.roll(misfit[which, :, lanes], back, 1)
            pulled = jnp.where(lane < DMAX - lag, turned, after)
            after = turned
            now[rows, lanes] = (now[rows, lanes] - pace * pulled).astype(BF).astype(F32)


def stage_kernel(plan, station_round, with_shot, first, split_in, split_out, *refs):
    refs = list(refs)
    take = lambda n: [refs.pop(0) for _ in range(n)]
    tallies, lags, order, paces = take(4)
    place = places(plan, first)
    sources = take(4 if split_in else 1)
    station = station_round is not None
    if station:
        energies, mixes = take(2)
        station_weights = take(2)
    if with_shot:
        edges = take(0 if first else 1)
        shot_weights = take(2)
    results = take({"parts": plan.each, "edge": 2}.get(split_out, 1))
    if with_shot and split_out != "parts":
        (energy,) = take(1)
    now, packed, hidden, total, ends, rim = take(6)
    scratch = (packed, hidden, total, ends)
    length = plan.slabs * SLAB
    if split_in == "parts":
        for d, part in enumerate(sources):
            at = pl.multiple_of((place[3] ^ d) * plan.span, plan.span)
            now[pl.ds(at, plan.span), :] = part[:, 0:length].astype(F32)
    elif split_in:
        share = length // plan.time_parts
        for d in range(2):
            lanes = pl.ds(pl.multiple_of((place[2] ^ d) * share, share), share)
            now[:, lanes] = sources[d][...].astype(F32)
            rim[:, lanes] = sources[2 + d][...].astype(F32)
    else:
        now[...] = sources[0][...].astype(F32)
    if station:
        station_stage(
            plan,
            place,
            tallies,
            lags,
            order,
            paces[station_round],
            energies,
            mixes,
            station_weights,
            now,
            scratch,
            refs,
        )
    if with_shot:
        if plan.paired and not first:
            rim[0 : plan.groups, :] = edges[0][...].astype(F32)
        outer = rim if plan.paired else edges[0]
        sums = shot_stage(plan, place, tallies, first, outer, shot_weights, now, scratch)
    if split_out == "parts":
        row = iota((plan.span, SLAB), 0)
        beside = jnp.zeros((plan.span, SLAB), F32)
        for i, part in enumerate(split_bias(sums)):
            beside = jnp.where(row == i, part, beside)
        for d, part in enumerate(results):
            at = pl.multiple_of((place[3] ^ d) * plan.span, plan.span)
            part[:, 0:length] = now[pl.ds(at, plan.span), :].astype(BF)
            part[:, length:] = beside.astype(BF)
        return
    if with_shot:
        energy[...] = sums
    if split_out == "final":
        share = length // plan.time_parts
        for n in range(results[0].shape[0]):
            b, k = divmod(n, plan.each)
            results[0][n] = now[k * plan.span : (k + 1) * plan.span, b * share : (b + 1) * share].astype(BF)
        return
    results[0][...] = now[...].astype(BF)
    if split_out == "edge":
        row, col = iota((16, plan.rows), 0), iota((16, plan.rows), 1)
        sent = jnp.where(place[4] == 0, plan.lines - 1, 0)
        choose = picks(col == row * plan.lines + sent)
        sent = jnp.dot(choose, now[...].astype(BF), preferred_element_type=F32)
        results[1][...] = sent[: plan.groups].astype(BF)


SMEM = pl.BlockSpec(memory_space=pltpu.SMEM)
VMEM = pl.BlockSpec(memory_space=pltpu.VMEM)
HBM = pl.BlockSpec(memory_space=pltpu.HBM)


def run_stage(plan, small, source, station=None, shot=None, first=False, split_in=None, split_out=None, name="stage"):
    operands = [*small, *source]
    specs = [SMEM] * len(small) + [VMEM] * len(source)
    station_round = None
    macs = 0
    pass_macs = plan.rows * plan.slabs * QS * WIDE * (WIDE * 3 + SLAB)
    if station is not None:
        station_round, energies, mixes, weights = station
        operands += [energies, mixes, *weights]
        specs += [VMEM] * 4
        macs += pass_macs
    if shot is not None:
        edges, weights = shot
        operands += [*edges, *weights]
        specs += [VMEM] * (len(edges) + 2)
        macs += pass_macs
    length = plan.slabs * SLAB
    if split_out == "parts":
        shapes = [jax.ShapeDtypeStruct((plan.span, length + SLAB), BF)] * plan.each
    elif split_out == "final":
        shapes = [jax.ShapeDtypeStruct((plan.each * plan.time_parts, plan.span, length // plan.time_parts), BF)]
    else:
        shapes = [jax.ShapeDtypeStruct((plan.rows, length), BF)]
        if split_out == "edge":
            shapes.append(jax.ShapeDtypeStruct((plan.groups, length), BF))
    if shot is not None and split_out != "parts":
        shapes.append(jax.ShapeDtypeStruct((1, SLAB), F32))
    scratch = [
        pltpu.VMEM((plan.rows, length), F32),
        pltpu.VMEM((2, plan.slabs, plan.rows, WIDE), BF),
        pltpu.VMEM((QS * (plan.slabs + 2), plan.rows, WIDE), BF),
        pltpu.VMEM((plan.slabs, plan.rows, SLAB), F32),
        pltpu.VMEM((2, plan.slabs * plan.rows, WIDE), BF),
        pltpu.VMEM((16, length), F32),
    ]
    if station is not None:
        scratch += [
            pltpu.VMEM((plan.shots, plan.span, length), F32),
            pltpu.VMEM((plan.mixtures, plan.span, length), F32),
            pltpu.VMEM((plan.rows, SLAB), F32),
        ]
    return pl.pallas_call(
        functools.partial(stage_kernel, plan, station_round, shot is not None, first, split_in, split_out),
        out_shape=shapes,
        in_specs=specs,
        out_specs=[VMEM] * len(shapes),
        scratch_shapes=scratch,
        compiler_params=pltpu.CompilerParams(vmem_limit_bytes=VMEM_LIMIT),
        cost_estimate=pl.CostEstimate(flops=2 * macs, bytes_accessed=1 << 20, transcendentals=0),
        name=name,
    )(*operands)


def bundled(entry, spaced, leave, bias):
    rows = [spaced.reshape(3 * FEAT, FEAT), leave, entry.transpose(1, 0, 2).reshape(12, FEAT), bias]
    return jnp.concatenate([r.astype(F32) for r in rows] + [jnp.zeros((6, FEAT), F32)], axis=0)


def run_prepare(bundle, name):
    return pl.pallas_call(
        prepare_kernel,
        out_shape=[
            jax.ShapeDtypeStruct((QH + 2, WIDE, WIDE), BF),
            jax.ShapeDtypeStruct((QS + 2, WIDE, SLAB), BF),
        ],
        in_specs=[VMEM],
        out_specs=[VMEM] * 2,
        scratch_shapes=[pltpu.VMEM((SLAB, WIDE), F32), pltpu.VMEM((SLAB, WIDE), F32)],
        compiler_params=pltpu.CompilerParams(vmem_limit_bytes=VMEM_LIMIT),
        cost_estimate=pl.CostEstimate(flops=2 * 8192 * WIDE * SLAB, bytes_accessed=4 << 20, transcendentals=0),
        name=name,
    )(bundle)


def run_pack(plan, traces, *nets):
    block, width = traces.shape
    operands = [traces]
    for entry, spaced, leave, bias in nets:
        operands += [entry.transpose(1, 0, 2), spaced, leave, bias]
    shapes = [jax.ShapeDtypeStruct((rows, width), BF) for rows in (block // 2, block // 2, 16, 16)]
    shapes += [jax.ShapeDtypeStruct((3 * FEAT + 24, FEAT), F32)] * len(nets)
    return pl.pallas_call(
        functools.partial(pack_kernel, plan),
        out_shape=shapes,
        in_specs=[HBM] * len(operands),
        out_specs=[VMEM] * len(shapes),
        scratch_shapes=[*(pltpu.VMEM(o.shape, o.dtype) for o in operands), pltpu.SemaphoreType.DMA((len(operands),))],
        compiler_params=pltpu.CompilerParams(vmem_limit_bytes=VMEM_FULL),
        cost_estimate=pl.CostEstimate(flops=2 * block * block * width, bytes_accessed=1 << 20, transcendentals=0),
        name="pack",
    )(*operands)


def run_pick(plan, mixes):
    return pl.pallas_call(
        functools.partial(pick_kernel, plan),
        out_shape=jax.ShapeDtypeStruct((plan.mixtures, plan.span, mixes.shape[2]), BF),
        in_specs=[VMEM],
        out_specs=VMEM,
        compiler_params=pltpu.CompilerParams(vmem_limit_bytes=VMEM_LIMIT),
        cost_estimate=pl.CostEstimate(flops=1 << 24, bytes_accessed=1 << 20, transcendentals=0),
        name="pick",
    )(mixes)


class Plan:
    def __init__(self, **sizes):
        self.__dict__.update(sizes)
        self.span = self.lines * self.per
        self.rows = self.shots * self.span
        self.groups = self.rows // self.lines


def exchanged(parts, axes):
    size = len(parts)
    return [parts[0]] + [lax.ppermute(parts[d], axes, [(i, i ^ d) for i in range(size)]) for d in range(1, size)]


def per_device(
    initial_guess,
    measured_mixtures,
    launch_lags,
    source_launch_order,
    station_portion_tallies,
    source_entry_kernel,
    source_spaced_kernel,
    source_exit_kernel,
    source_inner_offsets,
    station_entry_kernel,
    station_spaced_kernel,
    station_exit_kernel,
    station_inner_offsets,
    learned_pace_factors,
):
    shots_here, block, window = initial_guess.shape
    n_shot, n_line, n_tm = (lax.axis_size(a) for a in ("shot", "line", "tm"))
    at_shot, at_tm = lax.axis_index("shot"), lax.axis_index("tm")
    block_lines = block // RPL
    length = window * n_tm
    shots = shots_here * n_shot
    sections = station_portion_tallies.shape[0]
    mixtures = measured_mixtures.shape[0]
    paired = n_shot * n_line * n_tm == RPL and n_line == 2 and n_tm == 2 and block_lines == 8
    assert shots_here == 1 and (paired or n_shot == RPL)
    plan = Plan(
        paired=paired,
        shots=shots,
        lines=block_lines if paired else block_lines // n_tm,
        per=RPL // (n_shot * n_tm) if paired else 1,
        sections=sections,
        mixtures=mixtures,
        slabs=length // SLAB,
        each=n_shot,
        time_parts=n_tm,
    )
    lines = plan.lines

    shot_net = (source_entry_kernel, source_spaced_kernel, source_exit_kernel, source_inner_offsets)
    station_net = (station_entry_kernel, station_spaced_kernel, station_exit_kernel, station_inner_offsets)
    if paired:
        *source, shot_net, station_net = run_pack(plan, initial_guess.reshape(block, window), shot_net, station_net)
        source = exchanged(source, ("line", "tm"))
        mixes = measured_mixtures
    else:
        grid = initial_guess.reshape(n_tm, lines, RPL, window)
        leaving = grid.transpose(2, 0, 1, 3).reshape(RPL * n_tm, lines, window)
        arrived = lax.all_to_all(leaving, ("shot", "tm"), split_axis=0, concat_axis=0, tiled=True)
        source = arrived.reshape(n_shot, n_tm, lines, window).transpose(0, 2, 1, 3).reshape(plan.rows, length)
        grid = measured_mixtures.reshape(mixtures, n_tm, lines, RPL, length)
        mixes = lax.dynamic_slice(grid, (0, at_tm, 0, at_shot, 0), (mixtures, 1, lines, 1, length))
        mixes = mixes.reshape(mixtures, lines, length)
        shot_net, station_net = bundled(*shot_net), bundled(*station_net)

    shot_weights = run_prepare(shot_net, "prepare_shot")
    small = (station_portion_tallies, launch_lags, source_launch_order, learned_pace_factors)
    def edges_of(current):
        size = n_line * n_tm
        grid = current.reshape(shots, lines, length)
        up = [(i, i + 1) for i in range(size - 1)]
        down = [(j, i) for i, j in up]
        above = lax.ppermute(grid[:, -1], ("line", "tm"), up)
        below = lax.ppermute(grid[:, 0], ("line", "tm"), down)
        wide = jnp.broadcast_to(jnp.stack([above, below])[:, :, None, :], (2, shots, lines, length))
        return wide.reshape(2, plan.rows, length)

    def summed(value, axis):
        size = lax.axis_size(axis)
        if size <= 4:
            others = [lax.ppermute(value, axis, [(i, i ^ d) for i in range(size)]) for d in range(1, size)]
            return sum(others, value)
        step = 1
        while step < size:
            value = value + lax.ppermute(value, axis, [(i, i ^ step) for i in range(size)])
            step *= 2
        return value

    def shared(energy, along):
        for axis in along:
            energy = summed(energy, axis)
        return energy

    if paired:
        parts = run_stage(
            plan,
            small,
            source,
            shot=([], shot_weights),
            first=True,
            split_in="packets",
            split_out="parts",
            name="shot_pass",
        )
        station_net, mixes, own = lax.optimization_barrier((station_net, mixes, parts[0]))
        mixes, middle = lax.optimization_barrier((run_pick(plan, mixes), parts[2:-1]))
        station_weights = run_prepare(station_net, "prepare_station")
        station_weights, nearest = lax.optimization_barrier((station_weights, parts[1]))
        current = exchanged([own, nearest, *middle, parts[-1]], "shot")
        energy = sum(jnp.sum(p[0:3, length:].astype(F32), axis=0, keepdims=True) for p in current)
        energy = summed(energy, "tm")
    else:
        current, energy = run_stage(plan, small, [source], shot=([edges_of(source)], shot_weights), name="shot_pass")
        energy = shared(energy, ("tm", "shot"))
        station_weights = run_prepare(station_net, "prepare_station")
    for i in range(ITERS):
        station = (i, energy, mixes, station_weights)
        form = {"split_in": "parts"} if paired and i == 0 else {}
        came = current if form else [current]
        if i == ITERS - 1:
            form["split_out"] = "final" if paired else None
            (current,) = run_stage(plan, small, came, station=station, name="station_pass", **form)
        elif paired:
            current, edge = run_stage(
                plan, small, came, station=station, name="station_pass", split_out="edge", **form
            )
            edge = lax.ppermute(edge, "line", [(0, 1), (1, 0)])
            current, energy = run_stage(plan, small, [current], shot=([edge], shot_weights), name="shot_pass")
            fresh, energy = lax.optimization_barrier((station_net, energy))
            station_weights = run_prepare(fresh, "prepare_station")
            energy = shared(energy, ("tm", "shot"))
        else:
            (current,) = run_stage(plan, small, came, station=station, name="station_pass")
            edges = [edges_of(current)]
            current, energy = run_stage(plan, small, [current], shot=(edges, shot_weights), name="shot_pass")
            energy = shared(energy, ("tm", "shot"))
    if paired:
        back = lax.all_to_all(current, ("tm", "shot"), split_axis=0, concat_axis=0, tiled=True)
        back = back.reshape(RPL, lines, window).transpose(1, 0, 2)
    else:
        current = current.reshape(n_shot, lines, n_tm, window).transpose(0, 2, 1, 3).reshape(-1, lines, window)
        back = lax.all_to_all(current, ("shot", "tm"), split_axis=0, concat_axis=0, tiled=True)
        back = back.reshape(RPL, n_tm, lines, window).transpose(1, 2, 0, 3)
    return back.reshape(shots_here, block, window)


def solution(mesh):
    placed = (P(("group", "shot"), "line", "tm"), P("group", "line", None), P("group"), P("group"), P("group"))
    return jax.shard_map(
        per_device,
        mesh=mesh,
        in_specs=placed + (P(),) * 9,
        out_specs=P(("group", "shot"), "line", "tm"),
        check_vma=False,
    )
```

```python
import functools

import jax
import jax.numpy as jnp
from jax import lax
from jax.experimental import pallas as pl
from jax.experimental.pallas import tpu as pltpu
from jax.sharding import PartitionSpec as P

RPL = 16
DMAX = 128
ITERS = 2
EPSILON = 1e-05

SLAB = 128
HALF = 64
FEAT = 64
GROUP = 4
WIDE = GROUP * FEAT
QS = SLAB // (2 * GROUP)
QH = QS // 2
assert QH == 8
ONES = 3 * HALF + 6
VMEM_LIMIT = 24 * 1024 * 1024
VMEM_FULL = 63 * 1024 * 1024

BF = jnp.bfloat16
F32 = jnp.float32


def split_bias(bias):
    high = bias.astype(BF).astype(F32)
    middle = (bias - high).astype(BF).astype(F32)
    return high, middle, bias - high - middle


def iota(shape, axis):
    return lax.broadcasted_iota(jnp.int32, shape, axis)


def picks(mask):
    return mask.astype(F32).astype(BF)


def start_of(q):
    return 16 * (q // 2) + 2 * (q % 2)


def prepare_kernel(bundle, o_in, o_out, rhs, cols):
    rhs[...] = jnp.zeros_like(rhs)
    cols[...] = jnp.zeros_like(cols)
    base = 3 * FEAT
    bias = bundle[base + 16 : base + 24, :]
    parts = split_bias(bias[0:1, :])
    exits = bundle[base : base + 4, :]
    for p in range(GROUP):
        lanes = slice(p * FEAT, (p + 1) * FEAT)
        for c in range(3):
            row = base + 4 * (c + 1)
            rhs[p * 32 + c * 8 : p * 32 + c * 8 + 4, lanes] = bundle[row : row + 4, :]
            rhs[p * 32 + 24 + c : p * 32 + 25 + c, lanes] = parts[c]
        cols[p * 8 : p * 8 + 4, lanes] = exits
    taps = rhs[...].astype(BF)
    row, col = iota((WIDE, SLAB), 0), iota((WIDE, SLAB), 1)
    channel, j, target = (col >> 3) & 3, col & 7, 4 * (col >> 5) + (col & 7) - 1
    rest = row - 3 * HALF
    sample = jnp.where(rest < 0, row & (HALF - 1), jnp.where(rest & 1 == 1, HALF, -1))
    same = (jnp.where(rest < 0, row >> 6, rest >> 1) == channel) & (channel < 3) & (j < 4)
    offset = jnp.where(same, sample - target, -SLAB)
    ones = (channel == 3) & (j < 3) & (row == ONES + j)
    for q in range(QH):
        chosen = picks((offset == start_of(q)) | ones)
        o_in[q] = jnp.dot(chosen, taps, preferred_element_type=F32).astype(BF)
    o_in[QH:] = jnp.zeros((2, WIDE, WIDE), BF)
    for a, at in [(0, 0), (1, 1), (2, 2), (3, 3), (4, 4), (-1, 5)]:
        for b in range(GROUP):
            if abs(a - b) <= 1:
                tap = a - b + 1
                rows, lanes = slice(at % 4 * FEAT, (at % 4 + 1) * FEAT), slice(b * FEAT, (b + 1) * FEAT)
                o_in[QH + at // 4, rows, lanes] = bundle[tap * FEAT : (tap + 1) * FEAT, :].astype(BF)
    row = iota((16, FEAT), 0)
    below = jnp.zeros((16, FEAT), F32)
    for i, part in enumerate(split_bias(bias[1:2, :])):
        below = jnp.where(row == i, part, below)
    for b in range(GROUP):
        o_in[QH + 1, SLAB : SLAB + 16, b * FEAT : (b + 1) * FEAT] = below.astype(BF)
    row, col = iota((SLAB, SLAB), 0), iota((SLAB, SLAB), 1)
    p, j = row >> 3, row & 7
    offset = jnp.where((p < GROUP) & (j < 4), col - (4 * p + j - 1), -SLAB)
    back = jnp.transpose(cols[...]).astype(BF)
    follows = (p == GROUP - 1) & (j == 3) & (col == 0)
    precedes = (row == 0) & (col == SLAB - 1)
    for q in range(QS + 2):
        chosen = picks(offset == start_of(q) if q < QS else [follows, precedes][q - QS])
        o_out[q] = jnp.dot(back, chosen, preferred_element_type=F32).astype(BF)


def pack_kernel(plan, *refs):
    sources, outs, fetched, done = refs[:9], refs[9:15], refs[15:24], refs[24]
    held = fetched[0]
    _, _, at_tm, _, at_line = places(plan, True)
    block = held.shape[0]
    copies = [pltpu.make_async_copy(src, dst, done.at[i]) for i, (src, dst) in enumerate(zip(sources, fetched))]
    for copy in copies:
        copy.start()
    lines = plan.lines
    half = block // 2
    row, col = iota((block, block), 0), iota((block, block), 1)
    spot, line = split_index(row, lines)
    d, spot = split_index(spot, half // lines)
    order = picks(col == line * RPL + (at_tm ^ d) * (half // lines) + spot)
    row, col = iota((32, block), 0), iota((32, block), 1)
    d, spot = split_index(row, 16)
    sent = jnp.where(at_line == 0, lines - 1, 0)
    outer = picks((col == sent * RPL + (at_tm ^ d) * (half // lines) + spot) & (spot < half // lines))
    for copy in copies:
        copy.wait()
    moved = jnp.dot(order, held[...], preferred_element_type=F32).astype(BF)
    edge = jnp.dot(outer, held[...], preferred_element_type=F32).astype(BF)
    outs[0][...] = moved[:half]
    outs[1][...] = moved[half:]
    outs[2][...] = edge[:16]
    outs[3][...] = edge[16:]
    for n, bundle in enumerate(outs[4:6]):
        entry, spaced, leave, bias = fetched[1 + 4 * n : 5 + 4 * n]
        for j in range(3):
            bundle[j * FEAT : (j + 1) * FEAT, :] = spaced[j].astype(F32)
            row = 3 * FEAT + 4 * (j + 1)
            bundle[row : row + 4, :] = entry[j].astype(F32)
        bundle[3 * FEAT : 3 * FEAT + 4, :] = leave[...].astype(F32)
        bundle[3 * FEAT + 16 : 3 * FEAT + 24, :] = jnp.zeros((8, FEAT), F32)
        bundle[3 * FEAT + 16 : 3 * FEAT + 18, :] = bias[...]


def pick_kernel(plan, mixes, picked):
    base = places(plan, False)[0]
    row, col = iota((plan.span, mixes.shape[1]), 0), iota((plan.span, mixes.shape[1]), 1)
    spot, line = split_index(row, plan.lines)
    choose = picks(col == line * RPL + base + spot)
    for g in range(plan.mixtures):
        picked[g] = jnp.dot(choose, mixes[g], preferred_element_type=F32).astype(BF)


def places(plan, first):
    at_shot, at_line, at_tm = (lax.axis_index(a) for a in ("shot", "line", "tm"))
    if not plan.paired:
        return at_shot, at_tm * plan.lines, at_tm, at_shot, at_line
    return at_tm * (RPL // 2) + (0 if first else at_shot * plan.per), 0, at_tm, at_shot, at_line


def split_index(value, size):
    if size & (size - 1):
        return value // size, value % size
    return value >> (size.bit_length() - 1), value & (size - 1)


def section_map(plan, place, tallies, first):
    shape = (plan.rows, SLAB)
    lane = lax.broadcasted_iota(jnp.int32, shape, 1)
    apart, line = split_index(iota(shape, 0), plan.lines)
    if not first:
        apart = split_index(apart, plan.per)[1]
    spot = (line + place[1]) * RPL + place[0] + apart
    low = jnp.zeros(shape, jnp.int32)
    high = jnp.zeros(shape, jnp.int32)
    count = jnp.zeros(shape, jnp.int32)
    start = jnp.int32(0)
    for p in range(plan.sections):
        amount = tallies[p]
        here = lane == p
        low = jnp.where(here, start, low)
        high = jnp.where(here, start + amount, high)
        count = jnp.where(here, amount, count)
        start = start + amount
    member = (spot >= low) & (spot < high)
    return member, count


def shifted(values, by, ok, edge):
    return jnp.where(ok, pltpu.roll(values, by % values.shape[0], 0), edge)


def pack_inputs(plan, channels, packed):
    lane = lax.broadcasted_iota(jnp.int32, (plan.rows, SLAB), 1)
    low = lane < HALF
    ones = ((lane >= ONES - SLAB) & (lane < ONES - SLAB + 3)).astype(F32)
    slabs = [[x[:, t * SLAB : (t + 1) * SLAB] for t in range(plan.slabs)] for x in channels]
    far = [[pltpu.roll(s, HALF + 1 + 2 * c, 1) for s in slabs[c]] for c in range(3)]
    for t in range(plan.slabs):
        v = [slabs[c][t] for c in range(3)]
        w = [pltpu.roll(s, HALF, 1) for s in v]
        even = jnp.where(low, v[2], ones)
        odd = jnp.where(low, w[2], ones)
        for c in range(3):
            left, right = lane == HALF + 2 * c, lane == HALF + 2 * c + 1
            near = pltpu.roll(v[c], 1 + 2 * c, 1)
            even = jnp.where(right, near, even)
            odd = jnp.where(left, near, odd)
            if t > 0:
                even = jnp.where(left, far[c][t - 1], even)
            if t < plan.slabs - 1:
                odd = jnp.where(right, far[c][t + 1], odd)
        packed[0, t, :, 0:SLAB] = jnp.where(low, v[0], w[1]).astype(BF)
        packed[0, t, :, SLAB:WIDE] = even.astype(BF)
        packed[1, t, :, 0:SLAB] = jnp.where(low, w[0], v[1]).astype(BF)
        packed[1, t, :, SLAB:WIDE] = odd.astype(BF)


def network(plan, weights, scratch, regions):
    w_in, w_out = weights
    packed, hidden, total, ends = scratch
    slabs, rows = plan.slabs, plan.rows
    many = slabs * rows
    pitch = slabs + 2

    def first(q):
        taps = jnp.concatenate([w_in[q], w_in[q + 1]], axis=1)
        value = jnp.dot(packed[...].reshape(2 * many, WIDE), taps, preferred_element_type=F32)
        value = jnp.maximum(value.astype(BF), 0).reshape(2, slabs, rows, 2 * WIDE)
        for h in range(2):
            for k in range(2):
                at = pl.ds((q + k + h * QH) * pitch + 1, slabs)
                hidden[at] = value[h, :, :, k * WIDE : (k + 1) * WIDE]

    lane = iota((slabs, rows, SLAB), 2)
    ones = picks(lane < 3)

    def window(q):
        if isinstance(q, int):
            left_at = (q - 2) * pitch + 1 if q >= 2 else (q + QS - 2) * pitch
            right_at = (q + 2) * pitch + 1 if q < QS - 2 else (q + 2 - QS) * pitch + 2
        else:
            left_at = jnp.where(q >= 2, (q - 2) * pitch + 1, (q + QS - 2) * pitch)
            right_at = jnp.where(q < QS - 2, (q + 2) * pitch + 1, (q + 2 - QS) * pitch + 2)
        middle = hidden[pl.ds(q * pitch + 1, slabs)]
        left = hidden[pl.ds(left_at, slabs), :, SLAB:WIDE]
        right = hidden[pl.ds(right_at, slabs), :, 0:SLAB]
        beside = jnp.where(lane < FEAT, right, left)
        return jnp.concatenate([middle, beside, ones], axis=2).reshape(many, 2 * WIDE)

    def second(q):
        both = jnp.concatenate([window(q), window(q + 1)], axis=0)
        value = jnp.dot(both, w_in[QH:].reshape(2 * WIDE, WIDE), preferred_element_type=F32)
        value = jnp.maximum(value.astype(BF), 0)
        return value[:many], value[many:]

    def onto(layer, taps):
        return jnp.dot(layer, taps, preferred_element_type=F32).reshape(slabs, rows, SLAB)

    edge = jnp.zeros((rows, WIDE), BF)
    for k in range(2):
        hidden[(QS - 2 + k) * pitch] = edge
        hidden[(k + 1) * pitch - 1] = edge

    @regions[0]
    def _():
        for q in range(0, QH, 2):
            first(q)

    @regions[1]
    def _():
        for q in range(0, QS, 2):
            one, two = second(q)
            value = onto(jnp.concatenate([one, two], axis=1), w_out[q : q + 2].reshape(2 * WIDE, SLAB))
            total[...] = value if q == 0 else total[...] + value
            if q == 0:
                ends[0] = one
            if q == QS - 2:
                ends[1] = two

    total[0 : slabs - 1] += onto(ends[0], w_out[QS + 1])[1:]
    total[1:slabs] += onto(ends[1], w_out[QS])[: slabs - 1]


def add_total(plan, now, total, scale=None):
    for t in range(plan.slabs):
        lanes = slice(t * SLAB, (t + 1) * SLAB)
        more = total[t] if scale is None else scale * total[t]
        value = (now[:, lanes] + more).astype(BF).astype(F32)
        now[:, lanes] = value
        power = value * value if t == 0 else power + value * value
    return power


def shot_stage(plan, place, tallies, first, edges, weights, now, scratch):
    apart = pl.when(place[0] >= 0)

    @apart
    def _():
        x = now[...]
        line = split_index(iota(x.shape, 0), plan.lines)[1]
        if plan.paired:
            wide = [jnp.broadcast_to(edges[g : g + 1, :], (plan.lines, x.shape[1])) for g in range(plan.groups)]
            wide = jnp.concatenate(wide, axis=0)
            above = jnp.where(place[4] == 1, wide, 0.0)
            below = jnp.where(place[4] == 1, 0.0, wide)
        else:
            above, below = edges[0].astype(F32), edges[1].astype(F32)
        channels = [
            shifted(x, 1, line > 0, above),
            x,
            shifted(x, -1, line < plan.lines - 1, below),
        ]
        pack_inputs(plan, channels, scratch[0])

    network(plan, weights, scratch, (apart, apart))
    power = add_total(plan, now, scratch[2])
    member, _ = section_map(plan, place, tallies, first)
    each = jnp.where(member, jnp.sum(power, axis=1, keepdims=True), 0.0)
    return jnp.sum(each, axis=0, keepdims=True)


def station_stage(
    plan, place, tallies, lags, order, pace, energies, mixes, weights, now, scratch, blend
):
    fired, misfit, scale = blend
    inline = lambda body: body()

    @inline
    def _():
        member, count = section_map(plan, place, tallies, False)
        denominator = jnp.maximum(count, 1) * (plan.shots * plan.slabs * SLAB)
        level = jnp.sqrt(energies[...] / denominator.astype(F32) + EPSILON)
        rms = jnp.sum(jnp.where(member, level, 0.0), axis=1, keepdims=True)
        scale[...] = jnp.broadcast_to(rms, scale.shape)
        x = (now[...] / rms).astype(BF).astype(F32)
        row = iota(x.shape, 0)
        channels = [
            shifted(x, plan.span, row >= plan.span, 0.0),
            x,
            shifted(x, -plan.span, row < plan.rows - plan.span, 0.0),
        ]
        pack_inputs(plan, channels, scratch[0])

    network(plan, weights, scratch, (inline, inline))
    add_total(plan, now, scratch[2], scale[...])
    lane = lax.broadcasted_iota(jnp.int32, (plan.span, SLAB), 1)
    mixtures = misfit.shape[0]
    per = plan.shots // mixtures
    misfit[...] = mixes[...].astype(F32)
    for s in range(plan.shots):
        lag = lags[s]
        before = jnp.zeros((plan.span, SLAB), F32)
        for t in range(plan.slabs):
            lanes = slice(t * SLAB, (t + 1) * SLAB)
            turned = pltpu.roll(now[s * plan.span : (s + 1) * plan.span, lanes], lag, 1)
            fired[s, :, lanes] = jnp.where(lane < lag, before, turned)
            before = turned
    for g in range(mixtures):
        value = fired[order[g * per]]
        for k in range(1, per):
            value = value + fired[order[g * per + k]]
        misfit[g] = value - misfit[g]
    for s in range(plan.shots):
        lag = lags[s]
        spot = jnp.int32(0)
        for k in range(plan.shots):
            spot = spot + jnp.where(order[k] == s, k, 0)
        which = spot // per
        back = (DMAX - lag) % DMAX
        after = jnp.zeros((plan.span, SLAB), F32)
        rows = slice(s * plan.span, (s + 1) * plan.span)
        for t in range(plan.slabs - 1, -1, -1):
            lanes = slice(t * SLAB, (t + 1) * SLAB)
            turned = pltpu.roll(misfit[which, :, lanes], back, 1)
            pulled = jnp.where(lane < DMAX - lag, turned, after)
            after = turned
            now[rows, lanes] = (now[rows, lanes] - pace * pulled).astype(BF).astype(F32)


def stage_kernel(plan, station_round, with_shot, first, split_in, split_out, *refs):
    refs = list(refs)
    take = lambda n: [refs.pop(0) for _ in range(n)]
    tallies, lags, order, paces = take(4)
    place = places(plan, first)
    sources = take(4 if split_in else 1)
    station = station_round is not None
    if station:
        energies, mixes = take(2)
        station_weights = take(2)
    if with_shot:
        edges = take(0 if first else 1)
        shot_weights = take(2)
    results = take({"parts": plan.each, "edge": 2}.get(split_out, 1))
    if with_shot and split_out != "parts":
        (energy,) = take(1)
    now, packed, hidden, total, ends, rim = take(6)
    scratch = (packed, hidden, total, ends)
    length = plan.slabs * SLAB
    if split_in == "parts":
        for d, part in enumerate(sources):
            at = pl.multiple_of((place[3] ^ d) * plan.span, plan.span)
            now[pl.ds(at, plan.span), :] = part[:, 0:length].astype(F32)
    elif split_in:
        share = length // plan.time_parts
        for d in range(2):
            lanes = pl.ds(pl.multiple_of((place[2] ^ d) * share, share), share)
            now[:, lanes] = sources[d][...].astype(F32)
            rim[:, lanes] = sources[2 + d][...].astype(F32)
    else:
        now[...] = sources[0][...].astype(F32)
    if station:
        station_stage(
            plan,
            place,
            tallies,
            lags,
            order,
            paces[station_round],
            energies,
            mixes,
            station_weights,
            now,
            scratch,
            refs,
        )
    if with_shot:
        if plan.paired and not first:
            rim[0 : plan.groups, :] = edges[0][...].astype(F32)
        outer = rim if plan.paired else edges[0]
        sums = shot_stage(plan, place, tallies, first, outer, shot_weights, now, scratch)
    if split_out == "parts":
        row = iota((plan.span, SLAB), 0)
        beside = jnp.zeros((plan.span, SLAB), F32)
        for i, part in enumerate(split_bias(sums)):
            beside = jnp.where(row == i, part, beside)
        for d, part in enumerate(results):
            at = pl.multiple_of((place[3] ^ d) * plan.span, plan.span)
            part[:, 0:length] = now[pl.ds(at, plan.span), :].astype(BF)
            part[:, length:] = beside.astype(BF)
        return
    if with_shot:
        energy[...] = sums
    if split_out == "final":
        share = length // plan.time_parts
        for n in range(results[0].shape[0]):
            b, k = divmod(n, plan.each)
            results[0][n] = now[k * plan.span : (k + 1) * plan.span, b * share : (b + 1) * share].astype(BF)
        return
    results[0][...] = now[...].astype(BF)
    if split_out == "edge":
        row, col = iota((16, plan.rows), 0), iota((16, plan.rows), 1)
        sent = jnp.where(place[4] == 0, plan.lines - 1, 0)
        choose = picks(col == row * plan.lines + sent)
        sent = jnp.dot(choose, now[...].astype(BF), preferred_element_type=F32)
        results[1][...] = sent[: plan.groups].astype(BF)


SMEM = pl.BlockSpec(memory_space=pltpu.SMEM)
VMEM = pl.BlockSpec(memory_space=pltpu.VMEM)
HBM = pl.BlockSpec(memory_space=pltpu.HBM)


def run_stage(plan, small, source, station=None, shot=None, first=False, split_in=None, split_out=None, name="stage"):
    operands = [*small, *source]
    specs = [SMEM] * len(small) + [VMEM] * len(source)
    station_round = None
    macs = 0
    pass_macs = plan.rows * plan.slabs * QS * WIDE * (WIDE * 3 + SLAB)
    if station is not None:
        station_round, energies, mixes, weights = station
        operands += [energies, mixes, *weights]
        specs += [VMEM] * 4
        macs += pass_macs
    if shot is not None:
        edges, weights = shot
        operands += [*edges, *weights]
        specs += [VMEM] * (len(edges) + 2)
        macs += pass_macs
    length = plan.slabs * SLAB
    if split_out == "parts":
        shapes = [jax.ShapeDtypeStruct((plan.span, length + SLAB), BF)] * plan.each
    elif split_out == "final":
        shapes = [jax.ShapeDtypeStruct((plan.each * plan.time_parts, plan.span, length // plan.time_parts), BF)]
    else:
        shapes = [jax.ShapeDtypeStruct((plan.rows, length), BF)]
        if split_out == "edge":
            shapes.append(jax.ShapeDtypeStruct((plan.groups, length), BF))
    if shot is not None and split_out != "parts":
        shapes.append(jax.ShapeDtypeStruct((1, SLAB), F32))
    scratch = [
        pltpu.VMEM((plan.rows, length), F32),
        pltpu.VMEM((2, plan.slabs, plan.rows, WIDE), BF),
        pltpu.VMEM((QS * (plan.slabs + 2), plan.rows, WIDE), BF),
        pltpu.VMEM((plan.slabs, plan.rows, SLAB), F32),
        pltpu.VMEM((2, plan.slabs * plan.rows, WIDE), BF),
        pltpu.VMEM((16, length), F32),
    ]
    if station is not None:
        scratch += [
            pltpu.VMEM((plan.shots, plan.span, length), F32),
            pltpu.VMEM((plan.mixtures, plan.span, length), F32),
            pltpu.VMEM((plan.rows, SLAB), F32),
        ]
    return pl.pallas_call(
        functools.partial(stage_kernel, plan, station_round, shot is not None, first, split_in, split_out),
        out_shape=shapes,
        in_specs=specs,
        out_specs=[VMEM] * len(shapes),
        scratch_shapes=scratch,
        compiler_params=pltpu.CompilerParams(vmem_limit_bytes=VMEM_LIMIT),
        cost_estimate=pl.CostEstimate(flops=2 * macs, bytes_accessed=1 << 20, transcendentals=0),
        name=name,
    )(*operands)


def bundled(entry, spaced, leave, bias):
    rows = [spaced.reshape(3 * FEAT, FEAT), leave, entry.transpose(1, 0, 2).reshape(12, FEAT), bias]
    return jnp.concatenate([r.astype(F32) for r in rows] + [jnp.zeros((6, FEAT), F32)], axis=0)


def run_prepare(bundle, name):
    return pl.pallas_call(
        prepare_kernel,
        out_shape=[
            jax.ShapeDtypeStruct((QH + 2, WIDE, WIDE), BF),
            jax.ShapeDtypeStruct((QS + 2, WIDE, SLAB), BF),
        ],
        in_specs=[VMEM],
        out_specs=[VMEM] * 2,
        scratch_shapes=[pltpu.VMEM((SLAB, WIDE), F32), pltpu.VMEM((SLAB, WIDE), F32)],
        compiler_params=pltpu.CompilerParams(vmem_limit_bytes=VMEM_LIMIT),
        cost_estimate=pl.CostEstimate(flops=2 * 8192 * WIDE * SLAB, bytes_accessed=4 << 20, transcendentals=0),
        name=name,
    )(bundle)


def run_pack(plan, traces, *nets):
    block, width = traces.shape
    operands = [traces]
    for entry, spaced, leave, bias in nets:
        operands += [entry.transpose(1, 0, 2), spaced, leave, bias]
    shapes = [jax.ShapeDtypeStruct((rows, width), BF) for rows in (block // 2, block // 2, 16, 16)]
    shapes += [jax.ShapeDtypeStruct((3 * FEAT + 24, FEAT), F32)] * len(nets)
    return pl.pallas_call(
        functools.partial(pack_kernel, plan),
        out_shape=shapes,
        in_specs=[HBM] * len(operands),
        out_specs=[VMEM] * len(shapes),
        scratch_shapes=[*(pltpu.VMEM(o.shape, o.dtype) for o in operands), pltpu.SemaphoreType.DMA((len(operands),))],
        compiler_params=pltpu.CompilerParams(vmem_limit_bytes=VMEM_FULL),
        cost_estimate=pl.CostEstimate(flops=2 * block * block * width, bytes_accessed=1 << 20, transcendentals=0),
        name="pack",
    )(*operands)


def run_pick(plan, mixes):
    return pl.pallas_call(
        functools.partial(pick_kernel, plan),
        out_shape=jax.ShapeDtypeStruct((plan.mixtures, plan.span, mixes.shape[2]), BF),
        in_specs=[VMEM],
        out_specs=VMEM,
        compiler_params=pltpu.CompilerParams(vmem_limit_bytes=VMEM_LIMIT),
        cost_estimate=pl.CostEstimate(flops=1 << 24, bytes_accessed=1 << 20, transcendentals=0),
        name="pick",
    )(mixes)


class Plan:
    def __init__(self, **sizes):
        self.__dict__.update(sizes)
        self.span = self.lines * self.per
        self.rows = self.shots * self.span
        self.groups = self.rows // self.lines


def exchanged(parts, axes):
    size = len(parts)
    return [parts[0]] + [lax.ppermute(parts[d], axes, [(i, i ^ d) for i in range(size)]) for d in range(1, size)]


def per_device(
    initial_guess,
    measured_mixtures,
    launch_lags,
    source_launch_order,
    station_portion_tallies,
    source_entry_kernel,
    source_spaced_kernel,
    source_exit_kernel,
    source_inner_offsets,
    station_entry_kernel,
    station_spaced_kernel,
    station_exit_kernel,
    station_inner_offsets,
    learned_pace_factors,
):
    shots_here, block, window = initial_guess.shape
    n_shot, n_line, n_tm = (lax.axis_size(a) for a in ("shot", "line", "tm"))
    at_shot, at_tm = lax.axis_index("shot"), lax.axis_index("tm")
    block_lines = block // RPL
    length = window * n_tm
    shots = shots_here * n_shot
    sections = station_portion_tallies.shape[0]
    mixtures = measured_mixtures.shape[0]
    paired = n_shot * n_line * n_tm == RPL and n_line == 2 and n_tm == 2 and block_lines == 8
    assert shots_here == 1 and (paired or n_shot == RPL)
    plan = Plan(
        paired=paired,
        shots=shots,
        lines=block_lines if paired else block_lines // n_tm,
        per=RPL // (n_shot * n_tm) if paired else 1,
        sections=sections,
        mixtures=mixtures,
        slabs=length // SLAB,
        each=n_shot,
        time_parts=n_tm,
    )
    lines = plan.lines

    shot_net = (source_entry_kernel, source_spaced_kernel, source_exit_kernel, source_inner_offsets)
    station_net = (station_entry_kernel, station_spaced_kernel, station_exit_kernel, station_inner_offsets)
    if paired:
        *source, shot_net, station_net = run_pack(plan, initial_guess.reshape(block, window), shot_net, station_net)
        source = exchanged(source, ("line", "tm"))
        mixes = measured_mixtures
    else:
        grid = initial_guess.reshape(n_tm, lines, RPL, window)
        leaving = grid.transpose(2, 0, 1, 3).reshape(RPL * n_tm, lines, window)
        arrived = lax.all_to_all(leaving, ("shot", "tm"), split_axis=0, concat_axis=0, tiled=True)
        source = arrived.reshape(n_shot, n_tm, lines, window).transpose(0, 2, 1, 3).reshape(plan.rows, length)
        grid = measured_mixtures.reshape(mixtures, n_tm, lines, RPL, length)
        mixes = lax.dynamic_slice(grid, (0, at_tm, 0, at_shot, 0), (mixtures, 1, lines, 1, length))
        mixes = mixes.reshape(mixtures, lines, length)
        shot_net, station_net = bundled(*shot_net), bundled(*station_net)

    shot_weights = run_prepare(shot_net, "prepare_shot")
    small = (station_portion_tallies, launch_lags, source_launch_order, learned_pace_factors)
    def edges_of(current):
        size = n_line * n_tm
        grid = current.reshape(shots, lines, length)
        up = [(i, i + 1) for i in range(size - 1)]
        down = [(j, i) for i, j in up]
        above = lax.ppermute(grid[:, -1], ("line", "tm"), up)
        below = lax.ppermute(grid[:, 0], ("line", "tm"), down)
        wide = jnp.broadcast_to(jnp.stack([above, below])[:, :, None, :], (2, shots, lines, length))
        return wide.reshape(2, plan.rows, length)

    def summed(value, axis):
        size = lax.axis_size(axis)
        if size <= 4:
            others = [lax.ppermute(value, axis, [(i, i ^ d) for i in range(size)]) for d in range(1, size)]
            return sum(others, value)
        step = 1
        while step < size:
            value = value + lax.ppermute(value, axis, [(i, i ^ step) for i in range(size)])
            step *= 2
        return value

    def shared(energy, along):
        for axis in along:
            energy = summed(energy, axis)
        return energy

    if paired:
        parts = run_stage(
            plan,
            small,
            source,
            shot=([], shot_weights),
            first=True,
            split_in="packets",
            split_out="parts",
            name="shot_pass",
        )
        station_net, mixes, own = lax.optimization_barrier((station_net, mixes, parts[0]))
        mixes, middle = lax.optimization_barrier((run_pick(plan, mixes), parts[2:-1]))
        station_weights = run_prepare(station_net, "prepare_station")
        station_weights, nearest = lax.optimization_barrier((station_weights, parts[1]))
        current = exchanged([own, nearest, *middle, parts[-1]], "shot")
        energy = sum(jnp.sum(p[0:3, length:].astype(F32), axis=0, keepdims=True) for p in current)
        energy = summed(energy, "tm")
    else:
        current, energy = run_stage(plan, small, [source], shot=([edges_of(source)], shot_weights), name="shot_pass")
        energy = shared(energy, ("tm", "shot"))
        station_weights = run_prepare(station_net, "prepare_station")
    for i in range(ITERS):
        station = (i, energy, mixes, station_weights)
        form = {"split_in": "parts"} if paired and i == 0 else {}
        came = current if form else [current]
        if i == ITERS - 1:
            form["split_out"] = "final" if paired else None
            (current,) = run_stage(plan, small, came, station=station, name="station_pass", **form)
        elif paired:
            current, edge = run_stage(
                plan, small, came, station=station, name="station_pass", split_out="edge", **form
            )
            edge = lax.ppermute(edge, "line", [(0, 1), (1, 0)])
            current, energy = run_stage(plan, small, [current], shot=([edge], shot_weights), name="shot_pass")
            fresh, energy = lax.optimization_barrier((station_net, energy))
            station_weights = run_prepare(fresh, "prepare_station")
            energy = shared(energy, ("tm", "shot"))
        else:
            (current,) = run_stage(plan, small, came, station=station, name="station_pass")
            edges = [edges_of(current)]
            current, energy = run_stage(plan, small, [current], shot=(edges, shot_weights), name="shot_pass")
            energy = shared(energy, ("tm", "shot"))
    if paired:
        back = lax.all_to_all(current, ("tm", "shot"), split_axis=0, concat_axis=0, tiled=True)
        back = back.reshape(RPL, lines, window).transpose(1, 0, 2)
    else:
        current = current.reshape(n_shot, lines, n_tm, window).transpose(0, 2, 1, 3).reshape(-1, lines, window)
        back = lax.all_to_all(current, ("shot", "tm"), split_axis=0, concat_axis=0, tiled=True)
        back = back.reshape(RPL, n_tm, lines, window).transpose(1, 2, 0, 3)
    return back.reshape(shots_here, block, window)


def solution(mesh):
    placed = (P(("group", "shot"), "line", "tm"), P("group", "line", None), P("group"), P("group"), P("group"))
    return jax.shard_map(
        per_device,
        mesh=mesh,
        in_specs=placed + (P(),) * 9,
        out_specs=P(("group", "shot"), "line", "tm"),
        check_vma=False,
    )
```
